32 devices in a mesh: sx: 16 (over z, x, core), sy: 2 (over y).
Axes of the slice: x: 2, y: 2, z: 4, core: 2. Of those that a mesh axis runs over, the one named last changes fastest.
Arguments:
- object_field: float32 [2, 2048, 1024], P(None, 'sx', 'sy'), may hold values from -6 to 6
- probe_field: float32 [2, 256, 256], replicated, may hold values from -4.2 to 4.2
- amplitudes: float32 [16, 2, 2, 256, 256], P('sx', 'sy'), may hold values from 0 to 2
- centres: int32 [16, 2, 2, 2], P('sx', 'sy'), may hold values from 0 to 511, as said below
- counts: int32 [16, 2], P(None, 'sy'), may hold values from 1 to 2, as said below
Outputs:
- object_next: float32 [2, 2048, 1024], P(None, 'sx', 'sy')
The draws below stay inside these ranges and needn't reach their ends.
Inputs may be any that keep to these rules, and one draw needn't show every extreme that they name: centres[s, t, k, 0] is below 128 and centres[s, t, k, 1] below 512; slots from counts[s, t] on are unused. A device's live positions are its first counts[s, t] slots; 2 is reached in every draw.
All inputs are finite; a program needn't handle non-finite values.
Results may differ from the reference program's by a relative error of at most 0.0003.
Values sent between devices are 32-bit elements; how exact they have to be, the bound alone decides.
No kernel may reach another device: no remote copies, remote signals or barrier semaphores. Data moves between devices by JAX's collectives and lax.ppermute only.
A program may use at most 128 MiB of HBM per device.

```python
import math
import jax
import jax.numpy as jnp
from jax import lax

PS = 256
BR = 128
BC = 512
CAP = 2
ITERS = 2
NR = 2048
NC = 1024
N_SX = 16
N_SY = 2


def draw_counts(key, part):
    band_start = jax.random.randint(jax.random.fold_in(key, 11), (), 0, N_SX)
    band_width = max(N_SX // 4, 1)
    row_index = jnp.arange(N_SX, dtype=jnp.int32)
    dense_rows = (row_index - band_start) % N_SX < band_width
    light_counts = jax.random.randint(jax.random.fold_in(key, 12), (N_SX, N_SY), 1, 3)
    return jnp.where(dense_rows[:, None], CAP, light_counts).astype(jnp.int32)


def draw_centres(key, part):
    row_values = jax.random.randint(jax.random.fold_in(key, 21), (N_SX, N_SY, CAP), 0, BR)
    col_values = jax.random.randint(jax.random.fold_in(key, 22), (N_SX, N_SY, CAP), 0, BC)
    chosen_row = jax.random.randint(jax.random.fold_in(key, 23), (), 0, N_SX)
    chosen_col = jax.random.randint(jax.random.fold_in(key, 24), (), 0, N_SY)
    col_values = col_values.at[chosen_row, chosen_col, 0].set(BC - 1)
    return jnp.stack([row_values, col_values], axis=-1).astype(jnp.int32)


def shard_levels(key, extent, pieces, low, high):
    def one(position, parts):
        draws = jax.random.uniform(jax.random.fold_in(jax.random.fold_in(key, 6), position), (parts,), jnp.float32, low / len(pieces), high / len(pieces))
        return jnp.repeat(jnp.exp(draws), extent[position] // parts).reshape((-1,) + (1,) * (len(extent) - position - 1))

    gain = one(*pieces[0])
    for cut in pieces[1:]:
        gain = gain * one(*cut)
    return gain


def centred(own_key, extent, deviation, most, shards=(), kind=jnp.bfloat16):
    loudness = shard_levels(own_key, extent, shards, -0.22, 0.18) if shards else 1.0
    result = jax.random.normal(own_key, extent, jnp.float32) * deviation * loudness
    return jnp.minimum(jnp.maximum(result, -most), most).astype(kind)


def setup_inputs(seed: int = 0) -> dict:
    seeds = jax.random.split(jax.random.key(seed), 6)
    return {
        "object_field": centred(seeds[0], (2, NR, NC), 1.0, 6.0, ((1, 16), (2, 2)), jnp.float32),
        "probe_field": centred(seeds[1], (2, PS, PS), 0.7, 4.2, (), jnp.float32),
        "amplitudes": jnp.clip(2.0 * jax.random.uniform(seeds[2], (N_SX, N_SY, CAP, PS, PS), jnp.float32) ** shard_levels(seeds[2], (N_SX, N_SY, CAP, PS, PS), ((0, 16), (1, 2)), -0.2, 0.2), 0.0, 2.0),
        "centres": draw_centres(jax.random.fold_in(seeds[5], 71), 0),
        "counts": draw_counts(jax.random.fold_in(seeds[5], 71), 0),
    }


SMOOTH = 1.0
DAMPING = 1.0

def dft_tables(length):
    index_values = jnp.arange(length, dtype=jnp.int32)
    product_mod = index_values[:, None] * index_values[None, :] % length
    angles = product_mod.astype(jnp.float32) * (2.0 * math.pi / length)
    scaling = 1.0 / math.sqrt(length)
    return (jnp.cos(angles) * scaling, -jnp.sin(angles) * scaling)

def matmul_exact(left_side, right_side):
    return jnp.dot(left_side, right_side, precision=lax.Precision.HIGHEST)

def complex_left(table_real, table_imag, field_real, field_imag):
    out_real = matmul_exact(table_real, field_real) - matmul_exact(table_imag, field_imag)
    out_imag = matmul_exact(table_real, field_imag) + matmul_exact(table_imag, field_real)
    return (out_real, out_imag)

def complex_right(field_real, field_imag, table_real, table_imag):
    out_real = matmul_exact(field_real, table_real) - matmul_exact(field_imag, table_imag)
    out_imag = matmul_exact(field_real, table_imag) + matmul_exact(field_imag, table_real)
    return (out_real, out_imag)

def position_gradient(object_patch, probe_field, amplitude, table_real, table_imag):
    probe_real = probe_field[0]
    probe_imag = probe_field[1]
    exit_real = probe_real * object_patch[0] - probe_imag * object_patch[1]
    exit_imag = probe_real * object_patch[1] + probe_imag * object_patch[0]
    half_real, half_imag = complex_left(table_real, table_imag, exit_real, exit_imag)
    far_real, far_imag = complex_right(half_real, half_imag, table_real, table_imag)
    factor = 1.0 - amplitude / jnp.sqrt(far_real * far_real + far_imag * far_imag + SMOOTH)
    miss_real = far_real * factor
    miss_imag = far_imag * factor
    back_real, back_imag = complex_left(table_real, -table_imag, miss_real, miss_imag)
    near_real, near_imag = complex_right(back_real, back_imag, table_real, -table_imag)
    return jnp.stack([probe_real * near_real + probe_imag * near_imag, probe_real * near_imag - probe_imag * near_real])

def add_patch(canvas, patch_values, corner_row, corner_col):
    zero_index = jnp.zeros((), jnp.int32)
    starts = (zero_index, corner_row, corner_col)
    present = lax.dynamic_slice(canvas, starts, patch_values.shape)
    return lax.dynamic_update_slice(canvas, present + patch_values, starts)

def reference(object_field, probe_field, amplitudes, centres, counts):
    table_real, table_imag = dft_tables(PS)
    half_probe = PS // 2
    total_devices = N_SX * N_SY
    flat_centres = centres.reshape(total_devices, CAP, 2)
    flat_counts = counts.reshape(total_devices)
    flat_amps = amplitudes.reshape(total_devices, CAP, PS, PS)
    padding = ((0, 0), (half_probe, half_probe), (half_probe, half_probe))
    spot_power = (probe_field[0] * probe_field[0] + probe_field[1] * probe_field[1])[None]

    def corner_of(device, slot_index):
        corner_row = device // N_SY * BR + flat_centres[device, slot_index, 0]
        corner_col = device % N_SY * BC + flat_centres[device, slot_index, 1]
        return (corner_row.astype(jnp.int32), corner_col.astype(jnp.int32))

    def over_positions(device_step):

        def outer_step(device, state_carry):

            def inner_step(slot_index, inner_carry):
                return device_step(device, slot_index, inner_carry)
            return lax.fori_loop(0, flat_counts[device], inner_step, state_carry)
        return outer_step

    def add_power(device, slot_index, canvas):
        corner_row, corner_col = corner_of(device, slot_index)
        return add_patch(canvas, spot_power, corner_row, corner_col)
    blank_power = jnp.zeros((1, NR + PS, NC + PS), jnp.float32)
    power_canvas = lax.fori_loop(0, total_devices, over_positions(add_power), blank_power)
    illumination = power_canvas[:, half_probe:half_probe + NR, half_probe:half_probe + NC]
    current = object_field
    for sweep_index in range(ITERS):
        padded = jnp.pad(current, padding)

        def add_gradient(device, slot_index, canvas, padded=padded):
            corner_row, corner_col = corner_of(device, slot_index)
            zero_index = jnp.zeros((), jnp.int32)
            object_patch = lax.dynamic_slice(padded, (zero_index, corner_row, corner_col), (2, PS, PS))
            update = position_gradient(object_patch, probe_field, flat_amps[device, slot_index], table_real, table_imag)
            return add_patch(canvas, update, corner_row, corner_col)
        blank_grad = jnp.zeros((2, NR + PS, NC + PS), jnp.float32)
        grad_canvas = lax.fori_loop(0, total_devices, over_positions(add_gradient), blank_grad)
        gradient = grad_canvas[:, half_probe:half_probe + NR, half_probe:half_probe + NC]
        current = current - gradient / (illumination + DAMPING)
    return current
```

```python
import math

import jax
import jax.numpy as jnp
import ml_dtypes
import numpy as np
from jax import lax
from jax.experimental import pallas as pl
from jax.experimental.pallas import tpu as pltpu
from jax.sharding import PartitionSpec as P

ITERS = 2
SMOOTH = 1.0
DAMPING = 1.0
LANES = 128
INFO = 8
VMEM_BYTES = 32 * 1024 * 1024

VMEM = pl.BlockSpec(memory_space=pltpu.VMEM)
SMEM = pl.BlockSpec(memory_space=pltpu.SMEM)


def split_numpy(table):
    high = table.astype(np.float32).astype(ml_dtypes.bfloat16)
    low = (table - high.astype(np.float64)).astype(ml_dtypes.bfloat16)
    return high, low


def dft_tables(length):
    half = length // 2
    index = np.arange(half)
    tables = []
    for parity in range(2):
        angles = 2.0 * math.pi / length * (index[:, None] * (2 * index[None, :] + parity) % length)
        cosine = np.cos(angles) / math.sqrt(length)
        sine = np.sin(angles) / math.sqrt(length)
        forward = np.block([[cosine, -sine], [sine, cosine]])
        tables.append([split_numpy(forward), split_numpy(forward.T)])
    return np.array(tables, dtype=ml_dtypes.bfloat16)


def parity_order(length):
    half = length // 2
    order = np.zeros((length, length))
    for index in range(length):
        order[index, index % 2 * half + index // 2] = 1.0
    return np.stack([order, order.T]).astype(ml_dtypes.bfloat16)


def split(values):
    high = values.astype(jnp.bfloat16)
    low = (values - high.astype(jnp.float32)).astype(jnp.bfloat16)
    return high, low


def times_table(values, table):
    high, low = split(values)
    left = jnp.concatenate([high, low, high], axis=1)
    right = jnp.concatenate([table[0], table[0], table[1]], axis=0)
    return jnp.dot(left, right, preferred_element_type=jnp.float32)


def table_times(table, values):
    high, low = split(values)
    left = jnp.concatenate([table[0], table[0], table[1]], axis=1)
    right = jnp.concatenate([high, low, high], axis=0)
    return jnp.dot(left, right, preferred_element_type=jnp.float32)


class Plan:
    def __init__(self, sx_size, sy_size, block_cols):
        self.sx_size = sx_size
        self.sy_size = sy_size
        self.own = block_cols // LANES
        self.tiles = self.own + 2
        self.paired = sy_size == 2
        self.sides = 1 if self.paired else 2

    def rights(self, t):
        return [1 - t] if self.paired else [0, 1]

    def pair_starts(self, t):
        return [right * (self.tiles - 2) for right in self.rights(t)]

    def halo_tiles(self, t):
        return [right * (self.tiles - 1) for right in self.rights(t)]

    def edge_tiles(self, t):
        return [1 + right * (self.tiles - 3) for right in self.rights(t)]

    def mid_start(self, t):
        return 1 + t if self.paired else 2

    @property
    def mid_tiles(self):
        return self.tiles - 3 if self.paired else self.tiles - 4

    def across(self, values, axis_name="sy"):
        if self.paired:
            return [lax.ppermute(values[0], axis_name, [(0, 1), (1, 0)])]
        ends = self.sy_size - 1
        return [
            lax.ppermute(values[1], axis_name, [(i, i + 1) for i in range(ends)]),
            lax.ppermute(values[0], axis_name, [(i + 1, i) for i in range(ends)]),
        ]

    def from_above(self, values):
        return lax.ppermute(values, "sx", [(i, i + 1) for i in range(self.sx_size - 1)])

    def from_below(self, values):
        return lax.ppermute(values, "sx", [(i + 1, i) for i in range(self.sx_size - 1)])


def lanes(tile, count=1):
    if isinstance(tile, int):
        return pl.ds(tile * LANES, count * LANES)
    return pl.ds(pl.multiple_of(tile * LANES, LANES), count * LANES)


def assemble(canvas, pieces, starts, tiles):
    blank = jnp.zeros(canvas.shape[:-1] + (LANES,), jnp.float32)
    canvas[:, :, lanes(0)] = blank
    canvas[:, :, lanes(tiles - 1)] = blank
    for piece, start in zip(pieces, starts):
        canvas[:, :, lanes(start, piece.shape[2] // LANES)] = piece[...]


def rows_at(ref, start, count):
    offset = start % 8
    values = ref[pl.ds(pl.multiple_of(start - offset, 8), count + 8)]
    return pltpu.roll(values, (count + 8 - offset) % (count + 8), 0)[:count]


def prepare_kernel(centres, probe, amps, order, rolled, ordered, padded):
    size = probe.shape[1]
    half = size // 2
    padded[:, :half] = jnp.zeros((2, half, size), jnp.float32)
    padded[:, half + size :] = jnp.zeros((2, half + 8, size), jnp.float32)
    padded[:, half : half + size] = probe[...]
    for slot in range(amps.shape[0]):
        row = centres[2 * slot]
        col = centres[2 * slot + 1]
        for part in range(2):
            shape = padded.at[part]
            upper = rows_at(shape, half - row, half) + rows_at(shape, half + size - row, half)
            lower = rows_at(shape, size - row, half)
            rolled[slot, part] = pltpu.roll(jnp.concatenate([upper, lower], axis=0), col % size, 1)
        high, low = split(amps[slot])
        across = jnp.dot(
            jnp.concatenate([high, low], axis=1),
            jnp.concatenate([order[0], order[0]], axis=0),
            preferred_element_type=jnp.float32,
        )
        high, low = split(across)
        ordered[slot] = jnp.dot(
            jnp.concatenate([order[1], order[1]], axis=1),
            jnp.concatenate([high, low], axis=0),
            preferred_element_type=jnp.float32,
        )


def light_kernel(plan, slots, place, info, probe, inverse, *rest):
    pairs = rest[: plan.sides]
    padded, canvas = rest[plan.sides :]
    size = probe.shape[1]
    half = size // 2
    s = place[0]
    t = place[1]
    padded[:half] = jnp.zeros((half, size), jnp.float32)
    padded[half + size :] = jnp.zeros((half + 8, size), jnp.float32)
    padded[half : half + size] = probe[0] * probe[0] + probe[1] * probe[1]
    canvas[...] = jnp.zeros(canvas.shape, jnp.float32)
    reach = 2 if plan.paired else 3
    spare = jnp.zeros((half, LANES), jnp.float32)
    for down in (-1, 0, 1):

        def add(step, carry, down=down):
            turn = step // slots
            slot = step % slots
            over = turn * (1 - 2 * t) if plan.paired else turn - 1
            there_s = s + down
            there_t = t + over
            inside = (there_s >= 0) & (there_s < plan.sx_size) & (there_t >= 0) & (there_t < plan.sy_size)
            base = (jnp.clip(there_s, 0, plan.sx_size - 1) * plan.sy_size + jnp.clip(there_t, 0, plan.sy_size - 1)) * INFO

            @pl.when(inside & (slot < info[base + 2 * slots]))
            def _():
                row = info[base + 2 * slot]
                col = info[base + 2 * slot + 1]
                power = rows_at(padded, size - half * down - row, half)
                shifted = pltpu.roll(jnp.concatenate([power, spare], axis=1), col % LANES, 1)
                first = col // LANES + plan.own * (over + 1)
                canvas[:, lanes(first, 3)] += shifted

            return carry

        lax.fori_loop(0, reach * slots, add, 0)
    result = 1.0 / (canvas[:, lanes(plan.own, plan.tiles)] + DAMPING)
    inverse[...] = result
    for pair, start in zip(pairs, plan.pair_starts(t)):
        pair[...] = inverse[:, lanes(start, 2)]


def term_kernel(plan, slot, starts, place, centres, counts, *rest):
    pieces = len(starts(0))
    above, own, below = (rest[k * pieces : (k + 1) * pieces] for k in range(3))
    probe, amps, tables, outer, inner, window, canvas = rest[3 * pieces :]
    size = probe.shape[2]
    half = size // 2
    s = place[0]
    t = place[1]
    row = centres[2 * slot]
    col = centres[2 * slot + 1]
    alive = slot < counts[s, 0]

    @pl.when(jnp.logical_not(alive))
    def _():
        outer[...] = jnp.zeros(outer.shape, jnp.float32)
        inner[...] = jnp.zeros(inner.shape, jnp.float32)

    @pl.when(alive)
    def _():
        tile = col // LANES
        first = tile % 2
        rest_col = col % LANES
        from_tile = lax.broadcasted_iota(jnp.int32, (half, LANES), 1) >= rest_col
        from_upper = lax.broadcasted_iota(jnp.int32, (half, LANES), 0) >= row
        for kind, source in enumerate((above, own, below)):
            assemble(canvas.at[kind], source, starts(t), plan.tiles)

        def pick(kind, part, index):
            return canvas[kind, part, :, lanes(index)]

        for part in range(2):
            edge = [jnp.where(from_tile, pick(kind, part, tile), pick(kind, part, tile + 2)) for kind in range(3)]
            middle = [pick(kind, part, tile + 1) for kind in range(3)]
            window[part, :half, lanes(first)] = jnp.where(from_upper, edge[0], edge[2])
            window[part, half:, lanes(first)] = edge[1]
            window[part, :half, lanes(1 - first)] = jnp.where(from_upper, middle[0], middle[2])
            window[part, half:, lanes(1 - first)] = middle[1]

        probe_real = probe[0, 0]
        probe_imag = probe[0, 1]
        exit_real = probe_real * window[0] - probe_imag * window[1]
        exit_imag = probe_real * window[1] + probe_imag * window[0]

        halves = [
            jnp.concatenate([exit_real[:, :half] + sign * exit_real[:, half:], exit_imag[:, :half] + sign * exit_imag[:, half:]], axis=1)
            for sign in (1.0, -1.0)
        ]
        across = [times_table(halves[parity], tables[parity, 0]) for parity in range(2)]
        real = jnp.concatenate([across[0][:, :half], across[1][:, :half]], axis=1)
        imag = jnp.concatenate([across[0][:, half:], across[1][:, half:]], axis=1)
        halves = [
            jnp.concatenate([real[:half] + sign * real[half:], imag[:half] + sign * imag[half:]], axis=0)
            for sign in (1.0, -1.0)
        ]
        back = []
        for parity in range(2):
            far = table_times(tables[parity, 1], halves[parity])
            far_real = far[:half]
            far_imag = far[half:]
            amplitude = amps[0, parity * half : (parity + 1) * half]
            factor = 1.0 - amplitude * lax.rsqrt(far_real * far_real + far_imag * far_imag + SMOOTH)
            miss = jnp.concatenate([far_real * factor, far_imag * factor], axis=0)
            back.append(table_times(tables[parity, 0], miss))
        real = jnp.concatenate([back[0][:half] + back[1][:half], back[0][:half] - back[1][:half]], axis=0)
        imag = jnp.concatenate([back[0][half:] + back[1][half:], back[0][half:] - back[1][half:]], axis=0)
        near = []
        for parity in range(2):
            picked = slice(parity * half, (parity + 1) * half)
            near.append(times_table(jnp.concatenate([real[:, picked], imag[:, picked]], axis=1), tables[parity, 1]))
        near_real = jnp.concatenate([near[0][:, :half] + near[1][:, :half], near[0][:, :half] - near[1][:, :half]], axis=1)
        near_imag = jnp.concatenate([near[0][:, half:] + near[1][:, half:], near[0][:, half:] - near[1][:, half:]], axis=1)
        term_real = probe_real * near_real + probe_imag * near_imag
        term_imag = probe_real * near_imag - probe_imag * near_real
        outer[0] = term_real[:half]
        outer[1] = term_imag[:half]
        inner[0] = term_real[half:]
        inner[1] = term_imag[half:]


def gather_terms(plan, slots, place, info, own, above, below, canvas):
    half = canvas.shape[1]
    s = place[0]
    t = place[1]
    canvas[...] = jnp.zeros(canvas.shape, jnp.float32)
    lane = lax.broadcasted_iota(jnp.int32, (half, LANES), 1)
    line = lax.broadcasted_iota(jnp.int32, (half, LANES), 0)
    for down, patches in ((0, own), (-1, above), (1, below)):
        base = (jnp.clip(s + down, 0, plan.sx_size - 1) * plan.sy_size + t) * INFO
        for slot in range(slots):
            row = info[base + 2 * slot]
            col = info[base + 2 * slot + 1]
            tile = col // LANES
            first = tile % 2
            from_tile = lane >= col % LANES
            if down == 0:
                left_rows = right_rows = None
            elif down == 1:
                left_rows = line >= row
            else:
                left_rows = line < row
            for part in range(2):
                edge = patches[slot][part, :, lanes(first)]
                middle = patches[slot][part, :, lanes(1 - first)]
                if left_rows is not None:
                    edge = jnp.where(left_rows, edge, 0.0)
                    middle = jnp.where(left_rows, middle, 0.0)
                canvas[part, :, lanes(tile)] += jnp.where(from_tile, edge, 0.0)
                canvas[part, :, lanes(tile + 1)] += middle
                canvas[part, :, lanes(tile + 2)] += jnp.where(from_tile, 0.0, edge)


def step_kernel(plan, slots, starts, place, info, *rest):
    patches = [rest[k * slots : (k + 1) * slots] for k in range(3)]
    rest = rest[3 * slots :]
    pieces = len(starts(0))
    own = rest[:pieces]
    inverse, middle = rest[pieces : pieces + 2]
    bases = rest[pieces + 2 : pieces + 2 + plan.sides]
    sums = rest[pieces + 2 + plan.sides : pieces + 2 + 2 * plan.sides]
    current, canvas = rest[pieces + 2 + 2 * plan.sides :]
    t = place[1]
    gather_terms(plan, slots, place, info, *patches, canvas)
    assemble(current, own, starts(t), plan.tiles)
    where = lanes(plan.mid_start(t), plan.mid_tiles)
    middle[...] = current[:, :, where] - canvas[:, :, where] * inverse[:, where][None]
    for base, total, start in zip(bases, sums, plan.pair_starts(t)):
        where = lanes(start, 2)
        partial = canvas[:, :, where]
        total[...] = partial
        base[...] = current[:, :, where] - partial * inverse[:, where][None]


def last_kernel(plan, slots, starts, place, info, *rest):
    patches = [rest[k * slots : (k + 1) * slots] for k in range(3)]
    rest = rest[3 * slots :]
    pieces = len(starts(0))
    own = rest[:pieces]
    inverse, nearly = rest[pieces : pieces + 2]
    sums = rest[pieces + 2 : pieces + 2 + plan.sides]
    current, canvas = rest[pieces + 2 + plan.sides :]
    t = place[1]
    gather_terms(plan, slots, place, info, *patches, canvas)
    assemble(current, own, starts(t), plan.tiles)
    where = lanes(1, plan.own)
    nearly[...] = current[:, :, where] - canvas[:, :, where] * inverse[:, where][None]
    for total, tile in zip(sums, plan.halo_tiles(t)):
        total[...] = canvas[:, :, lanes(tile)]


def edge_kernel(place, nearly, received, inverse, result):
    result[...] = nearly[...] - received[...] * inverse[...][None]


def call(kernel, outs, scratch, ins, flops, size, **options):
    return pl.pallas_call(
        kernel,
        out_shape=outs,
        in_specs=[SMEM if value.dtype == jnp.int32 else VMEM for value in ins],
        out_specs=jax.tree.map(lambda _: VMEM, outs),
        scratch_shapes=scratch,
        compiler_params=pltpu.CompilerParams(vmem_limit_bytes=VMEM_BYTES),
        cost_estimate=pl.CostEstimate(flops=flops, bytes_accessed=size, transcendentals=0),
        **options,
    )(*ins)


def on_device(plan, object_field, probe_field, amplitudes, centres, counts):
    f32 = jnp.float32
    shape = jax.ShapeDtypeStruct
    size = probe_field.shape[1]
    half = size // 2
    slots = amplitudes.shape[2]
    block_rows = object_field.shape[1]
    block_cols = object_field.shape[2]
    assert block_rows == half and block_cols % LANES == 0 and half == LANES
    width = plan.tiles * LANES
    s = lax.axis_index("sx")
    t = lax.axis_index("sy")
    place = jnp.stack([s, t]).astype(jnp.int32)
    spots = centres.reshape(2 * slots)
    own_amps = amplitudes[0, 0]
    tables = jnp.asarray(dft_tables(size))
    order = jnp.asarray(parity_order(size))

    rows_above = plan.from_above(object_field)
    rows_below = plan.from_below(object_field)
    edges = [
        lax.dynamic_slice(object_field, (0, 0, (tile - 1) * LANES), (2, block_rows, LANES))
        for tile in plan.edge_tiles(t)
    ]
    halos = plan.across(edges)
    own_info = jnp.concatenate([spots, lax.dynamic_slice(counts, (s, 0), (1, 1)).reshape(1)])
    own_info = jnp.pad(own_info, (0, INFO - own_info.shape[0]))
    info = lax.all_gather(own_info, ("sx", "sy"), tiled=True)

    rolled, ordered = call(
        prepare_kernel,
        [shape((slots, 2, size, size), f32), shape((slots, size, size), f32)],
        [pltpu.VMEM((2, 2 * size + 8, size), f32)],
        [spots, probe_field, own_amps, order],
        10**9, 10**6,
    )
    inverse, *inverse_pairs = call(
        lambda *refs: light_kernel(plan, slots, *refs),
        [shape((half, width), f32)] + [shape((half, 2 * LANES), f32)] * plan.sides,
        [pltpu.VMEM((2 * size + 8, size), f32), pltpu.VMEM((half, width + 2 * plan.own * LANES), f32)],
        [place, info, probe_field],
        10**9, 10**6,
    )

    own = [object_field] + halos
    above = [rows_above] + [plan.from_above(halo) for halo in halos]
    below = [rows_below] + [plan.from_below(halo) for halo in halos]

    def starts(t):
        return [1] + plan.halo_tiles(t)

    def later_starts(t):
        return [plan.mid_start(t)] + plan.pair_starts(t)

    result = None
    for sweep in range(ITERS):
        inner, outer_above, outer_below = [], [], []
        for slot in range(slots):
            outer_part, inner_part = pl.pallas_call(
                lambda *refs, slot=slot, starts=starts: term_kernel(plan, slot, starts, *refs),
                out_shape=[shape((2, half, size), f32)] * 2,
                in_specs=[SMEM] * 3 + [VMEM] * (3 * len(own)) + [
                    pl.BlockSpec((1, 2, size, size), lambda i, slot=slot: (slot, 0, 0, 0)),
                    pl.BlockSpec((1, size, size), lambda i, slot=slot: (slot, 0, 0)),
                    VMEM,
                ],
                out_specs=[VMEM] * 2,
                grid=(1,),
                scratch_shapes=[pltpu.VMEM((2, size, size), f32), pltpu.VMEM((3, 2, half, width), f32)],
                compiler_params=pltpu.CompilerParams(vmem_limit_bytes=VMEM_BYTES),
                cost_estimate=pl.CostEstimate(flops=2 * 10**9, bytes_accessed=6 * 10**6, transcendentals=0),
            )(place, spots, counts, *above, *own, *below, rolled, ordered, tables)
            inner.append(inner_part)
            outer_above.append(plan.from_above(outer_part))
            outer_below.append(plan.from_below(outer_part))
        patches = inner + outer_above + outer_below
        if sweep < ITERS - 1:
            middle, *rest = call(
                lambda *refs, starts=starts: step_kernel(plan, slots, starts, *refs),
                [shape((2, half, plan.mid_tiles * LANES), f32)] + [shape((2, half, 2 * LANES), f32)] * (2 * plan.sides),
                [pltpu.VMEM((2, half, width), f32)] * 2,
                [place, info] + patches + own + [inverse],
                10**9, 10**6,
            )
            bases, sums = rest[: plan.sides], rest[plan.sides :]
            received = plan.across(sums)
            pairs = [base - other * inv[None] for base, other, inv in zip(bases, received, inverse_pairs)]
            own = [middle] + pairs
            above = [plan.from_above(piece) for piece in own]
            below = [plan.from_below(piece) for piece in own]
            starts = later_starts
        else:
            nearly, *sums = call(
                lambda *refs, starts=starts: last_kernel(plan, slots, starts, *refs),
                [shape((2, half, block_cols), f32)] + [shape((2, half, LANES), f32)] * plan.sides,
                [pltpu.VMEM((2, half, width), f32)] * 2,
                [place, info] + patches + own + [inverse],
                10**9, 10**6,
            )
            result = nearly
            for side, received in enumerate(plan.across(sums)):
                block = pl.BlockSpec((2, half, LANES), lambda i, place, side=side: (0, 0, plan.edge_tiles(place[1])[side] - 1))
                result = pl.pallas_call(
                    edge_kernel,
                    grid_spec=pltpu.PrefetchScalarGridSpec(
                        num_scalar_prefetch=1,
                        grid=(1,),
                        in_specs=[
                            block,
                            pl.BlockSpec((2, half, LANES), lambda i, place: (0, 0, 0)),
                            pl.BlockSpec((half, LANES), lambda i, place, side=side: (0, plan.edge_tiles(place[1])[side])),
                        ],
                        out_specs=block,
                    ),
                    out_shape=shape(result.shape, f32),
                    input_output_aliases={1: 0},
                )(place, result, received, inverse)
    return result


def solution(mesh):
    sizes = dict(mesh.shape)

    def per_device(object_field, *rest):
        plan = Plan(sizes["sx"], sizes["sy"], object_field.shape[2])
        return on_device(plan, object_field, *rest)

    return jax.shard_map(
        per_device,
        mesh=mesh,
        in_specs=(
            P(None, "sx", "sy"),
            P(),
            P("sx", "sy", None, None, None),
            P("sx", "sy", None, None),
            P(None, "sy"),
        ),
        out_specs=P(None, "sx", "sy"),
        check_vma=False,
    )
```

```python
import math

import jax
import jax.numpy as jnp
import ml_dtypes
import numpy as np
from jax import lax
from jax.experimental import pallas as pl
from jax.experimental.pallas import tpu as pltpu
from jax.sharding import PartitionSpec as P

ITERS = 2
SMOOTH = 1.0
DAMPING = 1.0
LANES = 128
INFO = 8
VMEM_BYTES = 12 * 1024 * 1024

VMEM = pl.BlockSpec(memory_space=pltpu.VMEM)
SMEM = pl.BlockSpec(memory_space=pltpu.SMEM)


def split_numpy(table):
    high = table.astype(np.float32).astype(ml_dtypes.bfloat16)
    low = (table - high.astype(np.float64)).astype(ml_dtypes.bfloat16)
    return high, low


def dft_tables(length):
    half = length // 2
    index = np.arange(half)
    tables = []
    for parity in range(2):
        angles = 2.0 * math.pi / length * (index[:, None] * (2 * index[None, :] + parity) % length)
        cosine = np.cos(angles) / math.sqrt(length)
        sine = np.sin(angles) / math.sqrt(length)
        forward = np.block([[cosine, -sine], [sine, cosine]])
        tables.append([split_numpy(forward), split_numpy(forward.T)])
    return np.array(tables, dtype=ml_dtypes.bfloat16)


def parity_order(length):
    half = length // 2
    order = np.zeros((length, length))
    for index in range(length):
        order[index, index % 2 * half + index // 2] = 1.0
    return np.stack([order, order.T]).astype(ml_dtypes.bfloat16)


def split(values):
    high = values.astype(jnp.bfloat16)
    low = (values - high.astype(jnp.float32)).astype(jnp.bfloat16)
    return high, low


def times_table(values, table):
    high, low = split(values)
    left = jnp.concatenate([high, low, high], axis=1)
    right = jnp.concatenate([table[0], table[0], table[1]], axis=0)
    return jnp.dot(left, right, preferred_element_type=jnp.float32)


def table_times(table, values):
    high, low = split(values)
    left = jnp.concatenate([table[0], table[0], table[1]], axis=1)
    right = jnp.concatenate([high, low, high], axis=0)
    return jnp.dot(left, right, preferred_element_type=jnp.float32)


class Plan:
    def __init__(self, sx_size, sy_size, block_cols):
        self.sx_size = sx_size
        self.sy_size = sy_size
        self.own = block_cols // LANES
        self.tiles = self.own + 2
        self.paired = sy_size == 2
        self.sides = 1 if self.paired else 2

    def rights(self, t):
        return [1 - t] if self.paired else [0, 1]

    def pair_starts(self, t):
        return [right * (self.tiles - 2) for right in self.rights(t)]

    def halo_tiles(self, t):
        return [right * (self.tiles - 1) for right in self.rights(t)]

    def edge_tiles(self, t):
        return [1 + right * (self.tiles - 3) for right in self.rights(t)]

    def mid_start(self, t):
        return 1 + t if self.paired else 2

    @property
    def mid_tiles(self):
        return self.tiles - 3 if self.paired else self.tiles - 4

    def across(self, values, axis_name="sy"):
        if self.paired:
            return [lax.ppermute(values[0], axis_name, [(0, 1), (1, 0)])]
        ends = self.sy_size - 1
        return [
            lax.ppermute(values[1], axis_name, [(i, i + 1) for i in range(ends)]),
            lax.ppermute(values[0], axis_name, [(i + 1, i) for i in range(ends)]),
        ]

    def far_rows(self, values):
        return lax.ppermute(values, "sx", self.swaps(1))

    def near_rows(self, values):
        return lax.ppermute(values, "sx", self.swaps(0))

    def swaps(self, first):
        pairs = [(i, i + 1) for i in range(first, self.sx_size - 1, 2)]
        return pairs + [(j, i) for i, j in pairs]


def far_side(s):
    return 2 * (s % 2) - 1


def lanes(tile, count=1):
    if isinstance(tile, int):
        return pl.ds(tile * LANES, count * LANES)
    return pl.ds(pl.multiple_of(tile * LANES, LANES), count * LANES)


def assemble(canvas, pieces, starts, tiles):
    blank = jnp.zeros(canvas.shape[:-1] + (LANES,), jnp.float32)
    canvas[:, :, lanes(0)] = blank
    canvas[:, :, lanes(tiles - 1)] = blank
    for piece, start in zip(pieces, starts):
        canvas[:, :, lanes(start, piece.shape[2] // LANES)] = piece[:, : canvas.shape[1]]


def rows_at(ref, start, count):
    offset = start % 8
    values = ref[pl.ds(pl.multiple_of(start - offset, 8), count + 8)]
    return pltpu.roll(values, (count + 8 - offset) % (count + 8), 0)[:count]


def prepare_kernel(centres, probe, amps, order, rolled, ordered, padded):
    size = probe.shape[1]
    half = size // 2
    padded[:, :half] = jnp.zeros((2, half, size), jnp.float32)
    padded[:, half + size :] = jnp.zeros((2, half + 8, size), jnp.float32)
    padded[:, half : half + size] = probe[...]
    for slot in range(amps.shape[0]):
        row = centres[2 * slot]
        col = centres[2 * slot + 1]
        for part in range(2):
            shape = padded.at[part]
            upper = rows_at(shape, half - row, half) + rows_at(shape, half + size - row, half)
            lower = rows_at(shape, size - row, half)
            rolled[slot, part] = pltpu.roll(jnp.concatenate([upper, lower], axis=0), col % size, 1)
        high, low = split(amps[slot])
        across = jnp.dot(
            jnp.concatenate([high, low], axis=1),
            jnp.concatenate([order[0], order[0]], axis=0),
            preferred_element_type=jnp.float32,
        )
        high, low = split(across)
        ordered[slot] = jnp.dot(
            jnp.concatenate([order[1], order[1]], axis=1),
            jnp.concatenate([high, low], axis=0),
            preferred_element_type=jnp.float32,
        )


def light_kernel(plan, slots, place, info, probe, inverse, *rest):
    pairs = rest[: plan.sides]
    padded, canvas = rest[plan.sides :]
    size = probe.shape[1]
    half = size // 2
    t = place[1]
    padded[:half] = jnp.zeros((half, size), jnp.float32)
    padded[half + size :] = jnp.zeros((half + 8, size), jnp.float32)
    padded[half : half + size] = probe[0] * probe[0] + probe[1] * probe[1]
    canvas[...] = jnp.zeros(canvas.shape, jnp.float32)
    reach = plan.sides + 1
    spare = jnp.zeros((half, LANES), jnp.float32)
    for down in (-1, 0, 1):

        def add(step, carry, down=down):
            turn = step // slots
            slot = step % slots
            over = turn * (1 - 2 * t) if plan.paired else jnp.where(turn == 0, 0, 2 * turn - 3)
            base = ((down + 1) * reach + turn) * INFO

            @pl.when(slot < info[base + 2 * slots])
            def _():
                row = info[base + 2 * slot]
                col = info[base + 2 * slot + 1]
                power = rows_at(padded, size - half * down - row, half)
                shifted = pltpu.roll(jnp.concatenate([power, spare], axis=1), col % LANES, 1)
                first = col // LANES + plan.own * (over + 1)
                canvas[:, lanes(first, 3)] += shifted

            return carry

        lax.fori_loop(0, reach * slots, add, 0)
    result = 1.0 / (canvas[:, lanes(plan.own, plan.tiles)] + DAMPING)
    inverse[...] = result
    for pair, start in zip(pairs, plan.pair_starts(t)):
        pair[...] = inverse[:, lanes(start, 2)]


def term_kernel(plan, slot, starts, place, centres, counts, *rest):
    pieces = len(starts(0))
    own, far, near = (rest[k * pieces : (k + 1) * pieces] for k in range(3))
    probe, amps, tables, outer, inner, window, canvas = rest[3 * pieces :]
    size = probe.shape[2]
    half = size // 2
    s = place[0]
    t = place[1]
    row = centres[2 * slot]
    col = centres[2 * slot + 1]
    alive = slot < counts[s, 0]

    @pl.when(jnp.logical_not(alive))
    def _():
        outer[...] = jnp.zeros(outer.shape, jnp.float32)
        inner[...] = jnp.zeros(inner.shape, jnp.float32)

    @pl.when(alive)
    def _():
        tile = col // LANES
        first = tile % 2
        rest_col = col % LANES
        from_tile = lax.broadcasted_iota(jnp.int32, (half, LANES), 1) >= rest_col
        from_upper = lax.broadcasted_iota(jnp.int32, (half, LANES), 0) >= row
        side = far_side(s)
        for kind, source in ((1, own), (1 + side, far), (1 - side, near)):
            assemble(canvas.at[kind], source, starts(t), plan.tiles)

        def pick(kind, part, index):
            return canvas[kind, part, :, lanes(index)]

        for part in range(2):
            edge = [jnp.where(from_tile, pick(kind, part, tile), pick(kind, part, tile + 2)) for kind in range(3)]
            middle = [pick(kind, part, tile + 1) for kind in range(3)]
            window[part, :half, lanes(first)] = jnp.where(from_upper, edge[0], edge[2])
            window[part, half:, lanes(first)] = edge[1]
            window[part, :half, lanes(1 - first)] = jnp.where(from_upper, middle[0], middle[2])
            window[part, half:, lanes(1 - first)] = middle[1]

        probe_real = probe[0, 0]
        probe_imag = probe[0, 1]
        exit_real = probe_real * window[0] - probe_imag * window[1]
        exit_imag = probe_real * window[1] + probe_imag * window[0]

        halves = [
            jnp.concatenate([exit_real[:, :half] + sign * exit_real[:, half:], exit_imag[:, :half] + sign * exit_imag[:, half:]], axis=1)
            for sign in (1.0, -1.0)
        ]
        across = [times_table(halves[parity], tables[parity, 0]) for parity in range(2)]
        real = jnp.concatenate([across[0][:, :half], across[1][:, :half]], axis=1)
        imag = jnp.concatenate([across[0][:, half:], across[1][:, half:]], axis=1)
        halves = [
            jnp.concatenate([real[:half] + sign * real[half:], imag[:half] + sign * imag[half:]], axis=0)
            for sign in (1.0, -1.0)
        ]
        back = []
        for parity in range(2):
            pattern = table_times(tables[parity, 1], halves[parity])
            far_real = pattern[:half]
            far_imag = pattern[half:]
            amplitude = amps[0, parity * half : (parity + 1) * half]
            factor = 1.0 - amplitude * lax.rsqrt(far_real * far_real + far_imag * far_imag + SMOOTH)
            miss = jnp.concatenate([far_real * factor, far_imag * factor], axis=0)
            back.append(table_times(tables[parity, 0], miss))
        real = jnp.concatenate([back[0][:half] + back[1][:half], back[0][:half] - back[1][:half]], axis=0)
        imag = jnp.concatenate([back[0][half:] + back[1][half:], back[0][half:] - back[1][half:]], axis=0)
        both = []
        for parity in range(2):
            picked = slice(parity * half, (parity + 1) * half)
            both.append(times_table(jnp.concatenate([real[:, picked], imag[:, picked]], axis=1), tables[parity, 1]))
        near_real = jnp.concatenate([both[0][:, :half] + both[1][:, :half], both[0][:, :half] - both[1][:, :half]], axis=1)
        near_imag = jnp.concatenate([both[0][:, half:] + both[1][:, half:], both[0][:, half:] - both[1][:, half:]], axis=1)
        term_real = probe_real * near_real + probe_imag * near_imag
        term_imag = probe_real * near_imag - probe_imag * near_real
        outer[0] = term_real[:half]
        outer[1] = term_imag[:half]
        inner[0] = term_real[half:]
        inner[1] = term_imag[half:]


def gather_terms(plan, slots, place, info, own, far, near, canvas):
    half = canvas.shape[1]
    side = far_side(place[0])
    canvas[...] = jnp.zeros(canvas.shape, jnp.float32)
    lane = lax.broadcasted_iota(jnp.int32, (half, LANES), 1)
    line = lax.broadcasted_iota(jnp.int32, (half, LANES), 0)
    for down, patches in ((None, own), (side, far), (-side, near)):
        base = (0 if down is None else down) * (plan.sides + 1) * INFO + (plan.sides + 1) * INFO
        for slot in range(slots):
            row = info[base + 2 * slot]
            col = info[base + 2 * slot + 1]
            tile = col // LANES
            first = tile % 2
            from_tile = lane >= col % LANES
            if down is not None:
                there = (line >= jnp.where(down > 0, row, 0)) & (line < jnp.where(down > 0, half, row))
            for part in range(2):
                edge = patches[slot][part, :, lanes(first)]
                middle = patches[slot][part, :, lanes(1 - first)]
                if down is not None:
                    edge = jnp.where(there, edge, 0.0)
                    middle = jnp.where(there, middle, 0.0)
                canvas[part, :, lanes(tile)] += jnp.where(from_tile, edge, 0.0)
                canvas[part, :, lanes(tile + 1)] += middle
                canvas[part, :, lanes(tile + 2)] += jnp.where(from_tile, 0.0, edge)


def step_kernel(plan, slots, starts, place, info, *rest):
    patches = [rest[k * slots : (k + 1) * slots] for k in range(3)]
    rest = rest[3 * slots :]
    pieces = len(starts(0))
    own = rest[:pieces]
    inverse, middle = rest[pieces : pieces + 2]
    bases = rest[pieces + 2 : pieces + 2 + plan.sides]
    sums = rest[pieces + 2 + plan.sides : pieces + 2 + 2 * plan.sides]
    current, canvas = rest[pieces + 2 + 2 * plan.sides :]
    t = place[1]
    gather_terms(plan, slots, place, info, *patches, canvas)
    assemble(current, own, starts(t), plan.tiles)
    where = lanes(plan.mid_start(t), plan.mid_tiles)
    middle[...] = current[:, :, where] - canvas[:, :, where] * inverse[:, where][None]
    for base, total, start in zip(bases, sums, plan.pair_starts(t)):
        where = lanes(start, 2)
        partial = canvas[:, :, where]
        total[...] = partial
        base[...] = current[:, :, where] - partial * inverse[:, where][None]


def last_kernel(plan, slots, starts, place, info, *rest):
    patches = [rest[k * slots : (k + 1) * slots] for k in range(3)]
    rest = rest[3 * slots :]
    pieces = len(starts(0))
    own = rest[:pieces]
    inverse, nearly = rest[pieces : pieces + 2]
    sums = rest[pieces + 2 : pieces + 2 + plan.sides]
    current, canvas = rest[pieces + 2 + plan.sides :]
    t = place[1]
    gather_terms(plan, slots, place, info, *patches, canvas)
    assemble(current, own, starts(t), plan.tiles)
    where = lanes(1, plan.own)
    nearly[...] = current[:, :, where] - canvas[:, :, where] * inverse[:, where][None]
    for total, tile in zip(sums, plan.halo_tiles(t)):
        total[...] = canvas[:, :, lanes(tile)]


def edge_kernel(place, nearly, received, inverse, result):
    result[...] = nearly[...] - received[...] * inverse[...][None]


def call(kernel, outs, scratch, ins, flops, size, **options):
    return pl.pallas_call(
        kernel,
        out_shape=outs,
        in_specs=[SMEM if value.dtype == jnp.int32 else VMEM for value in ins],
        out_specs=jax.tree.map(lambda _: VMEM, outs),
        scratch_shapes=scratch,
        compiler_params=pltpu.CompilerParams(vmem_limit_bytes=VMEM_BYTES),
        cost_estimate=pl.CostEstimate(flops=flops, bytes_accessed=size, transcendentals=0),
        **options,
    )(*ins)


def on_device(plan, object_field, probe_field, amplitudes, centres, counts):
    f32 = jnp.float32
    shape = jax.ShapeDtypeStruct
    size = probe_field.shape[1]
    half = size // 2
    slots = amplitudes.shape[2]
    block_rows = object_field.shape[1]
    block_cols = object_field.shape[2]
    assert block_rows == half and block_cols % LANES == 0 and half == LANES
    width = plan.tiles * LANES
    s = lax.axis_index("sx")
    t = lax.axis_index("sy")
    place = jnp.stack([s, t]).astype(jnp.int32)
    spots = centres.reshape(2 * slots)
    own_amps = amplitudes[0, 0]
    tables = jnp.asarray(dft_tables(size))
    order = jnp.asarray(parity_order(size))

    own_info = jnp.concatenate([spots, lax.dynamic_slice(counts, (s, 0), (1, 1)).reshape(1)])
    own_rows = jnp.pad(own_info.astype(f32).reshape(1, 1, -1), ((0, 1), (0, 7), (0, LANES - own_info.shape[0])))

    far_block = plan.far_rows(object_field)
    edges = [
        lax.dynamic_slice(object_field, (0, 0, (tile - 1) * LANES), (2, block_rows, LANES))
        for tile in plan.edge_tiles(t)
    ]
    halos = plan.across([jnp.concatenate([edge, own_rows], axis=1) for edge in edges])
    near_block = plan.near_rows(object_field)

    rolled, ordered = call(
        prepare_kernel,
        [shape((slots, 2, size, size), f32), shape((slots, size, size), f32)],
        [pltpu.VMEM((2, 2 * size + 8, size), f32)],
        [spots, probe_field, own_amps, order],
        10**9, 10**6,
    )
    halos, rolled, ordered = lax.optimization_barrier((halos, rolled, ordered))
    own = [object_field] + halos
    passed = [jnp.concatenate([halo, own_rows], axis=1) for halo in halos]
    far = [far_block] + [plan.far_rows(message) for message in passed]
    near = [near_block] + [plan.near_rows(message) for message in passed]

    def known(messages):
        lines = [messages[0][0, half + 8 : half + 9, :INFO]]
        return jnp.concatenate(lines + [message[0, half : half + 1, :INFO] for message in messages], axis=0)

    upper = s % 2 == 0
    far_info, own_known, near_info = known(far[1:]), known(passed), known(near[1:])
    info = jnp.stack([jnp.where(upper, far_info, near_info), own_known, jnp.where(upper, near_info, far_info)])
    info = info.astype(jnp.int32).reshape(-1)
    inverse, *inverse_pairs = call(
        lambda *refs: light_kernel(plan, slots, *refs),
        [shape((half, width), f32)] + [shape((half, 2 * LANES), f32)] * plan.sides,
        [pltpu.VMEM((2 * size + 8, size), f32), pltpu.VMEM((half, width + 2 * plan.own * LANES), f32)],
        [place, info, probe_field],
        10**9, 10**6,
    )

    def starts(t):
        return [1] + plan.halo_tiles(t)

    def later_starts(t):
        return [plan.mid_start(t)] + plan.pair_starts(t)

    result = None
    for sweep in range(ITERS):
        inner, outer_far, outer_near = [], [], []
        for slot in range(slots):
            outer_part, inner_part = pl.pallas_call(
                lambda *refs, slot=slot, starts=starts: term_kernel(plan, slot, starts, *refs),
                out_shape=[shape((2, half, size), f32)] * 2,
                in_specs=[SMEM] * 3 + [VMEM] * (3 * len(own)) + [
                    pl.BlockSpec((1, 2, size, size), lambda i, slot=slot: (slot, 0, 0, 0)),
                    pl.BlockSpec((1, size, size), lambda i, slot=slot: (slot, 0, 0)),
                    VMEM,
                ],
                out_specs=[VMEM] * 2,
                grid=(1,),
                scratch_shapes=[pltpu.VMEM((2, size, size), f32), pltpu.VMEM((3, 2, half, width), f32)],
                compiler_params=pltpu.CompilerParams(vmem_limit_bytes=VMEM_BYTES),
                cost_estimate=pl.CostEstimate(flops=2 * 10**9, bytes_accessed=6 * 10**6, transcendentals=0),
            )(place, spots, counts, *own, *far, *near, rolled, ordered, tables)
            inner.append(inner_part)
            outer_far.append(plan.far_rows(outer_part))
            outer_near.append(plan.near_rows(outer_part))
        patches = inner + outer_far + outer_near
        if sweep < ITERS - 1:
            middle, *rest = call(
                lambda *refs, starts=starts: step_kernel(plan, slots, starts, *refs),
                [shape((2, half, plan.mid_tiles * LANES), f32)] + [shape((2, half, 2 * LANES), f32)] * (2 * plan.sides),
                [pltpu.VMEM((2, half, width), f32)] * 2,
                [place, info] + patches + own + [inverse],
                10**9, 10**6,
            )
            bases, sums = rest[: plan.sides], rest[plan.sides :]
            received = plan.across(sums)
            pairs = [base - other * inv[None] for base, other, inv in zip(bases, received, inverse_pairs)]
            own = [middle] + pairs
            far = [plan.far_rows(piece) for piece in own]
            near = [plan.near_rows(piece) for piece in own]
            starts = later_starts
        else:
            nearly, *sums = call(
                lambda *refs, starts=starts: last_kernel(plan, slots, starts, *refs),
                [shape((2, half, block_cols), f32)] + [shape((2, half, LANES), f32)] * plan.sides,
                [pltpu.VMEM((2, half, width), f32)] * 2,
                [place, info] + patches + own + [inverse],
                10**9, 10**6,
            )
            result = nearly
            for side, received in enumerate(plan.across(sums)):
                block = pl.BlockSpec((2, half, LANES), lambda i, place, side=side: (0, 0, plan.edge_tiles(place[1])[side] - 1))
                result = pl.pallas_call(
                    edge_kernel,
                    grid_spec=pltpu.PrefetchScalarGridSpec(
                        num_scalar_prefetch=1,
                        grid=(1,),
                        in_specs=[
                            block,
                            pl.BlockSpec((2, half, LANES), lambda i, place: (0, 0, 0)),
                            pl.BlockSpec((half, LANES), lambda i, place, side=side: (0, plan.edge_tiles(place[1])[side])),
                        ],
                        out_specs=block,
                    ),
                    out_shape=shape(result.shape, f32),
                    input_output_aliases={1: 0},
                )(place, result, received, inverse)
    return result


def solution(mesh):
    sizes = dict(mesh.shape)

    def per_device(object_field, *rest):
        plan = Plan(sizes["sx"], sizes["sy"], object_field.shape[2])
        return on_device(plan, object_field, *rest)

    return jax.shard_map(
        per_device,
        mesh=mesh,
        in_specs=(
            P(None, "sx", "sy"),
            P(),
            P("sx", "sy", None, None, None),
            P("sx", "sy", None, None),
            P(None, "sy"),
        ),
        out_specs=P(None, "sx", "sy"),
        check_vma=False,
    )
```

```python
import math

import jax
import jax.numpy as jnp
import ml_dtypes
import numpy as np
from jax import lax
from jax.experimental import pallas as pl
from jax.experimental.pallas import tpu as pltpu
from jax.sharding import PartitionSpec as P

ITERS = 2
SMOOTH = 1.0
DAMPING = 1.0
LANES = 128
VMEM_BYTES = 12 * 1024 * 1024

VMEM = pl.BlockSpec(memory_space=pltpu.VMEM)
SMEM = pl.BlockSpec(memory_space=pltpu.SMEM)
HBM = pl.BlockSpec(memory_space=pltpu.HBM)


def split_numpy(table):
    high = table.astype(np.float32).astype(ml_dtypes.bfloat16)
    low = (table - high.astype(np.float64)).astype(ml_dtypes.bfloat16)
    return high, low


def dft_tables(length):
    half = length // 2
    index = np.arange(half)
    tables = []
    for parity in range(2):
        angles = 2.0 * math.pi / length * (index[:, None] * (2 * index[None, :] + parity) % length)
        cosine = np.cos(angles) / math.sqrt(length)
        sine = np.sin(angles) / math.sqrt(length)
        forward = np.block([[cosine, -sine], [sine, cosine]])
        tables.append([split_numpy(forward), split_numpy(forward.T)])
    return np.array(tables, dtype=ml_dtypes.bfloat16)


def parity_order(length):
    half = length // 2
    order = np.zeros((length, length))
    for index in range(length):
        order[index, index % 2 * half + index // 2] = 1.0
    return np.stack([order, order.T]).astype(ml_dtypes.bfloat16)


def split(values):
    high = values.astype(jnp.bfloat16)
    low = (values - high.astype(jnp.float32)).astype(jnp.bfloat16)
    return high, low


def times_table(values, table):
    high, low = split(values)
    left = jnp.concatenate([high, low, high], axis=1)
    right = jnp.concatenate([table[0], table[0], table[1]], axis=0)
    return jnp.dot(left, right, preferred_element_type=jnp.float32)


def table_times(table, values):
    high, low = split(values)
    left = jnp.concatenate([table[0], table[0], table[1]], axis=1)
    right = jnp.concatenate([high, low, high], axis=0)
    return jnp.dot(left, right, preferred_element_type=jnp.float32)


class Plan:
    def __init__(self, sx_size, sy_size, block_cols):
        self.sx_size = sx_size
        self.sy_size = sy_size
        self.own = block_cols // LANES
        self.tiles = self.own + 2
        self.paired = sy_size == 2
        self.sides = 1 if self.paired else 2

    def rights(self, t):
        return [1 - t] if self.paired else [0, 1]

    def pair_starts(self, t):
        return [right * (self.tiles - 2) for right in self.rights(t)]

    def halo_tiles(self, t):
        return [right * (self.tiles - 1) for right in self.rights(t)]

    def edge_tiles(self, t):
        return [1 + right * (self.tiles - 3) for right in self.rights(t)]

    def mid_start(self, t):
        return 1 + t if self.paired else 2

    @property
    def mid_tiles(self):
        return self.tiles - 3 if self.paired else self.tiles - 4

    def across(self, values, axis_name="sy"):
        if self.paired:
            return [lax.ppermute(values[0], axis_name, [(0, 1), (1, 0)])]
        ends = self.sy_size - 1
        return [
            lax.ppermute(values[1], axis_name, [(i, i + 1) for i in range(ends)]),
            lax.ppermute(values[0], axis_name, [(i + 1, i) for i in range(ends)]),
        ]

    def far_rows(self, values):
        return lax.ppermute(values, "sx", self.swaps(1))

    def near_rows(self, values):
        return lax.ppermute(values, "sx", self.swaps(0))

    def swaps(self, first):
        pairs = [(i, i + 1) for i in range(first, self.sx_size - 1, 2)]
        return pairs + [(j, i) for i, j in pairs]


def far_side(s):
    return 2 * (s % 2) - 1


def lanes(tile, count=1):
    if isinstance(tile, int):
        return pl.ds(tile * LANES, count * LANES)
    return pl.ds(pl.multiple_of(tile * LANES, LANES), count * LANES)


def assemble(canvas, pieces, starts, tiles):
    blank = jnp.zeros(canvas.shape[:-1] + (LANES,), jnp.float32)
    canvas[:, :, lanes(0)] = blank
    canvas[:, :, lanes(tiles - 1)] = blank
    for piece, start in zip(pieces, starts):
        canvas[:, :, lanes(start, piece.shape[2] // LANES)] = piece[:, : canvas.shape[1]]


def rows_at(ref, start, count):
    offset = start % 8
    values = ref[pl.ds(pl.multiple_of(start - offset, 8), count + 8)]
    return pltpu.roll(values, (count + 8 - offset) % (count + 8), 0)[:count]


def here():
    return lax.axis_index("sx"), lax.axis_index("sy")


def info_rows(centres, count):
    lane = lax.broadcasted_iota(jnp.int32, (8, LANES), 1)
    slots = centres.shape[0]
    values = [centres[slot, axis] for slot in range(slots) for axis in range(2)] + [count]
    line = jnp.zeros((8, LANES), jnp.int32)
    for index, value in enumerate(values):
        line = jnp.where(lane == index, value, line)
    return line.astype(jnp.float32)


def edge_message_kernel(plan, block, centres, counts, *rest):
    messages, sems = rest[: plan.sides], rest[plan.sides]
    s, t = here()
    half = block.shape[1]
    copies = [
        pltpu.make_async_copy(block.at[:, :, lanes(tile - 1)], message.at[:, :half], sems.at[side])
        for side, (message, tile) in enumerate(zip(messages, plan.edge_tiles(t)))
    ]
    for copy in copies:
        copy.start()
    rows = info_rows(centres, counts[s])
    for message in messages:
        message[0, half:] = rows
        message[1, half:] = rows
    for copy in copies:
        copy.wait()


def halo_message_kernel(centres, counts, received, message):
    s, _ = here()
    rows = received.shape[1]
    message[:, :rows] = received[...]
    own = info_rows(centres, counts[s])
    message[0, rows:] = own
    message[1, rows:] = own


def pair_kernel(base, received, inverse, result):
    result[...] = base[...] - received[...] * inverse[...][None]


def prepare_kernel(centres, probe, amps, order, rolled, ordered, padded):
    size = probe.shape[1]
    half = size // 2
    padded[:, :half] = jnp.zeros((2, half, size), jnp.float32)
    padded[:, half + size :] = jnp.zeros((2, half + 8, size), jnp.float32)
    padded[:, half : half + size] = probe[...]
    for slot in range(amps.shape[0]):
        row = centres[slot, 0]
        col = centres[slot, 1]
        for part in range(2):
            shape = padded.at[part]
            upper = rows_at(shape, half - row, half) + rows_at(shape, half + size - row, half)
            lower = rows_at(shape, size - row, half)
            rolled[slot, part] = pltpu.roll(jnp.concatenate([upper, lower], axis=0), col % size, 1)
        high, low = split(amps[slot])
        across = jnp.dot(
            jnp.concatenate([high, low], axis=1),
            jnp.concatenate([order[0], order[0]], axis=0),
            preferred_element_type=jnp.float32,
        )
        high, low = split(across)
        ordered[slot] = jnp.dot(
            jnp.concatenate([order[1], order[1]], axis=1),
            jnp.concatenate([high, low], axis=0),
            preferred_element_type=jnp.float32,
        )


def light_kernel(plan, slots, *rest):
    groups = [rest[k * plan.sides : (k + 1) * plan.sides] for k in range(3)]
    probe, inverse, info = rest[3 * plan.sides : 3 * plan.sides + 3]
    pairs = rest[3 * plan.sides + 3 : 4 * plan.sides + 3]
    padded, canvas, known, sem = rest[4 * plan.sides + 3 :]
    size = probe.shape[1]
    half = size // 2
    s, t = here()
    upper = s % 2 == 0
    height = half

    def lines(messages):
        return [messages[0][0, height + 8 : height + 16]] + [message[0, height : height + 8] for message in messages]

    own, far, near = (lines(messages) for messages in groups)
    for turn in range(plan.sides + 1):
        for kind, line in ((0, jnp.where(upper, far[turn], near[turn])), (1, own[turn]), (2, jnp.where(upper, near[turn], far[turn]))):
            known[kind * (plan.sides + 1) + turn] = line.astype(jnp.int32)
    copy = pltpu.make_async_copy(known.at[:, 0], info, sem)
    copy.start()
    padded[:half] = jnp.zeros((half, size), jnp.float32)
    padded[half + size :] = jnp.zeros((half + 8, size), jnp.float32)
    padded[half : half + size] = probe[0] * probe[0] + probe[1] * probe[1]
    canvas[...] = jnp.zeros(canvas.shape, jnp.float32)
    copy.wait()
    reach = plan.sides + 1
    spare = jnp.zeros((half, LANES), jnp.float32)
    for down in (-1, 0, 1):

        def add(step, carry, down=down):
            turn = step // slots
            slot = step % slots
            over = turn * (1 - 2 * t) if plan.paired else jnp.where(turn == 0, 0, 2 * turn - 3)
            index = (down + 1) * reach + turn

            @pl.when(slot < info[index, 2 * slots])
            def _():
                row = info[index, 2 * slot]
                col = info[index, 2 * slot + 1]
                power = rows_at(padded, size - half * down - row, half)
                shifted = pltpu.roll(jnp.concatenate([power, spare], axis=1), col % LANES, 1)
                first = col // LANES + plan.own * (over + 1)
                canvas[:, lanes(first, 3)] += shifted

            return carry

        lax.fori_loop(0, reach * slots, add, 0)
    result = 1.0 / (canvas[:, lanes(plan.own, plan.tiles)] + DAMPING)
    inverse[...] = result
    for pair, start in zip(pairs, plan.pair_starts(t)):
        pair[...] = inverse[:, lanes(start, 2)]


def term_kernel(plan, slot, starts, centres, counts, *rest):
    pieces = len(starts(0))
    own, far, near = (rest[k * pieces : (k + 1) * pieces] for k in range(3))
    probe, amps, tables, outer, inner, window, canvas = rest[3 * pieces :]
    size = probe.shape[2]
    half = size // 2
    s, t = here()
    row = centres[slot, 0]
    col = centres[slot, 1]
    alive = slot < counts[s]

    @pl.when(jnp.logical_not(alive))
    def _():
        outer[...] = jnp.zeros(outer.shape, jnp.float32)
        inner[...] = jnp.zeros(inner.shape, jnp.float32)

    @pl.when(alive)
    def _():
        tile = col // LANES
        first = tile % 2
        rest_col = col % LANES
        from_tile = lax.broadcasted_iota(jnp.int32, (half, LANES), 1) >= rest_col
        from_upper = lax.broadcasted_iota(jnp.int32, (half, LANES), 0) >= row
        side = far_side(s)
        for kind, source in ((1, own), (1 + side, far), (1 - side, near)):
            assemble(canvas.at[kind], source, starts(t), plan.tiles)

        def pick(kind, part, index):
            return canvas[kind, part, :, lanes(index)]

        for part in range(2):
            edge = [jnp.where(from_tile, pick(kind, part, tile), pick(kind, part, tile + 2)) for kind in range(3)]
            middle = [pick(kind, part, tile + 1) for kind in range(3)]
            window[part, :half, lanes(first)] = jnp.where(from_upper, edge[0], edge[2])
            window[part, half:, lanes(first)] = edge[1]
            window[part, :half, lanes(1 - first)] = jnp.where(from_upper, middle[0], middle[2])
            window[part, half:, lanes(1 - first)] = middle[1]

        probe_real = probe[0, 0]
        probe_imag = probe[0, 1]
        exit_real = probe_real * window[0] - probe_imag * window[1]
        exit_imag = probe_real * window[1] + probe_imag * window[0]

        halves = [
            jnp.concatenate([exit_real[:, :half] + sign * exit_real[:, half:], exit_imag[:, :half] + sign * exit_imag[:, half:]], axis=1)
            for sign in (1.0, -1.0)
        ]
        across = [times_table(halves[parity], tables[parity, 0]) for parity in range(2)]
        real = jnp.concatenate([across[0][:, :half], across[1][:, :half]], axis=1)
        imag = jnp.concatenate([across[0][:, half:], across[1][:, half:]], axis=1)
        halves = [
            jnp.concatenate([real[:half] + sign * real[half:], imag[:half] + sign * imag[half:]], axis=0)
            for sign in (1.0, -1.0)
        ]
        back = []
        for parity in range(2):
            pattern = table_times(tables[parity, 1], halves[parity])
            far_real = pattern[:half]
            far_imag = pattern[half:]
            amplitude = amps[0, parity * half : (parity + 1) * half]
            factor = 1.0 - amplitude * lax.rsqrt(far_real * far_real + far_imag * far_imag + SMOOTH)
            miss = jnp.concatenate([far_real * factor, far_imag * factor], axis=0)
            back.append(table_times(tables[parity, 0], miss))
        real = jnp.concatenate([back[0][:half] + back[1][:half], back[0][:half] - back[1][:half]], axis=0)
        imag = jnp.concatenate([back[0][half:] + back[1][half:], back[0][half:] - back[1][half:]], axis=0)
        both = []
        for parity in range(2):
            picked = slice(parity * half, (parity + 1) * half)
            both.append(times_table(jnp.concatenate([real[:, picked], imag[:, picked]], axis=1), tables[parity, 1]))
        near_real = jnp.concatenate([both[0][:, :half] + both[1][:, :half], both[0][:, :half] - both[1][:, :half]], axis=1)
        near_imag = jnp.concatenate([both[0][:, half:] + both[1][:, half:], both[0][:, half:] - both[1][:, half:]], axis=1)
        term_real = probe_real * near_real + probe_imag * near_imag
        term_imag = probe_real * near_imag - probe_imag * near_real
        outer[0] = term_real[:half]
        outer[1] = term_imag[:half]
        inner[0] = term_real[half:]
        inner[1] = term_imag[half:]


def gather_terms(plan, slots, s, info, own, far, near, canvas):
    half = canvas.shape[1]
    side = far_side(s)
    canvas[...] = jnp.zeros(canvas.shape, jnp.float32)
    lane = lax.broadcasted_iota(jnp.int32, (half, LANES), 1)
    line = lax.broadcasted_iota(jnp.int32, (half, LANES), 0)
    for down, patches in ((None, own), (side, far), (-side, near)):
        index = (1 if down is None else 1 + down) * (plan.sides + 1)
        for slot in range(slots):
            row = info[index, 2 * slot]
            col = info[index, 2 * slot + 1]
            tile = col // LANES
            first = tile % 2
            from_tile = lane >= col % LANES
            if down is not None:
                there = (line >= jnp.where(down > 0, row, 0)) & (line < jnp.where(down > 0, half, row))
            for part in range(2):
                edge = patches[slot][part, :, lanes(first)]
                middle = patches[slot][part, :, lanes(1 - first)]
                if down is not None:
                    edge = jnp.where(there, edge, 0.0)
                    middle = jnp.where(there, middle, 0.0)
                canvas[part, :, lanes(tile)] += jnp.where(from_tile, edge, 0.0)
                canvas[part, :, lanes(tile + 1)] += middle
                canvas[part, :, lanes(tile + 2)] += jnp.where(from_tile, 0.0, edge)


def step_kernel(plan, slots, starts, info, *rest):
    patches = [rest[k * slots : (k + 1) * slots] for k in range(3)]
    rest = rest[3 * slots :]
    pieces = len(starts(0))
    own = rest[:pieces]
    inverse, middle = rest[pieces : pieces + 2]
    bases = rest[pieces + 2 : pieces + 2 + plan.sides]
    sums = rest[pieces + 2 + plan.sides : pieces + 2 + 2 * plan.sides]
    current, canvas = rest[pieces + 2 + 2 * plan.sides :]
    s, t = here()
    gather_terms(plan, slots, s, info, *patches, canvas)
    assemble(current, own, starts(t), plan.tiles)
    where = lanes(plan.mid_start(t), plan.mid_tiles)
    middle[...] = current[:, :, where] - canvas[:, :, where] * inverse[:, where][None]
    for base, total, start in zip(bases, sums, plan.pair_starts(t)):
        where = lanes(start, 2)
        partial = canvas[:, :, where]
        total[...] = partial
        base[...] = current[:, :, where] - partial * inverse[:, where][None]


def halo_sum_kernel(plan, slots, info, *rest):
    patches = [rest[k * slots : (k + 1) * slots] for k in range(3)]
    sums = rest[3 * slots : 3 * slots + plan.sides]
    canvas = rest[3 * slots + plan.sides]
    s, t = here()
    gather_terms(plan, slots, s, info, *patches, canvas)
    for total, tile in zip(sums, plan.halo_tiles(t)):
        total[...] = canvas[:, :, lanes(tile)]


def last_kernel(plan, slots, starts, info, *rest):
    patches = [rest[k * slots : (k + 1) * slots] for k in range(3)]
    rest = rest[3 * slots :]
    pieces = len(starts(0))
    own = rest[:pieces]
    inverse, nearly = rest[pieces : pieces + 2]
    bases = rest[pieces + 2 : pieces + 2 + plan.sides]
    current, canvas, sem = rest[pieces + 2 + plan.sides :]
    s, t = here()
    gather_terms(plan, slots, s, info, *patches, canvas)
    assemble(current, own, starts(t), plan.tiles)
    where = lanes(1, plan.own)
    current[:, :, where] = current[:, :, where] - canvas[:, :, where] * inverse[:, where][None]
    copy = pltpu.make_async_copy(current.at[:, :, where], nearly, sem)
    copy.start()
    for base, tile in zip(bases, plan.edge_tiles(t)):
        base[...] = current[:, :, lanes(tile)]
    copy.wait()


def edge_kernel(plan, inverse, *rest):
    bases, received = rest[: plan.sides], rest[plan.sides : 2 * plan.sides]
    _, result, sums, sems = rest[2 * plan.sides :]
    _, t = here()
    copies = []
    for side, tile in enumerate(plan.edge_tiles(t)):
        sums[side] = bases[side][...] - received[side][...] * inverse[:, lanes(tile)][None]
        copies.append(pltpu.make_async_copy(sums.at[side], result.at[:, :, lanes(tile - 1)], sems.at[side]))
        copies[-1].start()
    for copy in copies:
        copy.wait()


def call(kernel, outs, scratch, ins, flops=10**9, size=10**6, in_specs=None, out_specs=None, **options):
    return pl.pallas_call(
        kernel,
        out_shape=outs,
        in_specs=in_specs or [SMEM if value.dtype == jnp.int32 else VMEM for value in ins],
        out_specs=out_specs or jax.tree.map(lambda _: VMEM, outs),
        scratch_shapes=scratch,
        compiler_params=pltpu.CompilerParams(vmem_limit_bytes=VMEM_BYTES),
        cost_estimate=pl.CostEstimate(flops=flops, bytes_accessed=size, transcendentals=0),
        **options,
    )(*ins)


def on_device(plan, object_field, probe_field, amplitudes, centres, counts):
    f32 = jnp.float32
    shape = jax.ShapeDtypeStruct
    size = probe_field.shape[1]
    half = size // 2
    slots = amplitudes.shape[2]
    block_rows = object_field.shape[1]
    block_cols = object_field.shape[2]
    assert block_rows == half and block_cols % LANES == 0 and half == LANES
    width = plan.tiles * LANES
    sides = plan.sides
    spots = centres[0, 0]
    counts = counts.reshape(-1)
    own_amps = amplitudes[0, 0]
    tables = jnp.asarray(dft_tables(size))
    order = jnp.asarray(parity_order(size))
    dma = pltpu.SemaphoreType.DMA

    messages = call(
        lambda *refs: edge_message_kernel(plan, *refs),
        [shape((2, half + 8, LANES), f32)] * sides,
        [dma((sides,))],
        [object_field, spots, counts],
        in_specs=[HBM, SMEM, SMEM],
    )
    halos = plan.across(messages)
    near_block = plan.near_rows(object_field)
    far_block = plan.far_rows(object_field)
    rolled, ordered = call(
        prepare_kernel,
        [shape((slots, 2, size, size), f32), shape((slots, size, size), f32)],
        [pltpu.VMEM((2, 2 * size + 8, size), f32)],
        [spots, probe_field, own_amps, order],
    )
    halos, rolled, ordered = lax.optimization_barrier((halos, rolled, ordered))
    passed = [
        call(halo_message_kernel, shape((2, half + 16, LANES), f32), [], [spots, counts, halo], flops=10**7)
        for halo in halos
    ]
    near = [near_block] + [plan.near_rows(message) for message in passed]
    far = [far_block] + [plan.far_rows(message) for message in passed]
    own = [object_field] + passed
    inverse, info, *inverse_pairs = call(
        lambda *refs: light_kernel(plan, slots, *refs),
        [shape((half, width), f32), shape((3 * (sides + 1), LANES), jnp.int32)] + [shape((half, 2 * LANES), f32)] * sides,
        [
            pltpu.VMEM((2 * size + 8, size), f32),
            pltpu.VMEM((half, width + 2 * plan.own * LANES), f32),
            pltpu.VMEM((3 * (sides + 1), 8, LANES), jnp.int32),
            dma,
        ],
        passed + far[1:] + near[1:] + [probe_field],
        out_specs=[VMEM, SMEM] + [VMEM] * sides,
    )

    def starts(t):
        return [1] + plan.halo_tiles(t)

    def later_starts(t):
        return [plan.mid_start(t)] + plan.pair_starts(t)

    for sweep in range(ITERS):
        inner, outer_far, outer_near = [], [], []
        for slot in range(slots):
            outer_part, inner_part = pl.pallas_call(
                lambda *refs, slot=slot, starts=starts: term_kernel(plan, slot, starts, *refs),
                out_shape=[shape((2, half, size), f32)] * 2,
                in_specs=[SMEM] * 2 + [VMEM] * (3 * len(own)) + [
                    pl.BlockSpec((1, 2, size, size), lambda i, slot=slot: (slot, 0, 0, 0)),
                    pl.BlockSpec((1, size, size), lambda i, slot=slot: (slot, 0, 0)),
                    VMEM,
                ],
                out_specs=[VMEM] * 2,
                grid=(1,),
                scratch_shapes=[pltpu.VMEM((2, size, size), f32), pltpu.VMEM((3, 2, half, width), f32)],
                compiler_params=pltpu.CompilerParams(vmem_limit_bytes=VMEM_BYTES),
                cost_estimate=pl.CostEstimate(flops=2 * 10**9, bytes_accessed=6 * 10**6, transcendentals=0),
            )(spots, counts, *own, *far, *near, rolled, ordered, tables)
            inner.append(inner_part)
            outer_near.append(plan.near_rows(outer_part))
            outer_far.append(plan.far_rows(outer_part))
        patches = inner + outer_far + outer_near
        if sweep < ITERS - 1:
            middle, *rest = call(
                lambda *refs, starts=starts: step_kernel(plan, slots, starts, *refs),
                [shape((2, half, plan.mid_tiles * LANES), f32)] + [shape((2, half, 2 * LANES), f32)] * (2 * sides),
                [pltpu.VMEM((2, half, width), f32)] * 2,
                [info] + patches + own + [inverse],
            )
            bases, sums = rest[:sides], rest[sides:]
            near_middle = plan.near_rows(middle)
            received = plan.across(sums)
            far_middle = plan.far_rows(middle)
            pairs = [
                call(pair_kernel, shape(base.shape, f32), [], [base, other, inv], flops=10**7)
                for base, other, inv in zip(bases, received, inverse_pairs)
            ]
            own = [middle] + pairs
            near = [near_middle] + [plan.near_rows(piece) for piece in pairs]
            far = [far_middle] + [plan.far_rows(piece) for piece in pairs]
            starts = later_starts
    sums = call(
        lambda *refs: halo_sum_kernel(plan, slots, *refs),
        [shape((2, half, LANES), f32)] * sides,
        [pltpu.VMEM((2, half, width), f32)],
        [info] + patches,
    )
    nearly, *bases = call(
        lambda *refs: last_kernel(plan, slots, starts, *refs),
        [shape((2, half, block_cols), f32)] + [shape((2, half, LANES), f32)] * sides,
        [pltpu.VMEM((2, half, width), f32)] * 2 + [dma],
        [info] + patches + own + [inverse],
        out_specs=[HBM] + [VMEM] * sides,
    )
    received = plan.across(sums)
    return call(
        lambda *refs: edge_kernel(plan, *refs),
        shape(nearly.shape, f32),
        [pltpu.VMEM((sides, 2, half, LANES), f32), dma((sides,))],
        [inverse, *bases, *received, nearly],
        in_specs=[VMEM] * (1 + 2 * sides) + [HBM],
        out_specs=HBM,
        input_output_aliases={1 + 2 * sides: 0},
    )


def solution(mesh):
    sizes = dict(mesh.shape)

    def per_device(object_field, *rest):
        plan = Plan(sizes["sx"], sizes["sy"], object_field.shape[2])
        return on_device(plan, object_field, *rest)

    return jax.shard_map(
        per_device,
        mesh=mesh,
        in_specs=(
            P(None, "sx", "sy"),
            P(),
            P("sx", "sy", None, None, None),
            P("sx", "sy", None, None),
            P(None, "sy"),
        ),
        out_specs=P(None, "sx", "sy"),
        check_vma=False,
    )
```

```python
import math

import jax
import jax.numpy as jnp
import ml_dtypes
import numpy as np
from jax import lax
from jax.experimental import pallas as pl
from jax.experimental.pallas import tpu as pltpu
from jax.sharding import PartitionSpec as P

ITERS = 2
SMOOTH = 1.0
DAMPING = 1.0
LANES = 128
VMEM_BYTES = 12 * 1024 * 1024

VMEM = pl.BlockSpec(memory_space=pltpu.VMEM)
SMEM = pl.BlockSpec(memory_space=pltpu.SMEM)
HBM = pl.BlockSpec(memory_space=pltpu.HBM)
ANY = pl.BlockSpec(memory_space=pl.ANY)


def split_numpy(table):
    high = table.astype(np.float32).astype(ml_dtypes.bfloat16)
    low = (table - high.astype(np.float64)).astype(ml_dtypes.bfloat16)
    return high, low


def dft_tables(length):
    half = length // 2
    index = np.arange(half)
    tables = []
    for parity in range(2):
        angles = 2.0 * math.pi / length * (index[:, None] * (2 * index[None, :] + parity) % length)
        cosine = np.cos(angles) / math.sqrt(length)
        sine = np.sin(angles) / math.sqrt(length)
        forward = np.block([[cosine, -sine], [sine, cosine]])
        tables.append([split_numpy(forward), split_numpy(forward.T)])
    return np.array(tables, dtype=ml_dtypes.bfloat16)


def parity_order(length):
    half = length // 2
    order = np.zeros((length, length))
    for index in range(length):
        order[index, index % 2 * half + index // 2] = 1.0
    return np.stack([order, order.T]).astype(ml_dtypes.bfloat16)


def split(values):
    high = values.astype(jnp.bfloat16)
    low = (values - high.astype(jnp.float32)).astype(jnp.bfloat16)
    return high, low


def times_table(values, table):
    high, low = split(values)
    left = jnp.concatenate([high, low, high], axis=1)
    right = jnp.concatenate([table[0], table[0], table[1]], axis=0)
    return jnp.dot(left, right, preferred_element_type=jnp.float32)


def table_times(table, values):
    high, low = split(values)
    left = jnp.concatenate([table[0], table[0], table[1]], axis=1)
    right = jnp.concatenate([high, low, high], axis=0)
    return jnp.dot(left, right, preferred_element_type=jnp.float32)


class Plan:
    def __init__(self, sx_size, sy_size, block_cols):
        self.sx_size = sx_size
        self.sy_size = sy_size
        self.own = block_cols // LANES
        self.tiles = self.own + 2
        self.paired = sy_size == 2
        self.sides = 1 if self.paired else 2

    def rights(self, t):
        return [1 - t] if self.paired else [0, 1]

    def pair_starts(self, t):
        return [right * (self.tiles - 2) for right in self.rights(t)]

    def halo_tiles(self, t):
        return [right * (self.tiles - 1) for right in self.rights(t)]

    def edge_tiles(self, t):
        return [1 + right * (self.tiles - 3) for right in self.rights(t)]

    def mid_start(self, t):
        return 1 + t if self.paired else 2

    @property
    def mid_tiles(self):
        return self.tiles - 3 if self.paired else self.tiles - 4

    def across(self, values, axis_name="sy"):
        if self.paired:
            return [lax.ppermute(values[0], axis_name, [(0, 1), (1, 0)])]
        ends = self.sy_size - 1
        return [
            lax.ppermute(values[1], axis_name, [(i, i + 1) for i in range(ends)]),
            lax.ppermute(values[0], axis_name, [(i + 1, i) for i in range(ends)]),
        ]

    def far_rows(self, values):
        return lax.ppermute(values, "sx", self.swaps(1))

    def near_rows(self, values):
        return lax.ppermute(values, "sx", self.swaps(0))

    def swaps(self, first):
        pairs = [(i, i + 1) for i in range(first, self.sx_size - 1, 2)]
        return pairs + [(j, i) for i, j in pairs]


def far_side(s):
    return 2 * (s % 2) - 1


def lanes(tile, count=1):
    if isinstance(tile, int):
        return pl.ds(tile * LANES, count * LANES)
    return pl.ds(pl.multiple_of(tile * LANES, LANES), count * LANES)


def pick_tile(plan, target, pieces, tile, t):
    rows = target.shape[1]
    if plan.paired:

        @pl.when(tile == (plan.tiles - 1) * t)
        def _():
            target[...] = jnp.zeros(target.shape, jnp.float32)

    for ref, offset, count, start in pieces:

        @pl.when((tile >= start) & (tile < start + count))
        def _(ref=ref, offset=offset, start=start):
            target[...] = ref[:, :rows, lanes(tile - start + offset)]


def lay_out(refs, starts):
    return [(ref, 0, ref.shape[2] // LANES, start) for ref, start in zip(refs, starts)]


def chunks(count):
    return [min(2, count - first) for first in range(0, count, 2)]


def chunk_starts(start, count):
    return [start + 2 * index for index in range(len(chunks(count)))]


def spread(source, targets):
    offset = 0
    for target in targets:
        columns = target.shape[2]
        target[...] = source[:, :, offset : offset + columns]
        offset += columns


def rows_at(ref, start, count):
    offset = start % 8
    values = ref[pl.ds(pl.multiple_of(start - offset, 8), count + 8)]
    return pltpu.roll(values, (count + 8 - offset) % (count + 8), 0)[:count]


def here():
    return lax.axis_index("sx"), lax.axis_index("sy")


def info_rows(centres, count):
    lane = lax.broadcasted_iota(jnp.int32, (8, LANES), 1)
    slots = centres.shape[0]
    values = [centres[slot, axis] for slot in range(slots) for axis in range(2)] + [count]
    line = jnp.zeros((8, LANES), jnp.int32)
    for index, value in enumerate(values):
        line = jnp.where(lane == index, value, line)
    return line.astype(jnp.float32)


def edge_message_kernel(plan, block, centres, counts, *rest):
    messages, sems = rest[: plan.sides], rest[plan.sides]
    s, t = here()
    half = block.shape[1]
    copies = [
        pltpu.make_async_copy(block.at[:, :, lanes(tile - 1)], message.at[:, :half], sems.at[side])
        for side, (message, tile) in enumerate(zip(messages, plan.edge_tiles(t)))
    ]
    for copy in copies:
        copy.start()
    rows = info_rows(centres, counts[s])
    for message in messages:
        message[0, half:] = rows
        message[1, half:] = rows
    for copy in copies:
        copy.wait()


def halo_message_kernel(plan, block, centres, counts, *rest):
    s, _ = here()
    received, messages, near = rest[: plan.sides], rest[plan.sides : 2 * plan.sides], rest[2 * plan.sides :]
    own = info_rows(centres, counts[s])
    for source, message in zip(received, messages):
        rows = source.shape[1]
        message[:, :rows] = source[...]
        message[0, rows:] = own
        message[1, rows:] = own
    spread(block, near)


def pair_kernel(sides, middle, *rest):
    bases, received, inverses, results = (rest[k * sides : (k + 1) * sides] for k in range(4))
    near = rest[4 * sides :]
    for base, other, inverse, result, copy in zip(bases, received, inverses, results, near):
        values = base[...] - other[...] * inverse[...][None]
        result[...] = values
        copy[...] = values
    spread(middle, near[sides:])


def prepare_kernel(centres, probe, amps, order, rolled, ordered, padded):
    size = probe.shape[1]
    half = size // 2
    padded[:, :half] = jnp.zeros((2, half, size), jnp.float32)
    padded[:, half + size :] = jnp.zeros((2, half + 8, size), jnp.float32)
    padded[:, half : half + size] = probe[...]
    for slot in range(amps.shape[0]):
        row = centres[slot, 0]
        col = centres[slot, 1]
        for part in range(2):
            shape = padded.at[part]
            upper = rows_at(shape, half - row, half) + rows_at(shape, half + size - row, half)
            lower = rows_at(shape, size - row, half)
            rolled[slot, part] = pltpu.roll(jnp.concatenate([upper, lower], axis=0), col % size, 1)
        high, low = split(amps[slot])
        across = jnp.dot(
            jnp.concatenate([high, low], axis=1),
            jnp.concatenate([order[0], order[0]], axis=0),
            preferred_element_type=jnp.float32,
        )
        high, low = split(across)
        ordered[slot] = jnp.dot(
            jnp.concatenate([order[1], order[1]], axis=1),
            jnp.concatenate([high, low], axis=0),
            preferred_element_type=jnp.float32,
        )


def light_kernel(plan, slots, *rest):
    groups = [rest[k * plan.sides : (k + 1) * plan.sides] for k in range(3)]
    probe, inverse, info = rest[3 * plan.sides : 3 * plan.sides + 3]
    pairs = rest[3 * plan.sides + 3 : 4 * plan.sides + 3]
    padded, canvas, known, sem = rest[4 * plan.sides + 3 :]
    size = probe.shape[1]
    half = size // 2
    s, t = here()
    upper = s % 2 == 0
    height = half

    def lines(messages):
        return [messages[0][0, height + 8 : height + 16]] + [message[0, height : height + 8] for message in messages]

    own, far, near = (lines(messages) for messages in groups)
    for turn in range(plan.sides + 1):
        for kind, line in ((0, jnp.where(upper, far[turn], near[turn])), (1, own[turn]), (2, jnp.where(upper, near[turn], far[turn]))):
            known[kind * (plan.sides + 1) + turn] = line.astype(jnp.int32)
    copy = pltpu.make_async_copy(known.at[:, 0], info, sem)
    copy.start()
    padded[:half] = jnp.zeros((half, size), jnp.float32)
    padded[half + size :] = jnp.zeros((half + 8, size), jnp.float32)
    padded[half : half + size] = probe[0] * probe[0] + probe[1] * probe[1]
    canvas[...] = jnp.zeros(canvas.shape, jnp.float32)
    copy.wait()
    reach = plan.sides + 1
    spare = jnp.zeros((half, LANES), jnp.float32)
    for down in (-1, 0, 1):

        def add(step, carry, down=down):
            turn = step // slots
            slot = step % slots
            over = turn * (1 - 2 * t) if plan.paired else jnp.where(turn == 0, 0, 2 * turn - 3)
            index = (down + 1) * reach + turn

            @pl.when(slot < info[index, 2 * slots])
            def _():
                row = info[index, 2 * slot]
                col = info[index, 2 * slot + 1]
                power = rows_at(padded, size - half * down - row, half)
                shifted = pltpu.roll(jnp.concatenate([power, spare], axis=1), col % LANES, 1)
                first = col // LANES + plan.own * (over + 1)
                canvas[:, lanes(first, 3)] += shifted

            return carry

        lax.fori_loop(0, reach * slots, add, 0)
    result = 1.0 / (canvas[:, lanes(plan.own, plan.tiles)] + DAMPING)
    inverse[...] = result
    for pair, start in zip(pairs, plan.pair_starts(t)):
        pair[...] = inverse[:, lanes(start, 2)]


def term_kernel(plan, slot, layout, pieces, copied, centres, counts, *rest):
    refs, rest = rest[:pieces], rest[pieces:]
    earlier, (probe, amps, tables, outer, inner), rest = rest[:copied], rest[copied : copied + 5], rest[copied + 5 :]
    near_outers, (window, picked) = rest[:-2], rest[-2:]
    size = probe.shape[2]
    half = size // 2
    s, t = here()
    row = centres[slot, 0]
    col = centres[slot, 1]
    alive = slot < counts[s]

    @pl.when(jnp.logical_not(alive))
    def _():
        outer[...] = jnp.zeros(outer.shape, jnp.float32)
        inner[...] = jnp.zeros(inner.shape, jnp.float32)

    @pl.when(alive)
    def _():
        tile = col // LANES
        first = tile % 2
        rest_col = col % LANES
        from_tile = lax.broadcasted_iota(jnp.int32, (half, LANES), 1) >= rest_col
        from_upper = lax.broadcasted_iota(jnp.int32, (half, LANES), 0) >= row
        side = far_side(s)
        own, far, near = layout(refs, t)
        for kind, source in ((1, own), (1 + side, far), (1 - side, near)):
            for step in range(3):
                pick_tile(plan, picked.at[kind, step], source, tile + step, t)

        for part in range(2):
            edge = [jnp.where(from_tile, picked[kind, 0, part], picked[kind, 2, part]) for kind in range(3)]
            window[part, :half, lanes(first)] = jnp.where(from_upper, edge[0], edge[2])
            window[part, half:, lanes(first)] = edge[1]
            window[part, :half, lanes(1 - first)] = jnp.where(from_upper, picked[0, 1, part], picked[2, 1, part])
            window[part, half:, lanes(1 - first)] = picked[1, 1, part]

        probe_real = probe[slot, 0]
        probe_imag = probe[slot, 1]
        exit_real = probe_real * window[0] - probe_imag * window[1]
        exit_imag = probe_real * window[1] + probe_imag * window[0]

        halves = [
            jnp.concatenate([exit_real[:, :half] + sign * exit_real[:, half:], exit_imag[:, :half] + sign * exit_imag[:, half:]], axis=1)
            for sign in (1.0, -1.0)
        ]
        across = [times_table(halves[parity], tables[parity, 0]) for parity in range(2)]
        real = jnp.concatenate([across[0][:, :half], across[1][:, :half]], axis=1)
        imag = jnp.concatenate([across[0][:, half:], across[1][:, half:]], axis=1)
        halves = [
            jnp.concatenate([real[:half] + sign * real[half:], imag[:half] + sign * imag[half:]], axis=0)
            for sign in (1.0, -1.0)
        ]
        back = []
        for parity in range(2):
            pattern = table_times(tables[parity, 1], halves[parity])
            far_real = pattern[:half]
            far_imag = pattern[half:]
            amplitude = amps[slot, parity * half : (parity + 1) * half]
            factor = 1.0 - amplitude * lax.rsqrt(far_real * far_real + far_imag * far_imag + SMOOTH)
            miss = jnp.concatenate([far_real * factor, far_imag * factor], axis=0)
            back.append(table_times(tables[parity, 0], miss))
        real = jnp.concatenate([back[0][:half] + back[1][:half], back[0][:half] - back[1][:half]], axis=0)
        imag = jnp.concatenate([back[0][half:] + back[1][half:], back[0][half:] - back[1][half:]], axis=0)
        both = []
        for parity in range(2):
            columns = slice(parity * half, (parity + 1) * half)
            both.append(times_table(jnp.concatenate([real[:, columns], imag[:, columns]], axis=1), tables[parity, 1]))
        near_real = jnp.concatenate([both[0][:, :half] + both[1][:, :half], both[0][:, :half] - both[1][:, :half]], axis=1)
        near_imag = jnp.concatenate([both[0][:, half:] + both[1][:, half:], both[0][:, half:] - both[1][:, half:]], axis=1)
        term_real = probe_real * near_real + probe_imag * near_imag
        term_imag = probe_real * near_imag - probe_imag * near_real
        outer[0] = term_real[:half]
        outer[1] = term_imag[:half]
        inner[0] = term_real[half:]
        inner[1] = term_imag[half:]

    for source, target in zip((*earlier, outer), near_outers):
        target[...] = source[...]


class Patch:
    def __init__(self, plan, info, s, patch, slot, down):
        half = patch.shape[1]
        index = (1 if down is None else 1 + down) * (plan.sides + 1)
        row = info[index, 2 * slot]
        col = info[index, 2 * slot + 1]
        self.patch = patch
        self.tile = col // LANES
        self.first = self.tile % 2
        self.from_tile = lax.broadcasted_iota(jnp.int32, (half, LANES), 1) >= col % LANES
        self.rows = None
        if down is not None:
            line = lax.broadcasted_iota(jnp.int32, (half, LANES), 0)
            self.rows = (line >= jnp.where(down > 0, row, 0)) & (line < jnp.where(down > 0, half, row))

    def lines(self, part, place):
        values = self.patch[part, :, lanes(place)]
        return values if self.rows is None else jnp.where(self.rows, values, 0.0)

    def tiles(self, part):
        edge = self.lines(part, self.first)
        middle = self.lines(part, 1 - self.first)
        return jnp.where(self.from_tile, edge, 0.0), middle, jnp.where(self.from_tile, 0.0, edge)

    def add_to(self, canvas):
        for part in range(2):
            for step, values in enumerate(self.tiles(part)):
                canvas[part, :, lanes(self.tile + step)] += values

    def add_tile_to(self, total, tile):
        for step in range(3):

            @pl.when(self.tile + step == tile)
            def _(step=step):
                for part in range(2):
                    total[part] += self.tiles(part)[step]


def early_sum_kernel(plan, slots, info, *rest):
    inner, far, canvas = rest[:slots], rest[slots : 2 * slots - 1], rest[2 * slots - 1]
    s, _ = here()
    canvas[...] = jnp.zeros(canvas.shape, jnp.float32)
    for slot in range(slots):
        Patch(plan, info, s, inner[slot], slot, None).add_to(canvas)
    for slot in range(slots - 1):
        Patch(plan, info, s, far[slot], slot, far_side(s)).add_to(canvas)


def near_sum_kernel(plan, slots, info, early, *rest):
    near, canvas = rest[:slots], rest[slots]
    s, _ = here()
    canvas[...] = early[...]
    for slot in range(slots):
        Patch(plan, info, s, near[slot], slot, -far_side(s)).add_to(canvas)


def last_patch(plan, slots, info, patch):
    s, _ = here()
    return Patch(plan, info, s, patch, slots - 1, far_side(s))


def middle_kernel(plan, slots, layout, pieces, info, early, patch, inverse, *rest):
    refs, (middle, canvas) = rest[:pieces], rest[pieces:]
    _, t = here()
    canvas[...] = early[...]
    last_patch(plan, slots, info, patch).add_to(canvas)
    for step in range(plan.mid_tiles):
        tile = plan.mid_start(t) + step
        where = lanes(step)
        pick_tile(plan, middle.at[:, :, where], layout(refs, t)[0], tile, t)
        middle[:, :, where] -= canvas[:, :, lanes(tile)] * inverse[:, lanes(tile)][None]


def boundary_kernel(plan, layout, pieces, canvas, inverse, _, *rest):
    refs, outs = rest[:pieces], rest[pieces:]
    bases, sums = outs[: plan.sides], outs[plan.sides :]
    _, t = here()
    for base, total, start in zip(bases, sums, plan.pair_starts(t)):
        total[...] = canvas[:, :, lanes(start, 2)]
        for step in range(2):
            where = lanes(step)
            pick_tile(plan, base.at[:, :, where], layout(refs, t)[0], start + step, t)
            base[:, :, where] -= total[:, :, where] * inverse[:, lanes(start + step)][None]


def halo_sum_kernel(plan, slots, info, early, patch, *sums):
    _, t = here()
    last = last_patch(plan, slots, info, patch)
    for total, tile in zip(sums, plan.halo_tiles(t)):
        total[...] = early[:, :, lanes(tile)]
        last.add_tile_to(total, tile)


def last_kernel(plan, slots, layout, pieces, info, early, patch, inverse, _, *rest):
    refs, rest = rest[:pieces], rest[pieces:]
    nearly, bases = rest[0], rest[1 : 1 + plan.sides]
    current, canvas, sem = rest[1 + plan.sides :]
    _, t = here()
    canvas[...] = early[...]
    last_patch(plan, slots, info, patch).add_to(canvas)
    for step in range(plan.own):
        tile = 1 + step
        where = lanes(step)
        pick_tile(plan, current.at[:, :, where], layout(refs, t)[0], tile, t)
        current[:, :, where] -= canvas[:, :, lanes(tile)] * inverse[:, lanes(tile)][None]
    copy = pltpu.make_async_copy(current, nearly, sem)
    copy.start()
    for base, tile in zip(bases, plan.edge_tiles(t)):
        base[...] = current[:, :, lanes(tile - 1)]
    copy.wait()


def edge_kernel(plan, inverse, *rest):
    bases, received = rest[: plan.sides], rest[plan.sides : 2 * plan.sides]
    _, result, sums, sems = rest[2 * plan.sides :]
    _, t = here()
    copies = []
    for side, tile in enumerate(plan.edge_tiles(t)):
        sums[side] = bases[side][...] - received[side][...] * inverse[:, lanes(tile)][None]
        copies.append(pltpu.make_async_copy(sums.at[side], result.at[:, :, lanes(tile - 1)], sems.at[side]))
        copies[-1].start()
    for copy in copies:
        copy.wait()


def call(kernel, outs, scratch, ins, flops=10**5, size=10**4, in_specs=None, out_specs=None, **options):
    result = pl.pallas_call(
        kernel,
        out_shape=outs,
        in_specs=in_specs or [SMEM if value.dtype == jnp.int32 else VMEM for value in ins],
        out_specs=out_specs or jax.tree.map(lambda _: VMEM, outs),
        scratch_shapes=scratch,
        compiler_params=pltpu.CompilerParams(vmem_limit_bytes=VMEM_BYTES),
        cost_estimate=pl.CostEstimate(flops=flops, bytes_accessed=size, transcendentals=0),
        **options,
    )(*ins)
    return list(result) if isinstance(outs, list) else result


def on_device(plan, object_field, probe_field, amplitudes, centres, counts):
    f32 = jnp.float32
    shape = jax.ShapeDtypeStruct
    size = probe_field.shape[1]
    half = size // 2
    slots = amplitudes.shape[2]
    block_rows = object_field.shape[1]
    block_cols = object_field.shape[2]
    assert block_rows == half and block_cols % LANES == 0 and half == LANES
    width = plan.tiles * LANES
    sides = plan.sides
    spots = centres[0, 0]
    counts = counts.reshape(-1)
    own_amps = amplitudes[0, 0]
    tables = jnp.asarray(dft_tables(size))
    order = jnp.asarray(parity_order(size))
    dma = pltpu.SemaphoreType.DMA

    messages = call(
        lambda *refs: edge_message_kernel(plan, *refs),
        [shape((2, half + 8, LANES), f32)] * sides,
        [dma((sides,))],
        [object_field, spots, counts],
        in_specs=[HBM, SMEM, SMEM],
    )
    halos = plan.across(messages)
    far_block = plan.far_rows(object_field)
    rolled, ordered = call(
        prepare_kernel,
        [shape((slots, 2, size, size), f32), shape((slots, size, size), f32)],
        [pltpu.VMEM((2, 2 * size + 8, size), f32)],
        [spots, probe_field, own_amps, order],
    )
    halos, rolled, ordered = lax.optimization_barrier((halos, rolled, ordered))
    near_runs = [shape((2, half, count * LANES), f32) for count in chunks(plan.own)]
    messages = call(
        lambda *refs: halo_message_kernel(plan, *refs),
        [shape((2, half + 16, LANES), f32)] * sides + near_runs,
        [],
        [object_field, spots, counts, *halos],
    )
    passed = messages[:sides]
    far = [far_block] + [plan.far_rows(message) for message in passed]
    near = [plan.near_rows(piece) for piece in messages]
    own = [object_field] + passed
    inverse, info, *inverse_pairs = call(
        lambda *refs: light_kernel(plan, slots, *refs),
        [shape((half, width), f32), shape((3 * (sides + 1), LANES), jnp.int32)] + [shape((half, 2 * LANES), f32)] * sides,
        [
            pltpu.VMEM((2 * size + 8, size), f32),
            pltpu.VMEM((half, width + 2 * plan.own * LANES), f32),
            pltpu.VMEM((3 * (sides + 1), 8, LANES), jnp.int32),
            dma,
        ],
        passed + far[1:] + near[:sides] + [probe_field],
        out_specs=[VMEM, SMEM] + [VMEM] * sides,
    )

    def runs_layout(refs, main, count, side_starts):
        starts = [main] + side_starts
        own, far, near = refs[: 1 + sides], refs[1 + sides : 2 + 2 * sides], refs[2 + 2 * sides :]
        return lay_out(own, starts), lay_out(far, starts), lay_out(near, side_starts + chunk_starts(main, count))

    def first_layout(refs, t):
        return runs_layout(refs, 1, plan.own, plan.halo_tiles(t))

    def later_layout(refs, t):
        return runs_layout(refs, plan.mid_start(t), plan.mid_tiles, plan.pair_starts(t))

    layout = first_layout

    for sweep in range(ITERS):
        pieces = own + far + near
        inner, outer, outer_far = [], [], []
        for slot in range(slots):
            last = slot == slots - 1
            earlier = outer if last else []
            patch = shape((2, half, size), f32)
            outer_part, inner_part, *copies = call(
                lambda *refs, slot=slot, layout=layout, copied=len(earlier): term_kernel(
                    plan, slot, layout, len(pieces), copied, *refs
                ),
                [patch] * (2 + slots * last),
                [pltpu.VMEM((2, size, size), f32), pltpu.VMEM((3, 3, 2, half, LANES), f32)],
                [spots, counts, *pieces, *earlier, rolled, ordered, tables],
            )
            inner.append(inner_part)
            outer.append(outer_part)
            outer_far.append(plan.far_rows(outer_part))
        outer_near = [plan.near_rows(copy) for copy in copies]
        early = call(
            lambda *refs: early_sum_kernel(plan, slots, *refs),
            shape((2, half, width), f32),
            [],
            [info, *inner, *outer_far[:-1]],
        )
        early = call(
            lambda *refs: near_sum_kernel(plan, slots, *refs),
            shape((2, half, width), f32),
            [],
            [info, early, *outer_near],
        )
        if sweep < ITERS - 1:
            middle, total = call(
                lambda *refs, layout=layout: middle_kernel(plan, slots, layout, len(own), *refs),
                [shape((2, half, plan.mid_tiles * LANES), f32), shape((2, half, width), f32)],
                [],
                [info, early, outer_far[-1], inverse, *own],
            )
            far_middle = plan.far_rows(middle)
            boundary = call(
                lambda *refs, layout=layout: boundary_kernel(plan, layout, len(own), *refs),
                [shape((2, half, 2 * LANES), f32)] * (2 * sides),
                [],
                [total, inverse, middle, *own],
                in_specs=[VMEM, VMEM, ANY] + [VMEM] * len(own),
            )
            bases, sums = boundary[:sides], boundary[sides:]
            received = plan.across(sums)
            near_runs = [shape((2, half, count * LANES), f32) for count in chunks(plan.mid_tiles)]
            updated = call(
                lambda *refs: pair_kernel(sides, *refs),
                [shape((2, half, 2 * LANES), f32)] * (2 * sides) + near_runs,
                [],
                [middle, *bases, *received, *inverse_pairs],
            )
            pairs = updated[:sides]
            own = [middle] + pairs
            far = [far_middle] + [plan.far_rows(piece) for piece in pairs]
            near = [plan.near_rows(piece) for piece in updated[sides:]]
            layout = later_layout
    sums = call(
        lambda *refs: halo_sum_kernel(plan, slots, *refs),
        [shape((2, half, LANES), f32)] * sides,
        [],
        [info, early, outer_far[-1]],
    )
    nearly, *bases = call(
        lambda *refs: last_kernel(plan, slots, layout, len(own), *refs),
        [shape((2, half, block_cols), f32)] + [shape((2, half, LANES), f32)] * sides,
        [pltpu.VMEM((2, half, block_cols), f32), pltpu.VMEM((2, half, width), f32), dma],
        [info, early, outer_far[-1], inverse, sums[0], *own],
        in_specs=[SMEM, VMEM, VMEM, VMEM, ANY] + [VMEM] * len(own),
        out_specs=[HBM] + [VMEM] * sides,
    )
    received = plan.across(sums)
    return call(
        lambda *refs: edge_kernel(plan, *refs),
        shape(nearly.shape, f32),
        [pltpu.VMEM((sides, 2, half, LANES), f32), dma((sides,))],
        [inverse, *bases, *received, nearly],
        in_specs=[VMEM] * (1 + 2 * sides) + [HBM],
        out_specs=HBM,
        input_output_aliases={1 + 2 * sides: 0},
    )


def solution(mesh):
    sizes = dict(mesh.shape)

    def per_device(object_field, *rest):
        plan = Plan(sizes["sx"], sizes["sy"], object_field.shape[2])
        return on_device(plan, object_field, *rest)

    return jax.shard_map(
        per_device,
        mesh=mesh,
        in_specs=(
            P(None, "sx", "sy"),
            P(),
            P("sx", "sy", None, None, None),
            P("sx", "sy", None, None),
            P(None, "sy"),
        ),
        out_specs=P(None, "sx", "sy"),
        check_vma=False,
    )
```

```python
import math

import jax
import jax.numpy as jnp
import ml_dtypes
import numpy as np
from jax import lax
from jax.experimental import pallas as pl
from jax.experimental.pallas import tpu as pltpu
from jax.sharding import PartitionSpec as P

ITERS = 2
SMOOTH = 1.0
DAMPING = 1.0
LANES = 128
VMEM_BYTES = 12 * 1024 * 1024

VMEM = pl.BlockSpec(memory_space=pltpu.VMEM)
SMEM = pl.BlockSpec(memory_space=pltpu.SMEM)
HBM = pl.BlockSpec(memory_space=pltpu.HBM)
ANY = pl.BlockSpec(memory_space=pl.ANY)


def split_numpy(table):
    high = table.astype(np.float32).astype(ml_dtypes.bfloat16)
    low = (table - high.astype(np.float64)).astype(ml_dtypes.bfloat16)
    return high, low


def dft_tables(length):
    half = length // 2
    index = np.arange(half)
    tables = []
    for parity in range(2):
        angles = 2.0 * math.pi / length * (index[:, None] * (2 * index[None, :] + parity) % length)
        cosine = np.cos(angles) / math.sqrt(length)
        sine = np.sin(angles) / math.sqrt(length)
        forward = np.block([[cosine, -sine], [sine, cosine]])
        tables.append([split_numpy(forward), split_numpy(forward.T)])
    return np.array(tables, dtype=ml_dtypes.bfloat16)


def parity_order(length):
    half = length // 2
    order = np.zeros((length, length))
    for index in range(length):
        order[index, index % 2 * half + index // 2] = 1.0
    return np.stack([order, order.T]).astype(ml_dtypes.bfloat16)


def split(values):
    high = values.astype(jnp.bfloat16)
    low = (values - high.astype(jnp.float32)).astype(jnp.bfloat16)
    return high, low


def times_table(values, table):
    high, low = split(values)
    left = jnp.concatenate([high, low, high], axis=1)
    right = jnp.concatenate([table[0], table[0], table[1]], axis=0)
    return jnp.dot(left, right, preferred_element_type=jnp.float32)


def table_times(table, values):
    high, low = split(values)
    left = jnp.concatenate([table[0], table[0], table[1]], axis=1)
    right = jnp.concatenate([high, low, high], axis=0)
    return jnp.dot(left, right, preferred_element_type=jnp.float32)


class Plan:
    def __init__(self, sx_size, sy_size, block_cols):
        self.sx_size = sx_size
        self.sy_size = sy_size
        self.own = block_cols // LANES
        self.tiles = self.own + 2
        self.paired = sy_size == 2
        self.sides = 1 if self.paired else 2

    def rights(self, t):
        return [1 - t] if self.paired else [0, 1]

    def pair_starts(self, t):
        return [right * (self.tiles - 2) for right in self.rights(t)]

    def halo_tiles(self, t):
        return [right * (self.tiles - 1) for right in self.rights(t)]

    def edge_tiles(self, t):
        return [1 + right * (self.tiles - 3) for right in self.rights(t)]

    def mid_start(self, t):
        return 1 + t if self.paired else 2

    @property
    def mid_tiles(self):
        return self.tiles - 3 if self.paired else self.tiles - 4

    def across(self, values, axis_name="sy"):
        if self.paired:
            return [lax.ppermute(values[0], axis_name, [(0, 1), (1, 0)])]
        ends = self.sy_size - 1
        return [
            lax.ppermute(values[1], axis_name, [(i, i + 1) for i in range(ends)]),
            lax.ppermute(values[0], axis_name, [(i + 1, i) for i in range(ends)]),
        ]

    def far_rows(self, values):
        return lax.ppermute(values, "sx", self.swaps(1))

    def near_rows(self, values):
        return lax.ppermute(values, "sx", self.swaps(0))

    def swaps(self, first):
        pairs = [(i, i + 1) for i in range(first, self.sx_size - 1, 2)]
        alone = [(i, i) for i in (0, self.sx_size - 1) if first]
        return pairs + [(j, i) for i, j in pairs] + alone

    def outermost(self, s):
        return (s == 0) | (s == self.sx_size - 1)


def far_side(s):
    return 2 * (s % 2) - 1


def lanes(tile, count=1):
    if isinstance(tile, int):
        return pl.ds(tile * LANES, count * LANES)
    return pl.ds(pl.multiple_of(tile * LANES, LANES), count * LANES)


def pick_tile(plan, target, pieces, tile, t):
    rows = target.shape[1]
    if plan.paired:

        @pl.when(tile == (plan.tiles - 1) * t)
        def _():
            target[...] = jnp.zeros(target.shape, jnp.float32)

    for ref, offset, count, start in pieces:

        @pl.when((tile >= start) & (tile < start + count))
        def _(ref=ref, offset=offset, start=start):
            target[...] = ref[:, :rows, lanes(tile - start + offset)]


def lay_out(refs, starts):
    return [(ref, 0, ref.shape[2] // LANES, start) for ref, start in zip(refs, starts)]


def chunks(count):
    return [min(2, count - first) for first in range(0, count, 2)]


def chunk_starts(start, count):
    return [start + 2 * index for index in range(len(chunks(count)))]


def spread(source, targets):
    offset = 0
    for target in targets:
        columns = target.shape[2]
        target[...] = source[:, :, offset : offset + columns]
        offset += columns


def rows_at(ref, start, count):
    offset = start % 8
    values = ref[pl.ds(pl.multiple_of(start - offset, 8), count + 8)]
    return pltpu.roll(values, (count + 8 - offset) % (count + 8), 0)[:count]


def here():
    return lax.axis_index("sx"), lax.axis_index("sy")


def info_rows(centres, count):
    lane = lax.broadcasted_iota(jnp.int32, (8, LANES), 1)
    slots = centres.shape[0]
    values = [centres[slot, axis] for slot in range(slots) for axis in range(2)] + [count]
    line = jnp.zeros((8, LANES), jnp.int32)
    for index, value in enumerate(values):
        line = jnp.where(lane == index, value, line)
    return line.astype(jnp.float32)


def edge_message_kernel(plan, block, centres, counts, *rest):
    messages, sems = rest[: plan.sides], rest[plan.sides]
    s, t = here()
    half = block.shape[1]
    copies = [
        pltpu.make_async_copy(block.at[:, :, lanes(tile - 1)], message.at[:, :half], sems.at[side])
        for side, (message, tile) in enumerate(zip(messages, plan.edge_tiles(t)))
    ]
    for copy in copies:
        copy.start()
    rows = info_rows(centres, counts[s])
    for message in messages:
        message[0, half:] = rows
        message[1, half:] = rows
    for copy in copies:
        copy.wait()


def halo_message_kernel(plan, block, centres, counts, *rest):
    s, _ = here()
    received, messages, near = rest[: plan.sides], rest[plan.sides : 2 * plan.sides], rest[2 * plan.sides :]
    own = info_rows(centres, counts[s])
    for source, message in zip(received, messages):
        rows = source.shape[1]
        message[:, :rows] = source[...]
        message[0, rows:] = own
        message[1, rows:] = own
    spread(block, near)


def pair_kernel(sides, middle, *rest):
    bases, received, inverses, results = (rest[k * sides : (k + 1) * sides] for k in range(4))
    near = rest[4 * sides :]
    for base, other, inverse, result, copy in zip(bases, received, inverses, results, near):
        values = base[...] - other[...] * inverse[...][None]
        result[...] = values
        copy[...] = values
    spread(middle, near[sides:])


def prepare_kernel(centres, probe, amps, order, rolled, ordered, padded):
    size = probe.shape[1]
    half = size // 2
    padded[:, :half] = jnp.zeros((2, half, size), jnp.float32)
    padded[:, half + size :] = jnp.zeros((2, half + 8, size), jnp.float32)
    padded[:, half : half + size] = probe[...]
    for slot in range(amps.shape[0]):
        row = centres[slot, 0]
        col = centres[slot, 1]
        for part in range(2):
            shape = padded.at[part]
            upper = rows_at(shape, half - row, half) + rows_at(shape, half + size - row, half)
            lower = rows_at(shape, size - row, half)
            rolled[slot, part] = pltpu.roll(jnp.concatenate([upper, lower], axis=0), col % size, 1)
        high, low = split(amps[slot])
        across = jnp.dot(
            jnp.concatenate([high, low], axis=1),
            jnp.concatenate([order[0], order[0]], axis=0),
            preferred_element_type=jnp.float32,
        )
        high, low = split(across)
        ordered[slot] = jnp.dot(
            jnp.concatenate([order[1], order[1]], axis=1),
            jnp.concatenate([high, low], axis=0),
            preferred_element_type=jnp.float32,
        )


def light_kernel(plan, slots, *rest):
    groups = [rest[k * plan.sides : (k + 1) * plan.sides] for k in range(3)]
    probe, inverse, info = rest[3 * plan.sides : 3 * plan.sides + 3]
    pairs = rest[3 * plan.sides + 3 : 4 * plan.sides + 3]
    padded, canvas, known, sem = rest[4 * plan.sides + 3 :]
    size = probe.shape[1]
    half = size // 2
    s, t = here()
    upper = s % 2 == 0
    height = half

    def lines(messages):
        return [messages[0][0, height + 8 : height + 16]] + [message[0, height : height + 8] for message in messages]

    own, far, near = (lines(messages) for messages in groups)
    far = [jnp.where(plan.outermost(s), 0.0, line) for line in far]
    for turn in range(plan.sides + 1):
        for kind, line in ((0, jnp.where(upper, far[turn], near[turn])), (1, own[turn]), (2, jnp.where(upper, near[turn], far[turn]))):
            known[kind * (plan.sides + 1) + turn] = line.astype(jnp.int32)
    copy = pltpu.make_async_copy(known.at[:, 0], info, sem)
    copy.start()
    padded[:half] = jnp.zeros((half, size), jnp.float32)
    padded[half + size :] = jnp.zeros((half + 8, size), jnp.float32)
    padded[half : half + size] = probe[0] * probe[0] + probe[1] * probe[1]
    canvas[...] = jnp.zeros(canvas.shape, jnp.float32)
    copy.wait()
    reach = plan.sides + 1
    spare = jnp.zeros((half, LANES), jnp.float32)
    for down in (-1, 0, 1):

        def add(step, carry, down=down):
            turn = step // slots
            slot = step % slots
            over = turn * (1 - 2 * t) if plan.paired else jnp.where(turn == 0, 0, 2 * turn - 3)
            index = (down + 1) * reach + turn

            @pl.when(slot < info[index, 2 * slots])
            def _():
                row = info[index, 2 * slot]
                col = info[index, 2 * slot + 1]
                power = rows_at(padded, size - half * down - row, half)
                shifted = pltpu.roll(jnp.concatenate([power, spare], axis=1), col % LANES, 1)
                first = col // LANES + plan.own * (over + 1)
                canvas[:, lanes(first, 3)] += shifted

            return carry

        lax.fori_loop(0, reach * slots, add, 0)
    result = 1.0 / (canvas[:, lanes(plan.own, plan.tiles)] + DAMPING)
    inverse[...] = result
    for pair, start in zip(pairs, plan.pair_starts(t)):
        pair[...] = inverse[:, lanes(start, 2)]


def term_kernel(plan, slot, layout, pieces, copied, centres, counts, *rest):
    refs, rest = rest[:pieces], rest[pieces:]
    earlier, (probe, amps, tables, outer, inner), rest = rest[:copied], rest[copied : copied + 5], rest[copied + 5 :]
    near_outers, (window, picked) = rest[:-2], rest[-2:]
    size = probe.shape[2]
    half = size // 2
    s, t = here()
    row = centres[slot, 0]
    col = centres[slot, 1]
    alive = slot < counts[s]

    @pl.when(jnp.logical_not(alive))
    def _():
        outer[...] = jnp.zeros(outer.shape, jnp.float32)
        inner[...] = jnp.zeros(inner.shape, jnp.float32)

    @pl.when(alive)
    def _():
        tile = col // LANES
        first = tile % 2
        rest_col = col % LANES
        from_tile = lax.broadcasted_iota(jnp.int32, (half, LANES), 1) >= rest_col
        from_upper = lax.broadcasted_iota(jnp.int32, (half, LANES), 0) >= row
        side = far_side(s)
        own, far, near = layout(refs, t)
        for kind, source in ((1, own), (1 + side, far), (1 - side, near)):
            for step in range(3):
                pick_tile(plan, picked.at[kind, step], source, tile + step, t)

        @pl.when(plan.outermost(s))
        def _():
            picked[1 + side] = jnp.zeros(picked.shape[1:], jnp.float32)

        for part in range(2):
            edge = [jnp.where(from_tile, picked[kind, 0, part], picked[kind, 2, part]) for kind in range(3)]
            window[part, :half, lanes(first)] = jnp.where(from_upper, edge[0], edge[2])
            window[part, half:, lanes(first)] = edge[1]
            window[part, :half, lanes(1 - first)] = jnp.where(from_upper, picked[0, 1, part], picked[2, 1, part])
            window[part, half:, lanes(1 - first)] = picked[1, 1, part]

        probe_real = probe[slot, 0]
        probe_imag = probe[slot, 1]
        exit_real = probe_real * window[0] - probe_imag * window[1]
        exit_imag = probe_real * window[1] + probe_imag * window[0]

        halves = [
            jnp.concatenate([exit_real[:, :half] + sign * exit_real[:, half:], exit_imag[:, :half] + sign * exit_imag[:, half:]], axis=1)
            for sign in (1.0, -1.0)
        ]
        across = [times_table(halves[parity], tables[parity, 0]) for parity in range(2)]
        real = jnp.concatenate([across[0][:, :half], across[1][:, :half]], axis=1)
        imag = jnp.concatenate([across[0][:, half:], across[1][:, half:]], axis=1)
        halves = [
            jnp.concatenate([real[:half] + sign * real[half:], imag[:half] + sign * imag[half:]], axis=0)
            for sign in (1.0, -1.0)
        ]
        back = []
        for parity in range(2):
            pattern = table_times(tables[parity, 1], halves[parity])
            far_real = pattern[:half]
            far_imag = pattern[half:]
            amplitude = amps[slot, parity * half : (parity + 1) * half]
            factor = 1.0 - amplitude * lax.rsqrt(far_real * far_real + far_imag * far_imag + SMOOTH)
            miss = jnp.concatenate([far_real * factor, far_imag * factor], axis=0)
            back.append(table_times(tables[parity, 0], miss))
        real = jnp.concatenate([back[0][:half] + back[1][:half], back[0][:half] - back[1][:half]], axis=0)
        imag = jnp.concatenate([back[0][half:] + back[1][half:], back[0][half:] - back[1][half:]], axis=0)
        both = []
        for parity in range(2):
            columns = slice(parity * half, (parity + 1) * half)
            both.append(times_table(jnp.concatenate([real[:, columns], imag[:, columns]], axis=1), tables[parity, 1]))
        near_real = jnp.concatenate([both[0][:, :half] + both[1][:, :half], both[0][:, :half] - both[1][:, :half]], axis=1)
        near_imag = jnp.concatenate([both[0][:, half:] + both[1][:, half:], both[0][:, half:] - both[1][:, half:]], axis=1)
        term_real = probe_real * near_real + probe_imag * near_imag
        term_imag = probe_real * near_imag - probe_imag * near_real
        outer[0] = term_real[:half]
        outer[1] = term_imag[:half]
        inner[0] = term_real[half:]
        inner[1] = term_imag[half:]

    for source, target in zip((*earlier, outer), near_outers):
        target[...] = source[...]


class Patch:
    def __init__(self, plan, info, s, patch, slot, down, far=False):
        half = patch.shape[1]
        index = (1 if down is None else 1 + down) * (plan.sides + 1)
        row = info[index, 2 * slot]
        col = info[index, 2 * slot + 1]
        self.patch = patch
        self.tile = col // LANES
        self.first = self.tile % 2
        self.from_tile = lax.broadcasted_iota(jnp.int32, (half, LANES), 1) >= col % LANES
        self.rows = None
        if down is not None:
            line = lax.broadcasted_iota(jnp.int32, (half, LANES), 0)
            after = jnp.where(down > 0, half, row)
            if far:
                after = jnp.where(plan.outermost(s), 0, after)
            self.rows = (line >= jnp.where(down > 0, row, 0)) & (line < after)

    def lines(self, part, place):
        values = self.patch[part, :, lanes(place)]
        return values if self.rows is None else jnp.where(self.rows, values, 0.0)

    def tiles(self, part):
        edge = self.lines(part, self.first)
        middle = self.lines(part, 1 - self.first)
        return jnp.where(self.from_tile, edge, 0.0), middle, jnp.where(self.from_tile, 0.0, edge)

    def add_to(self, canvas):
        for part in range(2):
            for step, values in enumerate(self.tiles(part)):
                canvas[part, :, lanes(self.tile + step)] += values

    def add_tile_to(self, total, tile):
        for step in range(3):

            @pl.when(self.tile + step == tile)
            def _(step=step):
                for part in range(2):
                    total[part] += self.tiles(part)[step]


def early_sum_kernel(plan, slots, info, *rest):
    inner, far, canvas = rest[:slots], rest[slots : 2 * slots - 1], rest[2 * slots - 1]
    s, _ = here()
    canvas[...] = jnp.zeros(canvas.shape, jnp.float32)
    for slot in range(slots):
        Patch(plan, info, s, inner[slot], slot, None).add_to(canvas)
    for slot in range(slots - 1):
        Patch(plan, info, s, far[slot], slot, far_side(s), True).add_to(canvas)


def near_sum_kernel(plan, slots, info, early, *rest):
    near, canvas = rest[:slots], rest[slots]
    s, _ = here()
    canvas[...] = early[...]
    for slot in range(slots):
        Patch(plan, info, s, near[slot], slot, -far_side(s)).add_to(canvas)


def last_patch(plan, slots, info, patch):
    s, _ = here()
    return Patch(plan, info, s, patch, slots - 1, far_side(s), True)


def middle_kernel(plan, slots, layout, pieces, info, early, patch, inverse, *rest):
    refs, (middle, canvas) = rest[:pieces], rest[pieces:]
    _, t = here()
    canvas[...] = early[...]
    last_patch(plan, slots, info, patch).add_to(canvas)
    for step in range(plan.mid_tiles):
        tile = plan.mid_start(t) + step
        where = lanes(step)
        pick_tile(plan, middle.at[:, :, where], layout(refs, t)[0], tile, t)
        middle[:, :, where] -= canvas[:, :, lanes(tile)] * inverse[:, lanes(tile)][None]


def boundary_kernel(plan, layout, pieces, canvas, inverse, _, *rest):
    refs, outs = rest[:pieces], rest[pieces:]
    bases, sums = outs[: plan.sides], outs[plan.sides :]
    _, t = here()
    for base, total, start in zip(bases, sums, plan.pair_starts(t)):
        total[...] = canvas[:, :, lanes(start, 2)]
        for step in range(2):
            where = lanes(step)
            pick_tile(plan, base.at[:, :, where], layout(refs, t)[0], start + step, t)
            base[:, :, where] -= total[:, :, where] * inverse[:, lanes(start + step)][None]


def halo_sum_kernel(plan, slots, info, early, patch, *sums):
    _, t = here()
    last = last_patch(plan, slots, info, patch)
    for total, tile in zip(sums, plan.halo_tiles(t)):
        total[...] = early[:, :, lanes(tile)]
        last.add_tile_to(total, tile)


def last_kernel(plan, slots, layout, pieces, info, early, patch, inverse, _, *rest):
    refs, rest = rest[:pieces], rest[pieces:]
    nearly, bases = rest[0], rest[1 : 1 + plan.sides]
    current, canvas, sem = rest[1 + plan.sides :]
    _, t = here()
    canvas[...] = early[...]
    last_patch(plan, slots, info, patch).add_to(canvas)
    for step in range(plan.own):
        tile = 1 + step
        where = lanes(step)
        pick_tile(plan, current.at[:, :, where], layout(refs, t)[0], tile, t)
        current[:, :, where] -= canvas[:, :, lanes(tile)] * inverse[:, lanes(tile)][None]
    copy = pltpu.make_async_copy(current, nearly, sem)
    copy.start()
    for base, tile in zip(bases, plan.edge_tiles(t)):
        base[...] = current[:, :, lanes(tile - 1)]
    copy.wait()


def edge_kernel(plan, inverse, *rest):
    bases, received = rest[: plan.sides], rest[plan.sides : 2 * plan.sides]
    _, result, sums, sems = rest[2 * plan.sides :]
    _, t = here()
    copies = []
    for side, tile in enumerate(plan.edge_tiles(t)):
        sums[side] = bases[side][...] - received[side][...] * inverse[:, lanes(tile)][None]
        copies.append(pltpu.make_async_copy(sums.at[side], result.at[:, :, lanes(tile - 1)], sems.at[side]))
        copies[-1].start()
    for copy in copies:
        copy.wait()


def call(kernel, outs, scratch, ins, flops=10**5, size=10**4, in_specs=None, out_specs=None, **options):
    result = pl.pallas_call(
        kernel,
        out_shape=outs,
        in_specs=in_specs or [SMEM if value.dtype == jnp.int32 else VMEM for value in ins],
        out_specs=out_specs or jax.tree.map(lambda _: VMEM, outs),
        scratch_shapes=scratch,
        compiler_params=pltpu.CompilerParams(vmem_limit_bytes=VMEM_BYTES),
        cost_estimate=pl.CostEstimate(flops=flops, bytes_accessed=size, transcendentals=0),
        **options,
    )(*ins)
    return list(result) if isinstance(outs, list) else result


def on_device(plan, object_field, probe_field, amplitudes, centres, counts):
    f32 = jnp.float32
    shape = jax.ShapeDtypeStruct
    size = probe_field.shape[1]
    half = size // 2
    slots = amplitudes.shape[2]
    block_rows = object_field.shape[1]
    block_cols = object_field.shape[2]
    assert block_rows == half and block_cols % LANES == 0 and half == LANES
    width = plan.tiles * LANES
    sides = plan.sides
    spots = centres[0, 0]
    counts = counts.reshape(-1)
    own_amps = amplitudes[0, 0]
    tables = jnp.asarray(dft_tables(size))
    order = jnp.asarray(parity_order(size))
    dma = pltpu.SemaphoreType.DMA

    messages = call(
        lambda *refs: edge_message_kernel(plan, *refs),
        [shape((2, half + 8, LANES), f32)] * sides,
        [dma((sides,))],
        [object_field, spots, counts],
        in_specs=[HBM, SMEM, SMEM],
    )
    halos = plan.across(messages)
    far_block = plan.far_rows(object_field)
    rolled, ordered = call(
        prepare_kernel,
        [shape((slots, 2, size, size), f32), shape((slots, size, size), f32)],
        [pltpu.VMEM((2, 2 * size + 8, size), f32)],
        [spots, probe_field, own_amps, order],
    )
    halos, rolled, ordered = lax.optimization_barrier((halos, rolled, ordered))
    near_runs = [shape((2, half, count * LANES), f32) for count in chunks(plan.own)]
    messages = call(
        lambda *refs: halo_message_kernel(plan, *refs),
        [shape((2, half + 16, LANES), f32)] * sides + near_runs,
        [],
        [object_field, spots, counts, *halos],
    )
    passed = messages[:sides]
    far = [far_block] + [plan.far_rows(message) for message in passed]
    near = [plan.near_rows(piece) for piece in messages]
    own = [object_field] + passed
    inverse, info, *inverse_pairs = call(
        lambda *refs: light_kernel(plan, slots, *refs),
        [shape((half, width), f32), shape((3 * (sides + 1), LANES), jnp.int32)] + [shape((half, 2 * LANES), f32)] * sides,
        [
            pltpu.VMEM((2 * size + 8, size), f32),
            pltpu.VMEM((half, width + 2 * plan.own * LANES), f32),
            pltpu.VMEM((3 * (sides + 1), 8, LANES), jnp.int32),
            dma,
        ],
        passed + far[1:] + near[:sides] + [probe_field],
        out_specs=[VMEM, SMEM] + [VMEM] * sides,
    )

    def runs_layout(refs, main, count, side_starts):
        starts = [main] + side_starts
        own, far, near = refs[: 1 + sides], refs[1 + sides : 2 + 2 * sides], refs[2 + 2 * sides :]
        return lay_out(own, starts), lay_out(far, starts), lay_out(near, side_starts + chunk_starts(main, count))

    def first_layout(refs, t):
        return runs_layout(refs, 1, plan.own, plan.halo_tiles(t))

    def later_layout(refs, t):
        return runs_layout(refs, plan.mid_start(t), plan.mid_tiles, plan.pair_starts(t))

    layout = first_layout

    for sweep in range(ITERS):
        pieces = own + far + near
        inner, outer, outer_far = [], [], []
        for slot in range(slots):
            last = slot == slots - 1
            earlier = outer if last else []
            patch = shape((2, half, size), f32)
            outer_part, inner_part, *copies = call(
                lambda *refs, slot=slot, layout=layout, copied=len(earlier): term_kernel(
                    plan, slot, layout, len(pieces), copied, *refs
                ),
                [patch] * (2 + slots * last),
                [pltpu.VMEM((2, size, size), f32), pltpu.VMEM((3, 3, 2, half, LANES), f32)],
                [spots, counts, *pieces, *earlier, rolled, ordered, tables],
            )
            inner.append(inner_part)
            outer.append(outer_part)
            outer_far.append(plan.far_rows(outer_part))
        outer_near = [plan.near_rows(copy) for copy in copies]
        early = call(
            lambda *refs: early_sum_kernel(plan, slots, *refs),
            shape((2, half, width), f32),
            [],
            [info, *inner, *outer_far[:-1]],
        )
        early = call(
            lambda *refs: near_sum_kernel(plan, slots, *refs),
            shape((2, half, width), f32),
            [],
            [info, early, *outer_near],
        )
        if sweep < ITERS - 1:
            middle, total = call(
                lambda *refs, layout=layout: middle_kernel(plan, slots, layout, len(own), *refs),
                [shape((2, half, plan.mid_tiles * LANES), f32), shape((2, half, width), f32)],
                [],
                [info, early, outer_far[-1], inverse, *own],
            )
            far_middle = plan.far_rows(middle)
            boundary = call(
                lambda *refs, layout=layout: boundary_kernel(plan, layout, len(own), *refs),
                [shape((2, half, 2 * LANES), f32)] * (2 * sides),
                [],
                [total, inverse, middle, *own],
                in_specs=[VMEM, VMEM, ANY] + [VMEM] * len(own),
            )
            bases, sums = boundary[:sides], boundary[sides:]
            received = plan.across(sums)
            near_runs = [shape((2, half, count * LANES), f32) for count in chunks(plan.mid_tiles)]
            updated = call(
                lambda *refs: pair_kernel(sides, *refs),
                [shape((2, half, 2 * LANES), f32)] * (2 * sides) + near_runs,
                [],
                [middle, *bases, *received, *inverse_pairs],
            )
            pairs = updated[:sides]
            own = [middle] + pairs
            far = [far_middle] + [plan.far_rows(piece) for piece in pairs]
            near = [plan.near_rows(piece) for piece in updated[sides:]]
            layout = later_layout
    sums = call(
        lambda *refs: halo_sum_kernel(plan, slots, *refs),
        [shape((2, half, LANES), f32)] * sides,
        [],
        [info, early, outer_far[-1]],
    )
    nearly, *bases = call(
        lambda *refs: last_kernel(plan, slots, layout, len(own), *refs),
        [shape((2, half, block_cols), f32)] + [shape((2, half, LANES), f32)] * sides,
        [pltpu.VMEM((2, half, block_cols), f32), pltpu.VMEM((2, half, width), f32), dma],
        [info, early, outer_far[-1], inverse, sums[0], *own],
        in_specs=[SMEM, VMEM, VMEM, VMEM, ANY] + [VMEM] * len(own),
        out_specs=[HBM] + [VMEM] * sides,
    )
    received = plan.across(sums)
    return call(
        lambda *refs: edge_kernel(plan, *refs),
        shape(nearly.shape, f32),
        [pltpu.VMEM((sides, 2, half, LANES), f32), dma((sides,))],
        [inverse, *bases, *received, nearly],
        in_specs=[VMEM] * (1 + 2 * sides) + [HBM],
        out_specs=HBM,
        input_output_aliases={1 + 2 * sides: 0},
    )


def solution(mesh):
    sizes = dict(mesh.shape)

    def per_device(object_field, *rest):
        plan = Plan(sizes["sx"], sizes["sy"], object_field.shape[2])
        return on_device(plan, object_field, *rest)

    return jax.shard_map(
        per_device,
        mesh=mesh,
        in_specs=(
            P(None, "sx", "sy"),
            P(),
            P("sx", "sy", None, None, None),
            P("sx", "sy", None, None),
            P(None, "sy"),
        ),
        out_specs=P(None, "sx", "sy"),
        check_vma=False,
    )
```

```python
import math

import jax
import jax.numpy as jnp
import ml_dtypes
import numpy as np
from jax import lax
from jax.experimental import pallas as pl
from jax.experimental.pallas import tpu as pltpu
from jax.sharding import PartitionSpec as P

ITERS = 2
SMOOTH = 1.0
DAMPING = 1.0
LANES = 128
VMEM_BYTES = 12 * 1024 * 1024

VMEM = pl.BlockSpec(memory_space=pltpu.VMEM)
SMEM = pl.BlockSpec(memory_space=pltpu.SMEM)
HBM = pl.BlockSpec(memory_space=pltpu.HBM)
ANY = pl.BlockSpec(memory_space=pl.ANY)


def split_numpy(table):
    high = table.astype(np.float32).astype(ml_dtypes.bfloat16)
    low = (table - high.astype(np.float64)).astype(ml_dtypes.bfloat16)
    return high, low


def dft_tables(length):
    half = length // 2
    index = np.arange(half)
    tables = []
    for parity in range(2):
        angles = 2.0 * math.pi / length * (index[:, None] * (2 * index[None, :] + parity) % length)
        cosine = np.cos(angles) / math.sqrt(length)
        sine = np.sin(angles) / math.sqrt(length)
        forward = np.block([[cosine, -sine], [sine, cosine]])
        tables.append([split_numpy(forward), split_numpy(forward.T)])
    return np.array(tables, dtype=ml_dtypes.bfloat16)


def parity_order(length):
    half = length // 2
    order = np.zeros((length, length))
    for index in range(length):
        order[index, index % 2 * half + index // 2] = 1.0
    return np.stack([order, order.T]).astype(ml_dtypes.bfloat16)


def split(values):
    high = values.astype(jnp.bfloat16)
    low = (values - high.astype(jnp.float32)).astype(jnp.bfloat16)
    return high, low


def times_table(values, table):
    high, low = split(values)
    left = jnp.concatenate([high, low, high], axis=1)
    right = jnp.concatenate([table[0], table[0], table[1]], axis=0)
    return jnp.dot(left, right, preferred_element_type=jnp.float32)


def table_times(table, values):
    high, low = split(values)
    left = jnp.concatenate([table[0], table[0], table[1]], axis=1)
    right = jnp.concatenate([high, low, high], axis=0)
    return jnp.dot(left, right, preferred_element_type=jnp.float32)


class Plan:
    def __init__(self, sx_size, sy_size, block_cols):
        self.sx_size = sx_size
        self.sy_size = sy_size
        self.own = block_cols // LANES
        self.tiles = self.own + 2
        self.paired = sy_size == 2
        self.sides = 1 if self.paired else 2

    def rights(self, t):
        return [1 - t] if self.paired else [0, 1]

    def pair_starts(self, t):
        return [right * (self.tiles - 2) for right in self.rights(t)]

    def halo_tiles(self, t):
        return [right * (self.tiles - 1) for right in self.rights(t)]

    def edge_tiles(self, t):
        return [1 + right * (self.tiles - 3) for right in self.rights(t)]

    def mid_start(self, t):
        return 1 + t if self.paired else 2

    @property
    def mid_tiles(self):
        return self.tiles - 3 if self.paired else self.tiles - 4

    def across(self, values, axis_name="sy"):
        if self.paired:
            return [lax.ppermute(values[0], axis_name, [(0, 1), (1, 0)])]
        ends = self.sy_size - 1
        return [
            lax.ppermute(values[1], axis_name, [(i, i + 1) for i in range(ends)]),
            lax.ppermute(values[0], axis_name, [(i + 1, i) for i in range(ends)]),
        ]

    def far_rows(self, values):
        pairs = [(2 * chip + (chip + 1) % 2, 2 * chip + 2 + (chip + 1) % 2) for chip in range(self.sx_size // 2 - 1)]
        return lax.ppermute(values, "sx", pairs + [(j, i) for i, j in pairs])

    def first_far_rows(self, values):
        pairs = []
        for chip in range(self.sx_size // 2 - 1):
            core = (chip + 1) % 2
            pairs += [(2 * chip + 2, 2 * chip + core), (2 * chip + 1, 2 * chip + 2 + core)]
        return lax.ppermute(values, "sx", pairs)

    def near_rows(self, values):
        return lax.ppermute(values, "sx", [(i, i ^ 1) for i in range(self.sx_size)])

    def swapped_rows(self, values):
        return lax.ppermute(values, "sx", [(i, i ^ 1) for i in range(self.sx_size) if i // 2 % 2])


def far_side(s):
    return 2 * (s % 2) - 1


def lanes(tile, count=1):
    if isinstance(tile, int):
        return pl.ds(tile * LANES, count * LANES)
    return pl.ds(pl.multiple_of(tile * LANES, LANES), count * LANES)


def pick_tile(plan, target, pieces, tile, t):
    rows = target.shape[1]
    if plan.paired:

        @pl.when(tile == (plan.tiles - 1) * t)
        def _():
            target[...] = jnp.zeros(target.shape, jnp.float32)

    for ref, offset, count, start, guard in pieces:
        inside = (tile >= start) & (tile < start + count)
        if inside is False:
            continue

        @pl.when(inside if guard is None else inside & guard)
        def _(ref=ref, offset=offset, start=start):
            target[...] = ref[:, :rows, lanes(tile - start + offset)]


def lay_out(refs, starts, guard=None):
    return [(ref, 0, ref.shape[2] // LANES, start, guard) for ref, start in zip(refs, starts)]


def chunks(count):
    return [min(2, count - first) for first in range(0, count, 2)]


def chunk_starts(start, count):
    return [start + 2 * index for index in range(len(chunks(count)))]


def spread(source, targets):
    offset = 0
    for target in targets:
        columns = target.shape[2]
        target[...] = source[:, :, offset : offset + columns]
        offset += columns


def rows_at(ref, start, count):
    offset = start % 8
    values = ref[pl.ds(pl.multiple_of(start - offset, 8), count + 8)]
    return pltpu.roll(values, (count + 8 - offset) % (count + 8), 0)[:count]


def traded():
    return lax.axis_index("sx") // 2 % 2


def here():
    s = lax.axis_index("sx")
    return s + traded() * (1 - 2 * (s % 2)), lax.axis_index("sy")


def role_centre(centres, near_centres, slot):
    swap = traded() == 1
    return tuple(jnp.where(swap, near_centres[slot, axis], centres[slot, axis]) for axis in range(2))


def info_rows(centres, count):
    lane = lax.broadcasted_iota(jnp.int32, (8, LANES), 1)
    slots = centres.shape[0]
    values = [centres[slot, axis] for slot in range(slots) for axis in range(2)] + [count]
    line = jnp.zeros((8, LANES), jnp.int32)
    for index, value in enumerate(values):
        line = jnp.where(lane == index, value, line)
    return line.astype(jnp.float32)


def edge_message_kernel(plan, block, centres, counts, *rest):
    messages, sems = rest[: plan.sides], rest[plan.sides]
    s, t = lax.axis_index("sx"), lax.axis_index("sy")
    half = block.shape[1]
    copies = [
        pltpu.make_async_copy(block.at[:, :, lanes(tile - 1)], message.at[:, :half], sems.at[side])
        for side, (message, tile) in enumerate(zip(messages, plan.edge_tiles(t)))
    ]
    for copy in copies:
        copy.start()
    rows = info_rows(centres, counts[s])
    for message in messages:
        message[0, half:] = rows
        message[1, half:] = rows
    for copy in copies:
        copy.wait()


def halo_message_kernel(plan, block, centres, counts, *rest):
    s = lax.axis_index("sx")
    received, messages, near = rest[: plan.sides], rest[plan.sides : 2 * plan.sides], rest[2 * plan.sides :]
    own = info_rows(centres, counts[s])
    for source, message in zip(received, messages):
        rows = source.shape[1]
        message[:, :rows] = source[...]
        message[0, rows:] = own
        message[1, rows:] = own
    spread(block, near)


def pair_kernel(sides, middle, *rest):
    bases, received, inverses, results = (rest[k * sides : (k + 1) * sides] for k in range(4))
    near = rest[4 * sides :]
    for base, other, inverse, result, copy in zip(bases, received, inverses, results, near):
        values = base[...] - other[...] * inverse[...][None]
        result[...] = values
        copy[...] = values
    spread(middle, near[sides:])


def token_kernel(_, token):
    token[...] = jnp.zeros(token.shape, jnp.float32)


def prepare_kernel(centres, near_centres, probe, amps, near_amps, order, rolled, ordered, padded):
    size = probe.shape[1]
    half = size // 2
    padded[:, :half] = jnp.zeros((2, half, size), jnp.float32)
    padded[:, half + size :] = jnp.zeros((2, half + 8, size), jnp.float32)
    padded[:, half : half + size] = probe[...]
    for slot in range(amps.shape[0]):
        row, col = role_centre(centres, near_centres, slot)
        for part in range(2):
            shape = padded.at[part]
            upper = rows_at(shape, half - row, half) + rows_at(shape, half + size - row, half)
            lower = rows_at(shape, size - row, half)
            rolled[slot, part] = pltpu.roll(jnp.concatenate([upper, lower], axis=0), col % size, 1)
        high, low = split(jnp.where(traded() == 1, near_amps[slot], amps[slot]))
        across = jnp.dot(
            jnp.concatenate([high, low], axis=1),
            jnp.concatenate([order[0], order[0]], axis=0),
            preferred_element_type=jnp.float32,
        )
        high, low = split(across)
        ordered[slot] = jnp.dot(
            jnp.concatenate([order[1], order[1]], axis=1),
            jnp.concatenate([high, low], axis=0),
            preferred_element_type=jnp.float32,
        )


def light_kernel(plan, slots, *rest):
    groups = [rest[k * plan.sides : (k + 1) * plan.sides] for k in range(3)]
    probe, inverse, info = rest[3 * plan.sides : 3 * plan.sides + 3]
    pairs = rest[3 * plan.sides + 3 : 4 * plan.sides + 3]
    padded, canvas, known, sem = rest[4 * plan.sides + 3 :]
    size = probe.shape[1]
    half = size // 2
    s, t = here()
    upper = s % 2 == 0
    height = half

    def lines(messages):
        return [messages[0][0, height + 8 : height + 16]] + [message[0, height : height + 8] for message in messages]

    swap = traded() == 1
    home, far, other = (lines(messages) for messages in groups)
    own = [jnp.where(swap, theirs, mine) for mine, theirs in zip(home, other)]
    near = [jnp.where(swap, mine, theirs) for mine, theirs in zip(home, other)]
    for turn in range(plan.sides + 1):
        for kind, line in ((0, jnp.where(upper, far[turn], near[turn])), (1, own[turn]), (2, jnp.where(upper, near[turn], far[turn]))):
            known[kind * (plan.sides + 1) + turn] = line.astype(jnp.int32)
    copy = pltpu.make_async_copy(known.at[:, 0], info, sem)
    copy.start()
    padded[:half] = jnp.zeros((half, size), jnp.float32)
    padded[half + size :] = jnp.zeros((half + 8, size), jnp.float32)
    padded[half : half + size] = probe[0] * probe[0] + probe[1] * probe[1]
    canvas[...] = jnp.zeros(canvas.shape, jnp.float32)
    copy.wait()
    reach = plan.sides + 1
    spare = jnp.zeros((half, LANES), jnp.float32)
    for down in (-1, 0, 1):

        def add(step, carry, down=down):
            turn = step // slots
            slot = step % slots
            over = turn * (1 - 2 * t) if plan.paired else jnp.where(turn == 0, 0, 2 * turn - 3)
            index = (down + 1) * reach + turn

            @pl.when(slot < info[index, 2 * slots])
            def _():
                row = info[index, 2 * slot]
                col = info[index, 2 * slot + 1]
                power = rows_at(padded, size - half * down - row, half)
                shifted = pltpu.roll(jnp.concatenate([power, spare], axis=1), col % LANES, 1)
                first = col // LANES + plan.own * (over + 1)
                canvas[:, lanes(first, 3)] += shifted

            return carry

        lax.fori_loop(0, reach * slots, add, 0)
    result = 1.0 / (canvas[:, lanes(plan.own, plan.tiles)] + DAMPING)
    inverse[...] = result
    for pair, start in zip(pairs, plan.pair_starts(t)):
        pair[...] = inverse[:, lanes(start, 2)]


def term_kernel(plan, slot, layout, pieces, copied, centres, near_centres, counts, *rest):
    refs, rest = rest[:pieces], rest[pieces:]
    earlier, (probe, amps, tables, _, outer, inner), rest = rest[:copied], rest[copied : copied + 6], rest[copied + 6 :]
    near_outers, (window, picked) = rest[:-2], rest[-2:]
    size = probe.shape[2]
    half = size // 2
    s, t = here()
    row, col = role_centre(centres, near_centres, slot)
    alive = slot < counts[s]

    @pl.when(jnp.logical_not(alive))
    def _():
        outer[...] = jnp.zeros(outer.shape, jnp.float32)
        inner[...] = jnp.zeros(inner.shape, jnp.float32)

    @pl.when(alive)
    def _():
        tile = col // LANES
        first = tile % 2
        rest_col = col % LANES
        from_tile = lax.broadcasted_iota(jnp.int32, (half, LANES), 1) >= rest_col
        from_upper = lax.broadcasted_iota(jnp.int32, (half, LANES), 0) >= row
        side = far_side(s)
        own, far, near = layout(refs, t)
        for kind, source in ((1, own), (1 + side, far), (1 - side, near)):
            for step in range(3):
                pick_tile(plan, picked.at[kind, step], source, tile + step, t)

        for part in range(2):
            edge = [jnp.where(from_tile, picked[kind, 0, part], picked[kind, 2, part]) for kind in range(3)]
            window[part, :half, lanes(first)] = jnp.where(from_upper, edge[0], edge[2])
            window[part, half:, lanes(first)] = edge[1]
            window[part, :half, lanes(1 - first)] = jnp.where(from_upper, picked[0, 1, part], picked[2, 1, part])
            window[part, half:, lanes(1 - first)] = picked[1, 1, part]

        probe_real = probe[slot, 0]
        probe_imag = probe[slot, 1]
        exit_real = probe_real * window[0] - probe_imag * window[1]
        exit_imag = probe_real * window[1] + probe_imag * window[0]

        halves = [
            jnp.concatenate([exit_real[:, :half] + sign * exit_real[:, half:], exit_imag[:, :half] + sign * exit_imag[:, half:]], axis=1)
            for sign in (1.0, -1.0)
        ]
        across = [times_table(halves[parity], tables[parity, 0]) for parity in range(2)]
        real = jnp.concatenate([across[0][:, :half], across[1][:, :half]], axis=1)
        imag = jnp.concatenate([across[0][:, half:], across[1][:, half:]], axis=1)
        halves = [
            jnp.concatenate([real[:half] + sign * real[half:], imag[:half] + sign * imag[half:]], axis=0)
            for sign in (1.0, -1.0)
        ]
        back = []
        for parity in range(2):
            pattern = table_times(tables[parity, 1], halves[parity])
            far_real = pattern[:half]
            far_imag = pattern[half:]
            amplitude = amps[slot, parity * half : (parity + 1) * half]
            factor = 1.0 - amplitude * lax.rsqrt(far_real * far_real + far_imag * far_imag + SMOOTH)
            miss = jnp.concatenate([far_real * factor, far_imag * factor], axis=0)
            back.append(table_times(tables[parity, 0], miss))
        real = jnp.concatenate([back[0][:half] + back[1][:half], back[0][:half] - back[1][:half]], axis=0)
        imag = jnp.concatenate([back[0][half:] + back[1][half:], back[0][half:] - back[1][half:]], axis=0)
        both = []
        for parity in range(2):
            columns = slice(parity * half, (parity + 1) * half)
            both.append(times_table(jnp.concatenate([real[:, columns], imag[:, columns]], axis=1), tables[parity, 1]))
        near_real = jnp.concatenate([both[0][:, :half] + both[1][:, :half], both[0][:, :half] - both[1][:, :half]], axis=1)
        near_imag = jnp.concatenate([both[0][:, half:] + both[1][:, half:], both[0][:, half:] - both[1][:, half:]], axis=1)
        term_real = probe_real * near_real + probe_imag * near_imag
        term_imag = probe_real * near_imag - probe_imag * near_real
        outer[0] = term_real[:half]
        outer[1] = term_imag[:half]
        inner[0] = term_real[half:]
        inner[1] = term_imag[half:]

    for index, source in enumerate((*earlier, outer)):
        for part in range(2 if near_outers else 0):
            near_outers[2 * index + part][0] = source[part]


class Patch:
    def __init__(self, plan, info, s, patch, slot, down):
        half = (patch[0] if isinstance(patch, (list, tuple)) else patch).shape[1]
        index = (1 if down is None else 1 + down) * (plan.sides + 1)
        row = info[index, 2 * slot]
        col = info[index, 2 * slot + 1]
        self.parts = patch if isinstance(patch, (list, tuple)) else [patch.at[0:1], patch.at[1:2]]
        self.tile = col // LANES
        self.first = self.tile % 2
        self.from_tile = lax.broadcasted_iota(jnp.int32, (half, LANES), 1) >= col % LANES
        self.rows = None
        if down is not None:
            line = lax.broadcasted_iota(jnp.int32, (half, LANES), 0)
            self.rows = (line >= jnp.where(down > 0, row, 0)) & (line < jnp.where(down > 0, half, row))

    def lines(self, part, place):
        values = self.parts[part][0, :, lanes(place)]
        return values if self.rows is None else jnp.where(self.rows, values, 0.0)

    def tiles(self, part):
        edge = self.lines(part, self.first)
        middle = self.lines(part, 1 - self.first)
        return jnp.where(self.from_tile, edge, 0.0), middle, jnp.where(self.from_tile, 0.0, edge)

    def add_to(self, canvas):
        for part in range(2):
            for step, values in enumerate(self.tiles(part)):
                canvas[part, :, lanes(self.tile + step)] += values

    def add_tile_to(self, total, tile):
        for step in range(3):

            @pl.when(self.tile + step == tile)
            def _(step=step):
                for part in range(2):
                    total[part] += self.tiles(part)[step]


def early_sum_kernel(plan, slots, info, *rest):
    inner, far, canvas = rest[:slots], rest[slots : 2 * slots - 1], rest[2 * slots - 1]
    s, _ = here()
    canvas[...] = jnp.zeros(canvas.shape, jnp.float32)
    for slot in range(slots):
        Patch(plan, info, s, inner[slot], slot, None).add_to(canvas)
    for slot in range(slots - 1):
        Patch(plan, info, s, far[slot], slot, far_side(s)).add_to(canvas)


def near_sum_kernel(plan, slots, info, early, *rest):
    near, canvas = rest[: 2 * slots], rest[2 * slots]
    s, _ = here()
    canvas[...] = early[...]
    for slot in range(slots):
        Patch(plan, info, s, near[2 * slot : 2 * slot + 2], slot, -far_side(s)).add_to(canvas)


def last_patch(plan, slots, info, patch):
    s, _ = here()
    return Patch(plan, info, s, patch, slots - 1, far_side(s))


def middle_kernel(plan, slots, layout, pieces, info, early, patch, inverse, *rest):
    refs, (middle, canvas) = rest[:pieces], rest[pieces:]
    _, t = here()
    canvas[...] = early[...]
    last_patch(plan, slots, info, patch).add_to(canvas)
    for step in range(plan.mid_tiles):
        tile = plan.mid_start(t) + step
        where = lanes(step)
        pick_tile(plan, middle.at[:, :, where], layout(refs, t)[0], tile, t)
        middle[:, :, where] -= canvas[:, :, lanes(tile)] * inverse[:, lanes(tile)][None]


def boundary_kernel(plan, layout, pieces, canvas, inverse, _, *rest):
    refs, outs = rest[:pieces], rest[pieces:]
    bases, sums = outs[: plan.sides], outs[plan.sides :]
    _, t = here()
    for base, total, start in zip(bases, sums, plan.pair_starts(t)):
        total[...] = canvas[:, :, lanes(start, 2)]
        for step in range(2):
            where = lanes(step)
            pick_tile(plan, base.at[:, :, where], layout(refs, t)[0], start + step, t)
            base[:, :, where] -= total[:, :, where] * inverse[:, lanes(start + step)][None]


def halo_sum_kernel(plan, slots, info, early, patch, inverse, *sums):
    _, t = here()
    last = last_patch(plan, slots, info, patch)
    for total, tile in zip(sums, plan.halo_tiles(t)):
        total[...] = early[:, :, lanes(tile)]
        last.add_tile_to(total, tile)
        total[...] *= inverse[:, lanes(tile)][None]


def last_kernel(plan, slots, layout, pieces, info, early, patch, inverse, _, *rest):
    refs, nearly, canvas = rest[:pieces], rest[pieces:-1], rest[-1]
    _, t = here()
    canvas[...] = early[...]
    last_patch(plan, slots, info, patch).add_to(canvas)
    for step in range(plan.own):
        tile = 1 + step
        target = nearly[step]
        pick_tile(plan, target, layout(refs, t)[0], tile, t)
        target[...] -= canvas[:, :, lanes(tile)] * inverse[:, lanes(tile)][None]


def home_kernel(plan, runs, *rest):
    nearly, near_nearly = rest[:runs], rest[runs : 2 * runs]
    result, bases, sem = rest[2 * runs], rest[2 * runs + 1 : -1], rest[-1]
    t = lax.axis_index("sy")
    for swap, source in ((0, nearly), (1, near_nearly)):

        @pl.when(traded() == swap)
        def _(source=source):
            copies = [
                pltpu.make_async_copy(run, result.at[:, :, lanes(index)], sem.at[index])
                for index, run in enumerate(source)
            ]
            for copy in copies:
                copy.start()
            for base, tile in zip(bases, plan.edge_tiles(t)):
                pick_tile(plan, base, lay_out(source, range(1, 1 + plan.own)), tile, t)
            for copy in copies:
                copy.wait()


def edge_kernel(plan, *rest):
    bases, received, others = (rest[k * plan.sides : (k + 1) * plan.sides] for k in range(3))
    _, result, sums, sems = rest[3 * plan.sides :]
    t = lax.axis_index("sy")
    copies = []
    for side, tile in enumerate(plan.edge_tiles(t)):
        terms = jnp.where(traded() == 1, others[side][...], received[side][...])
        sums[side] = bases[side][...] - terms
        copies.append(pltpu.make_async_copy(sums.at[side], result.at[:, :, lanes(tile - 1)], sems.at[side]))
        copies[-1].start()
    for copy in copies:
        copy.wait()


def call(kernel, outs, scratch, ins, flops=10**5, size=10**4, in_specs=None, out_specs=None, **options):
    result = pl.pallas_call(
        kernel,
        out_shape=outs,
        in_specs=in_specs or [SMEM if value.dtype == jnp.int32 else VMEM for value in ins],
        out_specs=out_specs or jax.tree.map(lambda _: VMEM, outs),
        scratch_shapes=scratch,
        compiler_params=pltpu.CompilerParams(vmem_limit_bytes=VMEM_BYTES),
        cost_estimate=pl.CostEstimate(flops=flops, bytes_accessed=size, transcendentals=0),
        **options,
    )(*ins)
    return list(result) if isinstance(outs, list) else result


def on_device(plan, object_field, probe_field, amplitudes, centres, counts):
    f32 = jnp.float32
    shape = jax.ShapeDtypeStruct
    size = probe_field.shape[1]
    half = size // 2
    slots = amplitudes.shape[2]
    block_rows = object_field.shape[1]
    block_cols = object_field.shape[2]
    assert block_rows == half and block_cols % LANES == 0 and half == LANES
    width = plan.tiles * LANES
    sides = plan.sides
    spots = centres[0, 0]
    counts = counts.reshape(-1)
    own_amps = amplitudes[0, 0]
    tables = jnp.asarray(dft_tables(size))
    order = jnp.asarray(parity_order(size))
    dma = pltpu.SemaphoreType.DMA

    messages = call(
        lambda *refs: edge_message_kernel(plan, *refs),
        [shape((2, half + 8, LANES), f32)] * sides,
        [dma((sides,))],
        [object_field, spots, counts],
        in_specs=[HBM, SMEM, SMEM],
    )
    halos = plan.across(messages)
    far_block = plan.first_far_rows(object_field)
    near_spots = plan.near_rows(spots)
    near_amps = plan.near_rows(own_amps)
    rolled, ordered = call(
        prepare_kernel,
        [shape((slots, 2, size, size), f32), shape((slots, size, size), f32)],
        [pltpu.VMEM((2, 2 * size + 8, size), f32)],
        [spots, near_spots, probe_field, own_amps, near_amps, order],
    )
    halos, rolled, ordered = lax.optimization_barrier((halos, rolled, ordered))
    near_runs = [shape((2, half, count * LANES), f32) for count in chunks(plan.own)]
    messages = call(
        lambda *refs: halo_message_kernel(plan, *refs),
        [shape((2, half + 16, LANES), f32)] * sides + near_runs,
        [],
        [object_field, spots, counts, *halos],
    )
    passed = messages[:sides]
    far = [far_block] + [plan.first_far_rows(message) for message in passed]
    near = [plan.near_rows(piece) for piece in messages]
    own = [object_field] + passed
    inverse, info, *inverse_pairs = call(
        lambda *refs: light_kernel(plan, slots, *refs),
        [shape((half, width), f32), shape((3 * (sides + 1), LANES), jnp.int32)] + [shape((half, 2 * LANES), f32)] * sides,
        [
            pltpu.VMEM((2 * size + 8, size), f32),
            pltpu.VMEM((half, width + 2 * plan.own * LANES), f32),
            pltpu.VMEM((3 * (sides + 1), 8, LANES), jnp.int32),
            dma,
        ],
        passed + far[1:] + near[:sides] + [probe_field],
        out_specs=[VMEM, SMEM] + [VMEM] * sides,
    )

    def runs(refs, main, count, side_starts):
        starts = [main] + side_starts
        own, far, near = refs[: 1 + sides], refs[1 + sides : 2 + 2 * sides], refs[2 + 2 * sides :]
        return (own, starts), (far, starts), (near, side_starts + chunk_starts(main, count))

    def first_layout(refs, t):
        home, far, other = runs(refs, 1, plan.own, plan.halo_tiles(t))
        stay, swap = traded() == 0, traded() == 1
        own = lay_out(*home, stay) + lay_out(*other, swap)
        return own, lay_out(*far), lay_out(*other, stay) + lay_out(*home, swap)

    def later_layout(refs, t):
        return tuple(lay_out(*group) for group in runs(refs, plan.mid_start(t), plan.mid_tiles, plan.pair_starts(t)))

    layout = first_layout
    token = spots

    for sweep in range(ITERS):
        pieces = own + far + near
        inner, outer, outer_far = [], [], []
        for slot in range(slots):
            last = slot == slots - 1
            earlier = outer if last else []
            patch = shape((2, half, size), f32)
            outer_part, inner_part, *copies = call(
                lambda *refs, slot=slot, layout=layout, copied=len(earlier): term_kernel(
                    plan, slot, layout, len(pieces), copied, *refs
                ),
                [patch] * 2 + [shape((1, half, size), f32)] * (2 * slots * last),
                [pltpu.VMEM((2, size, size), f32), pltpu.VMEM((3, 3, 2, half, LANES), f32)],
                [spots, near_spots, counts, *pieces, *earlier, rolled, ordered, tables, token],
            )
            inner.append(inner_part)
            outer.append(outer_part)
            outer_far.append(plan.far_rows(outer_part))
        outer_near = [plan.near_rows(copy) for copy in copies]
        early = call(
            lambda *refs: early_sum_kernel(plan, slots, *refs),
            shape((2, half, width), f32),
            [],
            [info, *inner, *outer_far[:-1]],
        )
        early = call(
            lambda *refs: near_sum_kernel(plan, slots, *refs),
            shape((2, half, width), f32),
            [],
            [info, early, *outer_near],
        )
        if sweep < ITERS - 1:
            middle, total = call(
                lambda *refs, layout=layout: middle_kernel(plan, slots, layout, len(pieces), *refs),
                [shape((2, half, plan.mid_tiles * LANES), f32), shape((2, half, width), f32)],
                [],
                [info, early, outer_far[-1], inverse, *pieces],
            )
            far_middle = plan.far_rows(middle)
            boundary = call(
                lambda *refs, layout=layout: boundary_kernel(plan, layout, len(pieces), *refs),
                [shape((2, half, 2 * LANES), f32)] * (2 * sides),
                [],
                [total, inverse, middle, *pieces],
                in_specs=[VMEM, VMEM, ANY] + [VMEM] * len(pieces),
            )
            bases, sums = boundary[:sides], boundary[sides:]
            received = plan.across(sums)
            near_runs = [shape((2, half, count * LANES), f32) for count in chunks(plan.mid_tiles)]
            updated = call(
                lambda *refs: pair_kernel(sides, *refs),
                [shape((2, half, 2 * LANES), f32)] * (2 * sides) + near_runs,
                [],
                [middle, *bases, *received, *inverse_pairs],
            )
            pairs = updated[:sides]
            own = [middle] + pairs
            far = [far_middle] + [plan.far_rows(piece) for piece in pairs]
            near = [plan.near_rows(piece) for piece in updated[sides:]]
            layout = later_layout
            token = call(
                token_kernel,
                shape((8, LANES), f32),
                [],
                [far_middle],
                in_specs=[ANY],
                flops=10**11,
            )
    sums = call(
        lambda *refs: halo_sum_kernel(plan, slots, *refs),
        [shape((2, half, LANES), f32)] * sides,
        [],
        [info, early, outer_far[-1], inverse],
    )
    received = plan.across(sums)
    nearly = call(
        lambda *refs: last_kernel(plan, slots, layout, len(pieces), *refs),
        [shape((2, half, LANES), f32)] * plan.own,
        [pltpu.VMEM((2, half, width), f32)],
        [info, early, outer_far[-1], inverse, sums[0], *pieces],
        in_specs=[SMEM, VMEM, VMEM, VMEM, ANY] + [VMEM] * len(pieces),
    )
    others = [plan.swapped_rows(terms) for terms in received]
    home, *bases = call(
        lambda *refs: home_kernel(plan, len(nearly), *refs),
        [shape((2, half, block_cols), f32)] + [shape((2, half, LANES), f32)] * sides,
        [dma((len(nearly),))],
        [*nearly, *[plan.swapped_rows(run) for run in nearly]],
        out_specs=[HBM] + [VMEM] * sides,
    )
    return call(
        lambda *refs: edge_kernel(plan, *refs),
        shape(home.shape, f32),
        [pltpu.VMEM((sides, 2, half, LANES), f32), dma((sides,))],
        [*bases, *received, *others, home],
        in_specs=[VMEM] * (3 * sides) + [HBM],
        out_specs=HBM,
        input_output_aliases={3 * sides: 0},
    )


def solution(mesh):
    sizes = dict(mesh.shape)

    def per_device(object_field, *rest):
        plan = Plan(sizes["sx"], sizes["sy"], object_field.shape[2])
        return on_device(plan, object_field, *rest)

    return jax.shard_map(
        per_device,
        mesh=mesh,
        in_specs=(
            P(None, "sx", "sy"),
            P(),
            P("sx", "sy", None, None, None),
            P("sx", "sy", None, None),
            P(None, "sy"),
        ),
        out_specs=P(None, "sx", "sy"),
        check_vma=False,
    )
```

```python
import math

import jax
import jax.numpy as jnp
import ml_dtypes
import numpy as np
from jax import lax
from jax.experimental import pallas as pl
from jax.experimental.pallas import tpu as pltpu
from jax.sharding import PartitionSpec as P

ITERS = 2
SMOOTH = 1.0
DAMPING = 1.0
LANES = 128
VMEM_BYTES = 12 * 1024 * 1024

VMEM = pl.BlockSpec(memory_space=pltpu.VMEM)
SMEM = pl.BlockSpec(memory_space=pltpu.SMEM)
HBM = pl.BlockSpec(memory_space=pltpu.HBM)
ANY = pl.BlockSpec(memory_space=pl.ANY)


def split_numpy(table):
    high = table.astype(np.float32).astype(ml_dtypes.bfloat16)
    low = (table - high.astype(np.float64)).astype(ml_dtypes.bfloat16)
    return high, low


def dft_tables(length):
    half = length // 2
    index = np.arange(half)
    tables = []
    for parity in range(2):
        angles = 2.0 * math.pi / length * (index[:, None] * (2 * index[None, :] + parity) % length)
        cosine = np.cos(angles) / math.sqrt(length)
        sine = np.sin(angles) / math.sqrt(length)
        forward = np.block([[cosine, -sine], [sine, cosine]])
        tables.append([split_numpy(forward), split_numpy(forward.T)])
    return np.array(tables, dtype=ml_dtypes.bfloat16)


def parity_order(length):
    half = length // 2
    order = np.zeros((length, length))
    for index in range(length):
        order[index, index % 2 * half + index // 2] = 1.0
    return np.stack([order, order.T]).astype(ml_dtypes.bfloat16)


def split(values):
    high = values.astype(jnp.bfloat16)
    low = (values - high.astype(jnp.float32)).astype(jnp.bfloat16)
    return high, low


def times_table(values, table):
    high, low = split(values)
    left = jnp.concatenate([high, low, high], axis=1)
    right = jnp.concatenate([table[0], table[0], table[1]], axis=0)
    return jnp.dot(left, right, preferred_element_type=jnp.float32)


def table_times(table, values):
    high, low = split(values)
    left = jnp.concatenate([table[0], table[0], table[1]], axis=1)
    right = jnp.concatenate([high, low, high], axis=0)
    return jnp.dot(left, right, preferred_element_type=jnp.float32)


class Plan:
    def __init__(self, sx_size, sy_size, block_cols):
        self.sx_size = sx_size
        self.sy_size = sy_size
        self.own = block_cols // LANES
        self.tiles = self.own + 2
        self.paired = sy_size == 2
        self.sides = 1 if self.paired else 2

    def rights(self, t):
        return [1 - t] if self.paired else [0, 1]

    def pair_starts(self, t):
        return [right * (self.tiles - 2) for right in self.rights(t)]

    def halo_tiles(self, t):
        return [right * (self.tiles - 1) for right in self.rights(t)]

    def edge_tiles(self, t):
        return [1 + right * (self.tiles - 3) for right in self.rights(t)]

    def mid_start(self, t):
        return 1 + t if self.paired else 2

    @property
    def mid_tiles(self):
        return self.tiles - 3 if self.paired else self.tiles - 4

    def across(self, values, axis_name="sy"):
        if self.paired:
            return [lax.ppermute(values[0], axis_name, [(0, 1), (1, 0)])]
        ends = self.sy_size - 1
        return [
            lax.ppermute(values[1], axis_name, [(i, i + 1) for i in range(ends)]),
            lax.ppermute(values[0], axis_name, [(i + 1, i) for i in range(ends)]),
        ]

    def far_rows(self, values):
        return lax.ppermute(values, "sx", self.swaps(1))

    def near_rows(self, values):
        return lax.ppermute(values, "sx", self.swaps(0))

    def swaps(self, first):
        pairs = [(i, i + 1) for i in range(first, self.sx_size - 1, 2)]
        pairs += [(0, self.sx_size - 1)] * first
        return pairs + [(j, i) for i, j in pairs]

    def outermost(self, s):
        return (s == 0) | (s == self.sx_size - 1)


def far_side(s):
    return 2 * (s % 2) - 1


def lanes(tile, count=1):
    if isinstance(tile, int):
        return pl.ds(tile * LANES, count * LANES)
    return pl.ds(pl.multiple_of(tile * LANES, LANES), count * LANES)


def pick_tile(plan, target, pieces, tile, t):
    rows = target.shape[1]
    if plan.paired:

        @pl.when(tile == (plan.tiles - 1) * t)
        def _():
            target[...] = jnp.zeros(target.shape, jnp.float32)

    for ref, offset, count, start in pieces:

        @pl.when((tile >= start) & (tile < start + count))
        def _(ref=ref, offset=offset, start=start):
            target[...] = ref[:, :rows, lanes(tile - start + offset)]


def lay_out(refs, starts):
    return [(ref, 0, ref.shape[2] // LANES, start) for ref, start in zip(refs, starts)]


def chunks(count):
    return [min(2, count - first) for first in range(0, count, 2)]


def chunk_starts(start, count):
    return [start + 2 * index for index in range(len(chunks(count)))]


def spread(source, targets):
    offset = 0
    for target in targets:
        columns = target.shape[2]
        target[...] = source[:, :, offset : offset + columns]
        offset += columns


def rows_at(ref, start, count):
    offset = start % 8
    values = ref[pl.ds(pl.multiple_of(start - offset, 8), count + 8)]
    return pltpu.roll(values, (count + 8 - offset) % (count + 8), 0)[:count]


def here():
    return lax.axis_index("sx"), lax.axis_index("sy")


def info_rows(centres, count):
    lane = lax.broadcasted_iota(jnp.int32, (8, LANES), 1)
    slots = centres.shape[0]
    values = [centres[slot, axis] for slot in range(slots) for axis in range(2)] + [count]
    line = jnp.zeros((8, LANES), jnp.int32)
    for index, value in enumerate(values):
        line = jnp.where(lane == index, value, line)
    return line.astype(jnp.float32)


def edge_message_kernel(plan, block, centres, counts, *rest):
    messages, sems = rest[: plan.sides], rest[plan.sides]
    s, t = here()
    half = block.shape[1]
    copies = [
        pltpu.make_async_copy(block.at[:, :, lanes(tile - 1)], message.at[:, :half], sems.at[side])
        for side, (message, tile) in enumerate(zip(messages, plan.edge_tiles(t)))
    ]
    for copy in copies:
        copy.start()
    rows = info_rows(centres, counts[s])
    for message in messages:
        message[0, half:] = rows
        message[1, half:] = rows
    for copy in copies:
        copy.wait()


def halo_message_kernel(plan, block, centres, counts, *rest):
    s, _ = here()
    received, messages, near = rest[: plan.sides], rest[plan.sides : 2 * plan.sides], rest[2 * plan.sides :]
    own = info_rows(centres, counts[s])
    for source, message in zip(received, messages):
        rows = source.shape[1]
        message[:, :rows] = source[...]
        message[0, rows:] = own
        message[1, rows:] = own
    spread(block, near)


def pair_kernel(sides, middle, *rest):
    bases, received, inverses, results = (rest[k * sides : (k + 1) * sides] for k in range(4))
    near = rest[4 * sides :]
    for base, other, inverse, result, copy in zip(bases, received, inverses, results, near):
        values = base[...] - other[...] * inverse[...][None]
        result[...] = values
        copy[...] = values
    spread(middle, near[sides:])


def token_kernel(_, token):
    token[...] = jnp.zeros(token.shape, jnp.float32)


def prepare_kernel(centres, probe, amps, order, rolled, ordered, padded):
    size = probe.shape[1]
    half = size // 2
    padded[:, :half] = jnp.zeros((2, half, size), jnp.float32)
    padded[:, half + size :] = jnp.zeros((2, half + 8, size), jnp.float32)
    padded[:, half : half + size] = probe[...]
    for slot in range(amps.shape[0]):
        row = centres[slot, 0]
        col = centres[slot, 1]
        for part in range(2):
            shape = padded.at[part]
            upper = rows_at(shape, half - row, half) + rows_at(shape, half + size - row, half)
            lower = rows_at(shape, size - row, half)
            rolled[slot, part] = pltpu.roll(jnp.concatenate([upper, lower], axis=0), col % size, 1)
        high, low = split(amps[slot])
        across = jnp.dot(
            jnp.concatenate([high, low], axis=1),
            jnp.concatenate([order[0], order[0]], axis=0),
            preferred_element_type=jnp.float32,
        )
        high, low = split(across)
        ordered[slot] = jnp.dot(
            jnp.concatenate([order[1], order[1]], axis=1),
            jnp.concatenate([high, low], axis=0),
            preferred_element_type=jnp.float32,
        )


def light_kernel(plan, slots, *rest):
    groups = [rest[k * plan.sides : (k + 1) * plan.sides] for k in range(3)]
    probe, inverse, info = rest[3 * plan.sides : 3 * plan.sides + 3]
    pairs = rest[3 * plan.sides + 3 : 4 * plan.sides + 3]
    padded, canvas, known, sem = rest[4 * plan.sides + 3 :]
    size = probe.shape[1]
    half = size // 2
    s, t = here()
    upper = s % 2 == 0
    height = half

    def lines(messages):
        return [messages[0][0, height + 8 : height + 16]] + [message[0, height : height + 8] for message in messages]

    own, far, near = (lines(messages) for messages in groups)
    far = [jnp.where(plan.outermost(s), 0.0, line) for line in far]
    for turn in range(plan.sides + 1):
        for kind, line in ((0, jnp.where(upper, far[turn], near[turn])), (1, own[turn]), (2, jnp.where(upper, near[turn], far[turn]))):
            known[kind * (plan.sides + 1) + turn] = line.astype(jnp.int32)
    copy = pltpu.make_async_copy(known.at[:, 0], info, sem)
    copy.start()
    padded[:half] = jnp.zeros((half, size), jnp.float32)
    padded[half + size :] = jnp.zeros((half + 8, size), jnp.float32)
    padded[half : half + size] = probe[0] * probe[0] + probe[1] * probe[1]
    canvas[...] = jnp.zeros(canvas.shape, jnp.float32)
    copy.wait()
    reach = plan.sides + 1
    spare = jnp.zeros((half, LANES), jnp.float32)
    for down in (-1, 0, 1):

        def add(step, carry, down=down):
            turn = step // slots
            slot = step % slots
            over = turn * (1 - 2 * t) if plan.paired else jnp.where(turn == 0, 0, 2 * turn - 3)
            index = (down + 1) * reach + turn

            @pl.when(slot < info[index, 2 * slots])
            def _():
                row = info[index, 2 * slot]
                col = info[index, 2 * slot + 1]
                power = rows_at(padded, size - half * down - row, half)
                shifted = pltpu.roll(jnp.concatenate([power, spare], axis=1), col % LANES, 1)
                first = col // LANES + plan.own * (over + 1)
                canvas[:, lanes(first, 3)] += shifted

            return carry

        lax.fori_loop(0, reach * slots, add, 0)
    result = 1.0 / (canvas[:, lanes(plan.own, plan.tiles)] + DAMPING)
    inverse[...] = result
    for pair, start in zip(pairs, plan.pair_starts(t)):
        pair[...] = inverse[:, lanes(start, 2)]


def term_kernel(plan, slot, layout, pieces, copied, centres, counts, *rest):
    refs, rest = rest[:pieces], rest[pieces:]
    earlier, (probe, amps, tables, _, outer, inner), rest = rest[:copied], rest[copied : copied + 6], rest[copied + 6 :]
    near_outers, (window, picked) = rest[:-2], rest[-2:]
    size = probe.shape[2]
    half = size // 2
    s, t = here()
    row = centres[slot, 0]
    col = centres[slot, 1]
    alive = slot < counts[s]

    @pl.when(jnp.logical_not(alive))
    def _():
        outer[...] = jnp.zeros(outer.shape, jnp.float32)
        inner[...] = jnp.zeros(inner.shape, jnp.float32)

    @pl.when(alive)
    def _():
        tile = col // LANES
        first = tile % 2
        rest_col = col % LANES
        from_tile = lax.broadcasted_iota(jnp.int32, (half, LANES), 1) >= rest_col
        from_upper = lax.broadcasted_iota(jnp.int32, (half, LANES), 0) >= row
        side = far_side(s)
        own, far, near = layout(refs, t)
        for kind, source in ((1, own), (1 + side, far), (1 - side, near)):
            for step in range(3):
                pick_tile(plan, picked.at[kind, step], source, tile + step, t)

        @pl.when(plan.outermost(s))
        def _():
            picked[1 + side] = jnp.zeros(picked.shape[1:], jnp.float32)

        for part in range(2):
            edge = [jnp.where(from_tile, picked[kind, 0, part], picked[kind, 2, part]) for kind in range(3)]
            window[part, :half, lanes(first)] = jnp.where(from_upper, edge[0], edge[2])
            window[part, half:, lanes(first)] = edge[1]
            window[part, :half, lanes(1 - first)] = jnp.where(from_upper, picked[0, 1, part], picked[2, 1, part])
            window[part, half:, lanes(1 - first)] = picked[1, 1, part]

        probe_real = probe[slot, 0]
        probe_imag = probe[slot, 1]
        exit_real = probe_real * window[0] - probe_imag * window[1]
        exit_imag = probe_real * window[1] + probe_imag * window[0]

        halves = [
            jnp.concatenate([exit_real[:, :half] + sign * exit_real[:, half:], exit_imag[:, :half] + sign * exit_imag[:, half:]], axis=1)
            for sign in (1.0, -1.0)
        ]
        across = [times_table(halves[parity], tables[parity, 0]) for parity in range(2)]
        real = jnp.concatenate([across[0][:, :half], across[1][:, :half]], axis=1)
        imag = jnp.concatenate([across[0][:, half:], across[1][:, half:]], axis=1)
        halves = [
            jnp.concatenate([real[:half] + sign * real[half:], imag[:half] + sign * imag[half:]], axis=0)
            for sign in (1.0, -1.0)
        ]
        back = []
        for parity in range(2):
            pattern = table_times(tables[parity, 1], halves[parity])
            far_real = pattern[:half]
            far_imag = pattern[half:]
            amplitude = amps[slot, parity * half : (parity + 1) * half]
            factor = 1.0 - amplitude * lax.rsqrt(far_real * far_real + far_imag * far_imag + SMOOTH)
            miss = jnp.concatenate([far_real * factor, far_imag * factor], axis=0)
            back.append(table_times(tables[parity, 0], miss))
        real = jnp.concatenate([back[0][:half] + back[1][:half], back[0][:half] - back[1][:half]], axis=0)
        imag = jnp.concatenate([back[0][half:] + back[1][half:], back[0][half:] - back[1][half:]], axis=0)
        both = []
        for parity in range(2):
            columns = slice(parity * half, (parity + 1) * half)
            both.append(times_table(jnp.concatenate([real[:, columns], imag[:, columns]], axis=1), tables[parity, 1]))
        near_real = jnp.concatenate([both[0][:, :half] + both[1][:, :half], both[0][:, :half] - both[1][:, :half]], axis=1)
        near_imag = jnp.concatenate([both[0][:, half:] + both[1][:, half:], both[0][:, half:] - both[1][:, half:]], axis=1)
        term_real = probe_real * near_real + probe_imag * near_imag
        term_imag = probe_real * near_imag - probe_imag * near_real
        outer[0] = term_real[:half]
        outer[1] = term_imag[:half]
        inner[0] = term_real[half:]
        inner[1] = term_imag[half:]

    for index, source in enumerate((*earlier, outer)):
        for part in range(2 if near_outers else 0):
            near_outers[2 * index + part][0] = source[part]


class Patch:
    def __init__(self, plan, info, s, patch, slot, down, far=False):
        half = (patch[0] if isinstance(patch, (list, tuple)) else patch).shape[1]
        index = (1 if down is None else 1 + down) * (plan.sides + 1)
        row = info[index, 2 * slot]
        col = info[index, 2 * slot + 1]
        self.parts = patch if isinstance(patch, (list, tuple)) else [patch.at[0:1], patch.at[1:2]]
        self.tile = col // LANES
        self.first = self.tile % 2
        self.from_tile = lax.broadcasted_iota(jnp.int32, (half, LANES), 1) >= col % LANES
        self.rows = None
        if down is not None:
            line = lax.broadcasted_iota(jnp.int32, (half, LANES), 0)
            after = jnp.where(down > 0, half, row)
            if far:
                after = jnp.where(plan.outermost(s), 0, after)
            self.rows = (line >= jnp.where(down > 0, row, 0)) & (line < after)

    def lines(self, part, place):
        values = self.parts[part][0, :, lanes(place)]
        return values if self.rows is None else jnp.where(self.rows, values, 0.0)

    def tiles(self, part):
        edge = self.lines(part, self.first)
        middle = self.lines(part, 1 - self.first)
        return jnp.where(self.from_tile, edge, 0.0), middle, jnp.where(self.from_tile, 0.0, edge)

    def add_to(self, canvas):
        for part in range(2):
            for step, values in enumerate(self.tiles(part)):
                canvas[part, :, lanes(self.tile + step)] += values

    def add_tile_to(self, total, tile):
        for step in range(3):

            @pl.when(self.tile + step == tile)
            def _(step=step):
                for part in range(2):
                    total[part] += self.tiles(part)[step]


def early_sum_kernel(plan, slots, info, *rest):
    inner, far, canvas = rest[:slots], rest[slots : 2 * slots - 1], rest[2 * slots - 1]
    s, _ = here()
    canvas[...] = jnp.zeros(canvas.shape, jnp.float32)
    for slot in range(slots):
        Patch(plan, info, s, inner[slot], slot, None).add_to(canvas)
    for slot in range(slots - 1):
        Patch(plan, info, s, far[slot], slot, far_side(s), True).add_to(canvas)


def near_sum_kernel(plan, slots, info, early, *rest):
    near, canvas = rest[: 2 * slots], rest[2 * slots]
    s, _ = here()
    canvas[...] = early[...]
    for slot in range(slots):
        Patch(plan, info, s, near[2 * slot : 2 * slot + 2], slot, -far_side(s)).add_to(canvas)


def last_patch(plan, slots, info, patch):
    s, _ = here()
    return Patch(plan, info, s, patch, slots - 1, far_side(s), True)


def middle_kernel(plan, slots, layout, pieces, info, early, patch, inverse, *rest):
    refs, (middle, canvas) = rest[:pieces], rest[pieces:]
    _, t = here()
    canvas[...] = early[...]
    last_patch(plan, slots, info, patch).add_to(canvas)
    for step in range(plan.mid_tiles):
        tile = plan.mid_start(t) + step
        where = lanes(step)
        pick_tile(plan, middle.at[:, :, where], layout(refs, t)[0], tile, t)
        middle[:, :, where] -= canvas[:, :, lanes(tile)] * inverse[:, lanes(tile)][None]


def boundary_kernel(plan, layout, pieces, canvas, inverse, _, *rest):
    refs, outs = rest[:pieces], rest[pieces:]
    bases, sums = outs[: plan.sides], outs[plan.sides :]
    _, t = here()
    for base, total, start in zip(bases, sums, plan.pair_starts(t)):
        total[...] = canvas[:, :, lanes(start, 2)]
        for step in range(2):
            where = lanes(step)
            pick_tile(plan, base.at[:, :, where], layout(refs, t)[0], start + step, t)
            base[:, :, where] -= total[:, :, where] * inverse[:, lanes(start + step)][None]


def halo_sum_kernel(plan, slots, info, early, patch, *sums):
    _, t = here()
    last = last_patch(plan, slots, info, patch)
    for total, tile in zip(sums, plan.halo_tiles(t)):
        total[...] = early[:, :, lanes(tile)]
        last.add_tile_to(total, tile)


def last_kernel(plan, slots, layout, pieces, info, early, patch, inverse, _, *rest):
    refs, rest = rest[:pieces], rest[pieces:]
    nearly, bases = rest[0], rest[1 : 1 + plan.sides]
    current, canvas, sem = rest[1 + plan.sides :]
    _, t = here()
    canvas[...] = early[...]
    last_patch(plan, slots, info, patch).add_to(canvas)
    for step in range(plan.own):
        tile = 1 + step
        where = lanes(step)
        pick_tile(plan, current.at[:, :, where], layout(refs, t)[0], tile, t)
        current[:, :, where] -= canvas[:, :, lanes(tile)] * inverse[:, lanes(tile)][None]
    copy = pltpu.make_async_copy(current, nearly, sem)
    copy.start()
    for base, tile in zip(bases, plan.edge_tiles(t)):
        base[...] = current[:, :, lanes(tile - 1)]
    copy.wait()


def edge_kernel(plan, inverse, *rest):
    bases, received = rest[: plan.sides], rest[plan.sides : 2 * plan.sides]
    _, result, sums, sems = rest[2 * plan.sides :]
    _, t = here()
    copies = []
    for side, tile in enumerate(plan.edge_tiles(t)):
        sums[side] = bases[side][...] - received[side][...] * inverse[:, lanes(tile)][None]
        copies.append(pltpu.make_async_copy(sums.at[side], result.at[:, :, lanes(tile - 1)], sems.at[side]))
        copies[-1].start()
    for copy in copies:
        copy.wait()


def call(kernel, outs, scratch, ins, flops=10**5, size=10**4, in_specs=None, out_specs=None, **options):
    result = pl.pallas_call(
        kernel,
        out_shape=outs,
        in_specs=in_specs or [SMEM if value.dtype == jnp.int32 else VMEM for value in ins],
        out_specs=out_specs or jax.tree.map(lambda _: VMEM, outs),
        scratch_shapes=scratch,
        compiler_params=pltpu.CompilerParams(vmem_limit_bytes=VMEM_BYTES),
        cost_estimate=pl.CostEstimate(flops=flops, bytes_accessed=size, transcendentals=0),
        **options,
    )(*ins)
    return list(result) if isinstance(outs, list) else result


def on_device(plan, object_field, probe_field, amplitudes, centres, counts):
    f32 = jnp.float32
    shape = jax.ShapeDtypeStruct
    size = probe_field.shape[1]
    half = size // 2
    slots = amplitudes.shape[2]
    block_rows = object_field.shape[1]
    block_cols = object_field.shape[2]
    assert block_rows == half and block_cols % LANES == 0 and half == LANES
    width = plan.tiles * LANES
    sides = plan.sides
    spots = centres[0, 0]
    counts = counts.reshape(-1)
    own_amps = amplitudes[0, 0]
    tables = jnp.asarray(dft_tables(size))
    order = jnp.asarray(parity_order(size))
    dma = pltpu.SemaphoreType.DMA

    messages = call(
        lambda *refs: edge_message_kernel(plan, *refs),
        [shape((2, half + 8, LANES), f32)] * sides,
        [dma((sides,))],
        [object_field, spots, counts],
        in_specs=[HBM, SMEM, SMEM],
    )
    halos = plan.across(messages)
    far_block = plan.far_rows(object_field)
    rolled, ordered = call(
        prepare_kernel,
        [shape((slots, 2, size, size), f32), shape((slots, size, size), f32)],
        [pltpu.VMEM((2, 2 * size + 8, size), f32)],
        [spots, probe_field, own_amps, order],
    )
    halos, rolled, ordered = lax.optimization_barrier((halos, rolled, ordered))
    near_runs = [shape((2, half, count * LANES), f32) for count in chunks(plan.own)]
    messages = call(
        lambda *refs: halo_message_kernel(plan, *refs),
        [shape((2, half + 16, LANES), f32)] * sides + near_runs,
        [],
        [object_field, spots, counts, *halos],
    )
    passed = messages[:sides]
    far = [far_block] + [plan.far_rows(message) for message in passed]
    near = [plan.near_rows(piece) for piece in messages]
    own = [object_field] + passed
    inverse, info, *inverse_pairs = call(
        lambda *refs: light_kernel(plan, slots, *refs),
        [shape((half, width), f32), shape((3 * (sides + 1), LANES), jnp.int32)] + [shape((half, 2 * LANES), f32)] * sides,
        [
            pltpu.VMEM((2 * size + 8, size), f32),
            pltpu.VMEM((half, width + 2 * plan.own * LANES), f32),
            pltpu.VMEM((3 * (sides + 1), 8, LANES), jnp.int32),
            dma,
        ],
        passed + far[1:] + near[:sides] + [probe_field],
        out_specs=[VMEM, SMEM] + [VMEM] * sides,
    )

    def runs_layout(refs, main, count, side_starts):
        starts = [main] + side_starts
        own, far, near = refs[: 1 + sides], refs[1 + sides : 2 + 2 * sides], refs[2 + 2 * sides :]
        return lay_out(own, starts), lay_out(far, starts), lay_out(near, side_starts + chunk_starts(main, count))

    def first_layout(refs, t):
        return runs_layout(refs, 1, plan.own, plan.halo_tiles(t))

    def later_layout(refs, t):
        return runs_layout(refs, plan.mid_start(t), plan.mid_tiles, plan.pair_starts(t))

    layout = first_layout
    token = spots

    for sweep in range(ITERS):
        pieces = own + far + near
        inner, outer, outer_far = [], [], []
        for slot in range(slots):
            last = slot == slots - 1
            earlier = outer if last else []
            patch = shape((2, half, size), f32)
            outer_part, inner_part, *copies = call(
                lambda *refs, slot=slot, layout=layout, copied=len(earlier): term_kernel(
                    plan, slot, layout, len(pieces), copied, *refs
                ),
                [patch] * 2 + [shape((1, half, size), f32)] * (2 * slots * last),
                [pltpu.VMEM((2, size, size), f32), pltpu.VMEM((3, 3, 2, half, LANES), f32)],
                [spots, counts, *pieces, *earlier, rolled, ordered, tables, token],
            )
            inner.append(inner_part)
            outer.append(outer_part)
            outer_far.append(plan.far_rows(outer_part))
        outer_near = [plan.near_rows(copy) for copy in copies]
        early = call(
            lambda *refs: early_sum_kernel(plan, slots, *refs),
            shape((2, half, width), f32),
            [],
            [info, *inner, *outer_far[:-1]],
        )
        early = call(
            lambda *refs: near_sum_kernel(plan, slots, *refs),
            shape((2, half, width), f32),
            [],
            [info, early, *outer_near],
        )
        if sweep < ITERS - 1:
            middle, total = call(
                lambda *refs, layout=layout: middle_kernel(plan, slots, layout, len(own), *refs),
                [shape((2, half, plan.mid_tiles * LANES), f32), shape((2, half, width), f32)],
                [],
                [info, early, outer_far[-1], inverse, *own],
            )
            far_middle = plan.far_rows(middle)
            boundary = call(
                lambda *refs, layout=layout: boundary_kernel(plan, layout, len(own), *refs),
                [shape((2, half, 2 * LANES), f32)] * (2 * sides),
                [],
                [total, inverse, middle, *own],
                in_specs=[VMEM, VMEM, ANY] + [VMEM] * len(own),
            )
            bases, sums = boundary[:sides], boundary[sides:]
            received = plan.across(sums)
            near_runs = [shape((2, half, count * LANES), f32) for count in chunks(plan.mid_tiles)]
            updated = call(
                lambda *refs: pair_kernel(sides, *refs),
                [shape((2, half, 2 * LANES), f32)] * (2 * sides) + near_runs,
                [],
                [middle, *bases, *received, *inverse_pairs],
            )
            pairs = updated[:sides]
            own = [middle] + pairs
            far = [far_middle] + [plan.far_rows(piece) for piece in pairs]
            near = [plan.near_rows(piece) for piece in updated[sides:]]
            layout = later_layout
            token = call(
                token_kernel,
                shape((8, LANES), f32),
                [],
                [far_middle],
                in_specs=[ANY],
                flops=10**11,
            )
    sums = call(
        lambda *refs: halo_sum_kernel(plan, slots, *refs),
        [shape((2, half, LANES), f32)] * sides,
        [],
        [info, early, outer_far[-1]],
    )
    nearly, *bases = call(
        lambda *refs: last_kernel(plan, slots, layout, len(own), *refs),
        [shape((2, half, block_cols), f32)] + [shape((2, half, LANES), f32)] * sides,
        [pltpu.VMEM((2, half, block_cols), f32), pltpu.VMEM((2, half, width), f32), dma],
        [info, early, outer_far[-1], inverse, sums[0], *own],
        in_specs=[SMEM, VMEM, VMEM, VMEM, ANY] + [VMEM] * len(own),
        out_specs=[HBM] + [VMEM] * sides,
    )
    received = plan.across(sums)
    return call(
        lambda *refs: edge_kernel(plan, *refs),
        shape(nearly.shape, f32),
        [pltpu.VMEM((sides, 2, half, LANES), f32), dma((sides,))],
        [inverse, *bases, *received, nearly],
        in_specs=[VMEM] * (1 + 2 * sides) + [HBM],
        out_specs=HBM,
        input_output_aliases={1 + 2 * sides: 0},
    )


def solution(mesh):
    sizes = dict(mesh.shape)

    def per_device(object_field, *rest):
        plan = Plan(sizes["sx"], sizes["sy"], object_field.shape[2])
        return on_device(plan, object_field, *rest)

    return jax.shard_map(
        per_device,
        mesh=mesh,
        in_specs=(
            P(None, "sx", "sy"),
            P(),
            P("sx", "sy", None, None, None),
            P("sx", "sy", None, None),
            P(None, "sy"),
        ),
        out_specs=P(None, "sx", "sy"),
        check_vma=False,
    )
```

```python
import math

import jax
import jax.numpy as jnp
import ml_dtypes
import numpy as np
from jax import lax
from jax.experimental import pallas as pl
from jax.experimental.pallas import tpu as pltpu
from jax.sharding import PartitionSpec as P

ITERS = 2
SMOOTH = 1.0
DAMPING = 1.0
LANES = 128
VMEM_BYTES = 12 * 1024 * 1024

VMEM = pl.BlockSpec(memory_space=pltpu.VMEM)
SMEM = pl.BlockSpec(memory_space=pltpu.SMEM)
HBM = pl.BlockSpec(memory_space=pltpu.HBM)
ANY = pl.BlockSpec(memory_space=pl.ANY)


def split_numpy(table):
    high = table.astype(np.float32).astype(ml_dtypes.bfloat16)
    low = (table - high.astype(np.float64)).astype(ml_dtypes.bfloat16)
    return high, low


def dft_tables(length):
    half = length // 2
    index = np.arange(half)
    tables = []
    for parity in range(2):
        angles = 2.0 * math.pi / length * (index[:, None] * (2 * index[None, :] + parity) % length)
        cosine = np.cos(angles) / math.sqrt(length)
        sine = np.sin(angles) / math.sqrt(length)
        forward = np.block([[cosine, -sine], [sine, cosine]])
        tables.append([split_numpy(forward), split_numpy(forward.T)])
    return np.array(tables, dtype=ml_dtypes.bfloat16)


def parity_order(length):
    half = length // 2
    order = np.zeros((length, length))
    for index in range(length):
        order[index, index % 2 * half + index // 2] = 1.0
    return np.stack([order, order.T]).astype(ml_dtypes.bfloat16)


def split(values):
    high = values.astype(jnp.bfloat16)
    low = (values - high.astype(jnp.float32)).astype(jnp.bfloat16)
    return high, low


def times_table(values, table):
    high, low = split(values)
    left = jnp.concatenate([high, low, high], axis=1)
    right = jnp.concatenate([table[0], table[0], table[1]], axis=0)
    return jnp.dot(left, right, preferred_element_type=jnp.float32)


def table_times(table, values):
    high, low = split(values)
    left = jnp.concatenate([table[0], table[0], table[1]], axis=1)
    right = jnp.concatenate([high, low, high], axis=0)
    return jnp.dot(left, right, preferred_element_type=jnp.float32)


class Plan:
    def __init__(self, sx_size, sy_size, block_cols):
        self.sx_size = sx_size
        self.sy_size = sy_size
        self.own = block_cols // LANES
        self.tiles = self.own + 2
        self.paired = sy_size == 2
        self.sides = 1 if self.paired else 2

    def rights(self, t):
        return [1 - t] if self.paired else [0, 1]

    def pair_starts(self, t):
        return [right * (self.tiles - 2) for right in self.rights(t)]

    def halo_tiles(self, t):
        return [right * (self.tiles - 1) for right in self.rights(t)]

    def edge_tiles(self, t):
        return [1 + right * (self.tiles - 3) for right in self.rights(t)]

    def mid_start(self, t):
        return 1 + t if self.paired else 2

    @property
    def mid_tiles(self):
        return self.tiles - 3 if self.paired else self.tiles - 4

    def across(self, values, axis_name="sy"):
        if self.paired:
            return [lax.ppermute(values[0], axis_name, [(0, 1), (1, 0)])]
        ends = self.sy_size - 1
        return [
            lax.ppermute(values[1], axis_name, [(i, i + 1) for i in range(ends)]),
            lax.ppermute(values[0], axis_name, [(i + 1, i) for i in range(ends)]),
        ]

    def far_rows(self, values):
        rows, columns = self.sx_size, self.sy_size
        pairs = [(i * columns + t, (i + 1) * columns + t) for i in range(1, rows - 1, 2) for t in range(columns)]
        for i in (0, rows - 1):
            pairs += [(i * columns + t, i * columns + t + 1) for t in range(0, columns - 1, 2)]
        return lax.ppermute(values, ("sx", "sy"), pairs + [(j, i) for i, j in pairs])

    def near_rows(self, values):
        return lax.ppermute(values, "sx", [(i, i ^ 1) for i in range(self.sx_size)])

    def outermost(self, s):
        return (s == 0) | (s == self.sx_size - 1)


def far_side(s):
    return 2 * (s % 2) - 1


def lanes(tile, count=1):
    if isinstance(tile, int):
        return pl.ds(tile * LANES, count * LANES)
    return pl.ds(pl.multiple_of(tile * LANES, LANES), count * LANES)


def pick_tile(plan, target, pieces, tile, t):
    rows = target.shape[1]
    if plan.paired:

        @pl.when(tile == (plan.tiles - 1) * t)
        def _():
            target[...] = jnp.zeros(target.shape, jnp.float32)

    for ref, offset, count, start in pieces:

        @pl.when((tile >= start) & (tile < start + count))
        def _(ref=ref, offset=offset, start=start):
            target[...] = ref[:, :rows, lanes(tile - start + offset)]


def lay_out(refs, starts):
    return [(ref, 0, ref.shape[2] // LANES, start) for ref, start in zip(refs, starts)]


def chunks(count):
    return [min(2, count - first) for first in range(0, count, 2)]


def chunk_starts(start, count):
    return [start + 2 * index for index in range(len(chunks(count)))]


def spread(source, targets):
    offset = 0
    for target in targets:
        columns = target.shape[2]
        target[...] = source[:, :, offset : offset + columns]
        offset += columns


def rows_at(ref, start, count):
    offset = start % 8
    values = ref[pl.ds(pl.multiple_of(start - offset, 8), count + 8)]
    return pltpu.roll(values, (count + 8 - offset) % (count + 8), 0)[:count]


def here():
    return lax.axis_index("sx"), lax.axis_index("sy")


def info_rows(centres, count):
    lane = lax.broadcasted_iota(jnp.int32, (8, LANES), 1)
    slots = centres.shape[0]
    values = [centres[slot, axis] for slot in range(slots) for axis in range(2)] + [count]
    line = jnp.zeros((8, LANES), jnp.int32)
    for index, value in enumerate(values):
        line = jnp.where(lane == index, value, line)
    return line.astype(jnp.float32)


def edge_message_kernel(plan, block, centres, counts, *rest):
    messages, sems = rest[: plan.sides], rest[plan.sides]
    s, t = here()
    half = block.shape[1]
    copies = [
        pltpu.make_async_copy(block.at[:, :, lanes(tile - 1)], message.at[:, :half], sems.at[side])
        for side, (message, tile) in enumerate(zip(messages, plan.edge_tiles(t)))
    ]
    for copy in copies:
        copy.start()
    rows = info_rows(centres, counts[s])
    for message in messages:
        message[0, half:] = rows
        message[1, half:] = rows
    for copy in copies:
        copy.wait()


def halo_message_kernel(plan, block, centres, counts, *rest):
    s, _ = here()
    received, messages, near = rest[: plan.sides], rest[plan.sides : 2 * plan.sides], rest[2 * plan.sides :]
    own = info_rows(centres, counts[s])
    for source, message in zip(received, messages):
        rows = source.shape[1]
        message[:, :rows] = source[...]
        message[0, rows:] = own
        message[1, rows:] = own
    spread(block, near)


def pair_kernel(sides, middle, *rest):
    bases, received, inverses, results = (rest[k * sides : (k + 1) * sides] for k in range(4))
    near = rest[4 * sides :]
    for base, other, inverse, result, copy in zip(bases, received, inverses, results, near):
        values = base[...] - other[...] * inverse[...][None]
        result[...] = values
        copy[...] = values
    spread(middle, near[sides:])


def token_kernel(_, token):
    token[...] = jnp.zeros(token.shape, jnp.float32)


def prepare_kernel(centres, probe, amps, order, rolled, ordered, padded):
    size = probe.shape[1]
    half = size // 2
    padded[:, :half] = jnp.zeros((2, half, size), jnp.float32)
    padded[:, half + size :] = jnp.zeros((2, half + 8, size), jnp.float32)
    padded[:, half : half + size] = probe[...]
    for slot in range(amps.shape[0]):
        row = centres[slot, 0]
        col = centres[slot, 1]
        for part in range(2):
            shape = padded.at[part]
            upper = rows_at(shape, half - row, half) + rows_at(shape, half + size - row, half)
            lower = rows_at(shape, size - row, half)
            rolled[slot, part] = pltpu.roll(jnp.concatenate([upper, lower], axis=0), col % size, 1)
        high, low = split(amps[slot])
        across = jnp.dot(
            jnp.concatenate([high, low], axis=1),
            jnp.concatenate([order[0], order[0]], axis=0),
            preferred_element_type=jnp.float32,
        )
        high, low = split(across)
        ordered[slot] = jnp.dot(
            jnp.concatenate([order[1], order[1]], axis=1),
            jnp.concatenate([high, low], axis=0),
            preferred_element_type=jnp.float32,
        )


def light_kernel(plan, slots, *rest):
    groups = [rest[k * plan.sides : (k + 1) * plan.sides] for k in range(3)]
    probe, inverse, info = rest[3 * plan.sides : 3 * plan.sides + 3]
    pairs = rest[3 * plan.sides + 3 : 4 * plan.sides + 3]
    padded, canvas, known, sem = rest[4 * plan.sides + 3 :]
    size = probe.shape[1]
    half = size // 2
    s, t = here()
    upper = s % 2 == 0
    height = half

    def lines(messages):
        return [messages[0][0, height + 8 : height + 16]] + [message[0, height : height + 8] for message in messages]

    own, far, near = (lines(messages) for messages in groups)
    far = [jnp.where(plan.outermost(s), 0.0, line) for line in far]
    for turn in range(plan.sides + 1):
        for kind, line in ((0, jnp.where(upper, far[turn], near[turn])), (1, own[turn]), (2, jnp.where(upper, near[turn], far[turn]))):
            known[kind * (plan.sides + 1) + turn] = line.astype(jnp.int32)
    copy = pltpu.make_async_copy(known.at[:, 0], info, sem)
    copy.start()
    padded[:half] = jnp.zeros((half, size), jnp.float32)
    padded[half + size :] = jnp.zeros((half + 8, size), jnp.float32)
    padded[half : half + size] = probe[0] * probe[0] + probe[1] * probe[1]
    canvas[...] = jnp.zeros(canvas.shape, jnp.float32)
    copy.wait()
    reach = plan.sides + 1
    spare = jnp.zeros((half, LANES), jnp.float32)
    for down in (-1, 0, 1):

        def add(step, carry, down=down):
            turn = step // slots
            slot = step % slots
            over = turn * (1 - 2 * t) if plan.paired else jnp.where(turn == 0, 0, 2 * turn - 3)
            index = (down + 1) * reach + turn

            @pl.when(slot < info[index, 2 * slots])
            def _():
                row = info[index, 2 * slot]
                col = info[index, 2 * slot + 1]
                power = rows_at(padded, size - half * down - row, half)
                shifted = pltpu.roll(jnp.concatenate([power, spare], axis=1), col % LANES, 1)
                first = col // LANES + plan.own * (over + 1)
                canvas[:, lanes(first, 3)] += shifted

            return carry

        lax.fori_loop(0, reach * slots, add, 0)
    result = 1.0 / (canvas[:, lanes(plan.own, plan.tiles)] + DAMPING)
    inverse[...] = result
    for pair, start in zip(pairs, plan.pair_starts(t)):
        pair[...] = inverse[:, lanes(start, 2)]


def term_kernel(plan, slot, layout, pieces, copied, centres, counts, *rest):
    refs, rest = rest[:pieces], rest[pieces:]
    earlier, (probe, amps, tables, _, outer, inner), rest = rest[:copied], rest[copied : copied + 6], rest[copied + 6 :]
    near_outers, (window, picked) = rest[:-2], rest[-2:]
    size = probe.shape[2]
    half = size // 2
    s, t = here()
    row = centres[slot, 0]
    col = centres[slot, 1]
    alive = slot < counts[s]

    @pl.when(jnp.logical_not(alive))
    def _():
        outer[...] = jnp.zeros(outer.shape, jnp.float32)
        inner[...] = jnp.zeros(inner.shape, jnp.float32)

    @pl.when(alive)
    def _():
        tile = col // LANES
        first = tile % 2
        rest_col = col % LANES
        from_tile = lax.broadcasted_iota(jnp.int32, (half, LANES), 1) >= rest_col
        from_upper = lax.broadcasted_iota(jnp.int32, (half, LANES), 0) >= row
        side = far_side(s)
        own, far, near = layout(refs, t)
        for kind, source in ((1, own), (1 + side, far), (1 - side, near)):
            for step in range(3):
                pick_tile(plan, picked.at[kind, step], source, tile + step, t)

        @pl.when(plan.outermost(s))
        def _():
            picked[1 + side] = jnp.zeros(picked.shape[1:], jnp.float32)

        for part in range(2):
            edge = [jnp.where(from_tile, picked[kind, 0, part], picked[kind, 2, part]) for kind in range(3)]
            window[part, :half, lanes(first)] = jnp.where(from_upper, edge[0], edge[2])
            window[part, half:, lanes(first)] = edge[1]
            window[part, :half, lanes(1 - first)] = jnp.where(from_upper, picked[0, 1, part], picked[2, 1, part])
            window[part, half:, lanes(1 - first)] = picked[1, 1, part]

        probe_real = probe[slot, 0]
        probe_imag = probe[slot, 1]
        exit_real = probe_real * window[0] - probe_imag * window[1]
        exit_imag = probe_real * window[1] + probe_imag * window[0]

        halves = [
            jnp.concatenate([exit_real[:, :half] + sign * exit_real[:, half:], exit_imag[:, :half] + sign * exit_imag[:, half:]], axis=1)
            for sign in (1.0, -1.0)
        ]
        across = [times_table(halves[parity], tables[parity, 0]) for parity in range(2)]
        real = jnp.concatenate([across[0][:, :half], across[1][:, :half]], axis=1)
        imag = jnp.concatenate([across[0][:, half:], across[1][:, half:]], axis=1)
        halves = [
            jnp.concatenate([real[:half] + sign * real[half:], imag[:half] + sign * imag[half:]], axis=0)
            for sign in (1.0, -1.0)
        ]
        back = []
        for parity in range(2):
            pattern = table_times(tables[parity, 1], halves[parity])
            far_real = pattern[:half]
            far_imag = pattern[half:]
            amplitude = amps[slot, parity * half : (parity + 1) * half]
            factor = 1.0 - amplitude * lax.rsqrt(far_real * far_real + far_imag * far_imag + SMOOTH)
            miss = jnp.concatenate([far_real * factor, far_imag * factor], axis=0)
            back.append(table_times(tables[parity, 0], miss))
        real = jnp.concatenate([back[0][:half] + back[1][:half], back[0][:half] - back[1][:half]], axis=0)
        imag = jnp.concatenate([back[0][half:] + back[1][half:], back[0][half:] - back[1][half:]], axis=0)
        both = []
        for parity in range(2):
            columns = slice(parity * half, (parity + 1) * half)
            both.append(times_table(jnp.concatenate([real[:, columns], imag[:, columns]], axis=1), tables[parity, 1]))
        near_real = jnp.concatenate([both[0][:, :half] + both[1][:, :half], both[0][:, :half] - both[1][:, :half]], axis=1)
        near_imag = jnp.concatenate([both[0][:, half:] + both[1][:, half:], both[0][:, half:] - both[1][:, half:]], axis=1)
        term_real = probe_real * near_real + probe_imag * near_imag
        term_imag = probe_real * near_imag - probe_imag * near_real
        outer[0] = term_real[:half]
        outer[1] = term_imag[:half]
        inner[0] = term_real[half:]
        inner[1] = term_imag[half:]

    for index, source in enumerate((*earlier, outer)):
        for part in range(2 if near_outers else 0):
            near_outers[2 * index + part][0] = source[part]


class Patch:
    def __init__(self, plan, info, s, patch, slot, down, far=False):
        half = (patch[0] if isinstance(patch, (list, tuple)) else patch).shape[1]
        index = (1 if down is None else 1 + down) * (plan.sides + 1)
        row = info[index, 2 * slot]
        col = info[index, 2 * slot + 1]
        self.parts = patch if isinstance(patch, (list, tuple)) else [patch.at[0:1], patch.at[1:2]]
        self.tile = col // LANES
        self.first = self.tile % 2
        self.from_tile = lax.broadcasted_iota(jnp.int32, (half, LANES), 1) >= col % LANES
        self.rows = None
        if down is not None:
            line = lax.broadcasted_iota(jnp.int32, (half, LANES), 0)
            after = jnp.where(down > 0, half, row)
            if far:
                after = jnp.where(plan.outermost(s), 0, after)
            self.rows = (line >= jnp.where(down > 0, row, 0)) & (line < after)

    def lines(self, part, place):
        values = self.parts[part][0, :, lanes(place)]
        return values if self.rows is None else jnp.where(self.rows, values, 0.0)

    def tiles(self, part):
        edge = self.lines(part, self.first)
        middle = self.lines(part, 1 - self.first)
        return jnp.where(self.from_tile, edge, 0.0), middle, jnp.where(self.from_tile, 0.0, edge)

    def add_to(self, canvas):
        for part in range(2):
            for step, values in enumerate(self.tiles(part)):
                canvas[part, :, lanes(self.tile + step)] += values

    def add_tile_to(self, total, tile):
        for step in range(3):

            @pl.when(self.tile + step == tile)
            def _(step=step):
                for part in range(2):
                    total[part] += self.tiles(part)[step]


def early_sum_kernel(plan, slots, info, *rest):
    inner, far, canvas = rest[:slots], rest[slots : 2 * slots - 1], rest[2 * slots - 1]
    s, _ = here()
    canvas[...] = jnp.zeros(canvas.shape, jnp.float32)
    for slot in range(slots):
        Patch(plan, info, s, inner[slot], slot, None).add_to(canvas)
    for slot in range(slots - 1):
        Patch(plan, info, s, far[slot], slot, far_side(s), True).add_to(canvas)


def near_sum_kernel(plan, slots, info, early, *rest):
    near, canvas = rest[: 2 * slots], rest[2 * slots]
    s, _ = here()
    canvas[...] = early[...]
    for slot in range(slots):
        Patch(plan, info, s, near[2 * slot : 2 * slot + 2], slot, -far_side(s)).add_to(canvas)


def last_patch(plan, slots, info, patch):
    s, _ = here()
    return Patch(plan, info, s, patch, slots - 1, far_side(s), True)


def middle_kernel(plan, slots, layout, pieces, info, early, patch, inverse, *rest):
    refs, (middle, canvas) = rest[:pieces], rest[pieces:]
    _, t = here()
    canvas[...] = early[...]
    last_patch(plan, slots, info, patch).add_to(canvas)
    for step in range(plan.mid_tiles):
        tile = plan.mid_start(t) + step
        where = lanes(step)
        pick_tile(plan, middle.at[:, :, where], layout(refs, t)[0], tile, t)
        middle[:, :, where] -= canvas[:, :, lanes(tile)] * inverse[:, lanes(tile)][None]


def boundary_kernel(plan, layout, pieces, canvas, inverse, _, *rest):
    refs, outs = rest[:pieces], rest[pieces:]
    bases, sums = outs[: plan.sides], outs[plan.sides :]
    _, t = here()
    for base, total, start in zip(bases, sums, plan.pair_starts(t)):
        total[...] = canvas[:, :, lanes(start, 2)]
        for step in range(2):
            where = lanes(step)
            pick_tile(plan, base.at[:, :, where], layout(refs, t)[0], start + step, t)
            base[:, :, where] -= total[:, :, where] * inverse[:, lanes(start + step)][None]


def halo_sum_kernel(plan, slots, info, early, patch, *sums):
    _, t = here()
    last = last_patch(plan, slots, info, patch)
    for total, tile in zip(sums, plan.halo_tiles(t)):
        total[...] = early[:, :, lanes(tile)]
        last.add_tile_to(total, tile)


def last_kernel(plan, slots, layout, pieces, info, early, patch, inverse, _, *rest):
    refs, rest = rest[:pieces], rest[pieces:]
    nearly, bases = rest[0], rest[1 : 1 + plan.sides]
    current, canvas, sem = rest[1 + plan.sides :]
    _, t = here()
    canvas[...] = early[...]
    last_patch(plan, slots, info, patch).add_to(canvas)
    for step in range(plan.own):
        tile = 1 + step
        where = lanes(step)
        pick_tile(plan, current.at[:, :, where], layout(refs, t)[0], tile, t)
        current[:, :, where] -= canvas[:, :, lanes(tile)] * inverse[:, lanes(tile)][None]
    copy = pltpu.make_async_copy(current, nearly, sem)
    copy.start()
    for base, tile in zip(bases, plan.edge_tiles(t)):
        base[...] = current[:, :, lanes(tile - 1)]
    copy.wait()


def edge_kernel(plan, inverse, *rest):
    bases, received = rest[: plan.sides], rest[plan.sides : 2 * plan.sides]
    _, result, sums, sems = rest[2 * plan.sides :]
    _, t = here()
    copies = []
    for side, tile in enumerate(plan.edge_tiles(t)):
        sums[side] = bases[side][...] - received[side][...] * inverse[:, lanes(tile)][None]
        copies.append(pltpu.make_async_copy(sums.at[side], result.at[:, :, lanes(tile - 1)], sems.at[side]))
        copies[-1].start()
    for copy in copies:
        copy.wait()


def call(kernel, outs, scratch, ins, flops=10**5, size=10**4, in_specs=None, out_specs=None, **options):
    result = pl.pallas_call(
        kernel,
        out_shape=outs,
        in_specs=in_specs or [SMEM if value.dtype == jnp.int32 else VMEM for value in ins],
        out_specs=out_specs or jax.tree.map(lambda _: VMEM, outs),
        scratch_shapes=scratch,
        compiler_params=pltpu.CompilerParams(vmem_limit_bytes=VMEM_BYTES),
        cost_estimate=pl.CostEstimate(flops=flops, bytes_accessed=size, transcendentals=0),
        **options,
    )(*ins)
    return list(result) if isinstance(outs, list) else result


def on_device(plan, object_field, probe_field, amplitudes, centres, counts):
    f32 = jnp.float32
    shape = jax.ShapeDtypeStruct
    size = probe_field.shape[1]
    half = size // 2
    slots = amplitudes.shape[2]
    block_rows = object_field.shape[1]
    block_cols = object_field.shape[2]
    assert block_rows == half and block_cols % LANES == 0 and half == LANES
    width = plan.tiles * LANES
    sides = plan.sides
    spots = centres[0, 0]
    counts = counts.reshape(-1)
    own_amps = amplitudes[0, 0]
    tables = jnp.asarray(dft_tables(size))
    order = jnp.asarray(parity_order(size))
    dma = pltpu.SemaphoreType.DMA

    messages = call(
        lambda *refs: edge_message_kernel(plan, *refs),
        [shape((2, half + 8, LANES), f32)] * sides,
        [dma((sides,))],
        [object_field, spots, counts],
        in_specs=[HBM, SMEM, SMEM],
    )
    halos = plan.across(messages)
    far_block = plan.far_rows(object_field)
    rolled, ordered = call(
        prepare_kernel,
        [shape((slots, 2, size, size), f32), shape((slots, size, size), f32)],
        [pltpu.VMEM((2, 2 * size + 8, size), f32)],
        [spots, probe_field, own_amps, order],
    )
    near_runs = [shape((2, half, count * LANES), f32) for count in chunks(plan.own)]
    messages = call(
        lambda *refs: halo_message_kernel(plan, *refs),
        [shape((2, half + 16, LANES), f32)] * sides + near_runs,
        [],
        [object_field, spots, counts, *halos],
    )
    passed = messages[:sides]
    far = [far_block] + [plan.far_rows(message) for message in passed]
    near = [plan.near_rows(piece) for piece in messages]
    own = [object_field] + passed
    inverse, info, *inverse_pairs = call(
        lambda *refs: light_kernel(plan, slots, *refs),
        [shape((half, width), f32), shape((3 * (sides + 1), LANES), jnp.int32)] + [shape((half, 2 * LANES), f32)] * sides,
        [
            pltpu.VMEM((2 * size + 8, size), f32),
            pltpu.VMEM((half, width + 2 * plan.own * LANES), f32),
            pltpu.VMEM((3 * (sides + 1), 8, LANES), jnp.int32),
            dma,
        ],
        passed + far[1:] + near[:sides] + [probe_field],
        out_specs=[VMEM, SMEM] + [VMEM] * sides,
    )

    def runs_layout(refs, main, count, side_starts):
        starts = [main] + side_starts
        own, far, near = refs[: 1 + sides], refs[1 + sides : 2 + 2 * sides], refs[2 + 2 * sides :]
        return lay_out(own, starts), lay_out(far, starts), lay_out(near, side_starts + chunk_starts(main, count))

    def first_layout(refs, t):
        return runs_layout(refs, 1, plan.own, plan.halo_tiles(t))

    def later_layout(refs, t):
        return runs_layout(refs, plan.mid_start(t), plan.mid_tiles, plan.pair_starts(t))

    layout = first_layout
    token = spots

    for sweep in range(ITERS):
        pieces = own + far + near
        inner, outer, outer_far = [], [], []
        for slot in range(slots):
            last = slot == slots - 1
            earlier = outer if last else []
            patch = shape((2, half, size), f32)
            outer_part, inner_part, *copies = call(
                lambda *refs, slot=slot, layout=layout, copied=len(earlier): term_kernel(
                    plan, slot, layout, len(pieces), copied, *refs
                ),
                [patch] * 2 + [shape((1, half, size), f32)] * (2 * slots * last),
                [pltpu.VMEM((2, size, size), f32), pltpu.VMEM((3, 3, 2, half, LANES), f32)],
                [spots, counts, *pieces, *earlier, rolled, ordered, tables, token],
            )
            inner.append(inner_part)
            outer.append(outer_part)
            outer_far.append(plan.far_rows(outer_part))
            token = info if sweep == 0 else token
        outer_near = [plan.near_rows(copy) for copy in copies]
        early = call(
            lambda *refs: early_sum_kernel(plan, slots, *refs),
            shape((2, half, width), f32),
            [],
            [info, *inner, *outer_far[:-1]],
        )
        early = call(
            lambda *refs: near_sum_kernel(plan, slots, *refs),
            shape((2, half, width), f32),
            [],
            [info, early, *outer_near],
        )
        if sweep < ITERS - 1:
            middle, total = call(
                lambda *refs, layout=layout: middle_kernel(plan, slots, layout, len(own), *refs),
                [shape((2, half, plan.mid_tiles * LANES), f32), shape((2, half, width), f32)],
                [],
                [info, early, outer_far[-1], inverse, *own],
            )
            far_middle = plan.far_rows(middle)
            boundary = call(
                lambda *refs, layout=layout: boundary_kernel(plan, layout, len(own), *refs),
                [shape((2, half, 2 * LANES), f32)] * (2 * sides),
                [],
                [total, inverse, middle, *own],
                in_specs=[VMEM, VMEM, ANY] + [VMEM] * len(own),
            )
            bases, sums = boundary[:sides], boundary[sides:]
            received = plan.across(sums)
            near_runs = [shape((2, half, count * LANES), f32) for count in chunks(plan.mid_tiles)]
            updated = call(
                lambda *refs: pair_kernel(sides, *refs),
                [shape((2, half, 2 * LANES), f32)] * (2 * sides) + near_runs,
                [],
                [middle, *bases, *received, *inverse_pairs],
            )
            pairs = updated[:sides]
            own = [middle] + pairs
            far = [far_middle] + [plan.far_rows(piece) for piece in pairs]
            near = [plan.near_rows(piece) for piece in updated[sides:]]
            layout = later_layout
            token = call(
                token_kernel,
                shape((8, LANES), f32),
                [],
                [far_middle],
                in_specs=[ANY],
                flops=10**11,
            )
    sums = call(
        lambda *refs: halo_sum_kernel(plan, slots, *refs),
        [shape((2, half, LANES), f32)] * sides,
        [],
        [info, early, outer_far[-1]],
    )
    nearly, *bases = call(
        lambda *refs: last_kernel(plan, slots, layout, len(own), *refs),
        [shape((2, half, block_cols), f32)] + [shape((2, half, LANES), f32)] * sides,
        [pltpu.VMEM((2, half, block_cols), f32), pltpu.VMEM((2, half, width), f32), dma],
        [info, early, outer_far[-1], inverse, sums[0], *own],
        in_specs=[SMEM, VMEM, VMEM, VMEM, ANY] + [VMEM] * len(own),
        out_specs=[HBM] + [VMEM] * sides,
    )
    received = plan.across(sums)
    return call(
        lambda *refs: edge_kernel(plan, *refs),
        shape(nearly.shape, f32),
        [pltpu.VMEM((sides, 2, half, LANES), f32), dma((sides,))],
        [inverse, *bases, *received, nearly],
        in_specs=[VMEM] * (1 + 2 * sides) + [HBM],
        out_specs=HBM,
        input_output_aliases={1 + 2 * sides: 0},
    )


def solution(mesh):
    sizes = dict(mesh.shape)

    def per_device(object_field, *rest):
        plan = Plan(sizes["sx"], sizes["sy"], object_field.shape[2])
        return on_device(plan, object_field, *rest)

    return jax.shard_map(
        per_device,
        mesh=mesh,
        in_specs=(
            P(None, "sx", "sy"),
            P(),
            P("sx", "sy", None, None, None),
            P("sx", "sy", None, None),
            P(None, "sy"),
        ),
        out_specs=P(None, "sx", "sy"),
        check_vma=False,
    )
```

```python
import math

import jax
import jax.numpy as jnp
import ml_dtypes
import numpy as np
from jax import lax
from jax.experimental import pallas as pl
from jax.experimental.pallas import tpu as pltpu
from jax.sharding import PartitionSpec as P

ITERS = 2
SMOOTH = 1.0
DAMPING = 1.0
LANES = 128
VMEM_BYTES = 12 * 1024 * 1024

VMEM = pl.BlockSpec(memory_space=pltpu.VMEM)
SMEM = pl.BlockSpec(memory_space=pltpu.SMEM)
HBM = pl.BlockSpec(memory_space=pltpu.HBM)
ANY = pl.BlockSpec(memory_space=pl.ANY)


def split_numpy(table):
    high = table.astype(np.float32).astype(ml_dtypes.bfloat16)
    low = (table - high.astype(np.float64)).astype(ml_dtypes.bfloat16)
    return high, low


def dft_tables(length):
    half = length // 2
    index = np.arange(half)
    tables = []
    for parity in range(2):
        angles = 2.0 * math.pi / length * (index[:, None] * (2 * index[None, :] + parity) % length)
        cosine = np.cos(angles) / math.sqrt(length)
        sine = np.sin(angles) / math.sqrt(length)
        forward = np.block([[cosine, -sine], [sine, cosine]])
        tables.append([split_numpy(forward), split_numpy(forward.T)])
    return np.array(tables, dtype=ml_dtypes.bfloat16)


def parity_order(length):
    half = length // 2
    order = np.zeros((length, length))
    for index in range(length):
        order[index, index % 2 * half + index // 2] = 1.0
    return np.stack([order, order.T]).astype(ml_dtypes.bfloat16)


def split(values):
    high = values.astype(jnp.bfloat16)
    low = (values - high.astype(jnp.float32)).astype(jnp.bfloat16)
    return high, low


def times_table(values, table):
    high, low = split(values)
    left = jnp.concatenate([high, low, high], axis=1)
    right = jnp.concatenate([table[0], table[0], table[1]], axis=0)
    return jnp.dot(left, right, preferred_element_type=jnp.float32)


def table_times(table, values):
    high, low = split(values)
    left = jnp.concatenate([table[0], table[0], table[1]], axis=1)
    right = jnp.concatenate([high, low, high], axis=0)
    return jnp.dot(left, right, preferred_element_type=jnp.float32)


class Plan:
    def __init__(self, sx_size, sy_size, block_cols):
        self.sx_size = sx_size
        self.sy_size = sy_size
        self.own = block_cols // LANES
        self.tiles = self.own + 2
        self.paired = sy_size == 2
        self.sides = 1 if self.paired else 2

    def rights(self, t):
        return [1 - t] if self.paired else [0, 1]

    def pair_starts(self, t):
        return [right * (self.tiles - 2) for right in self.rights(t)]

    def halo_tiles(self, t):
        return [right * (self.tiles - 1) for right in self.rights(t)]

    def edge_tiles(self, t):
        return [1 + right * (self.tiles - 3) for right in self.rights(t)]

    def mid_start(self, t):
        return 1 + t if self.paired else 2

    @property
    def mid_tiles(self):
        return self.tiles - 3 if self.paired else self.tiles - 4

    def across(self, values, axis_name="sy"):
        if self.paired:
            return [lax.ppermute(values[0], axis_name, [(0, 1), (1, 0)])]
        ends = self.sy_size - 1
        return [
            lax.ppermute(values[1], axis_name, [(i, i + 1) for i in range(ends)]),
            lax.ppermute(values[0], axis_name, [(i + 1, i) for i in range(ends)]),
        ]

    def far_rows(self, values):
        rows, columns = self.sx_size, self.sy_size
        pairs = [(i * columns + t, (i + 1) * columns + t) for i in range(1, rows - 1, 2) for t in range(columns)]
        for i in (0, rows - 1):
            pairs += [(i * columns + t, i * columns + t + 1) for t in range(0, columns - 1, 2)]
        return lax.ppermute(values, ("sx", "sy"), pairs + [(j, i) for i, j in pairs])

    def near_rows(self, values):
        return lax.ppermute(values, "sx", [(i, i ^ 1) for i in range(self.sx_size)])

    def outermost(self, s):
        return (s == 0) | (s == self.sx_size - 1)


def far_side(s):
    return 2 * (s % 2) - 1


def lanes(tile, count=1):
    if isinstance(tile, int):
        return pl.ds(tile * LANES, count * LANES)
    return pl.ds(pl.multiple_of(tile * LANES, LANES), count * LANES)


def pick_tile(plan, target, pieces, tile, t):
    rows = target.shape[1]
    if plan.paired:

        @pl.when(tile == (plan.tiles - 1) * t)
        def _():
            target[...] = jnp.zeros(target.shape, jnp.float32)

    for ref, offset, count, start in pieces:

        @pl.when((tile >= start) & (tile < start + count))
        def _(ref=ref, offset=offset, start=start):
            target[...] = ref[:, :rows, lanes(tile - start + offset)]


def lay_out(refs, starts):
    return [(ref, 0, ref.shape[2] // LANES, start) for ref, start in zip(refs, starts)]


def chunks(count):
    return [min(2, count - first) for first in range(0, count, 2)]


def chunk_starts(start, count):
    return [start + 2 * index for index in range(len(chunks(count)))]


def spread(source, targets):
    offset = 0
    for target in targets:
        columns = target.shape[2]
        target[...] = source[:, :, offset : offset + columns]
        offset += columns


def rows_at(ref, start, count):
    offset = start % 8
    values = ref[pl.ds(pl.multiple_of(start - offset, 8), count + 8)]
    return pltpu.roll(values, (count + 8 - offset) % (count + 8), 0)[:count]


def here():
    return lax.axis_index("sx"), lax.axis_index("sy")


def info_rows(centres, count):
    lane = lax.broadcasted_iota(jnp.int32, (8, LANES), 1)
    slots = centres.shape[0]
    values = [centres[slot, axis] for slot in range(slots) for axis in range(2)] + [count]
    line = jnp.zeros((8, LANES), jnp.int32)
    for index, value in enumerate(values):
        line = jnp.where(lane == index, value, line)
    return line.astype(jnp.float32)


def edge_message_kernel(plan, block, centres, counts, *rest):
    messages, sems = rest[: plan.sides], rest[plan.sides]
    s, t = here()
    half = block.shape[1]
    copies = [
        pltpu.make_async_copy(block.at[:, :, lanes(tile - 1)], message.at[:, :half], sems.at[side])
        for side, (message, tile) in enumerate(zip(messages, plan.edge_tiles(t)))
    ]
    for copy in copies:
        copy.start()
    rows = info_rows(centres, counts[s])
    for message in messages:
        message[0, half:] = rows
        message[1, half:] = rows
    for copy in copies:
        copy.wait()


def halo_message_kernel(plan, block, centres, counts, *rest):
    s, _ = here()
    received, messages, near = rest[: plan.sides], rest[plan.sides : 2 * plan.sides], rest[2 * plan.sides :]
    own = info_rows(centres, counts[s])
    for source, message in zip(received, messages):
        rows = source.shape[1]
        message[:, :rows] = source[...]
        message[0, rows:] = own
        message[1, rows:] = own
    spread(block, near)


def pair_kernel(sides, middle, *rest):
    bases, received, inverses, results = (rest[k * sides : (k + 1) * sides] for k in range(4))
    near = rest[4 * sides :]
    for base, other, inverse, result, copy in zip(bases, received, inverses, results, near):
        values = base[...] - other[...] * inverse[...][None]
        result[...] = values
        copy[...] = values
    spread(middle, near[sides:])


def token_kernel(_, token):
    token[...] = jnp.zeros(token.shape, jnp.float32)


def prepare_kernel(centres, probe, amps, order, rolled, ordered, padded):
    size = probe.shape[1]
    half = size // 2
    padded[:, :half] = jnp.zeros((2, half, size), jnp.float32)
    padded[:, half + size :] = jnp.zeros((2, half + 8, size), jnp.float32)
    padded[:, half : half + size] = probe[...]
    for slot in range(amps.shape[0]):
        row = centres[slot, 0]
        col = centres[slot, 1]
        for part in range(2):
            shape = padded.at[part]
            upper = rows_at(shape, half - row, half) + rows_at(shape, half + size - row, half)
            lower = rows_at(shape, size - row, half)
            rolled[slot, part] = pltpu.roll(jnp.concatenate([upper, lower], axis=0), col % size, 1)
        high, low = split(amps[slot])
        across = jnp.dot(
            jnp.concatenate([high, low], axis=1),
            jnp.concatenate([order[0], order[0]], axis=0),
            preferred_element_type=jnp.float32,
        )
        high, low = split(across)
        ordered[slot] = jnp.dot(
            jnp.concatenate([order[1], order[1]], axis=1),
            jnp.concatenate([high, low], axis=0),
            preferred_element_type=jnp.float32,
        )


def info_kernel(plan, *rest):
    groups = [rest[k * plan.sides : (k + 1) * plan.sides] for k in range(3)]
    info, known, sem = rest[3 * plan.sides :]
    s, _ = here()
    upper = s % 2 == 0
    height = groups[0][0].shape[1] - 16

    def lines(messages):
        return [messages[0][0, height + 8 : height + 16]] + [message[0, height : height + 8] for message in messages]

    own, far, near = (lines(messages) for messages in groups)
    far = [jnp.where(plan.outermost(s), 0.0, line) for line in far]
    for turn in range(plan.sides + 1):
        for kind, line in ((0, jnp.where(upper, far[turn], near[turn])), (1, own[turn]), (2, jnp.where(upper, near[turn], far[turn]))):
            known[kind * (plan.sides + 1) + turn] = line.astype(jnp.int32)
    copy = pltpu.make_async_copy(known.at[:, 0], info, sem)
    copy.start()
    copy.wait()


def light_kernel(plan, slots, info, probe, _, inverse, *rest):
    pairs, (padded, canvas) = rest[: plan.sides], rest[plan.sides :]
    size = probe.shape[1]
    half = size // 2
    _, t = here()
    padded[:half] = jnp.zeros((half, size), jnp.float32)
    padded[half + size :] = jnp.zeros((half + 8, size), jnp.float32)
    padded[half : half + size] = probe[0] * probe[0] + probe[1] * probe[1]
    canvas[...] = jnp.zeros(canvas.shape, jnp.float32)
    reach = plan.sides + 1
    spare = jnp.zeros((half, LANES), jnp.float32)
    for down in (-1, 0, 1):

        def add(step, carry, down=down):
            turn = step // slots
            slot = step % slots
            over = turn * (1 - 2 * t) if plan.paired else jnp.where(turn == 0, 0, 2 * turn - 3)
            index = (down + 1) * reach + turn

            @pl.when(slot < info[index, 2 * slots])
            def _():
                row = info[index, 2 * slot]
                col = info[index, 2 * slot + 1]
                power = rows_at(padded, size - half * down - row, half)
                shifted = pltpu.roll(jnp.concatenate([power, spare], axis=1), col % LANES, 1)
                first = col // LANES + plan.own * (over + 1)
                canvas[:, lanes(first, 3)] += shifted

            return carry

        lax.fori_loop(0, reach * slots, add, 0)
    result = 1.0 / (canvas[:, lanes(plan.own, plan.tiles)] + DAMPING)
    inverse[...] = result
    for pair, start in zip(pairs, plan.pair_starts(t)):
        pair[...] = inverse[:, lanes(start, 2)]


def term_kernel(plan, slot, layout, pieces, copied, centres, counts, *rest):
    refs, rest = rest[:pieces], rest[pieces:]
    earlier, (probe, amps, tables, _, outer, inner), rest = rest[:copied], rest[copied : copied + 6], rest[copied + 6 :]
    near_outers, (window, picked) = rest[:-2], rest[-2:]
    size = probe.shape[2]
    half = size // 2
    s, t = here()
    row = centres[slot, 0]
    col = centres[slot, 1]
    alive = slot < counts[s]

    @pl.when(jnp.logical_not(alive))
    def _():
        outer[...] = jnp.zeros(outer.shape, jnp.float32)
        inner[...] = jnp.zeros(inner.shape, jnp.float32)

    @pl.when(alive)
    def _():
        tile = col // LANES
        first = tile % 2
        rest_col = col % LANES
        from_tile = lax.broadcasted_iota(jnp.int32, (half, LANES), 1) >= rest_col
        from_upper = lax.broadcasted_iota(jnp.int32, (half, LANES), 0) >= row
        side = far_side(s)
        own, far, near = layout(refs, t)
        for kind, source in ((1, own), (1 + side, far), (1 - side, near)):
            for step in range(3):
                pick_tile(plan, picked.at[kind, step], source, tile + step, t)

        @pl.when(plan.outermost(s))
        def _():
            picked[1 + side] = jnp.zeros(picked.shape[1:], jnp.float32)

        for part in range(2):
            edge = [jnp.where(from_tile, picked[kind, 0, part], picked[kind, 2, part]) for kind in range(3)]
            window[part, :half, lanes(first)] = jnp.where(from_upper, edge[0], edge[2])
            window[part, half:, lanes(first)] = edge[1]
            window[part, :half, lanes(1 - first)] = jnp.where(from_upper, picked[0, 1, part], picked[2, 1, part])
            window[part, half:, lanes(1 - first)] = picked[1, 1, part]

        probe_real = probe[slot, 0]
        probe_imag = probe[slot, 1]
        exit_real = probe_real * window[0] - probe_imag * window[1]
        exit_imag = probe_real * window[1] + probe_imag * window[0]

        halves = [
            jnp.concatenate([exit_real[:, :half] + sign * exit_real[:, half:], exit_imag[:, :half] + sign * exit_imag[:, half:]], axis=1)
            for sign in (1.0, -1.0)
        ]
        across = [times_table(halves[parity], tables[parity, 0]) for parity in range(2)]
        real = jnp.concatenate([across[0][:, :half], across[1][:, :half]], axis=1)
        imag = jnp.concatenate([across[0][:, half:], across[1][:, half:]], axis=1)
        halves = [
            jnp.concatenate([real[:half] + sign * real[half:], imag[:half] + sign * imag[half:]], axis=0)
            for sign in (1.0, -1.0)
        ]
        back = []
        for parity in range(2):
            pattern = table_times(tables[parity, 1], halves[parity])
            far_real = pattern[:half]
            far_imag = pattern[half:]
            amplitude = amps[slot, parity * half : (parity + 1) * half]
            factor = 1.0 - amplitude * lax.rsqrt(far_real * far_real + far_imag * far_imag + SMOOTH)
            miss = jnp.concatenate([far_real * factor, far_imag * factor], axis=0)
            back.append(table_times(tables[parity, 0], miss))
        real = jnp.concatenate([back[0][:half] + back[1][:half], back[0][:half] - back[1][:half]], axis=0)
        imag = jnp.concatenate([back[0][half:] + back[1][half:], back[0][half:] - back[1][half:]], axis=0)
        both = []
        for parity in range(2):
            columns = slice(parity * half, (parity + 1) * half)
            both.append(times_table(jnp.concatenate([real[:, columns], imag[:, columns]], axis=1), tables[parity, 1]))
        near_real = jnp.concatenate([both[0][:, :half] + both[1][:, :half], both[0][:, :half] - both[1][:, :half]], axis=1)
        near_imag = jnp.concatenate([both[0][:, half:] + both[1][:, half:], both[0][:, half:] - both[1][:, half:]], axis=1)
        term_real = probe_real * near_real + probe_imag * near_imag
        term_imag = probe_real * near_imag - probe_imag * near_real
        outer[0] = term_real[:half]
        outer[1] = term_imag[:half]
        inner[0] = term_real[half:]
        inner[1] = term_imag[half:]

    for index, source in enumerate((*earlier, outer)):
        for part in range(2 if near_outers else 0):
            near_outers[2 * index + part][0] = source[part]


class Patch:
    def __init__(self, plan, info, s, patch, slot, down, far=False):
        half = (patch[0] if isinstance(patch, (list, tuple)) else patch).shape[1]
        index = (1 if down is None else 1 + down) * (plan.sides + 1)
        row = info[index, 2 * slot]
        col = info[index, 2 * slot + 1]
        self.parts = patch if isinstance(patch, (list, tuple)) else [patch.at[0:1], patch.at[1:2]]
        self.tile = col // LANES
        self.first = self.tile % 2
        self.from_tile = lax.broadcasted_iota(jnp.int32, (half, LANES), 1) >= col % LANES
        self.rows = None
        if down is not None:
            line = lax.broadcasted_iota(jnp.int32, (half, LANES), 0)
            after = jnp.where(down > 0, half, row)
            if far:
                after = jnp.where(plan.outermost(s), 0, after)
            self.rows = (line >= jnp.where(down > 0, row, 0)) & (line < after)

    def lines(self, part, place):
        values = self.parts[part][0, :, lanes(place)]
        return values if self.rows is None else jnp.where(self.rows, values, 0.0)

    def tiles(self, part):
        edge = self.lines(part, self.first)
        middle = self.lines(part, 1 - self.first)
        return jnp.where(self.from_tile, edge, 0.0), middle, jnp.where(self.from_tile, 0.0, edge)

    def add_to(self, canvas):
        for part in range(2):
            for step, values in enumerate(self.tiles(part)):
                canvas[part, :, lanes(self.tile + step)] += values

    def tiles_at(self, tile, act):
        for step in range(3):

            @pl.when(self.tile + step == tile)
            def _(step=step):
                for part in range(2):
                    act(part, self.tiles(part)[step])


def early_sum_kernel(plan, slots, info, *rest):
    inner, far, canvas = rest[:slots], rest[slots : 2 * slots - 1], rest[2 * slots - 1]
    s, _ = here()
    canvas[...] = jnp.zeros(canvas.shape, jnp.float32)
    for slot in range(slots):
        Patch(plan, info, s, inner[slot], slot, None).add_to(canvas)
    for slot in range(slots - 1):
        Patch(plan, info, s, far[slot], slot, far_side(s), True).add_to(canvas)


def base_kernel(plan, slots, layout, pieces, info, early, inverse, *rest):
    near, refs, (canvas, base) = rest[: 2 * slots], rest[2 * slots : 2 * slots + pieces], rest[2 * slots + pieces :]
    s, t = here()
    canvas[...] = early[...]
    for slot in range(slots):
        Patch(plan, info, s, near[2 * slot : 2 * slot + 2], slot, -far_side(s)).add_to(canvas)
    for tile in range(plan.tiles):
        where = lanes(tile)
        pick_tile(plan, base.at[:, :, where], layout(refs, t)[0], tile, t)
        base[:, :, where] -= canvas[:, :, where] * inverse[:, where][None]


def last_patch(plan, slots, info, patch):
    s, _ = here()
    return Patch(plan, info, s, patch, slots - 1, far_side(s), True)


def take_off(last, target, base, inverse, tile):
    target[...] = base[:, :, lanes(tile)]

    def act(part, values):
        target[part] -= values * inverse[:, lanes(tile)]

    last.tiles_at(tile, act)


def middle_kernel(plan, slots, info, base, patch, inverse, middle):
    _, t = here()
    last = last_patch(plan, slots, info, patch)
    for step in range(plan.mid_tiles):
        take_off(last, middle.at[:, :, lanes(step)], base, inverse, plan.mid_start(t) + step)


def boundary_kernel(plan, slots, info, early, base, patch, inverse, _, *outs):
    bases, sums = outs[: plan.sides], outs[plan.sides :]
    _, t = here()
    last = last_patch(plan, slots, info, patch)
    for pair, total, start in zip(bases, sums, plan.pair_starts(t)):
        total[...] = early[:, :, lanes(start, 2)]
        for step in range(2):
            part_sum = total.at[:, :, lanes(step)]

            def act(part, values, part_sum=part_sum):
                part_sum[part] += values

            last.tiles_at(start + step, act)
            take_off(last, pair.at[:, :, lanes(step)], base, inverse, start + step)


def halo_sum_kernel(plan, slots, info, early, patch, *sums):
    _, t = here()
    last = last_patch(plan, slots, info, patch)
    for total, tile in zip(sums, plan.halo_tiles(t)):
        total[...] = early[:, :, lanes(tile)]

        def act(part, values, total=total):
            total[part] += values

        last.tiles_at(tile, act)


def last_kernel(plan, slots, info, base, patch, inverse, _, *rest):
    nearly, bases, (current, sems) = rest[0], rest[1 : 1 + plan.sides], rest[1 + plan.sides :]
    _, t = here()
    last = last_patch(plan, slots, info, patch)
    copies = []
    for step in range(plan.own):
        where = lanes(step)
        take_off(last, current.at[:, :, where], base, inverse, 1 + step)
        copies.append(pltpu.make_async_copy(current.at[:, :, where], nearly.at[:, :, where], sems.at[step]))
        copies[-1].start()
    for edge, tile in zip(bases, plan.edge_tiles(t)):
        edge[...] = current[:, :, lanes(tile - 1)]
    for copy in copies:
        copy.wait()


def edge_kernel(plan, inverse, *rest):
    bases, received = rest[: plan.sides], rest[plan.sides : 2 * plan.sides]
    _, result, sums, sems = rest[2 * plan.sides :]
    _, t = here()
    copies = []
    for side, tile in enumerate(plan.edge_tiles(t)):
        sums[side] = bases[side][...] - received[side][...] * inverse[:, lanes(tile)][None]
        copies.append(pltpu.make_async_copy(sums.at[side], result.at[:, :, lanes(tile - 1)], sems.at[side]))
        copies[-1].start()
    for copy in copies:
        copy.wait()


def call(kernel, outs, scratch, ins, flops=10**5, size=10**4, in_specs=None, out_specs=None, **options):
    result = pl.pallas_call(
        kernel,
        out_shape=outs,
        in_specs=in_specs or [SMEM if value.dtype == jnp.int32 else VMEM for value in ins],
        out_specs=out_specs or jax.tree.map(lambda _: VMEM, outs),
        scratch_shapes=scratch,
        compiler_params=pltpu.CompilerParams(vmem_limit_bytes=VMEM_BYTES),
        cost_estimate=pl.CostEstimate(flops=flops, bytes_accessed=size, transcendentals=0),
        **options,
    )(*ins)
    return list(result) if isinstance(outs, list) else result


def on_device(plan, object_field, probe_field, amplitudes, centres, counts):
    f32 = jnp.float32
    shape = jax.ShapeDtypeStruct
    size = probe_field.shape[1]
    half = size // 2
    slots = amplitudes.shape[2]
    block_rows = object_field.shape[1]
    block_cols = object_field.shape[2]
    assert block_rows == half and block_cols % LANES == 0 and half == LANES
    width = plan.tiles * LANES
    sides = plan.sides
    spots = centres[0, 0]
    counts = counts.reshape(-1)
    own_amps = amplitudes[0, 0]
    tables = jnp.asarray(dft_tables(size))
    order = jnp.asarray(parity_order(size))
    dma = pltpu.SemaphoreType.DMA

    messages = call(
        lambda *refs: edge_message_kernel(plan, *refs),
        [shape((2, half + 8, LANES), f32)] * sides,
        [dma((sides,))],
        [object_field, spots, counts],
        in_specs=[HBM, SMEM, SMEM],
    )
    halos = plan.across(messages)
    far_block = plan.far_rows(object_field)
    rolled, ordered = call(
        prepare_kernel,
        [shape((slots, 2, size, size), f32), shape((slots, size, size), f32)],
        [pltpu.VMEM((2, 2 * size + 8, size), f32)],
        [spots, probe_field, own_amps, order],
    )
    near_runs = [shape((2, half, count * LANES), f32) for count in chunks(plan.own)]
    messages = call(
        lambda *refs: halo_message_kernel(plan, *refs),
        [shape((2, half + 16, LANES), f32)] * sides + near_runs,
        [],
        [object_field, spots, counts, *halos],
    )
    passed = messages[:sides]
    far = [far_block] + [plan.far_rows(message) for message in passed]
    near = [plan.near_rows(piece) for piece in messages]
    own = [object_field] + passed
    info = call(
        lambda *refs: info_kernel(plan, *refs),
        shape((3 * (sides + 1), LANES), jnp.int32),
        [pltpu.VMEM((3 * (sides + 1), 8, LANES), jnp.int32), dma],
        passed + far[1:] + near[:sides],
        out_specs=SMEM,
    )

    def runs_layout(refs, main, count, side_starts):
        starts = [main] + side_starts
        own, far, near = refs[: 1 + sides], refs[1 + sides : 2 + 2 * sides], refs[2 + 2 * sides :]
        return lay_out(own, starts), lay_out(far, starts), lay_out(near, side_starts + chunk_starts(main, count))

    def first_layout(refs, t):
        return runs_layout(refs, 1, plan.own, plan.halo_tiles(t))

    def later_layout(refs, t):
        return runs_layout(refs, plan.mid_start(t), plan.mid_tiles, plan.pair_starts(t))

    layout = first_layout
    token = spots

    for sweep in range(ITERS):
        pieces = own + far + near
        inner, outer, outer_far = [], [], []
        for slot in range(slots):
            last = slot == slots - 1
            earlier = outer if last else []
            patch = shape((2, half, size), f32)
            outer_part, inner_part, *copies = call(
                lambda *refs, slot=slot, layout=layout, copied=len(earlier): term_kernel(
                    plan, slot, layout, len(pieces), copied, *refs
                ),
                [patch] * 2 + [shape((1, half, size), f32)] * (2 * slots * last),
                [pltpu.VMEM((2, size, size), f32), pltpu.VMEM((3, 3, 2, half, LANES), f32)],
                [spots, counts, *pieces, *earlier, rolled, ordered, tables, token],
            )
            inner.append(inner_part)
            outer.append(outer_part)
            outer_far.append(plan.far_rows(outer_part))
            token = info if sweep == 0 else token
        outer_near = [plan.near_rows(copy) for copy in copies]
        early = call(
            lambda *refs: early_sum_kernel(plan, slots, *refs),
            shape((2, half, width), f32),
            [],
            [info, *inner, *outer_far[:-1]],
        )
        if sweep == 0:
            inverse, *inverse_pairs = call(
                lambda *refs: light_kernel(plan, slots, *refs),
                [shape((half, width), f32)] + [shape((half, 2 * LANES), f32)] * sides,
                [
                    pltpu.VMEM((2 * size + 8, size), f32),
                    pltpu.VMEM((half, width + 2 * plan.own * LANES), f32),
                ],
                [info, probe_field, early],
                in_specs=[SMEM, VMEM, ANY],
            )
        early, base = call(
            lambda *refs, layout=layout: base_kernel(plan, slots, layout, len(pieces), *refs),
            [shape((2, half, width), f32)] * 2,
            [],
            [info, early, inverse, *outer_near, *pieces],
        )
        if sweep < ITERS - 1:
            middle = call(
                lambda *refs: middle_kernel(plan, slots, *refs),
                shape((2, half, plan.mid_tiles * LANES), f32),
                [],
                [info, base, outer_far[-1], inverse],
            )
            far_middle = plan.far_rows(middle)
            boundary = call(
                lambda *refs: boundary_kernel(plan, slots, *refs),
                [shape((2, half, 2 * LANES), f32)] * (2 * sides),
                [],
                [info, early, base, outer_far[-1], inverse, middle],
                in_specs=[SMEM] + [VMEM] * 4 + [ANY],
            )
            bases, sums = boundary[:sides], boundary[sides:]
            received = plan.across(sums)
            near_runs = [shape((2, half, count * LANES), f32) for count in chunks(plan.mid_tiles)]
            updated = call(
                lambda *refs: pair_kernel(sides, *refs),
                [shape((2, half, 2 * LANES), f32)] * (2 * sides) + near_runs,
                [],
                [middle, *bases, *received, *inverse_pairs],
            )
            pairs = updated[:sides]
            own = [middle] + pairs
            far = [far_middle] + [plan.far_rows(piece) for piece in pairs]
            near = [plan.near_rows(piece) for piece in updated[sides:]]
            layout = later_layout
            token = call(
                token_kernel,
                shape((8, LANES), f32),
                [],
                [far_middle],
                in_specs=[ANY],
                flops=10**11,
            )
    sums = call(
        lambda *refs: halo_sum_kernel(plan, slots, *refs),
        [shape((2, half, LANES), f32)] * sides,
        [],
        [info, early, outer_far[-1]],
    )
    nearly, *bases = call(
        lambda *refs: last_kernel(plan, slots, *refs),
        [shape((2, half, block_cols), f32)] + [shape((2, half, LANES), f32)] * sides,
        [pltpu.VMEM((2, half, block_cols), f32), dma((plan.own,))],
        [info, base, outer_far[-1], inverse, sums[0]],
        in_specs=[SMEM, VMEM, VMEM, VMEM, ANY],
        out_specs=[HBM] + [VMEM] * sides,
    )
    received = plan.across(sums)
    return call(
        lambda *refs: edge_kernel(plan, *refs),
        shape(nearly.shape, f32),
        [pltpu.VMEM((sides, 2, half, LANES), f32), dma((sides,))],
        [inverse, *bases, *received, nearly],
        in_specs=[VMEM] * (1 + 2 * sides) + [HBM],
        out_specs=HBM,
        input_output_aliases={1 + 2 * sides: 0},
    )


def solution(mesh):
    sizes = dict(mesh.shape)

    def per_device(object_field, *rest):
        plan = Plan(sizes["sx"], sizes["sy"], object_field.shape[2])
        return on_device(plan, object_field, *rest)

    return jax.shard_map(
        per_device,
        mesh=mesh,
        in_specs=(
            P(None, "sx", "sy"),
            P(),
            P("sx", "sy", None, None, None),
            P("sx", "sy", None, None),
            P(None, "sy"),
        ),
        out_specs=P(None, "sx", "sy"),
        check_vma=False,
    )
```

```python
import math

import jax
import jax.numpy as jnp
import ml_dtypes
import numpy as np
from jax import lax
from jax.experimental import pallas as pl
from jax.experimental.pallas import tpu as pltpu
from jax.sharding import PartitionSpec as P

ITERS = 2
SMOOTH = 1.0
DAMPING = 1.0
LANES = 128
VMEM_BYTES = 12 * 1024 * 1024

VMEM = pl.BlockSpec(memory_space=pltpu.VMEM)
SMEM = pl.BlockSpec(memory_space=pltpu.SMEM)
HBM = pl.BlockSpec(memory_space=pltpu.HBM)
ANY = pl.BlockSpec(memory_space=pl.ANY)


def split_numpy(table):
    high = table.astype(np.float32).astype(ml_dtypes.bfloat16)
    low = (table - high.astype(np.float64)).astype(ml_dtypes.bfloat16)
    return high, low


def dft_tables(length):
    half = length // 2
    index = np.arange(half)
    tables = []
    for parity in range(2):
        angles = 2.0 * math.pi / length * (index[:, None] * (2 * index[None, :] + parity) % length)
        cosine = np.cos(angles) / math.sqrt(length)
        sine = np.sin(angles) / math.sqrt(length)
        forward = np.block([[cosine, -sine], [sine, cosine]])
        tables.append([split_numpy(forward), split_numpy(forward.T)])
    return np.array(tables, dtype=ml_dtypes.bfloat16)


def parity_order(length):
    half = length // 2
    order = np.zeros((length, length))
    for index in range(length):
        order[index, index % 2 * half + index // 2] = 1.0
    return np.stack([order, order.T]).astype(ml_dtypes.bfloat16)


def split(values):
    high = values.astype(jnp.bfloat16)
    low = (values - high.astype(jnp.float32)).astype(jnp.bfloat16)
    return high, low


def times_table(values, table):
    high, low = split(values)
    left = jnp.concatenate([high, low, high], axis=1)
    right = jnp.concatenate([table[0], table[0], table[1]], axis=0)
    return jnp.dot(left, right, preferred_element_type=jnp.float32)


def table_times(table, values):
    high, low = split(values)
    left = jnp.concatenate([table[0], table[0], table[1]], axis=1)
    right = jnp.concatenate([high, low, high], axis=0)
    return jnp.dot(left, right, preferred_element_type=jnp.float32)


class Plan:
    def __init__(self, sx_size, sy_size, block_cols):
        self.sx_size = sx_size
        self.sy_size = sy_size
        self.own = block_cols // LANES
        self.tiles = self.own + 2
        self.paired = sy_size == 2
        self.sides = 1 if self.paired else 2

    def rights(self, t):
        return [1 - t] if self.paired else [0, 1]

    def pair_starts(self, t):
        return [right * (self.tiles - 2) for right in self.rights(t)]

    def halo_tiles(self, t):
        return [right * (self.tiles - 1) for right in self.rights(t)]

    def edge_tiles(self, t):
        return [1 + right * (self.tiles - 3) for right in self.rights(t)]

    def mid_start(self, t):
        return 1 + t if self.paired else 2

    @property
    def mid_tiles(self):
        return self.tiles - 3 if self.paired else self.tiles - 4

    def across(self, values, axis_name="sy"):
        if self.paired:
            return [lax.ppermute(values[0], axis_name, [(0, 1), (1, 0)])]
        ends = self.sy_size - 1
        return [
            lax.ppermute(values[1], axis_name, [(i, i + 1) for i in range(ends)]),
            lax.ppermute(values[0], axis_name, [(i + 1, i) for i in range(ends)]),
        ]

    def far_rows(self, values):
        rows, columns = self.sx_size, self.sy_size
        pairs = [(i * columns + t, (i + 1) * columns + t) for i in range(1, rows - 1, 2) for t in range(columns)]
        for i in (0, rows - 1):
            pairs += [(i * columns + t, i * columns + t + 1) for t in range(0, columns - 1, 2)]
        return lax.ppermute(values, ("sx", "sy"), pairs + [(j, i) for i, j in pairs])

    def near_rows(self, values):
        return lax.ppermute(values, "sx", [(i, i ^ 1) for i in range(self.sx_size)])

    def outermost(self, s):
        return (s == 0) | (s == self.sx_size - 1)


def far_side(s):
    return 2 * (s % 2) - 1


def lanes(tile, count=1):
    if isinstance(tile, int):
        return pl.ds(tile * LANES, count * LANES)
    return pl.ds(pl.multiple_of(tile * LANES, LANES), count * LANES)


def pick_tile(plan, target, pieces, tile, t):
    rows = target.shape[1]
    if plan.paired:

        @pl.when(tile == (plan.tiles - 1) * t)
        def _():
            target[...] = jnp.zeros(target.shape, jnp.float32)

    for ref, offset, count, start in pieces:

        @pl.when((tile >= start) & (tile < start + count))
        def _(ref=ref, offset=offset, start=start):
            target[...] = ref[:, :rows, lanes(tile - start + offset)]


def lay_out(refs, starts):
    return [(ref, 0, ref.shape[2] // LANES, start) for ref, start in zip(refs, starts)]


def chunks(count):
    return [min(2, count - first) for first in range(0, count, 2)]


def chunk_starts(start, count):
    return [start + 2 * index for index in range(len(chunks(count)))]


def spread(source, targets):
    offset = 0
    for target in targets:
        columns = target.shape[2]
        target[...] = source[:, :, offset : offset + columns]
        offset += columns


def rows_at(ref, start, count):
    offset = start % 8
    values = ref[pl.ds(pl.multiple_of(start - offset, 8), count + 8)]
    return pltpu.roll(values, (count + 8 - offset) % (count + 8), 0)[:count]


def here():
    return lax.axis_index("sx"), lax.axis_index("sy")


def info_rows(centres, count):
    lane = lax.broadcasted_iota(jnp.int32, (8, LANES), 1)
    slots = centres.shape[0]
    values = [centres[slot, axis] for slot in range(slots) for axis in range(2)] + [count]
    line = jnp.zeros((8, LANES), jnp.int32)
    for index, value in enumerate(values):
        line = jnp.where(lane == index, value, line)
    return line.astype(jnp.float32)


def edge_message_kernel(plan, block, centres, counts, *rest):
    messages, sems = rest[: plan.sides], rest[plan.sides]
    s, t = here()
    half = block.shape[1]
    copies = [
        pltpu.make_async_copy(block.at[:, :, lanes(tile - 1)], message.at[:, :half], sems.at[side])
        for side, (message, tile) in enumerate(zip(messages, plan.edge_tiles(t)))
    ]
    for copy in copies:
        copy.start()
    rows = info_rows(centres, counts[s])
    for message in messages:
        message[0, half:] = rows
        message[1, half:] = rows
    for copy in copies:
        copy.wait()


def halo_message_kernel(plan, block, centres, counts, *rest):
    s, _ = here()
    received, messages, near = rest[: plan.sides], rest[plan.sides : 2 * plan.sides], rest[2 * plan.sides :]
    own = info_rows(centres, counts[s])
    for source, message in zip(received, messages):
        rows = source.shape[1]
        message[:, :rows] = source[...]
        message[0, rows:] = own
        message[1, rows:] = own
    spread(block, near)


def pair_kernel(plan, base, early, inverse, middle, *rest):
    sides = plan.sides
    sums, received, results = (rest[k * sides : (k + 1) * sides] for k in range(3))
    near = rest[3 * sides :]
    _, t = here()
    for total, other, result, copy, start in zip(sums, received, results, near, plan.pair_starts(t)):
        where = lanes(start, 2)
        missing = total[...] + other[...] - early[:, :, where]
        values = base[:, :, where] - missing * inverse[:, where][None]
        result[...] = values
        copy[...] = values
    spread(middle, near[sides:])


def prepare_kernel(centres, probe, amps, order, rolled, ordered, padded):
    size = probe.shape[1]
    half = size // 2
    padded[:, :half] = jnp.zeros((2, half, size), jnp.float32)
    padded[:, half + size :] = jnp.zeros((2, half + 8, size), jnp.float32)
    padded[:, half : half + size] = probe[...]
    for slot in range(amps.shape[0]):
        row = centres[slot, 0]
        col = centres[slot, 1]
        for part in range(2):
            shape = padded.at[part]
            upper = rows_at(shape, half - row, half) + rows_at(shape, half + size - row, half)
            lower = rows_at(shape, size - row, half)
            rolled[slot, part] = pltpu.roll(jnp.concatenate([upper, lower], axis=0), col % size, 1)
        high, low = split(amps[slot])
        across = jnp.dot(
            jnp.concatenate([high, low], axis=1),
            jnp.concatenate([order[0], order[0]], axis=0),
            preferred_element_type=jnp.float32,
        )
        high, low = split(across)
        ordered[slot] = jnp.dot(
            jnp.concatenate([order[1], order[1]], axis=1),
            jnp.concatenate([high, low], axis=0),
            preferred_element_type=jnp.float32,
        )


def info_kernel(plan, *rest):
    groups = [rest[k * plan.sides : (k + 1) * plan.sides] for k in range(3)]
    info, known, sem = rest[3 * plan.sides :]
    s, _ = here()
    upper = s % 2 == 0
    height = groups[0][0].shape[1] - 16

    def lines(messages):
        return [messages[0][0, height + 8 : height + 16]] + [message[0, height : height + 8] for message in messages]

    own, far, near = (lines(messages) for messages in groups)
    far = [jnp.where(plan.outermost(s), 0.0, line) for line in far]
    for turn in range(plan.sides + 1):
        for kind, line in ((0, jnp.where(upper, far[turn], near[turn])), (1, own[turn]), (2, jnp.where(upper, near[turn], far[turn]))):
            known[kind * (plan.sides + 1) + turn] = line.astype(jnp.int32)
    copy = pltpu.make_async_copy(known.at[:, 0], info, sem)
    copy.start()
    copy.wait()


def light_kernel(plan, slots, info, probe, _, inverse, padded, canvas):
    size = probe.shape[1]
    half = size // 2
    _, t = here()
    padded[:half] = jnp.zeros((half, size), jnp.float32)
    padded[half + size :] = jnp.zeros((half + 8, size), jnp.float32)
    padded[half : half + size] = probe[0] * probe[0] + probe[1] * probe[1]
    canvas[...] = jnp.zeros(canvas.shape, jnp.float32)
    reach = plan.sides + 1
    spare = jnp.zeros((half, LANES), jnp.float32)
    for down in (-1, 0, 1):

        def add(step, carry, down=down):
            turn = step // slots
            slot = step % slots
            over = turn * (1 - 2 * t) if plan.paired else jnp.where(turn == 0, 0, 2 * turn - 3)
            index = (down + 1) * reach + turn

            @pl.when(slot < info[index, 2 * slots])
            def _():
                row = info[index, 2 * slot]
                col = info[index, 2 * slot + 1]
                power = rows_at(padded, size - half * down - row, half)
                shifted = pltpu.roll(jnp.concatenate([power, spare], axis=1), col % LANES, 1)
                first = col // LANES + plan.own * (over + 1)
                canvas[:, lanes(first, 3)] += shifted

            return carry

        lax.fori_loop(0, reach * slots, add, 0)
    inverse[...] = 1.0 / (canvas[:, lanes(plan.own, plan.tiles)] + DAMPING)


def term_kernel(plan, slot, layout, pieces, copied, centres, counts, *rest):
    refs, rest = rest[:pieces], rest[pieces:]
    earlier, (probe, amps, tables, _, outer, inner), rest = rest[:copied], rest[copied : copied + 6], rest[copied + 6 :]
    near_outers, (window, picked) = rest[:-2], rest[-2:]
    size = probe.shape[2]
    half = size // 2
    s, t = here()
    row = centres[slot, 0]
    col = centres[slot, 1]
    alive = slot < counts[s]

    @pl.when(jnp.logical_not(alive))
    def _():
        outer[...] = jnp.zeros(outer.shape, jnp.float32)
        inner[...] = jnp.zeros(inner.shape, jnp.float32)

    @pl.when(alive)
    def _():
        tile = col // LANES
        first = tile % 2
        rest_col = col % LANES
        from_tile = lax.broadcasted_iota(jnp.int32, (half, LANES), 1) >= rest_col
        from_upper = lax.broadcasted_iota(jnp.int32, (half, LANES), 0) >= row
        side = far_side(s)
        own, far, near = layout(refs, t)
        for kind, source in ((1, own), (1 + side, far), (1 - side, near)):
            for step in range(3):
                pick_tile(plan, picked.at[kind, step], source, tile + step, t)

        @pl.when(plan.outermost(s))
        def _():
            picked[1 + side] = jnp.zeros(picked.shape[1:], jnp.float32)

        for part in range(2):
            edge = [jnp.where(from_tile, picked[kind, 0, part], picked[kind, 2, part]) for kind in range(3)]
            window[part, :half, lanes(first)] = jnp.where(from_upper, edge[0], edge[2])
            window[part, half:, lanes(first)] = edge[1]
            window[part, :half, lanes(1 - first)] = jnp.where(from_upper, picked[0, 1, part], picked[2, 1, part])
            window[part, half:, lanes(1 - first)] = picked[1, 1, part]

        probe_real = probe[slot, 0]
        probe_imag = probe[slot, 1]
        exit_real = probe_real * window[0] - probe_imag * window[1]
        exit_imag = probe_real * window[1] + probe_imag * window[0]

        halves = [
            jnp.concatenate([exit_real[:, :half] + sign * exit_real[:, half:], exit_imag[:, :half] + sign * exit_imag[:, half:]], axis=1)
            for sign in (1.0, -1.0)
        ]
        across = [times_table(halves[parity], tables[parity, 0]) for parity in range(2)]
        real = jnp.concatenate([across[0][:, :half], across[1][:, :half]], axis=1)
        imag = jnp.concatenate([across[0][:, half:], across[1][:, half:]], axis=1)
        halves = [
            jnp.concatenate([real[:half] + sign * real[half:], imag[:half] + sign * imag[half:]], axis=0)
            for sign in (1.0, -1.0)
        ]
        back = []
        for parity in range(2):
            pattern = table_times(tables[parity, 1], halves[parity])
            far_real = pattern[:half]
            far_imag = pattern[half:]
            amplitude = amps[slot, parity * half : (parity + 1) * half]
            factor = 1.0 - amplitude * lax.rsqrt(far_real * far_real + far_imag * far_imag + SMOOTH)
            miss = jnp.concatenate([far_real * factor, far_imag * factor], axis=0)
            back.append(table_times(tables[parity, 0], miss))
        real = jnp.concatenate([back[0][:half] + back[1][:half], back[0][:half] - back[1][:half]], axis=0)
        imag = jnp.concatenate([back[0][half:] + back[1][half:], back[0][half:] - back[1][half:]], axis=0)
        both = []
        for parity in range(2):
            columns = slice(parity * half, (parity + 1) * half)
            both.append(times_table(jnp.concatenate([real[:, columns], imag[:, columns]], axis=1), tables[parity, 1]))
        near_real = jnp.concatenate([both[0][:, :half] + both[1][:, :half], both[0][:, :half] - both[1][:, :half]], axis=1)
        near_imag = jnp.concatenate([both[0][:, half:] + both[1][:, half:], both[0][:, half:] - both[1][:, half:]], axis=1)
        term_real = probe_real * near_real + probe_imag * near_imag
        term_imag = probe_real * near_imag - probe_imag * near_real
        outer[0] = term_real[:half]
        outer[1] = term_imag[:half]
        inner[0] = term_real[half:]
        inner[1] = term_imag[half:]

    for index, source in enumerate((*earlier, outer)):
        line = 0
        for target in near_outers:
            rows = target.shape[1]
            target[2 * index : 2 * index + 2] = source[:, line : line + rows]
            line += rows


class Patch:
    def __init__(self, plan, info, s, patch, slot, down, far=False):
        runs = patch if isinstance(patch, (list, tuple)) else [patch]
        half = sum(run.shape[1] for run in runs)
        index = (1 if down is None else 1 + down) * (plan.sides + 1)
        row = info[index, 2 * slot]
        col = info[index, 2 * slot + 1]
        self.runs = runs
        self.tile = col // LANES
        self.first = self.tile % 2
        self.from_tile = lax.broadcasted_iota(jnp.int32, (half, LANES), 1) >= col % LANES
        self.rows = None
        if down is not None:
            line = lax.broadcasted_iota(jnp.int32, (half, LANES), 0)
            after = jnp.where(down > 0, half, row)
            if far:
                after = jnp.where(plan.outermost(s), 0, after)
            self.rows = (line >= jnp.where(down > 0, row, 0)) & (line < after)

    def lines(self, part, place):
        values = jnp.concatenate([run[part, :, lanes(place)] for run in self.runs], axis=0)
        return values if self.rows is None else jnp.where(self.rows, values, 0.0)

    def tiles(self, part):
        edge = self.lines(part, self.first)
        middle = self.lines(part, 1 - self.first)
        return jnp.where(self.from_tile, edge, 0.0), middle, jnp.where(self.from_tile, 0.0, edge)

    def add_to(self, canvas):
        for part in range(2):
            for step, values in enumerate(self.tiles(part)):
                canvas[part, :, lanes(self.tile + step)] += values

    def tiles_at(self, tile, act):
        for step in range(3):

            @pl.when(self.tile + step == tile)
            def _(step=step):
                for part in range(2):
                    act(part, self.tiles(part)[step])


def early_sum_kernel(plan, slots, info, *rest):
    inner, near, canvas = rest[:slots], rest[slots:-1], rest[-1]
    s, _ = here()
    canvas[...] = jnp.zeros(canvas.shape, jnp.float32)
    for slot in range(slots):
        Patch(plan, info, s, inner[slot], slot, None).add_to(canvas)
        runs = [run.at[2 * slot : 2 * slot + 2] for run in near]
        Patch(plan, info, s, runs, slot, -far_side(s)).add_to(canvas)


def base_kernel(plan, slots, layout, pieces, info, early, inverse, *rest):
    far, refs, (canvas, base) = rest[: slots - 1], rest[slots - 1 : slots - 1 + pieces], rest[slots - 1 + pieces :]
    s, t = here()
    canvas[...] = early[...]
    for slot in range(slots - 1):
        Patch(plan, info, s, far[slot], slot, far_side(s), True).add_to(canvas)
    for tile in range(plan.tiles):
        where = lanes(tile)
        pick_tile(plan, base.at[:, :, where], layout(refs, t)[0], tile, t)
        base[:, :, where] -= canvas[:, :, where] * inverse[:, where][None]


def last_patch(plan, slots, info, patch):
    s, _ = here()
    return Patch(plan, info, s, patch, slots - 1, far_side(s), True)


def take_off(last, target, base, inverse, tile):
    target[...] = base[:, :, lanes(tile)]

    def act(part, values):
        target[part] -= values * inverse[:, lanes(tile)]

    last.tiles_at(tile, act)


def middle_kernel(plan, slots, info, base, patch, inverse, _, middle):
    _, t = here()
    last = last_patch(plan, slots, info, patch)
    for step in range(plan.mid_tiles):
        take_off(last, middle.at[:, :, lanes(step)], base, inverse, plan.mid_start(t) + step)


def boundary_kernel(plan, slots, info, early, patch, *sums):
    _, t = here()
    last = last_patch(plan, slots, info, patch)
    for total, start in zip(sums, plan.pair_starts(t)):
        total[...] = early[:, :, lanes(start, 2)]
        for step in range(2):

            def act(part, values, total=total, step=step):
                total[part, :, lanes(step)] += values

            last.tiles_at(start + step, act)


def halo_sum_kernel(plan, slots, info, early, patch, *sums):
    _, t = here()
    last = last_patch(plan, slots, info, patch)
    for total, tile in zip(sums, plan.halo_tiles(t)):
        total[...] = early[:, :, lanes(tile)]

        def act(part, values, total=total):
            total[part] += values

        last.tiles_at(tile, act)


def last_kernel(plan, slots, info, base, patch, inverse, _, *rest):
    nearly, bases, (current, sems) = rest[0], rest[1 : 1 + plan.sides], rest[1 + plan.sides :]
    _, t = here()
    last = last_patch(plan, slots, info, patch)
    copies = []
    for step in range(plan.own):
        where = lanes(step)
        take_off(last, current.at[:, :, where], base, inverse, 1 + step)
        copies.append(pltpu.make_async_copy(current.at[:, :, where], nearly.at[:, :, where], sems.at[step]))
        copies[-1].start()
    for edge, tile in zip(bases, plan.edge_tiles(t)):
        edge[...] = current[:, :, lanes(tile - 1)]
    for copy in copies:
        copy.wait()


def edge_kernel(plan, inverse, *rest):
    bases, received = rest[: plan.sides], rest[plan.sides : 2 * plan.sides]
    _, result, sums, sems = rest[2 * plan.sides :]
    _, t = here()
    copies = []
    for side, tile in enumerate(plan.edge_tiles(t)):
        sums[side] = bases[side][...] - received[side][...] * inverse[:, lanes(tile)][None]
        copies.append(pltpu.make_async_copy(sums.at[side], result.at[:, :, lanes(tile - 1)], sems.at[side]))
        copies[-1].start()
    for copy in copies:
        copy.wait()


def call(kernel, outs, scratch, ins, flops=10**5, size=10**4, in_specs=None, out_specs=None, **options):
    result = pl.pallas_call(
        kernel,
        out_shape=outs,
        in_specs=in_specs or [SMEM if value.dtype == jnp.int32 else VMEM for value in ins],
        out_specs=out_specs or jax.tree.map(lambda _: VMEM, outs),
        scratch_shapes=scratch,
        compiler_params=pltpu.CompilerParams(vmem_limit_bytes=VMEM_BYTES),
        cost_estimate=pl.CostEstimate(flops=flops, bytes_accessed=size, transcendentals=0),
        **options,
    )(*ins)
    return list(result) if isinstance(outs, list) else result


def on_device(plan, object_field, probe_field, amplitudes, centres, counts):
    f32 = jnp.float32
    shape = jax.ShapeDtypeStruct
    size = probe_field.shape[1]
    half = size // 2
    slots = amplitudes.shape[2]
    block_rows = object_field.shape[1]
    block_cols = object_field.shape[2]
    assert block_rows == half and block_cols % LANES == 0 and half == LANES
    width = plan.tiles * LANES
    sides = plan.sides
    spots = centres[0, 0]
    counts = counts.reshape(-1)
    own_amps = amplitudes[0, 0]
    tables = jnp.asarray(dft_tables(size))
    order = jnp.asarray(parity_order(size))
    dma = pltpu.SemaphoreType.DMA

    messages = call(
        lambda *refs: edge_message_kernel(plan, *refs),
        [shape((2, half + 8, LANES), f32)] * sides,
        [dma((sides,))],
        [object_field, spots, counts],
        in_specs=[HBM, SMEM, SMEM],
    )
    halos = plan.across(messages)
    far_block = plan.far_rows(object_field)
    rolled, ordered = call(
        prepare_kernel,
        [shape((slots, 2, size, size), f32), shape((slots, size, size), f32)],
        [pltpu.VMEM((2, 2 * size + 8, size), f32)],
        [spots, probe_field, own_amps, order],
    )
    near_runs = [shape((2, half, count * LANES), f32) for count in chunks(plan.own)]
    messages = call(
        lambda *refs: halo_message_kernel(plan, *refs),
        [shape((2, half + 16, LANES), f32)] * sides + near_runs,
        [],
        [object_field, spots, counts, *halos],
    )
    passed = messages[:sides]
    far = [far_block] + [plan.far_rows(message) for message in passed]
    near = [plan.near_rows(piece) for piece in messages]
    own = [object_field] + passed
    info = call(
        lambda *refs: info_kernel(plan, *refs),
        shape((3 * (sides + 1), LANES), jnp.int32),
        [pltpu.VMEM((3 * (sides + 1), 8, LANES), jnp.int32), dma],
        passed + far[1:] + near[:sides],
        out_specs=SMEM,
    )

    def runs_layout(refs, main, count, side_starts):
        starts = [main] + side_starts
        own, far, near = refs[: 1 + sides], refs[1 + sides : 2 + 2 * sides], refs[2 + 2 * sides :]
        return lay_out(own, starts), lay_out(far, starts), lay_out(near, side_starts + chunk_starts(main, count))

    def first_layout(refs, t):
        return runs_layout(refs, 1, plan.own, plan.halo_tiles(t))

    def later_layout(refs, t):
        return runs_layout(refs, plan.mid_start(t), plan.mid_tiles, plan.pair_starts(t))

    layout = first_layout
    token = spots

    third = half // 24 * 8
    near_heights = [half - 2 * third, third, third]
    for sweep in range(ITERS):
        pieces = own + far + near
        inner, outer, outer_far = [], [], []
        for slot in range(slots):
            last = slot == slots - 1
            earlier = outer if last else []
            patch = shape((2, half, size), f32)
            outer_part, inner_part, *copies = call(
                lambda *refs, slot=slot, layout=layout, copied=len(earlier): term_kernel(
                    plan, slot, layout, len(pieces), copied, *refs
                ),
                [patch] * 2 + [shape((2 * slots, rows, size), f32) for rows in near_heights if last],
                [pltpu.VMEM((2, size, size), f32), pltpu.VMEM((3, 3, 2, half, LANES), f32)],
                [spots, counts, *pieces, *earlier, rolled, ordered, tables, token],
            )
            inner.append(inner_part)
            outer.append(outer_part)
            outer_far.append(plan.far_rows(outer_part))
            token = info if sweep == 0 else token
        outer_near = [plan.near_rows(copy) for copy in copies]
        if sweep == 0:
            inverse = call(
                lambda *refs: light_kernel(plan, slots, *refs),
                shape((half, width), f32),
                [
                    pltpu.VMEM((2 * size + 8, size), f32),
                    pltpu.VMEM((half, width + 2 * plan.own * LANES), f32),
                ],
                [info, probe_field, copies[0]],
                in_specs=[SMEM, VMEM, ANY],
            )
        early = call(
            lambda *refs: early_sum_kernel(plan, slots, *refs),
            shape((2, half, width), f32),
            [],
            [info, *inner, *outer_near],
        )
        early, base = call(
            lambda *refs, layout=layout: base_kernel(plan, slots, layout, len(pieces), *refs),
            [shape((2, half, width), f32)] * 2,
            [],
            [info, early, inverse, *outer_far[:-1], *pieces],
        )
        if sweep < ITERS - 1:
            sums = call(
                lambda *refs: boundary_kernel(plan, slots, *refs),
                [shape((2, half, 2 * LANES), f32)] * sides,
                [],
                [info, early, outer_far[-1]],
            )
            received = plan.across(sums)
            middle = call(
                lambda *refs: middle_kernel(plan, slots, *refs),
                shape((2, half, plan.mid_tiles * LANES), f32),
                [],
                [info, base, outer_far[-1], inverse, sums[0]],
                in_specs=[SMEM, VMEM, VMEM, VMEM, ANY],
            )
            far_middle = plan.far_rows(middle)
            near_runs = [shape((2, half, count * LANES), f32) for count in chunks(plan.mid_tiles)]
            updated = call(
                lambda *refs: pair_kernel(plan, *refs),
                [shape((2, half, 2 * LANES), f32)] * (2 * sides) + near_runs,
                [],
                [base, early, inverse, middle, *sums, *received],
            )
            pairs = updated[:sides]
            own = [middle] + pairs
            far = [far_middle] + [plan.far_rows(piece) for piece in pairs]
            near = [plan.near_rows(piece) for piece in updated[sides:]]
            layout = later_layout
            token = spots
    sums = call(
        lambda *refs: halo_sum_kernel(plan, slots, *refs),
        [shape((2, half, LANES), f32)] * sides,
        [],
        [info, early, outer_far[-1]],
    )
    nearly, *bases = call(
        lambda *refs: last_kernel(plan, slots, *refs),
        [shape((2, half, block_cols), f32)] + [shape((2, half, LANES), f32)] * sides,
        [pltpu.VMEM((2, half, block_cols), f32), dma((plan.own,))],
        [info, base, outer_far[-1], inverse, sums[0]],
        in_specs=[SMEM, VMEM, VMEM, VMEM, ANY],
        out_specs=[HBM] + [VMEM] * sides,
    )
    received = plan.across(sums)
    return call(
        lambda *refs: edge_kernel(plan, *refs),
        shape(nearly.shape, f32),
        [pltpu.VMEM((sides, 2, half, LANES), f32), dma((sides,))],
        [inverse, *bases, *received, nearly],
        in_specs=[VMEM] * (1 + 2 * sides) + [HBM],
        out_specs=HBM,
        input_output_aliases={1 + 2 * sides: 0},
    )


def solution(mesh):
    sizes = dict(mesh.shape)

    def per_device(object_field, *rest):
        plan = Plan(sizes["sx"], sizes["sy"], object_field.shape[2])
        return on_device(plan, object_field, *rest)

    return jax.shard_map(
        per_device,
        mesh=mesh,
        in_specs=(
            P(None, "sx", "sy"),
            P(),
            P("sx", "sy", None, None, None),
            P("sx", "sy", None, None),
            P(None, "sy"),
        ),
        out_specs=P(None, "sx", "sy"),
        check_vma=False,
    )
```

```python
import math

import jax
import jax.numpy as jnp
import ml_dtypes
import numpy as np
from jax import lax
from jax.experimental import pallas as pl
from jax.experimental.pallas import tpu as pltpu
from jax.sharding import PartitionSpec as P

ITERS = 2
SMOOTH = 1.0
DAMPING = 1.0
LANES = 128
VMEM_BYTES = 12 * 1024 * 1024

VMEM = pl.BlockSpec(memory_space=pltpu.VMEM)
SMEM = pl.BlockSpec(memory_space=pltpu.SMEM)
HBM = pl.BlockSpec(memory_space=pltpu.HBM)
ANY = pl.BlockSpec(memory_space=pl.ANY)


def split_numpy(table):
    high = table.astype(np.float32).astype(ml_dtypes.bfloat16)
    low = (table - high.astype(np.float64)).astype(ml_dtypes.bfloat16)
    return high, low


def dft_tables(length):
    half = length // 2
    index = np.arange(half)
    tables = []
    for parity in range(2):
        angles = 2.0 * math.pi / length * (index[:, None] * (2 * index[None, :] + parity) % length)
        cosine = np.cos(angles) / math.sqrt(length)
        sine = np.sin(angles) / math.sqrt(length)
        forward = np.block([[cosine, -sine], [sine, cosine]])
        tables.append([split_numpy(forward), split_numpy(forward.T)])
    return np.array(tables, dtype=ml_dtypes.bfloat16)


def parity_order(length):
    half = length // 2
    order = np.zeros((length, length))
    for index in range(length):
        order[index, index % 2 * half + index // 2] = 1.0
    return np.stack([order, order.T]).astype(ml_dtypes.bfloat16)


def split(values):
    high = values.astype(jnp.bfloat16)
    low = (values - high.astype(jnp.float32)).astype(jnp.bfloat16)
    return high, low


def times_table(values, table):
    high, low = split(values)
    left = jnp.concatenate([high, low, high], axis=1)
    right = jnp.concatenate([table[0], table[0], table[1]], axis=0)
    return jnp.dot(left, right, preferred_element_type=jnp.float32)


def table_times(table, values):
    high, low = split(values)
    left = jnp.concatenate([table[0], table[0], table[1]], axis=1)
    right = jnp.concatenate([high, low, high], axis=0)
    return jnp.dot(left, right, preferred_element_type=jnp.float32)


class Plan:
    def __init__(self, sx_size, sy_size, block_rows, block_cols):
        self.rows = block_rows
        self.sx_size = sx_size
        self.sy_size = sy_size
        self.own = block_cols // LANES
        self.tiles = self.own + 2
        self.paired = sy_size == 2
        self.sides = 1 if self.paired else 2

    def rights(self, t):
        return [1 - t] if self.paired else [0, 1]

    def pair_starts(self, t):
        return [right * (self.tiles - 2) for right in self.rights(t)]

    def halo_tiles(self, t):
        return [right * (self.tiles - 1) for right in self.rights(t)]

    def edge_tiles(self, t):
        return [1 + right * (self.tiles - 3) for right in self.rights(t)]

    def mid_start(self, t):
        return 1 + t if self.paired else 2

    @property
    def mid_tiles(self):
        return self.tiles - 3 if self.paired else self.tiles - 4

    def across(self, values, axis_name="sy"):
        if self.paired:
            return [lax.ppermute(values[0], axis_name, [(0, 1), (1, 0)])]
        ends = self.sy_size - 1
        return [
            lax.ppermute(values[1], axis_name, [(i, i + 1) for i in range(ends)]),
            lax.ppermute(values[0], axis_name, [(i + 1, i) for i in range(ends)]),
        ]

    def far_rows(self, values):
        rows, columns = self.sx_size, self.sy_size
        pairs = [(i * columns + t, (i + 1) * columns + t) for i in range(1, rows - 1, 2) for t in range(columns)]
        for i in (0, rows - 1):
            pairs += [(i * columns + t, i * columns + t + 1) for t in range(0, columns - 1, 2)]
        return lax.ppermute(values, ("sx", "sy"), pairs + [(j, i) for i, j in pairs])

    def near_rows(self, values):
        return lax.ppermute(values, "sx", [(i, i ^ 1) for i in range(self.sx_size)])

    def outermost(self, s):
        return (s == 0) | (s == self.sx_size - 1)


def far_side(s):
    return 2 * (s % 2) - 1


def lanes(tile, count=1):
    if isinstance(tile, int):
        return pl.ds(tile * LANES, count * LANES)
    return pl.ds(pl.multiple_of(tile * LANES, LANES), count * LANES)


def pick_tile(plan, target, pieces, tile, t):
    rows = target.shape[1]
    if plan.paired:

        @pl.when(tile == (plan.tiles - 1) * t)
        def _():
            target[...] = jnp.zeros(target.shape, jnp.float32)

    for ref, offset, count, start in pieces:

        @pl.when((tile >= start) & (tile < start + count))
        def _(ref=ref, offset=offset, start=start):
            target[...] = ref[:, :rows, lanes(tile - start + offset)]


def lay_out(refs, starts):
    return [(ref, 0, ref.shape[2] // LANES, start) for ref, start in zip(refs, starts)]


def chunks(count):
    return [min(2, count - first) for first in range(0, count, 2)]


def chunk_starts(start, count):
    return [start + 2 * index for index in range(len(chunks(count)))]


def spread(source, targets):
    offset = 0
    for target in targets:
        columns = target.shape[2]
        target[...] = source[:, :, offset : offset + columns]
        offset += columns


def rows_at(ref, start, count):
    offset = start % 8
    values = ref[pl.ds(pl.multiple_of(start - offset, 8), count + 8)]
    return pltpu.roll(values, (count + 8 - offset) % (count + 8), 0)[:count]


def here():
    return lax.axis_index("sx"), lax.axis_index("sy")


def info_rows(centres, count):
    lane = lax.broadcasted_iota(jnp.int32, (8, LANES), 1)
    slots = centres.shape[0]
    values = [centres[slot, axis] for slot in range(slots) for axis in range(2)] + [count]
    line = jnp.zeros((8, LANES), jnp.int32)
    for index, value in enumerate(values):
        line = jnp.where(lane == index, value, line)
    return line.astype(jnp.float32)


def edge_message_kernel(plan, block, centres, counts, *rest):
    messages, sems = rest[: plan.sides], rest[plan.sides]
    s, t = here()
    half = block.shape[1]
    copies = [
        pltpu.make_async_copy(block.at[:, :, lanes(tile - 1)], message.at[:, :half], sems.at[side])
        for side, (message, tile) in enumerate(zip(messages, plan.edge_tiles(t)))
    ]
    for copy in copies:
        copy.start()
    rows = info_rows(centres, counts[s])
    for message in messages:
        message[0, half:] = rows
        message[1, half:] = rows
    for copy in copies:
        copy.wait()


def halo_message_kernel(plan, centres, counts, *rest):
    received, far, near = (rest[k * plan.sides : (k + 1) * plan.sides] for k in range(3))
    own = info_rows(centres, counts[lax.axis_index("sx")])
    for source, *messages in zip(received, far, near):
        for message in messages:
            rows = source.shape[1]
            message[:, :rows] = source[...]
            for line in range(rows, message.shape[1], 8):
                message[0, line : line + 8] = own
                message[1, line : line + 8] = own


def pair_kernel(plan, base, early, inverse, middle, *rest):
    sides = plan.sides
    sums, received, results = (rest[k * sides : (k + 1) * sides] for k in range(3))
    near = rest[3 * sides :]
    _, t = here()
    for total, other, result, copy, start in zip(sums, received, results, near, plan.pair_starts(t)):
        where = lanes(start, 2)
        missing = total[...] + other[...] - early[:, :, where]
        values = base[:, :, where] - missing * inverse[:, where][None]
        result[...] = values
        copy[...] = values
    spread(middle, near[sides:])


def prepare_kernel(centres, probe, amps, order, rolled, ordered, padded):
    size = probe.shape[1]
    half = size // 2
    padded[:, :half] = jnp.zeros((2, half, size), jnp.float32)
    padded[:, half + size :] = jnp.zeros((2, half + 8, size), jnp.float32)
    padded[:, half : half + size] = probe[...]
    for slot in range(amps.shape[0]):
        row = centres[slot, 0]
        col = centres[slot, 1]
        for part in range(2):
            shape = padded.at[part]
            upper = rows_at(shape, half - row, half) + rows_at(shape, half + size - row, half)
            lower = rows_at(shape, size - row, half)
            rolled[slot, part] = pltpu.roll(jnp.concatenate([upper, lower], axis=0), col % size, 1)
        high, low = split(amps[slot])
        across = jnp.dot(
            jnp.concatenate([high, low], axis=1),
            jnp.concatenate([order[0], order[0]], axis=0),
            preferred_element_type=jnp.float32,
        )
        high, low = split(across)
        ordered[slot] = jnp.dot(
            jnp.concatenate([order[1], order[1]], axis=1),
            jnp.concatenate([high, low], axis=0),
            preferred_element_type=jnp.float32,
        )


def info_kernel(plan, *rest):
    groups = [rest[k * plan.sides : (k + 1) * plan.sides] for k in range(3)]
    _, info, known, sem = rest[3 * plan.sides :]
    s, _ = here()
    upper = s % 2 == 0
    height = plan.rows

    def lines(messages):
        return [messages[0][0, height + 8 : height + 16]] + [message[0, height : height + 8] for message in messages]

    own, far, near = (lines(messages) for messages in groups)
    far = [jnp.where(plan.outermost(s), 0.0, line) for line in far]
    for turn in range(plan.sides + 1):
        for kind, line in ((0, jnp.where(upper, far[turn], near[turn])), (1, own[turn]), (2, jnp.where(upper, near[turn], far[turn]))):
            known[kind * (plan.sides + 1) + turn] = line.astype(jnp.int32)
    copy = pltpu.make_async_copy(known.at[:, 0], info, sem)
    copy.start()
    copy.wait()


def light_kernel(plan, slots, info, probe, _, inverse, padded, canvas):
    size = probe.shape[1]
    half = size // 2
    _, t = here()
    padded[:half] = jnp.zeros((half, size), jnp.float32)
    padded[half + size :] = jnp.zeros((half + 8, size), jnp.float32)
    padded[half : half + size] = probe[0] * probe[0] + probe[1] * probe[1]
    canvas[...] = jnp.zeros(canvas.shape, jnp.float32)
    reach = plan.sides + 1
    spare = jnp.zeros((half, LANES), jnp.float32)
    for down in (-1, 0, 1):

        def add(step, carry, down=down):
            turn = step // slots
            slot = step % slots
            over = turn * (1 - 2 * t) if plan.paired else jnp.where(turn == 0, 0, 2 * turn - 3)
            index = (down + 1) * reach + turn

            @pl.when(slot < info[index, 2 * slots])
            def _():
                row = info[index, 2 * slot]
                col = info[index, 2 * slot + 1]
                power = rows_at(padded, size - half * down - row, half)
                shifted = pltpu.roll(jnp.concatenate([power, spare], axis=1), col % LANES, 1)
                first = col // LANES + plan.own * (over + 1)
                canvas[:, lanes(first, 3)] += shifted

            return carry

        lax.fori_loop(0, reach * slots, add, 0)
    inverse[...] = 1.0 / (canvas[:, lanes(plan.own, plan.tiles)] + DAMPING)


def term_kernel(plan, slot, layout, pieces, copied, centres, counts, *rest):
    refs, rest = rest[:pieces], rest[pieces:]
    earlier, (probe, amps, tables, outer, inner), rest = rest[:copied], rest[copied : copied + 5], rest[copied + 5 :]
    near_outers, (window, picked) = rest[:-2], rest[-2:]
    size = probe.shape[2]
    half = size // 2
    s, t = here()
    row = centres[slot, 0]
    col = centres[slot, 1]
    alive = slot < counts[s]

    @pl.when(jnp.logical_not(alive))
    def _():
        outer[...] = jnp.zeros(outer.shape, jnp.float32)
        inner[...] = jnp.zeros(inner.shape, jnp.float32)

    @pl.when(alive)
    def _():
        tile = col // LANES
        first = tile % 2
        rest_col = col % LANES
        from_tile = lax.broadcasted_iota(jnp.int32, (half, LANES), 1) >= rest_col
        from_upper = lax.broadcasted_iota(jnp.int32, (half, LANES), 0) >= row
        side = far_side(s)
        own, far, near = layout(refs, t)
        for kind, source in ((1, own), (1 + side, far), (1 - side, near)):
            for step in range(3):
                pick_tile(plan, picked.at[kind, step], source, tile + step, t)

        @pl.when(plan.outermost(s))
        def _():
            picked[1 + side] = jnp.zeros(picked.shape[1:], jnp.float32)

        for part in range(2):
            edge = [jnp.where(from_tile, picked[kind, 0, part], picked[kind, 2, part]) for kind in range(3)]
            window[part, :half, lanes(first)] = jnp.where(from_upper, edge[0], edge[2])
            window[part, half:, lanes(first)] = edge[1]
            window[part, :half, lanes(1 - first)] = jnp.where(from_upper, picked[0, 1, part], picked[2, 1, part])
            window[part, half:, lanes(1 - first)] = picked[1, 1, part]

        probe_real = probe[slot, 0]
        probe_imag = probe[slot, 1]
        exit_real = probe_real * window[0] - probe_imag * window[1]
        exit_imag = probe_real * window[1] + probe_imag * window[0]

        halves = [
            jnp.concatenate([exit_real[:, :half] + sign * exit_real[:, half:], exit_imag[:, :half] + sign * exit_imag[:, half:]], axis=1)
            for sign in (1.0, -1.0)
        ]
        across = [times_table(halves[parity], tables[parity, 0]) for parity in range(2)]
        real = jnp.concatenate([across[0][:, :half], across[1][:, :half]], axis=1)
        imag = jnp.concatenate([across[0][:, half:], across[1][:, half:]], axis=1)
        halves = [
            jnp.concatenate([real[:half] + sign * real[half:], imag[:half] + sign * imag[half:]], axis=0)
            for sign in (1.0, -1.0)
        ]
        back = []
        for parity in range(2):
            pattern = table_times(tables[parity, 1], halves[parity])
            far_real = pattern[:half]
            far_imag = pattern[half:]
            amplitude = amps[slot, parity * half : (parity + 1) * half]
            factor = 1.0 - amplitude * lax.rsqrt(far_real * far_real + far_imag * far_imag + SMOOTH)
            miss = jnp.concatenate([far_real * factor, far_imag * factor], axis=0)
            back.append(table_times(tables[parity, 0], miss))
        real = jnp.concatenate([back[0][:half] + back[1][:half], back[0][:half] - back[1][:half]], axis=0)
        imag = jnp.concatenate([back[0][half:] + back[1][half:], back[0][half:] - back[1][half:]], axis=0)
        both = []
        for parity in range(2):
            columns = slice(parity * half, (parity + 1) * half)
            both.append(times_table(jnp.concatenate([real[:, columns], imag[:, columns]], axis=1), tables[parity, 1]))
        near_real = jnp.concatenate([both[0][:, :half] + both[1][:, :half], both[0][:, :half] - both[1][:, :half]], axis=1)
        near_imag = jnp.concatenate([both[0][:, half:] + both[1][:, half:], both[0][:, half:] - both[1][:, half:]], axis=1)
        term_real = probe_real * near_real + probe_imag * near_imag
        term_imag = probe_real * near_imag - probe_imag * near_real
        outer[0] = term_real[:half]
        outer[1] = term_imag[:half]
        inner[0] = term_real[half:]
        inner[1] = term_imag[half:]

    for index, source in enumerate((*earlier, outer)):
        line = 0
        for target in near_outers:
            rows = target.shape[1]
            target[2 * index : 2 * index + 2] = source[:, line : line + rows]
            line += rows


class Patch:
    def __init__(self, plan, info, s, patch, slot, down, far=False):
        runs = patch if isinstance(patch, (list, tuple)) else [patch]
        half = sum(run.shape[1] for run in runs)
        index = (1 if down is None else 1 + down) * (plan.sides + 1)
        row = info[index, 2 * slot]
        col = info[index, 2 * slot + 1]
        self.runs = runs
        self.tile = col // LANES
        self.first = self.tile % 2
        self.rest = col % LANES
        self.lane = lax.broadcasted_iota(jnp.int32, (half, LANES), 1)
        self.from_tile = self.lane >= self.rest
        self.rows = None
        if down is not None:
            line = lax.broadcasted_iota(jnp.int32, (half, LANES), 0)
            after = jnp.where(down > 0, half, row)
            if far:
                after = jnp.where(plan.outermost(s), 0, after)
            self.rows = (line >= jnp.where(down > 0, row, 0)) & (line < after)

    def lines(self, part, place):
        values = jnp.concatenate([run[part, :, lanes(place)] for run in self.runs], axis=0)
        return values if self.rows is None else jnp.where(self.rows, values, 0.0)

    def tiles(self, part):
        edge = self.lines(part, self.first)
        middle = self.lines(part, 1 - self.first)
        return jnp.where(self.from_tile, edge, 0.0), middle, jnp.where(self.from_tile, 0.0, edge)

    def add_to(self, canvas):
        for part in range(2):
            for step, values in enumerate(self.tiles(part)):
                canvas[part, :, lanes(self.tile + step)] += values

    def at(self, part, tile):
        step = tile - self.tile
        first = jnp.where(step == 0, self.rest, 0)
        after = jnp.where(step == 2, self.rest, jnp.where((step < 0) | (step > 2), 0, LANES))
        inside = (self.lane >= first) & (self.lane < after)
        return jnp.where(inside, self.lines(part, tile % 2), 0.0)


def early_sum_kernel(plan, slots, info, *rest):
    inner, near, canvas = rest[:slots], rest[slots:-1], rest[-1]
    s, _ = here()
    canvas[...] = jnp.zeros(canvas.shape, jnp.float32)
    for slot in range(slots):
        Patch(plan, info, s, inner[slot], slot, None).add_to(canvas)
        runs = [run.at[2 * slot : 2 * slot + 2] for run in near]
        Patch(plan, info, s, runs, slot, -far_side(s)).add_to(canvas)


def base_kernel(plan, slots, layout, pieces, info, early, inverse, *rest):
    far, refs, (canvas, base) = rest[: slots - 1], rest[slots - 1 : slots - 1 + pieces], rest[slots - 1 + pieces :]
    s, t = here()
    canvas[...] = early[...]
    for slot in range(slots - 1):
        Patch(plan, info, s, far[slot], slot, far_side(s), True).add_to(canvas)
    for tile in range(plan.tiles):
        where = lanes(tile)
        pick_tile(plan, base.at[:, :, where], layout(refs, t)[0], tile, t)
        base[:, :, where] -= canvas[:, :, where] * inverse[:, where][None]


def last_patch(plan, slots, info, patch):
    s, _ = here()
    return Patch(plan, info, s, patch, slots - 1, far_side(s), True)


def take_off(last, target, base, inverse, tile):
    for part in range(2):
        target[part] = base[part, :, lanes(tile)] - last.at(part, tile) * inverse[:, lanes(tile)]


def middle_kernel(plan, slots, info, base, patch, inverse, _, middle):
    _, t = here()
    last = last_patch(plan, slots, info, patch)
    for step in range(plan.mid_tiles):
        take_off(last, middle.at[:, :, lanes(step)], base, inverse, plan.mid_start(t) + step)


def boundary_kernel(plan, slots, info, early, patch, *sums):
    _, t = here()
    last = last_patch(plan, slots, info, patch)
    for total, start in zip(sums, plan.pair_starts(t)):
        for step in range(2):
            for part in range(2):
                total[part, :, lanes(step)] = early[part, :, lanes(start + step)] + last.at(part, start + step)


def halo_sum_kernel(plan, slots, info, early, patch, *sums):
    _, t = here()
    last = last_patch(plan, slots, info, patch)
    for total, tile in zip(sums, plan.halo_tiles(t)):
        for part in range(2):
            total[part] = early[part, :, lanes(tile)] + last.at(part, tile)


def last_kernel(plan, slots, info, base, patch, inverse, _, *rest):
    nearly, bases, (current, sems) = rest[0], rest[1 : 1 + plan.sides], rest[1 + plan.sides :]
    _, t = here()
    last = last_patch(plan, slots, info, patch)
    copies = []
    for step in range(plan.own):
        where = lanes(step)
        take_off(last, current.at[:, :, where], base, inverse, 1 + step)
        copies.append(pltpu.make_async_copy(current.at[:, :, where], nearly.at[:, :, where], sems.at[step]))
        copies[-1].start()
    for edge, tile in zip(bases, plan.edge_tiles(t)):
        edge[...] = current[:, :, lanes(tile - 1)]
    for copy in copies:
        copy.wait()


def edge_kernel(plan, inverse, *rest):
    bases, received = rest[: plan.sides], rest[plan.sides : 2 * plan.sides]
    _, result, sums, sems = rest[2 * plan.sides :]
    _, t = here()
    copies = []
    for side, tile in enumerate(plan.edge_tiles(t)):
        sums[side] = bases[side][...] - received[side][...] * inverse[:, lanes(tile)][None]
        copies.append(pltpu.make_async_copy(sums.at[side], result.at[:, :, lanes(tile - 1)], sems.at[side]))
        copies[-1].start()
    for copy in copies:
        copy.wait()


def call(kernel, outs, scratch, ins, flops=10**5, size=10**4, in_specs=None, out_specs=None, **options):
    result = pl.pallas_call(
        kernel,
        out_shape=outs,
        in_specs=in_specs or [SMEM if value.dtype == jnp.int32 else VMEM for value in ins],
        out_specs=out_specs or jax.tree.map(lambda _: VMEM, outs),
        scratch_shapes=scratch,
        compiler_params=pltpu.CompilerParams(vmem_limit_bytes=VMEM_BYTES),
        cost_estimate=pl.CostEstimate(flops=flops, bytes_accessed=size, transcendentals=0),
        **options,
    )(*ins)
    return list(result) if isinstance(outs, list) else result


def on_device(plan, object_field, probe_field, amplitudes, centres, counts):
    f32 = jnp.float32
    shape = jax.ShapeDtypeStruct
    size = probe_field.shape[1]
    half = size // 2
    slots = amplitudes.shape[2]
    block_rows = object_field.shape[1]
    block_cols = object_field.shape[2]
    assert block_rows == half and block_cols % LANES == 0 and half == LANES
    width = plan.tiles * LANES
    sides = plan.sides
    spots = centres[0, 0]
    counts = counts.reshape(-1)
    own_amps = amplitudes[0, 0]
    tables = jnp.asarray(dft_tables(size))
    order = jnp.asarray(parity_order(size))
    dma = pltpu.SemaphoreType.DMA

    messages = call(
        lambda *refs: edge_message_kernel(plan, *refs),
        [shape((2, half + 8, LANES), f32)] * sides,
        [dma((sides,))],
        [object_field, spots, counts],
        in_specs=[HBM, SMEM, SMEM],
    )
    halos = plan.across(messages)
    far_block = plan.far_rows(object_field)
    near_block = plan.near_rows(object_field)
    rolled, ordered = call(
        prepare_kernel,
        [shape((slots, 2, size, size), f32), shape((slots, size, size), f32)],
        [pltpu.VMEM((2, 2 * size + 8, size), f32)],
        [spots, probe_field, own_amps, order],
    )
    messages = call(
        lambda *refs: halo_message_kernel(plan, *refs),
        [shape((2, half + 24, LANES), f32)] * sides + [shape((2, half + 16, LANES), f32)] * sides,
        [],
        [spots, counts, *halos],
    )
    passed = messages[sides:]
    far = [far_block] + [plan.far_rows(message) for message in messages[:sides]]
    near = [plan.near_rows(message) for message in passed] + [near_block]
    own = [object_field] + passed
    def runs_layout(refs, main, count, side_starts):
        starts = [main] + side_starts
        own, far, near = refs[: 1 + sides], refs[1 + sides : 2 + 2 * sides], refs[2 + 2 * sides :]
        return lay_out(own, starts), lay_out(far, starts), lay_out(near, side_starts + (chunk_starts(main, count) if len(near) > 1 + sides else [main]))

    def first_layout(refs, t):
        return runs_layout(refs, 1, plan.own, plan.halo_tiles(t))

    def later_layout(refs, t):
        return runs_layout(refs, plan.mid_start(t), plan.mid_tiles, plan.pair_starts(t))

    layout = first_layout

    third = half // 24 * 8
    near_heights = [half - 2 * third, third, third]
    for sweep in range(ITERS):
        pieces = own + far + near
        inner, outer, outer_far = [], [], []
        for slot in range(slots):
            last = slot == slots - 1
            earlier = outer if last else []
            patch = shape((2, half, size), f32)
            outer_part, inner_part, *copies = call(
                lambda *refs, slot=slot, layout=layout, copied=len(earlier): term_kernel(
                    plan, slot, layout, len(pieces), copied, *refs
                ),
                [patch] * 2 + [shape((2 * slots, rows, size), f32) for rows in near_heights if last],
                [pltpu.VMEM((2, size, size), f32), pltpu.VMEM((3, 3, 2, half, LANES), f32)],
                [spots, counts, *pieces, *earlier, rolled, ordered, tables],
            )
            inner.append(inner_part)
            outer.append(outer_part)
            outer_far.append(plan.far_rows(outer_part))
            if sweep == 0 and last:
                info = call(
                    lambda *refs: info_kernel(plan, *refs),
                    shape((3 * (sides + 1), LANES), jnp.int32),
                    [pltpu.VMEM((3 * (sides + 1), 8, LANES), jnp.int32), dma],
                    passed + far[1:] + near[:sides] + [outer_part],
                    in_specs=[VMEM] * (3 * sides) + [ANY],
                    out_specs=SMEM,
                )
        outer_near = [plan.near_rows(copy) for copy in copies]
        if sweep == 0:
            inverse = call(
                lambda *refs: light_kernel(plan, slots, *refs),
                shape((half, width), f32),
                [
                    pltpu.VMEM((2 * size + 8, size), f32),
                    pltpu.VMEM((half, width + 2 * plan.own * LANES), f32),
                ],
                [info, probe_field, copies[0]],
                in_specs=[SMEM, VMEM, ANY],
            )
        early = call(
            lambda *refs: early_sum_kernel(plan, slots, *refs),
            shape((2, half, width), f32),
            [],
            [info, *inner, *outer_near],
        )
        early, base = call(
            lambda *refs, layout=layout: base_kernel(plan, slots, layout, len(pieces), *refs),
            [shape((2, half, width), f32)] * 2,
            [],
            [info, early, inverse, *outer_far[:-1], *pieces],
        )
        if sweep < ITERS - 1:
            sums = call(
                lambda *refs: boundary_kernel(plan, slots, *refs),
                [shape((2, half, 2 * LANES), f32)] * sides,
                [],
                [info, early, outer_far[-1]],
            )
            received = plan.across(sums)
            middle = call(
                lambda *refs: middle_kernel(plan, slots, *refs),
                shape((2, half, plan.mid_tiles * LANES), f32),
                [],
                [info, base, outer_far[-1], inverse, sums[0]],
                in_specs=[SMEM, VMEM, VMEM, VMEM, ANY],
            )
            far_middle = plan.far_rows(middle)
            near_runs = [shape((2, half, count * LANES), f32) for count in chunks(plan.mid_tiles)]
            updated = call(
                lambda *refs: pair_kernel(plan, *refs),
                [shape((2, half, 2 * LANES), f32)] * (2 * sides) + near_runs,
                [],
                [base, early, inverse, middle, *sums, *received],
            )
            pairs = updated[:sides]
            own = [middle] + pairs
            far = [far_middle] + [plan.far_rows(piece) for piece in pairs]
            near = [plan.near_rows(piece) for piece in updated[sides:]]
            layout = later_layout
    sums = call(
        lambda *refs: halo_sum_kernel(plan, slots, *refs),
        [shape((2, half, LANES), f32)] * sides,
        [],
        [info, early, outer_far[-1]],
    )
    nearly, *bases = call(
        lambda *refs: last_kernel(plan, slots, *refs),
        [shape((2, half, block_cols), f32)] + [shape((2, half, LANES), f32)] * sides,
        [pltpu.VMEM((2, half, block_cols), f32), dma((plan.own,))],
        [info, base, outer_far[-1], inverse, sums[0]],
        in_specs=[SMEM, VMEM, VMEM, VMEM, ANY],
        out_specs=[HBM] + [VMEM] * sides,
    )
    received = plan.across(sums)
    return call(
        lambda *refs: edge_kernel(plan, *refs),
        shape(nearly.shape, f32),
        [pltpu.VMEM((sides, 2, half, LANES), f32), dma((sides,))],
        [inverse, *bases, *received, nearly],
        in_specs=[VMEM] * (1 + 2 * sides) + [HBM],
        out_specs=HBM,
        input_output_aliases={1 + 2 * sides: 0},
    )


def solution(mesh):
    sizes = dict(mesh.shape)

    def per_device(object_field, *rest):
        plan = Plan(sizes["sx"], sizes["sy"], *object_field.shape[1:])
        return on_device(plan, object_field, *rest)

    return jax.shard_map(
        per_device,
        mesh=mesh,
        in_specs=(
            P(None, "sx", "sy"),
            P(),
            P("sx", "sy", None, None, None),
            P("sx", "sy", None, None),
            P(None, "sy"),
        ),
        out_specs=P(None, "sx", "sy"),
        check_vma=False,
    )
```

```python
import math

import jax
import jax.numpy as jnp
import ml_dtypes
import numpy as np
from jax import lax
from jax.experimental import pallas as pl
from jax.experimental.pallas import tpu as pltpu
from jax.sharding import PartitionSpec as P

ITERS = 2
SMOOTH = 1.0
DAMPING = 1.0
LANES = 128
VMEM_BYTES = 12 * 1024 * 1024

VMEM = pl.BlockSpec(memory_space=pltpu.VMEM)
SMEM = pl.BlockSpec(memory_space=pltpu.SMEM)
HBM = pl.BlockSpec(memory_space=pltpu.HBM)
ANY = pl.BlockSpec(memory_space=pl.ANY)


def split_numpy(table):
    high = table.astype(np.float32).astype(ml_dtypes.bfloat16)
    low = (table - high.astype(np.float64)).astype(ml_dtypes.bfloat16)
    return high, low


def dft_tables(length):
    half = length // 2
    index = np.arange(half)
    tables = []
    for parity in range(2):
        angles = 2.0 * math.pi / length * (index[:, None] * (2 * index[None, :] + parity) % length)
        cosine = np.cos(angles) / math.sqrt(length)
        sine = np.sin(angles) / math.sqrt(length)
        forward = np.block([[cosine, -sine], [sine, cosine]])
        tables.append([split_numpy(forward), split_numpy(forward.T)])
    return np.array(tables, dtype=ml_dtypes.bfloat16)


def parity_order(length):
    half = length // 2
    order = np.zeros((length, length))
    for index in range(length):
        order[index, index % 2 * half + index // 2] = 1.0
    return np.stack([order, order.T]).astype(ml_dtypes.bfloat16)


def split(values):
    high = values.astype(jnp.bfloat16)
    low = (values - high.astype(jnp.float32)).astype(jnp.bfloat16)
    return high, low


def times_table(values, table):
    high, low = split(values)
    left = jnp.concatenate([high, low, high], axis=1)
    right = jnp.concatenate([table[0], table[0], table[1]], axis=0)
    return jnp.dot(left, right, preferred_element_type=jnp.float32)


def table_times(table, values):
    high, low = split(values)
    left = jnp.concatenate([table[0], table[0], table[1]], axis=1)
    right = jnp.concatenate([high, low, high], axis=0)
    return jnp.dot(left, right, preferred_element_type=jnp.float32)


class Plan:
    def __init__(self, sx_size, sy_size, block_rows, block_cols):
        self.rows = block_rows
        self.sx_size = sx_size
        self.sy_size = sy_size
        self.own = block_cols // LANES
        self.tiles = self.own + 2
        self.paired = sy_size == 2
        self.sides = 1 if self.paired else 2

    def rights(self, t):
        return [1 - t] if self.paired else [0, 1]

    def pair_starts(self, t):
        return [right * (self.tiles - 2) for right in self.rights(t)]

    def halo_tiles(self, t):
        return [right * (self.tiles - 1) for right in self.rights(t)]

    def edge_tiles(self, t):
        return [1 + right * (self.tiles - 3) for right in self.rights(t)]

    def mid_start(self, t):
        return 1 + t if self.paired else 2

    @property
    def mid_tiles(self):
        return self.tiles - 3 if self.paired else self.tiles - 4

    def across(self, values, axis_name="sy"):
        if self.paired:
            return [lax.ppermute(values[0], axis_name, [(0, 1), (1, 0)])]
        ends = self.sy_size - 1
        return [
            lax.ppermute(values[1], axis_name, [(i, i + 1) for i in range(ends)]),
            lax.ppermute(values[0], axis_name, [(i + 1, i) for i in range(ends)]),
        ]

    def far_rows(self, values):
        rows, columns = self.sx_size, self.sy_size
        pairs = [(i * columns + t, (i + 1) * columns + t) for i in range(1, rows - 1, 2) for t in range(columns)]
        for i in (0, rows - 1):
            pairs += [(i * columns + t, i * columns + t + 1) for t in range(0, columns - 1, 2)]
        return lax.ppermute(values, ("sx", "sy"), pairs + [(j, i) for i, j in pairs])

    def near_rows(self, values):
        return lax.ppermute(values, "sx", [(i, i ^ 1) for i in range(self.sx_size)])

    def outermost(self, s):
        return (s == 0) | (s == self.sx_size - 1)


def far_side(s):
    return 2 * (s % 2) - 1


def lanes(tile, count=1):
    if isinstance(tile, int):
        return pl.ds(tile * LANES, count * LANES)
    return pl.ds(pl.multiple_of(tile * LANES, LANES), count * LANES)


def pick_tile(plan, target, pieces, tile, t):
    rows = target.shape[1]
    if plan.paired:

        @pl.when(tile == (plan.tiles - 1) * t)
        def _():
            target[...] = jnp.zeros(target.shape, jnp.float32)

    for ref, offset, count, start in pieces:

        @pl.when((tile >= start) & (tile < start + count))
        def _(ref=ref, offset=offset, start=start):
            target[...] = ref[:, :rows, lanes(tile - start + offset)]


def lay_out(refs, starts):
    return [(ref, 0, ref.shape[2] // LANES, start) for ref, start in zip(refs, starts)]


def chunks(count):
    return [min(2, count - first) for first in range(0, count, 2)]


def chunk_starts(start, count):
    return [start + 2 * index for index in range(len(chunks(count)))]


def spread(source, targets):
    offset = 0
    for target in targets:
        columns = target.shape[2]
        target[...] = source[:, :, offset : offset + columns]
        offset += columns


def rows_at(ref, start, count):
    offset = start % 8
    values = ref[pl.ds(pl.multiple_of(start - offset, 8), count + 8)]
    return pltpu.roll(values, (count + 8 - offset) % (count + 8), 0)[:count]


def here():
    return lax.axis_index("sx"), lax.axis_index("sy")


def info_rows(centres, count):
    lane = lax.broadcasted_iota(jnp.int32, (8, LANES), 1)
    slots = centres.shape[0]
    values = [centres[slot, axis] for slot in range(slots) for axis in range(2)] + [count]
    line = jnp.zeros((8, LANES), jnp.int32)
    for index, value in enumerate(values):
        line = jnp.where(lane == index, value, line)
    return line.astype(jnp.float32)


def edge_message_kernel(plan, block, centres, counts, *rest):
    messages, sems = rest[: plan.sides], rest[plan.sides]
    s, t = here()
    half = block.shape[1]
    copies = [
        pltpu.make_async_copy(block.at[:, :, lanes(tile - 1)], message.at[:, :half], sems.at[side])
        for side, (message, tile) in enumerate(zip(messages, plan.edge_tiles(t)))
    ]
    for copy in copies:
        copy.start()
    rows = info_rows(centres, counts[s])
    for message in messages:
        message[0, half:] = rows
        message[1, half:] = rows
    for copy in copies:
        copy.wait()


def halo_message_kernel(plan, centres, counts, _, *rest):
    received, far, near = (rest[k * plan.sides : (k + 1) * plan.sides] for k in range(3))
    own = info_rows(centres, counts[lax.axis_index("sx")])
    rest[-1][...] = own
    for source, *messages in zip(received, far, near):
        for message in messages:
            rows = source.shape[1]
            message[:, :rows] = source[...]
            for line in range(rows, message.shape[1], 8):
                message[0, line : line + 8] = own
                message[1, line : line + 8] = own


def pair_kernel(plan, base, early, inverse, middle, *rest):
    sides = plan.sides
    sums, received, results = (rest[k * sides : (k + 1) * sides] for k in range(3))
    near = rest[3 * sides :]
    _, t = here()
    for total, other, result, copy, start in zip(sums, received, results, near, plan.pair_starts(t)):
        where = lanes(start, 2)
        missing = total[...] + other[...] - early[:, :, where]
        values = base[:, :, where] - missing * inverse[:, where][None]
        result[...] = values
        copy[...] = values
    spread(middle, near[sides:])


def prepare_kernel(centres, probe, amps, order, rolled, ordered, padded):
    size = probe.shape[1]
    half = size // 2
    padded[:, :half] = jnp.zeros((2, half, size), jnp.float32)
    padded[:, half + size :] = jnp.zeros((2, half + 8, size), jnp.float32)
    padded[:, half : half + size] = probe[...]
    for slot in range(amps.shape[0]):
        row = centres[slot, 0]
        col = centres[slot, 1]
        for part in range(2):
            shape = padded.at[part]
            upper = rows_at(shape, half - row, half) + rows_at(shape, half + size - row, half)
            lower = rows_at(shape, size - row, half)
            rolled[slot, part] = pltpu.roll(jnp.concatenate([upper, lower], axis=0), col % size, 1)
        high, low = split(amps[slot])
        across = jnp.dot(
            jnp.concatenate([high, low], axis=1),
            jnp.concatenate([order[0], order[0]], axis=0),
            preferred_element_type=jnp.float32,
        )
        high, low = split(across)
        ordered[slot] = jnp.dot(
            jnp.concatenate([order[1], order[1]], axis=1),
            jnp.concatenate([high, low], axis=0),
            preferred_element_type=jnp.float32,
        )


def info_kernel(plan, *rest):
    groups = [rest[k * plan.sides : (k + 1) * plan.sides] for k in range(3)]
    _, info, known, sem = rest[3 * plan.sides :]
    s, _ = here()
    upper = s % 2 == 0
    height = plan.rows

    def lines(messages):
        return [messages[0][0, height + 8 : height + 16]] + [message[0, height : height + 8] for message in messages]

    own, far, near = (lines(messages) for messages in groups)
    far = [jnp.where(plan.outermost(s), 0.0, line) for line in far]
    for turn in range(plan.sides + 1):
        for kind, line in ((0, jnp.where(upper, far[turn], near[turn])), (1, own[turn]), (2, jnp.where(upper, near[turn], far[turn]))):
            known[kind * (plan.sides + 1) + turn] = line.astype(jnp.int32)
    copy = pltpu.make_async_copy(known.at[:, 0], info, sem)
    copy.start()
    copy.wait()


def light_kernel(plan, slots, info, probe, _, inverse, padded, canvas):
    size = probe.shape[1]
    half = size // 2
    _, t = here()
    padded[:half] = jnp.zeros((half, size), jnp.float32)
    padded[half + size :] = jnp.zeros((half + 8, size), jnp.float32)
    padded[half : half + size] = probe[0] * probe[0] + probe[1] * probe[1]
    canvas[...] = jnp.zeros(canvas.shape, jnp.float32)
    reach = plan.sides + 1
    spare = jnp.zeros((half, LANES), jnp.float32)
    for down in (-1, 0, 1):

        def add(step, carry, down=down):
            turn = step // slots
            slot = step % slots
            over = turn * (1 - 2 * t) if plan.paired else jnp.where(turn == 0, 0, 2 * turn - 3)
            index = (down + 1) * reach + turn

            @pl.when(slot < info[index, 2 * slots])
            def _():
                row = info[index, 2 * slot]
                col = info[index, 2 * slot + 1]
                power = rows_at(padded, size - half * down - row, half)
                shifted = pltpu.roll(jnp.concatenate([power, spare], axis=1), col % LANES, 1)
                first = col // LANES + plan.own * (over + 1)
                canvas[:, lanes(first, 3)] += shifted

            return carry

        lax.fori_loop(0, reach * slots, add, 0)
    inverse[...] = 1.0 / (canvas[:, lanes(plan.own, plan.tiles)] + DAMPING)


def term_kernel(plan, slot, layout, pieces, copied, slots, spot, *rest):
    refs, rest = rest[:pieces], rest[pieces:]
    earlier, (probe, amps, tables, outer, inner), rest = rest[:copied], rest[copied : copied + 5], rest[copied + 5 :]
    near_outers, (window, picked) = rest[:-2], rest[-2:]
    size = probe.shape[2]
    half = size // 2
    s, t = here()
    line = spot[0:1]
    lane = lax.broadcasted_iota(jnp.int32, line.shape, 1)
    row, col, count = (jnp.sum(jnp.where(lane == k, line, 0.0)).astype(jnp.int32) for k in (2 * slot, 2 * slot + 1, 2 * slots))
    alive = slot < count

    @pl.when(jnp.logical_not(alive))
    def _():
        outer[...] = jnp.zeros(outer.shape, jnp.float32)
        inner[...] = jnp.zeros(inner.shape, jnp.float32)

    @pl.when(alive)
    def _():
        tile = col // LANES
        first = tile % 2
        rest_col = col % LANES
        from_tile = lax.broadcasted_iota(jnp.int32, (half, LANES), 1) >= rest_col
        from_upper = lax.broadcasted_iota(jnp.int32, (half, LANES), 0) >= row
        side = far_side(s)
        own, far, near = layout(refs, t)
        for kind, source in ((1, own), (1 + side, far), (1 - side, near)):
            for step in range(3):
                pick_tile(plan, picked.at[kind, step], source, tile + step, t)

        @pl.when(plan.outermost(s))
        def _():
            picked[1 + side] = jnp.zeros(picked.shape[1:], jnp.float32)

        for part in range(2):
            edge = [jnp.where(from_tile, picked[kind, 0, part], picked[kind, 2, part]) for kind in range(3)]
            window[part, :half, lanes(first)] = jnp.where(from_upper, edge[0], edge[2])
            window[part, half:, lanes(first)] = edge[1]
            window[part, :half, lanes(1 - first)] = jnp.where(from_upper, picked[0, 1, part], picked[2, 1, part])
            window[part, half:, lanes(1 - first)] = picked[1, 1, part]

        probe_real = probe[slot, 0]
        probe_imag = probe[slot, 1]
        exit_real = probe_real * window[0] - probe_imag * window[1]
        exit_imag = probe_real * window[1] + probe_imag * window[0]

        halves = [
            jnp.concatenate([exit_real[:, :half] + sign * exit_real[:, half:], exit_imag[:, :half] + sign * exit_imag[:, half:]], axis=1)
            for sign in (1.0, -1.0)
        ]
        across = [times_table(halves[parity], tables[parity, 0]) for parity in range(2)]
        real = jnp.concatenate([across[0][:, :half], across[1][:, :half]], axis=1)
        imag = jnp.concatenate([across[0][:, half:], across[1][:, half:]], axis=1)
        halves = [
            jnp.concatenate([real[:half] + sign * real[half:], imag[:half] + sign * imag[half:]], axis=0)
            for sign in (1.0, -1.0)
        ]
        back = []
        for parity in range(2):
            pattern = table_times(tables[parity, 1], halves[parity])
            far_real = pattern[:half]
            far_imag = pattern[half:]
            amplitude = amps[slot, parity * half : (parity + 1) * half]
            factor = 1.0 - amplitude * lax.rsqrt(far_real * far_real + far_imag * far_imag + SMOOTH)
            miss = jnp.concatenate([far_real * factor, far_imag * factor], axis=0)
            back.append(table_times(tables[parity, 0], miss))
        real = jnp.concatenate([back[0][:half] + back[1][:half], back[0][:half] - back[1][:half]], axis=0)
        imag = jnp.concatenate([back[0][half:] + back[1][half:], back[0][half:] - back[1][half:]], axis=0)
        both = []
        for parity in range(2):
            columns = slice(parity * half, (parity + 1) * half)
            both.append(times_table(jnp.concatenate([real[:, columns], imag[:, columns]], axis=1), tables[parity, 1]))
        near_real = jnp.concatenate([both[0][:, :half] + both[1][:, :half], both[0][:, :half] - both[1][:, :half]], axis=1)
        near_imag = jnp.concatenate([both[0][:, half:] + both[1][:, half:], both[0][:, half:] - both[1][:, half:]], axis=1)
        term_real = probe_real * near_real + probe_imag * near_imag
        term_imag = probe_real * near_imag - probe_imag * near_real
        outer[0] = term_real[:half]
        outer[1] = term_imag[:half]
        inner[0] = term_real[half:]
        inner[1] = term_imag[half:]

    for index, source in enumerate((*earlier, outer)):
        line = 0
        for target in near_outers:
            rows = target.shape[1]
            target[2 * index : 2 * index + 2] = source[:, line : line + rows]
            line += rows


class Patch:
    def __init__(self, plan, info, s, patch, slot, down, far=False):
        runs = patch if isinstance(patch, (list, tuple)) else [patch]
        half = sum(run.shape[1] for run in runs)
        index = (1 if down is None else 1 + down) * (plan.sides + 1)
        row = info[index, 2 * slot]
        col = info[index, 2 * slot + 1]
        self.runs = runs
        self.tile = col // LANES
        self.first = self.tile % 2
        self.rest = col % LANES
        self.lane = lax.broadcasted_iota(jnp.int32, (half, LANES), 1)
        self.from_tile = self.lane >= self.rest
        self.rows = None
        if down is not None:
            line = lax.broadcasted_iota(jnp.int32, (half, LANES), 0)
            after = jnp.where(down > 0, half, row)
            if far:
                after = jnp.where(plan.outermost(s), 0, after)
            self.rows = (line >= jnp.where(down > 0, row, 0)) & (line < after)

    def lines(self, part, place):
        values = jnp.concatenate([run[part, :, lanes(place)] for run in self.runs], axis=0)
        return values if self.rows is None else jnp.where(self.rows, values, 0.0)

    def tiles(self, part):
        edge = self.lines(part, self.first)
        middle = self.lines(part, 1 - self.first)
        return jnp.where(self.from_tile, edge, 0.0), middle, jnp.where(self.from_tile, 0.0, edge)

    def add_to(self, canvas):
        for part in range(2):
            for step, values in enumerate(self.tiles(part)):
                canvas[part, :, lanes(self.tile + step)] += values

    def mask(self, tile):
        step = tile - self.tile
        first = jnp.where(step == 0, self.rest, 0)
        after = jnp.where(step == 2, self.rest, jnp.where((step < 0) | (step > 2), 0, LANES))
        inside = (self.lane >= first) & (self.lane < after)
        if self.rows is not None:
            inside = inside & self.rows
        return jnp.where(inside, 1.0, 0.0)


def part_of(patch, mask, part, tile):
    return patch[part, :, lanes(tile % 2)] * mask[:, lanes(tile)]


def early_sum_kernel(plan, slots, info, *rest):
    inner, near, canvas = rest[:slots], rest[slots:-1], rest[-1]
    s, _ = here()
    canvas[...] = jnp.zeros(canvas.shape, jnp.float32)
    for slot in range(slots):
        Patch(plan, info, s, inner[slot], slot, None).add_to(canvas)
        runs = [run.at[2 * slot : 2 * slot + 2] for run in near]
        Patch(plan, info, s, runs, slot, -far_side(s)).add_to(canvas)


def base_kernel(plan, slots, layout, pieces, info, early, inverse, *rest):
    far, refs, (canvas, base, mask) = rest[: slots - 1], rest[slots - 1 : slots - 1 + pieces], rest[slots - 1 + pieces :]
    s, t = here()
    canvas[...] = early[...]
    for slot in range(slots - 1):
        Patch(plan, info, s, far[slot], slot, far_side(s), True).add_to(canvas)
    last = Patch(plan, info, s, canvas, slots - 1, far_side(s), True)
    for tile in range(plan.tiles):
        where = lanes(tile)
        pick_tile(plan, base.at[:, :, where], layout(refs, t)[0], tile, t)
        base[:, :, where] -= canvas[:, :, where] * inverse[:, where][None]
        mask[:, where] = last.mask(tile)


def take_off(patch, mask, target, base, inverse, tile):
    for part in range(2):
        target[part] = base[part, :, lanes(tile)] - part_of(patch, mask, part, tile) * inverse[:, lanes(tile)]


def middle_kernel(plan, base, patch, mask, inverse, _, middle):
    _, t = here()
    for step in range(plan.mid_tiles):
        take_off(patch, mask, middle.at[:, :, lanes(step)], base, inverse, plan.mid_start(t) + step)


def boundary_kernel(plan, early, patch, mask, *sums):
    _, t = here()
    for total, start in zip(sums, plan.pair_starts(t)):
        for step in range(2):
            tile = start + step
            for part in range(2):
                total[part, :, lanes(step)] = early[part, :, lanes(tile)] + part_of(patch, mask, part, tile)


def halo_sum_kernel(plan, early, patch, mask, *sums):
    _, t = here()
    for total, tile in zip(sums, plan.halo_tiles(t)):
        for part in range(2):
            total[part] = early[part, :, lanes(tile)] + part_of(patch, mask, part, tile)


def last_kernel(plan, base, patch, mask, inverse, _, *rest):
    nearly, bases, (current, sems) = rest[0], rest[1 : 1 + plan.sides], rest[1 + plan.sides :]
    _, t = here()
    copies = []
    for step in range(plan.own):
        where = lanes(step)
        take_off(patch, mask, current.at[:, :, where], base, inverse, 1 + step)
        copies.append(pltpu.make_async_copy(current.at[:, :, where], nearly.at[:, :, where], sems.at[step]))
        copies[-1].start()
    for edge, tile in zip(bases, plan.edge_tiles(t)):
        edge[...] = current[:, :, lanes(tile - 1)]
    for copy in copies:
        copy.wait()


def edge_kernel(plan, inverse, *rest):
    bases, received = rest[: plan.sides], rest[plan.sides : 2 * plan.sides]
    _, result, sums, sems = rest[2 * plan.sides :]
    _, t = here()
    copies = []
    for side, tile in enumerate(plan.edge_tiles(t)):
        sums[side] = bases[side][...] - received[side][...] * inverse[:, lanes(tile)][None]
        copies.append(pltpu.make_async_copy(sums.at[side], result.at[:, :, lanes(tile - 1)], sems.at[side]))
        copies[-1].start()
    for copy in copies:
        copy.wait()


def call(kernel, outs, scratch, ins, flops=10**5, size=10**4, in_specs=None, out_specs=None, **options):
    result = pl.pallas_call(
        kernel,
        out_shape=outs,
        in_specs=in_specs or [SMEM if value.dtype == jnp.int32 else VMEM for value in ins],
        out_specs=out_specs or jax.tree.map(lambda _: VMEM, outs),
        scratch_shapes=scratch,
        compiler_params=pltpu.CompilerParams(vmem_limit_bytes=VMEM_BYTES),
        cost_estimate=pl.CostEstimate(flops=flops, bytes_accessed=size, transcendentals=0),
        **options,
    )(*ins)
    return list(result) if isinstance(outs, list) else result


def on_device(plan, object_field, probe_field, amplitudes, centres, counts):
    f32 = jnp.float32
    shape = jax.ShapeDtypeStruct
    size = probe_field.shape[1]
    half = size // 2
    slots = amplitudes.shape[2]
    block_rows = object_field.shape[1]
    block_cols = object_field.shape[2]
    assert block_rows == half and block_cols % LANES == 0 and half == LANES
    width = plan.tiles * LANES
    sides = plan.sides
    spots = centres[0, 0]
    counts = counts.reshape(-1)
    own_amps = amplitudes[0, 0]
    tables = jnp.asarray(dft_tables(size))
    order = jnp.asarray(parity_order(size))
    dma = pltpu.SemaphoreType.DMA

    messages = call(
        lambda *refs: edge_message_kernel(plan, *refs),
        [shape((2, half + 8, LANES), f32)] * sides,
        [dma((sides,))],
        [object_field, spots, counts],
        in_specs=[HBM, SMEM, SMEM],
    )
    halos = plan.across(messages)
    far_block = plan.far_rows(object_field)
    near_block = plan.near_rows(object_field)
    rolled, ordered = call(
        prepare_kernel,
        [shape((slots, 2, size, size), f32), shape((slots, size, size), f32)],
        [pltpu.VMEM((2, 2 * size + 8, size), f32)],
        [spots, probe_field, own_amps, order],
    )
    messages = call(
        lambda *refs: halo_message_kernel(plan, *refs),
        [shape((2, half + 24, LANES), f32)] * sides + [shape((2, half + 16, LANES), f32)] * sides + [shape((8, LANES), f32)],
        [],
        [spots, counts, ordered, *halos],
        in_specs=[SMEM, SMEM, ANY] + [VMEM] * sides,
    )
    passed, own_spot = messages[sides:-1], messages[-1]
    far = [far_block] + [plan.far_rows(message) for message in messages[:sides]]
    near = [plan.near_rows(message) for message in passed] + [near_block]
    own = [object_field] + passed
    def runs_layout(refs, main, count, side_starts):
        starts = [main] + side_starts
        own, far, near = refs[: 1 + sides], refs[1 + sides : 2 + 2 * sides], refs[2 + 2 * sides :]
        return lay_out(own, starts), lay_out(far, starts), lay_out(near, side_starts + (chunk_starts(main, count) if len(near) > 1 + sides else [main]))

    def first_layout(refs, t):
        return runs_layout(refs, 1, plan.own, plan.halo_tiles(t))

    def later_layout(refs, t):
        return runs_layout(refs, plan.mid_start(t), plan.mid_tiles, plan.pair_starts(t))

    layout = first_layout

    third = half // 24 * 8
    near_heights = [half - 2 * third, third, third]
    for sweep in range(ITERS):
        pieces = own + far + near
        inner, outer, outer_far = [], [], []
        for slot in range(slots):
            last = slot == slots - 1
            earlier = outer if last else []
            patch = shape((2, half, size), f32)
            outer_part, inner_part, *copies = call(
                lambda *refs, slot=slot, layout=layout, copied=len(earlier): term_kernel(
                    plan, slot, layout, len(pieces), copied, slots, *refs
                ),
                [patch] * 2 + [shape((2 * slots, rows, size), f32) for rows in near_heights if last],
                [pltpu.VMEM((2, size, size), f32), pltpu.VMEM((3, 3, 2, half, LANES), f32)],
                [own_spot, *pieces, *earlier, rolled, ordered, tables],
            )
            inner.append(inner_part)
            outer.append(outer_part)
            outer_far.append(plan.far_rows(outer_part))
            if sweep == 0 and last:
                info = call(
                    lambda *refs: info_kernel(plan, *refs),
                    shape((3 * (sides + 1), LANES), jnp.int32),
                    [pltpu.VMEM((3 * (sides + 1), 8, LANES), jnp.int32), dma],
                    passed + far[1:] + near[:sides] + [outer_part],
                    in_specs=[VMEM] * (3 * sides) + [ANY],
                    out_specs=SMEM,
                )
        outer_near = [plan.near_rows(copy) for copy in copies]
        if sweep == 0:
            inverse = call(
                lambda *refs: light_kernel(plan, slots, *refs),
                shape((half, width), f32),
                [
                    pltpu.VMEM((2 * size + 8, size), f32),
                    pltpu.VMEM((half, width + 2 * plan.own * LANES), f32),
                ],
                [info, probe_field, copies[0]],
                in_specs=[SMEM, VMEM, ANY],
            )
        early = call(
            lambda *refs: early_sum_kernel(plan, slots, *refs),
            shape((2, half, width), f32),
            [],
            [info, *inner, *outer_near],
        )
        early, base, mask = call(
            lambda *refs, layout=layout: base_kernel(plan, slots, layout, len(pieces), *refs),
            [shape((2, half, width), f32)] * 2 + [shape((half, width), f32)],
            [],
            [info, early, inverse, *outer_far[:-1], *pieces],
        )
        if sweep < ITERS - 1:
            sums = call(
                lambda *refs: boundary_kernel(plan, *refs),
                [shape((2, half, 2 * LANES), f32)] * sides,
                [],
                [early, outer_far[-1], mask],
            )
            received = plan.across(sums)
            middle = call(
                lambda *refs: middle_kernel(plan, *refs),
                shape((2, half, plan.mid_tiles * LANES), f32),
                [],
                [base, outer_far[-1], mask, inverse, sums[0]],
                in_specs=[VMEM] * 4 + [ANY],
            )
            far_middle = plan.far_rows(middle)
            near_runs = [shape((2, half, count * LANES), f32) for count in chunks(plan.mid_tiles)]
            updated = call(
                lambda *refs: pair_kernel(plan, *refs),
                [shape((2, half, 2 * LANES), f32)] * (2 * sides) + near_runs,
                [],
                [base, early, inverse, middle, *sums, *received],
            )
            pairs = updated[:sides]
            own = [middle] + pairs
            far = [far_middle] + [plan.far_rows(piece) for piece in pairs]
            near = [plan.near_rows(piece) for piece in updated[sides:]]
            layout = later_layout
    sums = call(
        lambda *refs: halo_sum_kernel(plan, *refs),
        [shape((2, half, LANES), f32)] * sides,
        [],
        [early, outer_far[-1], mask],
    )
    nearly, *bases = call(
        lambda *refs: last_kernel(plan, *refs),
        [shape((2, half, block_cols), f32)] + [shape((2, half, LANES), f32)] * sides,
        [pltpu.VMEM((2, half, block_cols), f32), dma((plan.own,))],
        [base, outer_far[-1], mask, inverse, sums[0]],
        in_specs=[VMEM] * 4 + [ANY],
        out_specs=[HBM] + [VMEM] * sides,
    )
    received = plan.across(sums)
    return call(
        lambda *refs: edge_kernel(plan, *refs),
        shape(nearly.shape, f32),
        [pltpu.VMEM((sides, 2, half, LANES), f32), dma((sides,))],
        [inverse, *bases, *received, nearly],
        in_specs=[VMEM] * (1 + 2 * sides) + [HBM],
        out_specs=HBM,
        input_output_aliases={1 + 2 * sides: 0},
    )


def solution(mesh):
    sizes = dict(mesh.shape)

    def per_device(object_field, *rest):
        plan = Plan(sizes["sx"], sizes["sy"], *object_field.shape[1:])
        return on_device(plan, object_field, *rest)

    return jax.shard_map(
        per_device,
        mesh=mesh,
        in_specs=(
            P(None, "sx", "sy"),
            P(),
            P("sx", "sy", None, None, None),
            P("sx", "sy", None, None),
            P(None, "sy"),
        ),
        out_specs=P(None, "sx", "sy"),
        check_vma=False,
    )
```

```python
import math

import jax
import jax.numpy as jnp
import ml_dtypes
import numpy as np
from jax import lax
from jax.experimental import pallas as pl
from jax.experimental.pallas import tpu as pltpu
from jax.sharding import PartitionSpec as P

ITERS = 2
SMOOTH = 1.0
DAMPING = 1.0
LANES = 128
VMEM_BYTES = 12 * 1024 * 1024

VMEM = pl.BlockSpec(memory_space=pltpu.VMEM)
SMEM = pl.BlockSpec(memory_space=pltpu.SMEM)
HBM = pl.BlockSpec(memory_space=pltpu.HBM)
ANY = pl.BlockSpec(memory_space=pl.ANY)


def split_numpy(table):
    high = table.astype(np.float32).astype(ml_dtypes.bfloat16)
    low = (table - high.astype(np.float64)).astype(ml_dtypes.bfloat16)
    return high, low


def dft_tables(length):
    half = length // 2
    index = np.arange(half)
    tables = []
    for parity in range(2):
        angles = 2.0 * math.pi / length * (index[:, None] * (2 * index[None, :] + parity) % length)
        cosine = np.cos(angles) / math.sqrt(length)
        sine = np.sin(angles) / math.sqrt(length)
        forward = np.block([[cosine, -sine], [sine, cosine]])
        tables.append([split_numpy(forward), split_numpy(forward.T)])
    return np.array(tables, dtype=ml_dtypes.bfloat16)


def parity_order(length):
    half = length // 2
    order = np.zeros((length, length))
    for index in range(length):
        order[index, index % 2 * half + index // 2] = 1.0
    return np.stack([order, order.T]).astype(ml_dtypes.bfloat16)


def split(values):
    high = values.astype(jnp.bfloat16)
    low = (values - high.astype(jnp.float32)).astype(jnp.bfloat16)
    return high, low


def times_table(values, table):
    high, low = split(values)
    left = jnp.concatenate([high, low, high], axis=1)
    right = jnp.concatenate([table[0], table[0], table[1]], axis=0)
    return jnp.dot(left, right, preferred_element_type=jnp.float32)


def table_times(table, values):
    high, low = split(values)
    left = jnp.concatenate([table[0], table[0], table[1]], axis=1)
    right = jnp.concatenate([high, low, high], axis=0)
    return jnp.dot(left, right, preferred_element_type=jnp.float32)


class Plan:
    def __init__(self, sx_size, sy_size, block_rows, block_cols):
        self.rows = block_rows
        self.sx_size = sx_size
        self.sy_size = sy_size
        self.own = block_cols // LANES
        self.tiles = self.own + 2
        self.paired = sy_size == 2
        self.sides = 1 if self.paired else 2

    def rights(self, t):
        return [1 - t] if self.paired else [0, 1]

    def pair_starts(self, t):
        return [right * (self.tiles - 2) for right in self.rights(t)]

    def halo_tiles(self, t):
        return [right * (self.tiles - 1) for right in self.rights(t)]

    def edge_tiles(self, t):
        return [1 + right * (self.tiles - 3) for right in self.rights(t)]

    def first_parity(self, t):
        return 1 - t if self.paired else 0

    def mid_start(self, t):
        return 1 + t if self.paired else 2

    @property
    def mid_tiles(self):
        return self.tiles - 3 if self.paired else self.tiles - 4

    def across(self, values, axis_name="sy"):
        if self.paired:
            return [lax.ppermute(values[0], axis_name, [(0, 1), (1, 0)])]
        ends = self.sy_size - 1
        return [
            lax.ppermute(values[1], axis_name, [(i, i + 1) for i in range(ends)]),
            lax.ppermute(values[0], axis_name, [(i + 1, i) for i in range(ends)]),
        ]

    def far_rows(self, values):
        rows, columns = self.sx_size, self.sy_size
        pairs = [(i * columns + t, (i + 1) * columns + t) for i in range(1, rows - 1, 2) for t in range(columns)]
        for i in (0, rows - 1):
            pairs += [(i * columns + t, i * columns + t + 1) for t in range(0, columns - 1, 2)]
        return lax.ppermute(values, ("sx", "sy"), pairs + [(j, i) for i, j in pairs])

    def near_rows(self, values):
        return lax.ppermute(values, "sx", [(i, i ^ 1) for i in range(self.sx_size)])

    def outermost(self, s):
        return (s == 0) | (s == self.sx_size - 1)


def far_side(s):
    return 2 * (s % 2) - 1


def lanes(tile, count=1):
    if isinstance(tile, int):
        return pl.ds(tile * LANES, count * LANES)
    return pl.ds(pl.multiple_of(tile * LANES, LANES), count * LANES)


def pick_tile(plan, target, pieces, tile, t):
    rows = target.shape[1]
    if plan.paired:

        @pl.when(tile == (plan.tiles - 1) * t)
        def _():
            target[...] = jnp.zeros(target.shape, jnp.float32)

    for ref, offset, count, start in pieces:

        @pl.when((tile >= start) & (tile < start + count))
        def _(ref=ref, offset=offset, start=start):
            target[...] = ref[:, :rows, lanes(tile - start + offset)]


def lay_out(refs, starts):
    return [(ref, 0, ref.shape[2] // LANES, start) for ref, start in zip(refs, starts)]


def chunks(count):
    return [min(2, count - first) for first in range(0, count, 2)]


def chunk_starts(start, count):
    return [start + 2 * index for index in range(len(chunks(count)))]


def spread(source, targets):
    offset = 0
    for target in targets:
        columns = target.shape[2]
        target[...] = source[:, :, offset : offset + columns]
        offset += columns


def rows_at(ref, start, count):
    offset = start % 8
    values = ref[pl.ds(pl.multiple_of(start - offset, 8), count + 8)]
    return pltpu.roll(values, (count + 8 - offset) % (count + 8), 0)[:count]


def here():
    return lax.axis_index("sx"), lax.axis_index("sy")


def info_rows(centres, count):
    lane = lax.broadcasted_iota(jnp.int32, (8, LANES), 1)
    slots = centres.shape[0]
    values = [centres[slot, axis] for slot in range(slots) for axis in range(2)] + [count]
    line = jnp.zeros((8, LANES), jnp.int32)
    for index, value in enumerate(values):
        line = jnp.where(lane == index, value, line)
    return line.astype(jnp.float32)


def edge_message_kernel(plan, block, centres, counts, *rest):
    messages, sems = rest[: plan.sides], rest[plan.sides]
    s, t = here()
    half = block.shape[1]
    copies = [
        pltpu.make_async_copy(block.at[:, :, lanes(tile - 1)], message.at[:, :half], sems.at[side])
        for side, (message, tile) in enumerate(zip(messages, plan.edge_tiles(t)))
    ]
    for copy in copies:
        copy.start()
    rows = info_rows(centres, counts[s])
    for message in messages:
        message[0, half:] = rows
        message[1, half:] = rows
    for copy in copies:
        copy.wait()


def halo_message_kernel(plan, centres, counts, _, *rest):
    received, far, near = (rest[k * plan.sides : (k + 1) * plan.sides] for k in range(3))
    own = info_rows(centres, counts[lax.axis_index("sx")])
    rest[-1][...] = own
    for source, *messages in zip(received, far, near):
        for message in messages:
            rows = source.shape[1]
            message[:, :rows] = source[...]
            for line in range(rows, message.shape[1], 8):
                message[0, line : line + 8] = own
                message[1, line : line + 8] = own


def pair_kernel(plan, base, early, inverse, middle, *rest):
    sides = plan.sides
    sums, received, results = (rest[k * sides : (k + 1) * sides] for k in range(3))
    near = rest[3 * sides :]
    _, t = here()
    for total, other, result, copy, start in zip(sums, received, results, near, plan.pair_starts(t)):
        where = lanes(start, 2)
        missing = total[...] + other[...] - early[:, :, where]
        values = base[:, :, where] - missing * inverse[:, where][None]
        result[...] = values
        copy[...] = values
    spread(middle, near[sides:])


def prepare_kernel(centres, probe, amps, order, rolled, ordered, padded):
    size = probe.shape[1]
    half = size // 2
    padded[:, :half] = jnp.zeros((2, half, size), jnp.float32)
    padded[:, half + size :] = jnp.zeros((2, half + 8, size), jnp.float32)
    padded[:, half : half + size] = probe[...]
    for slot in range(amps.shape[0]):
        row = centres[slot, 0]
        col = centres[slot, 1]
        for part in range(2):
            shape = padded.at[part]
            upper = rows_at(shape, half - row, half) + rows_at(shape, half + size - row, half)
            lower = rows_at(shape, size - row, half)
            rolled[slot, part] = pltpu.roll(jnp.concatenate([upper, lower], axis=0), col % size, 1)
        high, low = split(amps[slot])
        across = jnp.dot(
            jnp.concatenate([high, low], axis=1),
            jnp.concatenate([order[0], order[0]], axis=0),
            preferred_element_type=jnp.float32,
        )
        high, low = split(across)
        ordered[slot] = jnp.dot(
            jnp.concatenate([order[1], order[1]], axis=1),
            jnp.concatenate([high, low], axis=0),
            preferred_element_type=jnp.float32,
        )


def info_kernel(plan, *rest):
    groups = [rest[k * plan.sides : (k + 1) * plan.sides] for k in range(3)]
    _, info, known, sem = rest[3 * plan.sides :]
    s, _ = here()
    upper = s % 2 == 0
    height = plan.rows

    def lines(messages):
        return [messages[0][0, height + 8 : height + 16]] + [message[0, height : height + 8] for message in messages]

    own, far, near = (lines(messages) for messages in groups)
    far = [jnp.where(plan.outermost(s), 0.0, line) for line in far]
    for turn in range(plan.sides + 1):
        for kind, line in ((0, jnp.where(upper, far[turn], near[turn])), (1, own[turn]), (2, jnp.where(upper, near[turn], far[turn]))):
            known[kind * (plan.sides + 1) + turn] = line.astype(jnp.int32)
    copy = pltpu.make_async_copy(known.at[:, 0], info, sem)
    copy.start()
    copy.wait()


def light_kernel(plan, slots, info, probe, _, inverse, padded, canvas):
    size = probe.shape[1]
    half = size // 2
    _, t = here()
    padded[:half] = jnp.zeros((half, size), jnp.float32)
    padded[half + size :] = jnp.zeros((half + 8, size), jnp.float32)
    padded[half : half + size] = probe[0] * probe[0] + probe[1] * probe[1]
    canvas[...] = jnp.zeros(canvas.shape, jnp.float32)
    reach = plan.sides + 1
    spare = jnp.zeros((half, LANES), jnp.float32)
    for down in (-1, 0, 1):

        def add(step, carry, down=down):
            turn = step // slots
            slot = step % slots
            over = turn * (1 - 2 * t) if plan.paired else jnp.where(turn == 0, 0, 2 * turn - 3)
            index = (down + 1) * reach + turn

            @pl.when(slot < info[index, 2 * slots])
            def _():
                row = info[index, 2 * slot]
                col = info[index, 2 * slot + 1]
                power = rows_at(padded, size - half * down - row, half)
                shifted = pltpu.roll(jnp.concatenate([power, spare], axis=1), col % LANES, 1)
                first = col // LANES + plan.own * (over + 1)
                canvas[:, lanes(first, 3)] += shifted

            return carry

        lax.fori_loop(0, reach * slots, add, 0)
    inverse[...] = 1.0 / (canvas[:, lanes(plan.own, plan.tiles)] + DAMPING)


def term_kernel(plan, slot, layout, pieces, copied, halves, slots, spot, *rest):
    refs, rest = rest[:pieces], rest[pieces:]
    earlier, (probe, amps, tables, outer, inner), rest = rest[:copied], rest[copied : copied + 5], rest[copied + 5 :]
    outer_halves, near_outers, (window, picked) = rest[:halves], rest[halves:-2], rest[-2:]
    size = probe.shape[2]
    half = size // 2
    s, t = here()
    line = spot[0:1]
    lane = lax.broadcasted_iota(jnp.int32, line.shape, 1)
    row, col, count = (jnp.sum(jnp.where(lane == k, line, 0.0)).astype(jnp.int32) for k in (2 * slot, 2 * slot + 1, 2 * slots))
    alive = slot < count

    @pl.when(jnp.logical_not(alive))
    def _():
        outer[...] = jnp.zeros(outer.shape, jnp.float32)
        inner[...] = jnp.zeros(inner.shape, jnp.float32)

    @pl.when(alive)
    def _():
        tile = col // LANES
        first = tile % 2
        rest_col = col % LANES
        from_tile = lax.broadcasted_iota(jnp.int32, (half, LANES), 1) >= rest_col
        from_upper = lax.broadcasted_iota(jnp.int32, (half, LANES), 0) >= row
        side = far_side(s)
        own, far, near = layout(refs, t)
        for kind, source in ((1, own), (1 + side, far), (1 - side, near)):
            for step in range(3):
                pick_tile(plan, picked.at[kind, step], source, tile + step, t)

        @pl.when(plan.outermost(s))
        def _():
            picked[1 + side] = jnp.zeros(picked.shape[1:], jnp.float32)

        for part in range(2):
            edge = [jnp.where(from_tile, picked[kind, 0, part], picked[kind, 2, part]) for kind in range(3)]
            window[part, :half, lanes(first)] = jnp.where(from_upper, edge[0], edge[2])
            window[part, half:, lanes(first)] = edge[1]
            window[part, :half, lanes(1 - first)] = jnp.where(from_upper, picked[0, 1, part], picked[2, 1, part])
            window[part, half:, lanes(1 - first)] = picked[1, 1, part]

        probe_real = probe[slot, 0]
        probe_imag = probe[slot, 1]
        exit_real = probe_real * window[0] - probe_imag * window[1]
        exit_imag = probe_real * window[1] + probe_imag * window[0]

        halves = [
            jnp.concatenate([exit_real[:, :half] + sign * exit_real[:, half:], exit_imag[:, :half] + sign * exit_imag[:, half:]], axis=1)
            for sign in (1.0, -1.0)
        ]
        across = [times_table(halves[parity], tables[parity, 0]) for parity in range(2)]
        real = jnp.concatenate([across[0][:, :half], across[1][:, :half]], axis=1)
        imag = jnp.concatenate([across[0][:, half:], across[1][:, half:]], axis=1)
        halves = [
            jnp.concatenate([real[:half] + sign * real[half:], imag[:half] + sign * imag[half:]], axis=0)
            for sign in (1.0, -1.0)
        ]
        back = []
        for parity in range(2):
            pattern = table_times(tables[parity, 1], halves[parity])
            far_real = pattern[:half]
            far_imag = pattern[half:]
            amplitude = amps[slot, parity * half : (parity + 1) * half]
            factor = 1.0 - amplitude * lax.rsqrt(far_real * far_real + far_imag * far_imag + SMOOTH)
            miss = jnp.concatenate([far_real * factor, far_imag * factor], axis=0)
            back.append(table_times(tables[parity, 0], miss))
        real = jnp.concatenate([back[0][:half] + back[1][:half], back[0][:half] - back[1][:half]], axis=0)
        imag = jnp.concatenate([back[0][half:] + back[1][half:], back[0][half:] - back[1][half:]], axis=0)
        both = []
        for parity in range(2):
            columns = slice(parity * half, (parity + 1) * half)
            both.append(times_table(jnp.concatenate([real[:, columns], imag[:, columns]], axis=1), tables[parity, 1]))
        near_real = jnp.concatenate([both[0][:, :half] + both[1][:, :half], both[0][:, :half] - both[1][:, :half]], axis=1)
        near_imag = jnp.concatenate([both[0][:, half:] + both[1][:, half:], both[0][:, half:] - both[1][:, half:]], axis=1)
        term_real = probe_real * near_real + probe_imag * near_imag
        term_imag = probe_real * near_imag - probe_imag * near_real
        outer[0] = term_real[:half]
        outer[1] = term_imag[:half]
        inner[0] = term_real[half:]
        inner[1] = term_imag[half:]

    for index, target in enumerate(outer_halves):
        first = plan.first_parity(t)
        target[...] = outer[:, :, lanes(first if index == 0 else 1 - first)]
    for index, source in enumerate((*earlier, outer)):
        line = 0
        for target in near_outers:
            rows = target.shape[1]
            target[2 * index : 2 * index + 2] = source[:, line : line + rows]
            line += rows


class Patch:
    def __init__(self, plan, info, s, patch, slot, down, far=False):
        runs = patch if isinstance(patch, (list, tuple)) else [patch]
        half = sum(run.shape[1] for run in runs)
        index = (1 if down is None else 1 + down) * (plan.sides + 1)
        row = info[index, 2 * slot]
        col = info[index, 2 * slot + 1]
        self.runs = runs
        self.tile = col // LANES
        self.first = self.tile % 2
        self.rest = col % LANES
        self.lane = lax.broadcasted_iota(jnp.int32, (half, LANES), 1)
        self.from_tile = self.lane >= self.rest
        self.rows = None
        if down is not None:
            line = lax.broadcasted_iota(jnp.int32, (half, LANES), 0)
            after = jnp.where(down > 0, half, row)
            if far:
                after = jnp.where(plan.outermost(s), 0, after)
            self.rows = (line >= jnp.where(down > 0, row, 0)) & (line < after)

    def lines(self, part, place):
        values = jnp.concatenate([run[part, :, lanes(place)] for run in self.runs], axis=0)
        return values if self.rows is None else jnp.where(self.rows, values, 0.0)

    def tiles(self, part):
        edge = self.lines(part, self.first)
        middle = self.lines(part, 1 - self.first)
        return jnp.where(self.from_tile, edge, 0.0), middle, jnp.where(self.from_tile, 0.0, edge)

    def add_to(self, canvas):
        for part in range(2):
            for step, values in enumerate(self.tiles(part)):
                canvas[part, :, lanes(self.tile + step)] += values

    def mask(self, tile):
        step = tile - self.tile
        first = jnp.where(step == 0, self.rest, 0)
        after = jnp.where(step == 2, self.rest, jnp.where((step < 0) | (step > 2), 0, LANES))
        inside = (self.lane >= first) & (self.lane < after)
        if self.rows is not None:
            inside = inside & self.rows
        return jnp.where(inside, 1.0, 0.0)


def part_of(plan, patch, mask, part, tile):
    if isinstance(patch, (list, tuple)):
        first = plan.first_parity(lax.axis_index("sy"))
        values = jnp.where(tile % 2 == first, patch[0][part], patch[1][part])
    else:
        values = patch[part, :, lanes(tile % 2)]
    return values * mask[:, lanes(tile)]


def early_sum_kernel(plan, slots, info, *rest):
    inner, near, canvas = rest[:slots], rest[slots:-1], rest[-1]
    s, _ = here()
    canvas[...] = jnp.zeros(canvas.shape, jnp.float32)
    for slot in range(slots):
        Patch(plan, info, s, inner[slot], slot, None).add_to(canvas)
        runs = [run.at[2 * slot : 2 * slot + 2] for run in near]
        Patch(plan, info, s, runs, slot, -far_side(s)).add_to(canvas)


def base_kernel(plan, slots, layout, pieces, info, early, inverse, *rest):
    far, refs, (canvas, base, mask) = rest[: slots - 1], rest[slots - 1 : slots - 1 + pieces], rest[slots - 1 + pieces :]
    s, t = here()
    canvas[...] = early[...]
    for slot in range(slots - 1):
        Patch(plan, info, s, far[slot], slot, far_side(s), True).add_to(canvas)
    last = Patch(plan, info, s, canvas, slots - 1, far_side(s), True)
    for tile in range(plan.tiles):
        where = lanes(tile)
        pick_tile(plan, base.at[:, :, where], layout(refs, t)[0], tile, t)
        base[:, :, where] -= canvas[:, :, where] * inverse[:, where][None]
        mask[:, where] = last.mask(tile)


def take_off(plan, patch, mask, target, base, inverse, tile):
    for part in range(2):
        target[part] = base[part, :, lanes(tile)] - part_of(plan, patch, mask, part, tile) * inverse[:, lanes(tile)]


def middle_kernel(plan, base, patch, mask, inverse, _, middle):
    _, t = here()
    for step in range(plan.mid_tiles):
        take_off(plan, patch, mask, middle.at[:, :, lanes(step)], base, inverse, plan.mid_start(t) + step)


def boundary_kernel(plan, early, patch, mask, *sums):
    _, t = here()
    for total, start in zip(sums, plan.pair_starts(t)):
        for step in range(2):
            tile = start + step
            for part in range(2):
                total[part, :, lanes(step)] = early[part, :, lanes(tile)] + part_of(plan, patch, mask, part, tile)


def halo_sum_kernel(plan, early, mask, *rest):
    halves, sums = rest[: plan.sides], rest[plan.sides :]
    _, t = here()
    for half, total, tile in zip(halves, sums, plan.halo_tiles(t)):
        for part in range(2):
            total[part] = early[part, :, lanes(tile)] + half[part] * mask[:, lanes(tile)]


def last_kernel(plan, base, mask, inverse, _, first, second, *rest):
    nearly, bases, (current, sems) = rest[0], rest[1 : 1 + plan.sides], rest[1 + plan.sides :]
    patch = [first, second]
    _, t = here()
    copies = []
    for step in range(plan.own):
        where = lanes(step)
        take_off(plan, patch, mask, current.at[:, :, where], base, inverse, 1 + step)
        copies.append(pltpu.make_async_copy(current.at[:, :, where], nearly.at[:, :, where], sems.at[step]))
        copies[-1].start()
    for edge, tile in zip(bases, plan.edge_tiles(t)):
        edge[...] = current[:, :, lanes(tile - 1)]
    for copy in copies:
        copy.wait()


def edge_kernel(plan, inverse, *rest):
    bases, received = rest[: plan.sides], rest[plan.sides : 2 * plan.sides]
    _, result, sums, sems = rest[2 * plan.sides :]
    _, t = here()
    copies = []
    for side, tile in enumerate(plan.edge_tiles(t)):
        sums[side] = bases[side][...] - received[side][...] * inverse[:, lanes(tile)][None]
        copies.append(pltpu.make_async_copy(sums.at[side], result.at[:, :, lanes(tile - 1)], sems.at[side]))
        copies[-1].start()
    for copy in copies:
        copy.wait()


def call(kernel, outs, scratch, ins, flops=10**5, size=10**4, in_specs=None, out_specs=None, **options):
    result = pl.pallas_call(
        kernel,
        out_shape=outs,
        in_specs=in_specs or [SMEM if value.dtype == jnp.int32 else VMEM for value in ins],
        out_specs=out_specs or jax.tree.map(lambda _: VMEM, outs),
        scratch_shapes=scratch,
        compiler_params=pltpu.CompilerParams(vmem_limit_bytes=VMEM_BYTES),
        cost_estimate=pl.CostEstimate(flops=flops, bytes_accessed=size, transcendentals=0),
        **options,
    )(*ins)
    return list(result) if isinstance(outs, list) else result


def on_device(plan, object_field, probe_field, amplitudes, centres, counts):
    f32 = jnp.float32
    shape = jax.ShapeDtypeStruct
    size = probe_field.shape[1]
    half = size // 2
    slots = amplitudes.shape[2]
    block_rows = object_field.shape[1]
    block_cols = object_field.shape[2]
    assert block_rows == half and block_cols % (2 * LANES) == 0 and half == LANES
    width = plan.tiles * LANES
    sides = plan.sides
    spots = centres[0, 0]
    counts = counts.reshape(-1)
    own_amps = amplitudes[0, 0]
    tables = jnp.asarray(dft_tables(size))
    order = jnp.asarray(parity_order(size))
    dma = pltpu.SemaphoreType.DMA

    messages = call(
        lambda *refs: edge_message_kernel(plan, *refs),
        [shape((2, half + 8, LANES), f32)] * sides,
        [dma((sides,))],
        [object_field, spots, counts],
        in_specs=[HBM, SMEM, SMEM],
    )
    halos = plan.across(messages)
    far_block = plan.far_rows(object_field)
    near_block = plan.near_rows(object_field)
    rolled, ordered = call(
        prepare_kernel,
        [shape((slots, 2, size, size), f32), shape((slots, size, size), f32)],
        [pltpu.VMEM((2, 2 * size + 8, size), f32)],
        [spots, probe_field, own_amps, order],
    )
    messages = call(
        lambda *refs: halo_message_kernel(plan, *refs),
        [shape((2, half + 24, LANES), f32)] * sides + [shape((2, half + 16, LANES), f32)] * sides + [shape((8, LANES), f32)],
        [],
        [spots, counts, ordered, *halos],
        in_specs=[SMEM, SMEM, ANY] + [VMEM] * sides,
    )
    passed, own_spot = messages[sides:-1], messages[-1]
    far = [far_block] + [plan.far_rows(message) for message in messages[:sides]]
    near = [plan.near_rows(message) for message in passed] + [near_block]
    own = [object_field] + passed
    def runs_layout(refs, main, count, side_starts):
        starts = [main] + side_starts
        own, far, near = refs[: 1 + sides], refs[1 + sides : 2 + 2 * sides], refs[2 + 2 * sides :]
        return lay_out(own, starts), lay_out(far, starts), lay_out(near, side_starts + (chunk_starts(main, count) if len(near) > 1 + sides else [main]))

    def first_layout(refs, t):
        return runs_layout(refs, 1, plan.own, plan.halo_tiles(t))

    def later_layout(refs, t):
        return runs_layout(refs, plan.mid_start(t), plan.mid_tiles, plan.pair_starts(t))

    layout = first_layout

    third = half // 24 * 8
    near_heights = [half - 2 * third, third, third]
    for sweep in range(ITERS):
        pieces = own + far + near
        inner, outer, outer_far = [], [], []
        for slot in range(slots):
            last = slot == slots - 1
            earlier = outer if last else []
            patch = shape((2, half, size), f32)
            halves = 2 if last and sweep == ITERS - 1 else 0
            outer_part, inner_part, *copies = call(
                lambda *refs, slot=slot, layout=layout, copied=len(earlier), halves=halves: term_kernel(
                    plan, slot, layout, len(pieces), copied, halves, slots, *refs
                ),
                [patch] * 2
                + [shape((2, half, LANES), f32)] * halves
                + [shape((2 * slots, rows, size), f32) for rows in near_heights if last],
                [pltpu.VMEM((2, size, size), f32), pltpu.VMEM((3, 3, 2, half, LANES), f32)],
                [own_spot, *pieces, *earlier, rolled, ordered, tables],
            )
            outer_halves, copies = copies[:halves], copies[halves:]
            inner.append(inner_part)
            outer.append(outer_part)
            outer_far.append([plan.far_rows(part) for part in outer_halves] if halves else plan.far_rows(outer_part))
            if sweep == 0 and last:
                info = call(
                    lambda *refs: info_kernel(plan, *refs),
                    shape((3 * (sides + 1), LANES), jnp.int32),
                    [pltpu.VMEM((3 * (sides + 1), 8, LANES), jnp.int32), dma],
                    passed + far[1:] + near[:sides] + [outer_part],
                    in_specs=[VMEM] * (3 * sides) + [ANY],
                    out_specs=SMEM,
                )
        outer_near = [plan.near_rows(copy) for copy in copies]
        if sweep == 0:
            inverse = call(
                lambda *refs: light_kernel(plan, slots, *refs),
                shape((half, width), f32),
                [
                    pltpu.VMEM((2 * size + 8, size), f32),
                    pltpu.VMEM((half, width + 2 * plan.own * LANES), f32),
                ],
                [info, probe_field, copies[0]],
                in_specs=[SMEM, VMEM, ANY],
            )
        early = call(
            lambda *refs: early_sum_kernel(plan, slots, *refs),
            shape((2, half, width), f32),
            [],
            [info, *inner, *outer_near],
        )
        early, base, mask = call(
            lambda *refs, layout=layout: base_kernel(plan, slots, layout, len(pieces), *refs),
            [shape((2, half, width), f32)] * 2 + [shape((half, width), f32)],
            [],
            [info, early, inverse, *outer_far[:-1], *pieces],
        )
        if sweep < ITERS - 1:
            sums = call(
                lambda *refs: boundary_kernel(plan, *refs),
                [shape((2, half, 2 * LANES), f32)] * sides,
                [],
                [early, outer_far[-1], mask],
            )
            received = plan.across(sums)
            middle = call(
                lambda *refs: middle_kernel(plan, *refs),
                shape((2, half, plan.mid_tiles * LANES), f32),
                [],
                [base, outer_far[-1], mask, inverse, sums[0]],
                in_specs=[VMEM] * 4 + [ANY],
            )
            far_middle = plan.far_rows(middle)
            near_runs = [shape((2, half, count * LANES), f32) for count in chunks(plan.mid_tiles)]
            updated = call(
                lambda *refs: pair_kernel(plan, *refs),
                [shape((2, half, 2 * LANES), f32)] * (2 * sides) + near_runs,
                [],
                [base, early, inverse, middle, *sums, *received],
            )
            pairs = updated[:sides]
            own = [middle] + pairs
            far = [far_middle] + [plan.far_rows(piece) for piece in pairs]
            near = [plan.near_rows(piece) for piece in updated[sides:]]
            layout = later_layout
    sums = call(
        lambda *refs: halo_sum_kernel(plan, *refs),
        [shape((2, half, LANES), f32)] * sides,
        [],
        [early, mask, *outer_far[-1][:sides]],
    )
    nearly, *bases = call(
        lambda *refs: last_kernel(plan, *refs),
        [shape((2, half, block_cols), f32)] + [shape((2, half, LANES), f32)] * sides,
        [pltpu.VMEM((2, half, block_cols), f32), dma((plan.own,))],
        [base, mask, inverse, sums[0], *outer_far[-1]],
        in_specs=[VMEM] * 3 + [ANY] + [VMEM] * 2,
        out_specs=[HBM] + [VMEM] * sides,
    )
    received = plan.across(sums)
    return call(
        lambda *refs: edge_kernel(plan, *refs),
        shape(nearly.shape, f32),
        [pltpu.VMEM((sides, 2, half, LANES), f32), dma((sides,))],
        [inverse, *bases, *received, nearly],
        in_specs=[VMEM] * (1 + 2 * sides) + [HBM],
        out_specs=HBM,
        input_output_aliases={1 + 2 * sides: 0},
    )


def solution(mesh):
    sizes = dict(mesh.shape)

    def per_device(object_field, *rest):
        plan = Plan(sizes["sx"], sizes["sy"], *object_field.shape[1:])
        return on_device(plan, object_field, *rest)

    return jax.shard_map(
        per_device,
        mesh=mesh,
        in_specs=(
            P(None, "sx", "sy"),
            P(),
            P("sx", "sy", None, None, None),
            P("sx", "sy", None, None),
            P(None, "sy"),
        ),
        out_specs=P(None, "sx", "sy"),
        check_vma=False,
    )
```

```python
import math

import jax
import jax.numpy as jnp
import ml_dtypes
import numpy as np
from jax import lax
from jax.experimental import pallas as pl
from jax.experimental.pallas import tpu as pltpu
from jax.sharding import PartitionSpec as P

ITERS = 2
SMOOTH = 1.0
DAMPING = 1.0
LANES = 128
VMEM_BYTES = 12 * 1024 * 1024

VMEM = pl.BlockSpec(memory_space=pltpu.VMEM)
SMEM = pl.BlockSpec(memory_space=pltpu.SMEM)
HBM = pl.BlockSpec(memory_space=pltpu.HBM)
ANY = pl.BlockSpec(memory_space=pl.ANY)


def split_numpy(table):
    high = table.astype(np.float32).astype(ml_dtypes.bfloat16)
    low = (table - high.astype(np.float64)).astype(ml_dtypes.bfloat16)
    return high, low


def dft_tables(length):
    half = length // 2
    index = np.arange(half)
    tables = []
    for parity in range(2):
        angles = 2.0 * math.pi / length * (index[:, None] * (2 * index[None, :] + parity) % length)
        cosine = np.cos(angles) / math.sqrt(length)
        sine = np.sin(angles) / math.sqrt(length)
        forward = np.block([[cosine, -sine], [sine, cosine]])
        tables.append([split_numpy(forward), split_numpy(forward.T)])
    return np.array(tables, dtype=ml_dtypes.bfloat16)


def parity_order(length):
    half = length // 2
    order = np.zeros((length, length))
    for index in range(length):
        order[index, index % 2 * half + index // 2] = 1.0
    return np.stack([order, order.T]).astype(ml_dtypes.bfloat16)


def split(values):
    high = values.astype(jnp.bfloat16)
    low = (values - high.astype(jnp.float32)).astype(jnp.bfloat16)
    return high, low


def times_table(values, table):
    high, low = split(values)
    left = jnp.concatenate([high, low, high], axis=1)
    right = jnp.concatenate([table[0], table[0], table[1]], axis=0)
    return jnp.dot(left, right, preferred_element_type=jnp.float32)


def table_times(table, values):
    high, low = split(values)
    left = jnp.concatenate([table[0], table[0], table[1]], axis=1)
    right = jnp.concatenate([high, low, high], axis=0)
    return jnp.dot(left, right, preferred_element_type=jnp.float32)


class Plan:
    def __init__(self, sx_size, sy_size, block_rows, block_cols):
        self.rows = block_rows
        self.sx_size = sx_size
        self.sy_size = sy_size
        self.own = block_cols // LANES
        self.tiles = self.own + 2
        self.paired = sy_size == 2
        self.sides = 1 if self.paired else 2

    def rights(self, t):
        return [1 - t] if self.paired else [0, 1]

    def pair_starts(self, t):
        return [right * (self.tiles - 2) for right in self.rights(t)]

    def halo_tiles(self, t):
        return [right * (self.tiles - 1) for right in self.rights(t)]

    def edge_tiles(self, t):
        return [1 + right * (self.tiles - 3) for right in self.rights(t)]

    def first_parity(self, t):
        return 1 - t if self.paired else 0

    def mid_start(self, t):
        return 1 + t if self.paired else 2

    @property
    def mid_tiles(self):
        return self.tiles - 3 if self.paired else self.tiles - 4

    def across(self, values, axis_name="sy"):
        if self.paired:
            return [lax.ppermute(values[0], axis_name, [(0, 1), (1, 0)])]
        ends = self.sy_size - 1
        return [
            lax.ppermute(values[1], axis_name, [(i, i + 1) for i in range(ends)]),
            lax.ppermute(values[0], axis_name, [(i + 1, i) for i in range(ends)]),
        ]

    def far_rows(self, values):
        rows, columns = self.sx_size, self.sy_size
        pairs = [(i * columns + t, (i + 1) * columns + t) for i in range(1, rows - 1, 2) for t in range(columns)]
        for i in (0, rows - 1):
            pairs += [(i * columns + t, i * columns + t + 1) for t in range(0, columns - 1, 2)]
        return lax.ppermute(values, ("sx", "sy"), pairs + [(j, i) for i, j in pairs])

    def near_rows(self, values):
        return lax.ppermute(values, "sx", [(i, i ^ 1) for i in range(self.sx_size)])

    def outermost(self, s):
        return (s == 0) | (s == self.sx_size - 1)


def far_side(s):
    return 2 * (s % 2) - 1


def lanes(tile, count=1):
    if isinstance(tile, int):
        return pl.ds(tile * LANES, count * LANES)
    return pl.ds(pl.multiple_of(tile * LANES, LANES), count * LANES)


def pick_tile(plan, target, pieces, tile, t):
    rows = target.shape[1]
    if plan.paired:

        @pl.when(tile == (plan.tiles - 1) * t)
        def _():
            target[...] = jnp.zeros(target.shape, jnp.float32)

    for ref, offset, count, start in pieces:

        @pl.when((tile >= start) & (tile < start + count))
        def _(ref=ref, offset=offset, start=start):
            target[...] = ref[:, :rows, lanes(tile - start + offset)]


def lay_out(refs, starts):
    return [(ref, 0, ref.shape[2] // LANES, start) for ref, start in zip(refs, starts)]


def chunks(count):
    return [min(2, count - first) for first in range(0, count, 2)]


def chunk_starts(start, count):
    return [start + 2 * index for index in range(len(chunks(count)))]


def spread(source, targets):
    offset = 0
    for target in targets:
        columns = target.shape[2]
        target[...] = source[:, :, offset : offset + columns]
        offset += columns


def rows_at(ref, start, count):
    offset = start % 8
    values = ref[pl.ds(pl.multiple_of(start - offset, 8), count + 8)]
    return pltpu.roll(values, (count + 8 - offset) % (count + 8), 0)[:count]


def here():
    return lax.axis_index("sx"), lax.axis_index("sy")


def info_rows(centres, count):
    lane = lax.broadcasted_iota(jnp.int32, (8, LANES), 1)
    slots = centres.shape[0]
    values = [centres[slot, axis] for slot in range(slots) for axis in range(2)] + [count]
    line = jnp.zeros((8, LANES), jnp.int32)
    for index, value in enumerate(values):
        line = jnp.where(lane == index, value, line)
    return line.astype(jnp.float32)


def edge_message_kernel(plan, block, centres, counts, *rest):
    messages, sems = rest[: plan.sides], rest[plan.sides]
    s, t = here()
    half = block.shape[1]
    copies = [
        pltpu.make_async_copy(block.at[:, :, lanes(tile - 1)], message.at[:, :half], sems.at[side])
        for side, (message, tile) in enumerate(zip(messages, plan.edge_tiles(t)))
    ]
    for copy in copies:
        copy.start()
    rows = info_rows(centres, counts[s])
    for message in messages:
        message[0, half:] = rows
        message[1, half:] = rows
    for copy in copies:
        copy.wait()


def halo_message_kernel(plan, centres, counts, _, *rest):
    received, far, near = (rest[k * plan.sides : (k + 1) * plan.sides] for k in range(3))
    own = info_rows(centres, counts[lax.axis_index("sx")])
    rest[-1][...] = own
    for source, *messages in zip(received, far, near):
        for message in messages:
            rows = source.shape[1]
            message[:, :rows] = source[...]
            for line in range(rows, message.shape[1], 8):
                message[0, line : line + 8] = own
                message[1, line : line + 8] = own


def pair_kernel(plan, base, early, inverse, middle, *rest):
    sides = plan.sides
    sums, received, results = (rest[k * sides : (k + 1) * sides] for k in range(3))
    near = rest[3 * sides :]
    _, t = here()
    for total, other, result, copy, start in zip(sums, received, results, near, plan.pair_starts(t)):
        where = lanes(start, 2)
        missing = total[...] + other[...] - early[:, :, where]
        values = base[:, :, where] - missing * inverse[:, where][None]
        result[...] = values
        copy[...] = values
    spread(middle, near[sides:])


def spot_kernel(spot, _, copy):
    copy[...] = spot[...]


def prepare_kernel(centres, probe, amps, order, rolled, ordered, padded):
    size = probe.shape[1]
    half = size // 2
    padded[:, :half] = jnp.zeros((2, half, size), jnp.float32)
    padded[:, half + size :] = jnp.zeros((2, half + 8, size), jnp.float32)
    padded[:, half : half + size] = probe[...]
    for slot in range(amps.shape[0]):
        row = centres[slot, 0]
        col = centres[slot, 1]
        for part in range(2):
            shape = padded.at[part]
            upper = rows_at(shape, half - row, half) + rows_at(shape, half + size - row, half)
            lower = rows_at(shape, size - row, half)
            rolled[slot, part] = pltpu.roll(jnp.concatenate([upper, lower], axis=0), col % size, 1)
        high, low = split(amps[slot])
        across = jnp.dot(
            jnp.concatenate([high, low], axis=1),
            jnp.concatenate([order[0], order[0]], axis=0),
            preferred_element_type=jnp.float32,
        )
        high, low = split(across)
        ordered[slot] = jnp.dot(
            jnp.concatenate([order[1], order[1]], axis=1),
            jnp.concatenate([high, low], axis=0),
            preferred_element_type=jnp.float32,
        )


def info_kernel(plan, *rest):
    groups = [rest[k * plan.sides : (k + 1) * plan.sides] for k in range(3)]
    _, info, known, sem = rest[3 * plan.sides :]
    s, _ = here()
    upper = s % 2 == 0
    height = plan.rows

    def lines(messages):
        return [messages[0][0, height + 8 : height + 16]] + [message[0, height : height + 8] for message in messages]

    own, far, near = (lines(messages) for messages in groups)
    far = [jnp.where(plan.outermost(s), 0.0, line) for line in far]
    for turn in range(plan.sides + 1):
        for kind, line in ((0, jnp.where(upper, far[turn], near[turn])), (1, own[turn]), (2, jnp.where(upper, near[turn], far[turn]))):
            known[kind * (plan.sides + 1) + turn] = line.astype(jnp.int32)
    copy = pltpu.make_async_copy(known.at[:, 0], info, sem)
    copy.start()
    copy.wait()


def light_kernel(plan, slots, info, probe, _, inverse, padded, canvas):
    size = probe.shape[1]
    half = size // 2
    _, t = here()
    padded[:half] = jnp.zeros((half, size), jnp.float32)
    padded[half + size :] = jnp.zeros((half + 8, size), jnp.float32)
    padded[half : half + size] = probe[0] * probe[0] + probe[1] * probe[1]
    canvas[...] = jnp.zeros(canvas.shape, jnp.float32)
    reach = plan.sides + 1
    spare = jnp.zeros((half, LANES), jnp.float32)
    for down in (-1, 0, 1):

        def add(step, carry, down=down):
            turn = step // slots
            slot = step % slots
            over = turn * (1 - 2 * t) if plan.paired else jnp.where(turn == 0, 0, 2 * turn - 3)
            index = (down + 1) * reach + turn

            @pl.when(slot < info[index, 2 * slots])
            def _():
                row = info[index, 2 * slot]
                col = info[index, 2 * slot + 1]
                power = rows_at(padded, size - half * down - row, half)
                shifted = pltpu.roll(jnp.concatenate([power, spare], axis=1), col % LANES, 1)
                first = col // LANES + plan.own * (over + 1)
                canvas[:, lanes(first, 3)] += shifted

            return carry

        lax.fori_loop(0, reach * slots, add, 0)
    inverse[...] = 1.0 / (canvas[:, lanes(plan.own, plan.tiles)] + DAMPING)


def term_kernel(plan, slot, layout, pieces, copied, halves, slots, spot, *rest):
    refs, rest = rest[:pieces], rest[pieces:]
    earlier, (probe, amps, tables, inner), rest = rest[:copied], rest[copied : copied + 4], rest[copied + 4 :]
    if halves:
        outer, rest = rest[-1], rest[:-1]
    else:
        outer, rest = rest[0], rest[1:]
    outer_halves, near_outers, (window, picked) = rest[:halves], rest[halves:-2], rest[-2:]
    size = probe.shape[2]
    half = size // 2
    s, t = here()
    line = spot[0:1]
    lane = lax.broadcasted_iota(jnp.int32, line.shape, 1)
    row, col, count = (jnp.sum(jnp.where(lane == k, line, 0.0)).astype(jnp.int32) for k in (2 * slot, 2 * slot + 1, 2 * slots))
    alive = slot < count

    @pl.when(jnp.logical_not(alive))
    def _():
        outer[...] = jnp.zeros(outer.shape, jnp.float32)
        inner[...] = jnp.zeros(inner.shape, jnp.float32)

    @pl.when(alive)
    def _():
        tile = col // LANES
        first = tile % 2
        rest_col = col % LANES
        from_tile = lax.broadcasted_iota(jnp.int32, (half, LANES), 1) >= rest_col
        from_upper = lax.broadcasted_iota(jnp.int32, (half, LANES), 0) >= row
        side = far_side(s)
        own, far, near = layout(refs, t)
        for kind, source in ((1, own), (1 + side, far), (1 - side, near)):
            for step in range(3):
                pick_tile(plan, picked.at[kind, step], source, tile + step, t)

        @pl.when(plan.outermost(s))
        def _():
            picked[1 + side] = jnp.zeros(picked.shape[1:], jnp.float32)

        for part in range(2):
            edge = [jnp.where(from_tile, picked[kind, 0, part], picked[kind, 2, part]) for kind in range(3)]
            window[part, :half, lanes(first)] = jnp.where(from_upper, edge[0], edge[2])
            window[part, half:, lanes(first)] = edge[1]
            window[part, :half, lanes(1 - first)] = jnp.where(from_upper, picked[0, 1, part], picked[2, 1, part])
            window[part, half:, lanes(1 - first)] = picked[1, 1, part]

        probe_real = probe[slot, 0]
        probe_imag = probe[slot, 1]
        exit_real = probe_real * window[0] - probe_imag * window[1]
        exit_imag = probe_real * window[1] + probe_imag * window[0]

        halves = [
            jnp.concatenate([exit_real[:, :half] + sign * exit_real[:, half:], exit_imag[:, :half] + sign * exit_imag[:, half:]], axis=1)
            for sign in (1.0, -1.0)
        ]
        across = [times_table(halves[parity], tables[parity, 0]) for parity in range(2)]
        real = jnp.concatenate([across[0][:, :half], across[1][:, :half]], axis=1)
        imag = jnp.concatenate([across[0][:, half:], across[1][:, half:]], axis=1)
        halves = [
            jnp.concatenate([real[:half] + sign * real[half:], imag[:half] + sign * imag[half:]], axis=0)
            for sign in (1.0, -1.0)
        ]
        back = []
        for parity in range(2):
            pattern = table_times(tables[parity, 1], halves[parity])
            far_real = pattern[:half]
            far_imag = pattern[half:]
            amplitude = amps[slot, parity * half : (parity + 1) * half]
            factor = 1.0 - amplitude * lax.rsqrt(far_real * far_real + far_imag * far_imag + SMOOTH)
            miss = jnp.concatenate([far_real * factor, far_imag * factor], axis=0)
            back.append(table_times(tables[parity, 0], miss))
        real = jnp.concatenate([back[0][:half] + back[1][:half], back[0][:half] - back[1][:half]], axis=0)
        imag = jnp.concatenate([back[0][half:] + back[1][half:], back[0][half:] - back[1][half:]], axis=0)
        both = []
        for parity in range(2):
            columns = slice(parity * half, (parity + 1) * half)
            both.append(times_table(jnp.concatenate([real[:, columns], imag[:, columns]], axis=1), tables[parity, 1]))
        near_real = jnp.concatenate([both[0][:, :half] + both[1][:, :half], both[0][:, :half] - both[1][:, :half]], axis=1)
        near_imag = jnp.concatenate([both[0][:, half:] + both[1][:, half:], both[0][:, half:] - both[1][:, half:]], axis=1)
        term_real = probe_real * near_real + probe_imag * near_imag
        term_imag = probe_real * near_imag - probe_imag * near_real
        outer[0] = term_real[:half]
        outer[1] = term_imag[:half]
        inner[0] = term_real[half:]
        inner[1] = term_imag[half:]

    for index, target in enumerate(outer_halves):
        first = plan.first_parity(t)
        target[...] = outer[:, :, lanes(first if index == 0 else 1 - first)]
    for index, source in enumerate((*earlier, outer)):
        line = 0
        for target in near_outers:
            rows = target.shape[1]
            target[2 * index : 2 * index + 2] = source[:, line : line + rows]
            line += rows


class Patch:
    def __init__(self, plan, info, s, patch, slot, down, far=False):
        runs = patch if isinstance(patch, (list, tuple)) else [patch]
        half = sum(run.shape[1] for run in runs)
        index = (1 if down is None else 1 + down) * (plan.sides + 1)
        row = info[index, 2 * slot]
        col = info[index, 2 * slot + 1]
        self.runs = runs
        self.tile = col // LANES
        self.first = self.tile % 2
        self.rest = col % LANES
        self.lane = lax.broadcasted_iota(jnp.int32, (half, LANES), 1)
        self.from_tile = self.lane >= self.rest
        self.rows = None
        if down is not None:
            line = lax.broadcasted_iota(jnp.int32, (half, LANES), 0)
            after = jnp.where(down > 0, half, row)
            if far:
                after = jnp.where(plan.outermost(s), 0, after)
            self.rows = (line >= jnp.where(down > 0, row, 0)) & (line < after)

    def lines(self, part, place):
        values = jnp.concatenate([run[part, :, lanes(place)] for run in self.runs], axis=0)
        return values if self.rows is None else jnp.where(self.rows, values, 0.0)

    def tiles(self, part):
        edge = self.lines(part, self.first)
        middle = self.lines(part, 1 - self.first)
        return jnp.where(self.from_tile, edge, 0.0), middle, jnp.where(self.from_tile, 0.0, edge)

    def add_to(self, canvas):
        for part in range(2):
            for step, values in enumerate(self.tiles(part)):
                canvas[part, :, lanes(self.tile + step)] += values

    def mask(self, tile):
        step = tile - self.tile
        first = jnp.where(step == 0, self.rest, 0)
        after = jnp.where(step == 2, self.rest, jnp.where((step < 0) | (step > 2), 0, LANES))
        inside = (self.lane >= first) & (self.lane < after)
        if self.rows is not None:
            inside = inside & self.rows
        return jnp.where(inside, 1.0, 0.0)


def part_of(plan, patch, mask, part, tile):
    if isinstance(patch, (list, tuple)):
        first = plan.first_parity(lax.axis_index("sy"))
        values = jnp.where(tile % 2 == first, patch[0][part], patch[1][part])
    else:
        values = patch[part, :, lanes(tile % 2)]
    return values * mask[:, lanes(tile)]


def early_sum_kernel(plan, slots, info, *rest):
    inner, near, canvas = rest[:slots], rest[slots:-1], rest[-1]
    s, _ = here()
    canvas[...] = jnp.zeros(canvas.shape, jnp.float32)
    for slot in range(slots):
        Patch(plan, info, s, inner[slot], slot, None).add_to(canvas)
        runs = [run.at[2 * slot : 2 * slot + 2] for run in near]
        Patch(plan, info, s, runs, slot, -far_side(s)).add_to(canvas)


def base_kernel(plan, slots, layout, pieces, info, early, inverse, *rest):
    far, refs, (canvas, base, mask) = rest[: slots - 1], rest[slots - 1 : slots - 1 + pieces], rest[slots - 1 + pieces :]
    s, t = here()
    canvas[...] = early[...]
    for slot in range(slots - 1):
        Patch(plan, info, s, far[slot], slot, far_side(s), True).add_to(canvas)
    last = Patch(plan, info, s, canvas, slots - 1, far_side(s), True)
    for tile in range(plan.tiles):
        where = lanes(tile)
        pick_tile(plan, base.at[:, :, where], layout(refs, t)[0], tile, t)
        base[:, :, where] -= canvas[:, :, where] * inverse[:, where][None]
        mask[:, where] = last.mask(tile)


def take_off(plan, patch, mask, target, base, inverse, tile):
    for part in range(2):
        target[part] = base[part, :, lanes(tile)] - part_of(plan, patch, mask, part, tile) * inverse[:, lanes(tile)]


def middle_kernel(plan, base, patch, mask, inverse, middle):
    _, t = here()
    for step in range(plan.mid_tiles):
        take_off(plan, patch, mask, middle.at[:, :, lanes(step)], base, inverse, plan.mid_start(t) + step)


def boundary_kernel(plan, early, patch, mask, _, *sums):
    _, t = here()
    for total, start in zip(sums, plan.pair_starts(t)):
        for step in range(2):
            tile = start + step
            for part in range(2):
                total[part, :, lanes(step)] = early[part, :, lanes(tile)] + part_of(plan, patch, mask, part, tile)


def halo_sum_kernel(plan, early, mask, *rest):
    halves, sums = rest[: plan.sides], rest[plan.sides :]
    _, t = here()
    for half, total, tile in zip(halves, sums, plan.halo_tiles(t)):
        for part in range(2):
            total[part] = early[part, :, lanes(tile)] + half[part] * mask[:, lanes(tile)]


def last_kernel(plan, base, mask, inverse, _, first, second, *rest):
    nearly, bases, (current, sems) = rest[0], rest[1 : 1 + plan.sides], rest[1 + plan.sides :]
    patch = [first, second]
    _, t = here()
    copies = []
    for step in range(plan.own):
        where = lanes(step)
        take_off(plan, patch, mask, current.at[:, :, where], base, inverse, 1 + step)
        copies.append(pltpu.make_async_copy(current.at[:, :, where], nearly.at[:, :, where], sems.at[step]))
        copies[-1].start()
    for edge, tile in zip(bases, plan.edge_tiles(t)):
        edge[...] = current[:, :, lanes(tile - 1)]
    for copy in copies:
        copy.wait()


def edge_kernel(plan, inverse, *rest):
    bases, received = rest[: plan.sides], rest[plan.sides : 2 * plan.sides]
    _, result, sums, sems = rest[2 * plan.sides :]
    _, t = here()
    copies = []
    for side, tile in enumerate(plan.edge_tiles(t)):
        sums[side] = bases[side][...] - received[side][...] * inverse[:, lanes(tile)][None]
        copies.append(pltpu.make_async_copy(sums.at[side], result.at[:, :, lanes(tile - 1)], sems.at[side]))
        copies[-1].start()
    for copy in copies:
        copy.wait()


def call(kernel, outs, scratch, ins, flops=10**5, size=10**4, in_specs=None, out_specs=None, **options):
    result = pl.pallas_call(
        kernel,
        out_shape=outs,
        in_specs=in_specs or [SMEM if value.dtype == jnp.int32 else VMEM for value in ins],
        out_specs=out_specs or jax.tree.map(lambda _: VMEM, outs),
        scratch_shapes=scratch,
        compiler_params=pltpu.CompilerParams(vmem_limit_bytes=VMEM_BYTES),
        cost_estimate=pl.CostEstimate(flops=flops, bytes_accessed=size, transcendentals=0),
        **options,
    )(*ins)
    return list(result) if isinstance(outs, list) else result


def on_device(plan, object_field, probe_field, amplitudes, centres, counts):
    f32 = jnp.float32
    shape = jax.ShapeDtypeStruct
    size = probe_field.shape[1]
    half = size // 2
    slots = amplitudes.shape[2]
    block_rows = object_field.shape[1]
    block_cols = object_field.shape[2]
    assert block_rows == half and block_cols % (2 * LANES) == 0 and half == LANES
    width = plan.tiles * LANES
    sides = plan.sides
    spots = centres[0, 0]
    counts = counts.reshape(-1)
    own_amps = amplitudes[0, 0]
    tables = jnp.asarray(dft_tables(size))
    order = jnp.asarray(parity_order(size))
    dma = pltpu.SemaphoreType.DMA

    messages = call(
        lambda *refs: edge_message_kernel(plan, *refs),
        [shape((2, half + 8, LANES), f32)] * sides,
        [dma((sides,))],
        [object_field, spots, counts],
        in_specs=[HBM, SMEM, SMEM],
    )
    halos = plan.across(messages)
    far_block = plan.far_rows(object_field)
    near_block = plan.near_rows(object_field)
    rolled, ordered = call(
        prepare_kernel,
        [shape((slots, 2, size, size), f32), shape((slots, size, size), f32)],
        [pltpu.VMEM((2, 2 * size + 8, size), f32)],
        [spots, probe_field, own_amps, order],
    )
    messages = call(
        lambda *refs: halo_message_kernel(plan, *refs),
        [shape((2, half + 24, LANES), f32)] * sides + [shape((2, half + 16, LANES), f32)] * sides + [shape((8, LANES), f32)],
        [],
        [spots, counts, ordered, *halos],
        in_specs=[SMEM, SMEM, ANY] + [VMEM] * sides,
    )
    passed, own_spot = messages[sides:-1], messages[-1]
    far = [far_block] + [plan.far_rows(message) for message in messages[:sides]]
    near = [plan.near_rows(message) for message in passed] + [near_block]
    own = [object_field] + passed
    def runs_layout(refs, main, count, side_starts):
        starts = [main] + side_starts
        own, far, near = refs[: 1 + sides], refs[1 + sides : 2 + 2 * sides], refs[2 + 2 * sides :]
        return lay_out(own, starts), lay_out(far, starts), lay_out(near, side_starts + (chunk_starts(main, count) if len(near) > 1 + sides else [main]))

    def first_layout(refs, t):
        return runs_layout(refs, 1, plan.own, plan.halo_tiles(t))

    def later_layout(refs, t):
        return runs_layout(refs, plan.mid_start(t), plan.mid_tiles, plan.pair_starts(t))

    layout = first_layout

    third = half // 24 * 8
    near_heights = [half - 2 * third, third, third]
    for sweep in range(ITERS):
        pieces = own + far + near
        inner, outer, outer_far = [], [], []
        for slot in range(slots):
            last = slot == slots - 1
            earlier = outer if last else []
            patch = shape((2, half, size), f32)
            halves = 2 if last and sweep == ITERS - 1 else 0
            inner_part, *copies = call(
                lambda *refs, slot=slot, layout=layout, copied=len(earlier), halves=halves: term_kernel(
                    plan, slot, layout, len(pieces), copied, halves, slots, *refs
                ),
                [patch]
                + ([shape((2, half, LANES), f32)] * halves or [patch])
                + [shape((2 * slots, rows, size), f32) for rows in near_heights if last],
                [pltpu.VMEM((2, size, size), f32), pltpu.VMEM((3, 3, 2, half, LANES), f32)]
                + [pltpu.VMEM((2, half, size), f32)] * (halves > 0),
                [own_spot, *pieces, *earlier, rolled, ordered, tables],
            )
            outer_part = None if halves else copies.pop(0)
            outer_halves, copies = copies[:halves], copies[halves:]
            inner.append(inner_part)
            outer.append(outer_part)
            outer_far.append([plan.far_rows(part) for part in outer_halves] if halves else plan.far_rows(outer_part))
            if sweep == 0 and last:
                info = call(
                    lambda *refs: info_kernel(plan, *refs),
                    shape((3 * (sides + 1), LANES), jnp.int32),
                    [pltpu.VMEM((3 * (sides + 1), 8, LANES), jnp.int32), dma],
                    passed + far[1:] + near[:sides] + [outer_part],
                    in_specs=[VMEM] * (3 * sides) + [ANY],
                    out_specs=SMEM,
                )
        outer_near = [plan.near_rows(copy) for copy in copies]
        if sweep == 0:
            inverse = call(
                lambda *refs: light_kernel(plan, slots, *refs),
                shape((half, width), f32),
                [
                    pltpu.VMEM((2 * size + 8, size), f32),
                    pltpu.VMEM((half, width + 2 * plan.own * LANES), f32),
                ],
                [info, probe_field, copies[0]],
                in_specs=[SMEM, VMEM, ANY],
            )
        early = call(
            lambda *refs: early_sum_kernel(plan, slots, *refs),
            shape((2, half, width), f32),
            [],
            [info, *inner, *outer_near],
        )
        early, base, mask = call(
            lambda *refs, layout=layout: base_kernel(plan, slots, layout, len(pieces), *refs),
            [shape((2, half, width), f32)] * 2 + [shape((half, width), f32)],
            [],
            [info, early, inverse, *outer_far[:-1], *pieces],
        )
        if sweep < ITERS - 1:
            middle = call(
                lambda *refs: middle_kernel(plan, *refs),
                shape((2, half, plan.mid_tiles * LANES), f32),
                [],
                [base, outer_far[-1], mask, inverse],
            )
            far_middle = plan.far_rows(middle)
            sums = call(
                lambda *refs: boundary_kernel(plan, *refs),
                [shape((2, half, 2 * LANES), f32)] * sides,
                [],
                [early, outer_far[-1], mask, middle],
                in_specs=[VMEM] * 3 + [ANY],
            )
            received = plan.across(sums)
            near_runs = [shape((2, half, count * LANES), f32) for count in chunks(plan.mid_tiles)]
            updated = call(
                lambda *refs: pair_kernel(plan, *refs),
                [shape((2, half, 2 * LANES), f32)] * (2 * sides) + near_runs,
                [],
                [base, early, inverse, middle, *sums, *received],
            )
            pairs = updated[:sides]
            own = [middle] + pairs
            far = [far_middle] + [plan.far_rows(piece) for piece in pairs]
            near = [plan.near_rows(piece) for piece in updated[sides:]]
            layout = later_layout
            own_spot = call(
                spot_kernel,
                shape(own_spot.shape, f32),
                [],
                [own_spot, far_middle],
                in_specs=[VMEM, ANY],
                flops=10**11,
            )
    sums = call(
        lambda *refs: halo_sum_kernel(plan, *refs),
        [shape((2, half, LANES), f32)] * sides,
        [],
        [early, mask, *outer_far[-1][:sides]],
    )
    nearly, *bases = call(
        lambda *refs: last_kernel(plan, *refs),
        [shape((2, half, block_cols), f32)] + [shape((2, half, LANES), f32)] * sides,
        [pltpu.VMEM((2, half, block_cols), f32), dma((plan.own,))],
        [base, mask, inverse, sums[0], *outer_far[-1]],
        in_specs=[VMEM] * 3 + [ANY] + [VMEM] * 2,
        out_specs=[HBM] + [VMEM] * sides,
    )
    received = plan.across(sums)
    return call(
        lambda *refs: edge_kernel(plan, *refs),
        shape(nearly.shape, f32),
        [pltpu.VMEM((sides, 2, half, LANES), f32), dma((sides,))],
        [inverse, *bases, *received, nearly],
        in_specs=[VMEM] * (1 + 2 * sides) + [HBM],
        out_specs=HBM,
        input_output_aliases={1 + 2 * sides: 0},
    )


def solution(mesh):
    sizes = dict(mesh.shape)

    def per_device(object_field, *rest):
        plan = Plan(sizes["sx"], sizes["sy"], *object_field.shape[1:])
        return on_device(plan, object_field, *rest)

    return jax.shard_map(
        per_device,
        mesh=mesh,
        in_specs=(
            P(None, "sx", "sy"),
            P(),
            P("sx", "sy", None, None, None),
            P("sx", "sy", None, None),
            P(None, "sy"),
        ),
        out_specs=P(None, "sx", "sy"),
        check_vma=False,
    )
```

```python
import math

import jax
import jax.numpy as jnp
import ml_dtypes
import numpy as np
from jax import lax
from jax.experimental import pallas as pl
from jax.experimental.pallas import tpu as pltpu
from jax.sharding import PartitionSpec as P

ITERS = 2
SMOOTH = 1.0
DAMPING = 1.0
LANES = 128
VMEM_BYTES = 12 * 1024 * 1024

VMEM = pl.BlockSpec(memory_space=pltpu.VMEM)
SMEM = pl.BlockSpec(memory_space=pltpu.SMEM)
HBM = pl.BlockSpec(memory_space=pltpu.HBM)
ANY = pl.BlockSpec(memory_space=pl.ANY)


def split_numpy(table):
    high = table.astype(np.float32).astype(ml_dtypes.bfloat16)
    low = (table - high.astype(np.float64)).astype(ml_dtypes.bfloat16)
    return high, low


def dft_tables(length):
    half = length // 2
    index = np.arange(half)
    tables = []
    for parity in range(2):
        angles = 2.0 * math.pi / length * (index[:, None] * (2 * index[None, :] + parity) % length)
        cosine = np.cos(angles) / math.sqrt(length)
        sine = np.sin(angles) / math.sqrt(length)
        forward = np.block([[cosine, -sine], [sine, cosine]])
        tables.append([split_numpy(forward), split_numpy(forward.T)])
    return np.array(tables, dtype=ml_dtypes.bfloat16)


def parity_order(length):
    half = length // 2
    order = np.zeros((length, length))
    for index in range(length):
        order[index, index % 2 * half + index // 2] = 1.0
    return np.stack([order, order.T]).astype(ml_dtypes.bfloat16)


def split(values):
    high = values.astype(jnp.bfloat16)
    low = (values - high.astype(jnp.float32)).astype(jnp.bfloat16)
    return high, low


def times_table(values, table):
    high, low = split(values)
    left = jnp.concatenate([high, low, high], axis=1)
    right = jnp.concatenate([table[0], table[0], table[1]], axis=0)
    return jnp.dot(left, right, preferred_element_type=jnp.float32)


def table_times(table, values):
    high, low = split(values)
    left = jnp.concatenate([table[0], table[0], table[1]], axis=1)
    right = jnp.concatenate([high, low, high], axis=0)
    return jnp.dot(left, right, preferred_element_type=jnp.float32)


class Plan:
    def __init__(self, sx_size, sy_size, block_rows, block_cols):
        self.rows = block_rows
        self.sx_size = sx_size
        self.sy_size = sy_size
        self.own = block_cols // LANES
        self.tiles = self.own + 2
        self.paired = sy_size == 2
        self.sides = 1 if self.paired else 2

    def rights(self, t):
        return [1 - t] if self.paired else [0, 1]

    def pair_starts(self, t):
        return [right * (self.tiles - 2) for right in self.rights(t)]

    def halo_tiles(self, t):
        return [right * (self.tiles - 1) for right in self.rights(t)]

    def edge_tiles(self, t):
        return [1 + right * (self.tiles - 3) for right in self.rights(t)]

    def first_parity(self, t):
        return 1 - t if self.paired else 0

    def mid_start(self, t):
        return 1 + t if self.paired else 2

    @property
    def mid_tiles(self):
        return self.tiles - 3 if self.paired else self.tiles - 4

    def across(self, values, axis_name="sy"):
        if self.paired:
            return [lax.ppermute(values[0], axis_name, [(0, 1), (1, 0)])]
        ends = self.sy_size - 1
        return [
            lax.ppermute(values[1], axis_name, [(i, i + 1) for i in range(ends)]),
            lax.ppermute(values[0], axis_name, [(i + 1, i) for i in range(ends)]),
        ]

    def far_rows(self, values):
        rows, columns = self.sx_size, self.sy_size
        pairs = [(i * columns + t, (i + 1) * columns + t) for i in range(1, rows - 1, 2) for t in range(columns)]
        for i in (0, rows - 1):
            pairs += [(i * columns + t, i * columns + t + 1) for t in range(0, columns - 1, 2)]
        return lax.ppermute(values, ("sx", "sy"), pairs + [(j, i) for i, j in pairs])

    def near_rows(self, values):
        return lax.ppermute(values, "sx", [(i, i ^ 1) for i in range(self.sx_size)])

    def outermost(self, s):
        return (s == 0) | (s == self.sx_size - 1)


def far_side(s):
    return 2 * (s % 2) - 1


def lanes(tile, count=1):
    if isinstance(tile, int):
        return pl.ds(tile * LANES, count * LANES)
    return pl.ds(pl.multiple_of(tile * LANES, LANES), count * LANES)


def pick_tile(plan, target, pieces, tile, t):
    rows = target.shape[1]
    if plan.paired:

        @pl.when(tile == (plan.tiles - 1) * t)
        def _():
            target[...] = jnp.zeros(target.shape, jnp.float32)

    for ref, offset, count, start in pieces:

        @pl.when((tile >= start) & (tile < start + count))
        def _(ref=ref, offset=offset, start=start):
            target[...] = ref[:, :rows, lanes(tile - start + offset)]


def lay_out(refs, starts):
    return [(ref, 0, ref.shape[2] // LANES, start) for ref, start in zip(refs, starts)]


def chunks(count):
    return [min(2, count - first) for first in range(0, count, 2)]


def chunk_starts(start, count):
    return [start + 2 * index for index in range(len(chunks(count)))]


def spread(source, targets):
    offset = 0
    for target in targets:
        columns = target.shape[2]
        target[...] = source[:, :, offset : offset + columns]
        offset += columns


def rows_at(ref, start, count):
    offset = start % 8
    values = ref[pl.ds(pl.multiple_of(start - offset, 8), count + 8)]
    return pltpu.roll(values, (count + 8 - offset) % (count + 8), 0)[:count]


def here():
    return lax.axis_index("sx"), lax.axis_index("sy")


def info_rows(centres, count):
    lane = lax.broadcasted_iota(jnp.int32, (8, LANES), 1)
    slots = centres.shape[0]
    values = [centres[slot, axis] for slot in range(slots) for axis in range(2)] + [count]
    line = jnp.zeros((8, LANES), jnp.int32)
    for index, value in enumerate(values):
        line = jnp.where(lane == index, value, line)
    return line.astype(jnp.float32)


def edge_message_kernel(plan, block, centres, counts, *rest):
    messages, sems = rest[: plan.sides], rest[plan.sides]
    s, t = here()
    half = block.shape[1]
    copies = [
        pltpu.make_async_copy(block.at[:, :, lanes(tile - 1)], message.at[:, :half], sems.at[side])
        for side, (message, tile) in enumerate(zip(messages, plan.edge_tiles(t)))
    ]
    for copy in copies:
        copy.start()
    rows = info_rows(centres, counts[s])
    for message in messages:
        message[0, half:] = rows
        message[1, half:] = rows
    for copy in copies:
        copy.wait()


def halo_message_kernel(plan, centres, counts, _, *rest):
    sides = plan.sides
    received, far, halos, infos = (rest[k * sides : (k + 1) * sides] for k in range(4))
    own = info_rows(centres, counts[lax.axis_index("sx")])
    rest[-1][...] = own
    upper_line = lax.broadcasted_iota(jnp.int32, own.shape, 0) == 0
    for source, message, halo, info in zip(received, far, halos, infos):
        rows = halo.shape[1]
        both = jnp.where(upper_line, own, pltpu.roll(source[0, rows : rows + 8], 1, 0))
        halo[...] = source[:, :rows]
        info[...] = both
        message[:, :rows] = source[:, :rows]
        message[0, rows:] = both
        message[1, rows:] = both


def pair_kernel(plan, base, early, inverse, middle, *rest):
    sides = plan.sides
    sums, received, results = (rest[k * sides : (k + 1) * sides] for k in range(3))
    near = rest[3 * sides :]
    _, t = here()
    for total, other, result, copy, start in zip(sums, received, results, near, plan.pair_starts(t)):
        where = lanes(start, 2)
        missing = total[...] + other[...] - early[:, :, where]
        values = base[:, :, where] - missing * inverse[:, where][None]
        result[...] = values
        copy[...] = values
    spread(middle, near[sides:])


def prepare_kernel(centres, probe, amps, order, rolled, ordered, padded):
    size = probe.shape[1]
    half = size // 2
    padded[:, :half] = jnp.zeros((2, half, size), jnp.float32)
    padded[:, half + size :] = jnp.zeros((2, half + 8, size), jnp.float32)
    padded[:, half : half + size] = probe[...]
    for slot in range(amps.shape[0]):
        row = centres[slot, 0]
        col = centres[slot, 1]
        for part in range(2):
            shape = padded.at[part]
            upper = rows_at(shape, half - row, half) + rows_at(shape, half + size - row, half)
            lower = rows_at(shape, size - row, half)
            rolled[slot, part] = pltpu.roll(jnp.concatenate([upper, lower], axis=0), col % size, 1)
        high, low = split(amps[slot])
        across = jnp.dot(
            jnp.concatenate([high, low], axis=1),
            jnp.concatenate([order[0], order[0]], axis=0),
            preferred_element_type=jnp.float32,
        )
        high, low = split(across)
        ordered[slot] = jnp.dot(
            jnp.concatenate([order[1], order[1]], axis=1),
            jnp.concatenate([high, low], axis=0),
            preferred_element_type=jnp.float32,
        )


def info_kernel(plan, *rest):
    home, far, other = (rest[k * plan.sides : (k + 1) * plan.sides] for k in range(3))
    _, info, known, sem = rest[3 * plan.sides :]
    s, _ = here()
    upper = s % 2 == 0
    width = plan.sides + 1

    def lines(messages):
        return [messages[0]] + [pltpu.roll(message, 7, 0) for message in messages]

    own = lines([line[...] for line in home])
    near = lines([line[...] for line in other])
    far = lines([jnp.where(plan.outermost(s), 0.0, message[0, plan.rows :]) for message in far])
    for turn in range(width):
        for kind, line in ((0, jnp.where(upper, far[turn], near[turn])), (1, own[turn]), (2, jnp.where(upper, near[turn], far[turn]))):
            known[kind * width + turn] = line.astype(jnp.int32)
    copy = pltpu.make_async_copy(known.at[:, 0], info, sem)
    copy.start()
    copy.wait()


def light_kernel(plan, slots, info, probe, _, inverse, padded, canvas):
    size = probe.shape[1]
    half = size // 2
    _, t = here()
    padded[:half] = jnp.zeros((half, size), jnp.float32)
    padded[half + size :] = jnp.zeros((half + 8, size), jnp.float32)
    padded[half : half + size] = probe[0] * probe[0] + probe[1] * probe[1]
    canvas[...] = jnp.zeros(canvas.shape, jnp.float32)
    reach = plan.sides + 1
    spare = jnp.zeros((half, LANES), jnp.float32)
    for down in (-1, 0, 1):

        def add(step, carry, down=down):
            turn = step // slots
            slot = step % slots
            over = turn * (1 - 2 * t) if plan.paired else jnp.where(turn == 0, 0, 2 * turn - 3)
            index = (down + 1) * reach + turn

            @pl.when(slot < info[index, 2 * slots])
            def _():
                row = info[index, 2 * slot]
                col = info[index, 2 * slot + 1]
                power = rows_at(padded, size - half * down - row, half)
                shifted = pltpu.roll(jnp.concatenate([power, spare], axis=1), col % LANES, 1)
                first = col // LANES + plan.own * (over + 1)
                canvas[:, lanes(first, 3)] += shifted

            return carry

        lax.fori_loop(0, reach * slots, add, 0)
    inverse[...] = 1.0 / (canvas[:, lanes(plan.own, plan.tiles)] + DAMPING)


def term_kernel(plan, slot, layout, pieces, copied, halves, slots, spot, *rest):
    refs, rest = rest[:pieces], rest[pieces:]
    earlier, (probe, amps, tables, inner), rest = rest[:copied], rest[copied : copied + 4], rest[copied + 4 :]
    if halves:
        outer, rest = rest[-1], rest[:-1]
    else:
        outer, rest = rest[0], rest[1:]
    outer_halves, near_outers, (window, picked) = rest[:halves], rest[halves:-2], rest[-2:]
    size = probe.shape[2]
    half = size // 2
    s, t = here()
    line = spot[0:1]
    lane = lax.broadcasted_iota(jnp.int32, line.shape, 1)
    row, col, count = (jnp.sum(jnp.where(lane == k, line, 0.0)).astype(jnp.int32) for k in (2 * slot, 2 * slot + 1, 2 * slots))
    alive = slot < count

    @pl.when(jnp.logical_not(alive))
    def _():
        outer[...] = jnp.zeros(outer.shape, jnp.float32)
        inner[...] = jnp.zeros(inner.shape, jnp.float32)

    @pl.when(alive)
    def _():
        tile = col // LANES
        first = tile % 2
        rest_col = col % LANES
        from_tile = lax.broadcasted_iota(jnp.int32, (half, LANES), 1) >= rest_col
        from_upper = lax.broadcasted_iota(jnp.int32, (half, LANES), 0) >= row
        side = far_side(s)
        own, far, near = layout(refs, t)
        for kind, source in ((1, own), (1 + side, far), (1 - side, near)):
            for step in range(3):
                pick_tile(plan, picked.at[kind, step], source, tile + step, t)

        @pl.when(plan.outermost(s))
        def _():
            picked[1 + side] = jnp.zeros(picked.shape[1:], jnp.float32)

        for part in range(2):
            edge = [jnp.where(from_tile, picked[kind, 0, part], picked[kind, 2, part]) for kind in range(3)]
            window[part, :half, lanes(first)] = jnp.where(from_upper, edge[0], edge[2])
            window[part, half:, lanes(first)] = edge[1]
            window[part, :half, lanes(1 - first)] = jnp.where(from_upper, picked[0, 1, part], picked[2, 1, part])
            window[part, half:, lanes(1 - first)] = picked[1, 1, part]

        probe_real = probe[slot, 0]
        probe_imag = probe[slot, 1]
        exit_real = probe_real * window[0] - probe_imag * window[1]
        exit_imag = probe_real * window[1] + probe_imag * window[0]

        halves = [
            jnp.concatenate([exit_real[:, :half] + sign * exit_real[:, half:], exit_imag[:, :half] + sign * exit_imag[:, half:]], axis=1)
            for sign in (1.0, -1.0)
        ]
        across = [times_table(halves[parity], tables[parity, 0]) for parity in range(2)]
        real = jnp.concatenate([across[0][:, :half], across[1][:, :half]], axis=1)
        imag = jnp.concatenate([across[0][:, half:], across[1][:, half:]], axis=1)
        halves = [
            jnp.concatenate([real[:half] + sign * real[half:], imag[:half] + sign * imag[half:]], axis=0)
            for sign in (1.0, -1.0)
        ]
        back = []
        for parity in range(2):
            pattern = table_times(tables[parity, 1], halves[parity])
            far_real = pattern[:half]
            far_imag = pattern[half:]
            amplitude = amps[slot, parity * half : (parity + 1) * half]
            factor = 1.0 - amplitude * lax.rsqrt(far_real * far_real + far_imag * far_imag + SMOOTH)
            miss = jnp.concatenate([far_real * factor, far_imag * factor], axis=0)
            back.append(table_times(tables[parity, 0], miss))
        real = jnp.concatenate([back[0][:half] + back[1][:half], back[0][:half] - back[1][:half]], axis=0)
        imag = jnp.concatenate([back[0][half:] + back[1][half:], back[0][half:] - back[1][half:]], axis=0)
        both = []
        for parity in range(2):
            columns = slice(parity * half, (parity + 1) * half)
            both.append(times_table(jnp.concatenate([real[:, columns], imag[:, columns]], axis=1), tables[parity, 1]))
        near_real = jnp.concatenate([both[0][:, :half] + both[1][:, :half], both[0][:, :half] - both[1][:, :half]], axis=1)
        near_imag = jnp.concatenate([both[0][:, half:] + both[1][:, half:], both[0][:, half:] - both[1][:, half:]], axis=1)
        term_real = probe_real * near_real + probe_imag * near_imag
        term_imag = probe_real * near_imag - probe_imag * near_real
        outer[0] = term_real[:half]
        outer[1] = term_imag[:half]
        inner[0] = term_real[half:]
        inner[1] = term_imag[half:]

    for index, target in enumerate(outer_halves):
        first = plan.first_parity(t)
        target[...] = outer[:, :, lanes(first if index == 0 else 1 - first)]
    for index, source in enumerate((*earlier, outer)):
        line = 0
        for target in near_outers:
            rows = target.shape[1]
            target[2 * index : 2 * index + 2] = source[:, line : line + rows]
            line += rows


class Patch:
    def __init__(self, plan, info, s, patch, slot, down, far=False):
        runs = patch if isinstance(patch, (list, tuple)) else [patch]
        half = sum(run.shape[1] for run in runs)
        index = (1 if down is None else 1 + down) * (plan.sides + 1)
        row = info[index, 2 * slot]
        col = info[index, 2 * slot + 1]
        self.runs = runs
        self.tile = col // LANES
        self.first = self.tile % 2
        self.rest = col % LANES
        self.lane = lax.broadcasted_iota(jnp.int32, (half, LANES), 1)
        self.from_tile = self.lane >= self.rest
        self.rows = None
        if down is not None:
            line = lax.broadcasted_iota(jnp.int32, (half, LANES), 0)
            after = jnp.where(down > 0, half, row)
            if far:
                after = jnp.where(plan.outermost(s), 0, after)
            self.rows = (line >= jnp.where(down > 0, row, 0)) & (line < after)

    def lines(self, part, place):
        values = jnp.concatenate([run[part, :, lanes(place)] for run in self.runs], axis=0)
        return values if self.rows is None else jnp.where(self.rows, values, 0.0)

    def tiles(self, part):
        edge = self.lines(part, self.first)
        middle = self.lines(part, 1 - self.first)
        return jnp.where(self.from_tile, edge, 0.0), middle, jnp.where(self.from_tile, 0.0, edge)

    def add_to(self, canvas):
        for part in range(2):
            for step, values in enumerate(self.tiles(part)):
                canvas[part, :, lanes(self.tile + step)] += values

    def mask(self, tile):
        step = tile - self.tile
        first = jnp.where(step == 0, self.rest, 0)
        after = jnp.where(step == 2, self.rest, jnp.where((step < 0) | (step > 2), 0, LANES))
        inside = (self.lane >= first) & (self.lane < after)
        if self.rows is not None:
            inside = inside & self.rows
        return jnp.where(inside, 1.0, 0.0)


def part_of(plan, patch, mask, part, tile):
    if isinstance(patch, (list, tuple)):
        first = plan.first_parity(lax.axis_index("sy"))
        values = jnp.where(tile % 2 == first, patch[0][part], patch[1][part])
    else:
        values = patch[part, :, lanes(tile % 2)]
    return values * mask[:, lanes(tile)]


def early_sum_kernel(plan, slots, info, *rest):
    inner, near, canvas = rest[:slots], rest[slots:-1], rest[-1]
    s, _ = here()
    canvas[...] = jnp.zeros(canvas.shape, jnp.float32)
    for slot in range(slots):
        Patch(plan, info, s, inner[slot], slot, None).add_to(canvas)
        runs = [run.at[2 * slot : 2 * slot + 2] for run in near]
        Patch(plan, info, s, runs, slot, -far_side(s)).add_to(canvas)


def base_kernel(plan, slots, layout, pieces, info, early, inverse, *rest):
    far, refs, (canvas, base, mask) = rest[: slots - 1], rest[slots - 1 : slots - 1 + pieces], rest[slots - 1 + pieces :]
    s, t = here()
    canvas[...] = early[...]
    for slot in range(slots - 1):
        Patch(plan, info, s, far[slot], slot, far_side(s), True).add_to(canvas)
    last = Patch(plan, info, s, canvas, slots - 1, far_side(s), True)
    for tile in range(plan.tiles):
        where = lanes(tile)
        pick_tile(plan, base.at[:, :, where], layout(refs, t)[0], tile, t)
        base[:, :, where] -= canvas[:, :, where] * inverse[:, where][None]
        mask[:, where] = last.mask(tile)


def take_off(plan, patch, mask, target, base, inverse, tile):
    for part in range(2):
        target[part] = base[part, :, lanes(tile)] - part_of(plan, patch, mask, part, tile) * inverse[:, lanes(tile)]


def middle_kernel(plan, base, patch, mask, inverse, _, middle):
    _, t = here()
    for step in range(plan.mid_tiles):
        take_off(plan, patch, mask, middle.at[:, :, lanes(step)], base, inverse, plan.mid_start(t) + step)


def boundary_kernel(plan, early, patch, mask, *sums):
    _, t = here()
    for total, start in zip(sums, plan.pair_starts(t)):
        for step in range(2):
            tile = start + step
            for part in range(2):
                total[part, :, lanes(step)] = early[part, :, lanes(tile)] + part_of(plan, patch, mask, part, tile)


def halo_sum_kernel(plan, early, mask, *rest):
    halves, sums = rest[: plan.sides], rest[plan.sides :]
    _, t = here()
    for half, total, tile in zip(halves, sums, plan.halo_tiles(t)):
        for part in range(2):
            total[part] = early[part, :, lanes(tile)] + half[part] * mask[:, lanes(tile)]


def last_kernel(plan, base, mask, inverse, _, first, second, *rest):
    nearly, bases, (current, sems) = rest[0], rest[1 : 1 + plan.sides], rest[1 + plan.sides :]
    patch = [first, second]
    _, t = here()
    copies = []
    for step in range(plan.own):
        where = lanes(step)
        take_off(plan, patch, mask, current.at[:, :, where], base, inverse, 1 + step)
        copies.append(pltpu.make_async_copy(current.at[:, :, where], nearly.at[:, :, where], sems.at[step]))
        copies[-1].start()
    for edge, tile in zip(bases, plan.edge_tiles(t)):
        edge[...] = current[:, :, lanes(tile - 1)]
    for copy in copies:
        copy.wait()


def edge_kernel(plan, inverse, *rest):
    bases, received = rest[: plan.sides], rest[plan.sides : 2 * plan.sides]
    _, result, sums, sems = rest[2 * plan.sides :]
    _, t = here()
    copies = []
    for side, tile in enumerate(plan.edge_tiles(t)):
        sums[side] = bases[side][...] - received[side][...] * inverse[:, lanes(tile)][None]
        copies.append(pltpu.make_async_copy(sums.at[side], result.at[:, :, lanes(tile - 1)], sems.at[side]))
        copies[-1].start()
    for copy in copies:
        copy.wait()


def call(kernel, outs, scratch, ins, flops=10**5, size=10**4, in_specs=None, out_specs=None, **options):
    result = pl.pallas_call(
        kernel,
        out_shape=outs,
        in_specs=in_specs or [SMEM if value.dtype == jnp.int32 else VMEM for value in ins],
        out_specs=out_specs or jax.tree.map(lambda _: VMEM, outs),
        scratch_shapes=scratch,
        compiler_params=pltpu.CompilerParams(vmem_limit_bytes=VMEM_BYTES),
        cost_estimate=pl.CostEstimate(flops=flops, bytes_accessed=size, transcendentals=0),
        **options,
    )(*ins)
    return list(result) if isinstance(outs, list) else result


def on_device(plan, object_field, probe_field, amplitudes, centres, counts):
    f32 = jnp.float32
    shape = jax.ShapeDtypeStruct
    size = probe_field.shape[1]
    half = size // 2
    slots = amplitudes.shape[2]
    block_rows = object_field.shape[1]
    block_cols = object_field.shape[2]
    assert block_rows == half and block_cols % (2 * LANES) == 0 and half == LANES
    width = plan.tiles * LANES
    sides = plan.sides
    spots = centres[0, 0]
    counts = counts.reshape(-1)
    own_amps = amplitudes[0, 0]
    tables = jnp.asarray(dft_tables(size))
    order = jnp.asarray(parity_order(size))
    dma = pltpu.SemaphoreType.DMA

    messages = call(
        lambda *refs: edge_message_kernel(plan, *refs),
        [shape((2, half + 8, LANES), f32)] * sides,
        [dma((sides,))],
        [object_field, spots, counts],
        in_specs=[HBM, SMEM, SMEM],
    )
    halos = plan.across(messages)
    far_block = plan.far_rows(object_field)
    near_block = plan.near_rows(object_field)
    rolled, ordered = call(
        prepare_kernel,
        [shape((slots, 2, size, size), f32), shape((slots, size, size), f32)],
        [pltpu.VMEM((2, 2 * size + 8, size), f32)],
        [spots, probe_field, own_amps, order],
    )
    messages = call(
        lambda *refs: halo_message_kernel(plan, *refs),
        [shape((2, half + 8, LANES), f32)] * sides
        + [shape((2, half, LANES), f32)] * sides
        + [shape((8, LANES), f32)] * (sides + 1),
        [],
        [spots, counts, ordered, *halos],
        in_specs=[SMEM, SMEM, ANY] + [VMEM] * sides,
    )
    passed, lines, own_spot = messages[sides : 2 * sides], messages[2 * sides : -1], messages[-1]
    near_lines = [plan.near_rows(line) for line in lines]
    far = [far_block] + [plan.far_rows(message) for message in messages[:sides]]
    near = [plan.near_rows(message) for message in passed] + [near_block]
    own = [object_field] + passed
    def runs_layout(refs, main, count, side_starts):
        starts = [main] + side_starts
        own, far, near = refs[: 1 + sides], refs[1 + sides : 2 + 2 * sides], refs[2 + 2 * sides :]
        return lay_out(own, starts), lay_out(far, starts), lay_out(near, side_starts + (chunk_starts(main, count) if len(near) > 1 + sides else [main]))

    def first_layout(refs, t):
        return runs_layout(refs, 1, plan.own, plan.halo_tiles(t))

    def later_layout(refs, t):
        return runs_layout(refs, plan.mid_start(t), plan.mid_tiles, plan.pair_starts(t))

    layout = first_layout

    third = half // 24 * 8
    near_heights = [half - 2 * third, third, third]
    for sweep in range(ITERS):
        pieces = own + far + near
        inner, outer, outer_far = [], [], []
        for slot in range(slots):
            last = slot == slots - 1
            earlier = outer if last else []
            patch = shape((2, half, size), f32)
            halves = 2 if last and sweep == ITERS - 1 else 0
            inner_part, *copies = call(
                lambda *refs, slot=slot, layout=layout, copied=len(earlier), halves=halves: term_kernel(
                    plan, slot, layout, len(pieces), copied, halves, slots, *refs
                ),
                [patch]
                + ([shape((2, half, LANES), f32)] * halves or [patch])
                + [shape((2 * slots, rows, size), f32) for rows in near_heights if last],
                [pltpu.VMEM((2, size, size), f32), pltpu.VMEM((3, 3, 2, half, LANES), f32)]
                + [pltpu.VMEM((2, half, size), f32)] * (halves > 0),
                [own_spot, *pieces, *earlier, rolled, ordered, tables],
            )
            outer_part = None if halves else copies.pop(0)
            outer_halves, copies = copies[:halves], copies[halves:]
            inner.append(inner_part)
            outer.append(outer_part)
            outer_far.append([plan.far_rows(part) for part in outer_halves] if halves else plan.far_rows(outer_part))
            if sweep == 0 and last:
                info = call(
                    lambda *refs: info_kernel(plan, *refs),
                    shape((3 * (sides + 1), LANES), jnp.int32),
                    [pltpu.VMEM((3 * (sides + 1), 8, LANES), jnp.int32), dma],
                    lines + far[1:] + near_lines + [outer_part],
                    in_specs=[VMEM] * (3 * sides) + [ANY],
                    out_specs=SMEM,
                )
        outer_near = [plan.near_rows(copy) for copy in copies]
        if sweep == 0:
            inverse = call(
                lambda *refs: light_kernel(plan, slots, *refs),
                shape((half, width), f32),
                [
                    pltpu.VMEM((2 * size + 8, size), f32),
                    pltpu.VMEM((half, width + 2 * plan.own * LANES), f32),
                ],
                [info, probe_field, copies[0]],
                in_specs=[SMEM, VMEM, ANY],
            )
        early = call(
            lambda *refs: early_sum_kernel(plan, slots, *refs),
            shape((2, half, width), f32),
            [],
            [info, *inner, *outer_near],
        )
        early, base, mask = call(
            lambda *refs, layout=layout: base_kernel(plan, slots, layout, len(pieces), *refs),
            [shape((2, half, width), f32)] * 2 + [shape((half, width), f32)],
            [],
            [info, early, inverse, *outer_far[:-1], *pieces],
        )
        if sweep < ITERS - 1:
            sums = call(
                lambda *refs: boundary_kernel(plan, *refs),
                [shape((2, half, 2 * LANES), f32)] * sides,
                [],
                [early, outer_far[-1], mask],
            )
            received = plan.across(sums)
            middle = call(
                lambda *refs: middle_kernel(plan, *refs),
                shape((2, half, plan.mid_tiles * LANES), f32),
                [],
                [base, outer_far[-1], mask, inverse, sums[0]],
                in_specs=[VMEM] * 4 + [ANY],
            )
            far_middle = plan.far_rows(middle)
            near_runs = [shape((2, half, count * LANES), f32) for count in chunks(plan.mid_tiles)]
            updated = call(
                lambda *refs: pair_kernel(plan, *refs),
                [shape((2, half, 2 * LANES), f32)] * (2 * sides) + near_runs,
                [],
                [base, early, inverse, middle, *sums, *received],
            )
            pairs = updated[:sides]
            own = [middle] + pairs
            far = [far_middle] + [plan.far_rows(piece) for piece in pairs]
            near = [plan.near_rows(piece) for piece in updated[sides:]]
            layout = later_layout
    sums = call(
        lambda *refs: halo_sum_kernel(plan, *refs),
        [shape((2, half, LANES), f32)] * sides,
        [],
        [early, mask, *outer_far[-1][:sides]],
    )
    nearly, *bases = call(
        lambda *refs: last_kernel(plan, *refs),
        [shape((2, half, block_cols), f32)] + [shape((2, half, LANES), f32)] * sides,
        [pltpu.VMEM((2, half, block_cols), f32), dma((plan.own,))],
        [base, mask, inverse, sums[0], *outer_far[-1]],
        in_specs=[VMEM] * 3 + [ANY] + [VMEM] * 2,
        out_specs=[HBM] + [VMEM] * sides,
    )
    received = plan.across(sums)
    return call(
        lambda *refs: edge_kernel(plan, *refs),
        shape(nearly.shape, f32),
        [pltpu.VMEM((sides, 2, half, LANES), f32), dma((sides,))],
        [inverse, *bases, *received, nearly],
        in_specs=[VMEM] * (1 + 2 * sides) + [HBM],
        out_specs=HBM,
        input_output_aliases={1 + 2 * sides: 0},
    )


def solution(mesh):
    sizes = dict(mesh.shape)

    def per_device(object_field, *rest):
        plan = Plan(sizes["sx"], sizes["sy"], *object_field.shape[1:])
        return on_device(plan, object_field, *rest)

    return jax.shard_map(
        per_device,
        mesh=mesh,
        in_specs=(
            P(None, "sx", "sy"),
            P(),
            P("sx", "sy", None, None, None),
            P("sx", "sy", None, None),
            P(None, "sy"),
        ),
        out_specs=P(None, "sx", "sy"),
        check_vma=False,
    )
```

```python
import math

import jax
import jax.numpy as jnp
import ml_dtypes
import numpy as np
from jax import lax
from jax.experimental import pallas as pl
from jax.experimental.pallas import tpu as pltpu
from jax.sharding import PartitionSpec as P

ITERS = 2
SMOOTH = 1.0
DAMPING = 1.0
LANES = 128
VMEM_BYTES = 12 * 1024 * 1024

VMEM = pl.BlockSpec(memory_space=pltpu.VMEM)
SMEM = pl.BlockSpec(memory_space=pltpu.SMEM)
HBM = pl.BlockSpec(memory_space=pltpu.HBM)
ANY = pl.BlockSpec(memory_space=pl.ANY)


def split_numpy(table):
    high = table.astype(np.float32).astype(ml_dtypes.bfloat16)
    low = (table - high.astype(np.float64)).astype(ml_dtypes.bfloat16)
    return high, low


def dft_tables(length):
    half = length // 2
    index = np.arange(half)
    tables = []
    for parity in range(2):
        angles = 2.0 * math.pi / length * (index[:, None] * (2 * index[None, :] + parity) % length)
        cosine = np.cos(angles) / math.sqrt(length)
        sine = np.sin(angles) / math.sqrt(length)
        forward = np.block([[cosine, -sine], [sine, cosine]])
        tables.append([split_numpy(forward), split_numpy(forward.T)])
    return np.array(tables, dtype=ml_dtypes.bfloat16)


def parity_order(length):
    half = length // 2
    order = np.zeros((length, length))
    for index in range(length):
        order[index, index % 2 * half + index // 2] = 1.0
    return np.stack([order, order.T]).astype(ml_dtypes.bfloat16)


def split(values):
    high = values.astype(jnp.bfloat16)
    low = (values - high.astype(jnp.float32)).astype(jnp.bfloat16)
    return high, low


def times_table(values, table):
    high, low = split(values)
    left = jnp.concatenate([high, low, high], axis=1)
    right = jnp.concatenate([table[0], table[0], table[1]], axis=0)
    return jnp.dot(left, right, preferred_element_type=jnp.float32)


def table_times(table, values):
    high, low = split(values)
    left = jnp.concatenate([table[0], table[0], table[1]], axis=1)
    right = jnp.concatenate([high, low, high], axis=0)
    return jnp.dot(left, right, preferred_element_type=jnp.float32)


class Plan:
    def __init__(self, sx_size, sy_size, block_rows, block_cols):
        self.rows = block_rows
        self.sx_size = sx_size
        self.sy_size = sy_size
        self.own = block_cols // LANES
        self.tiles = self.own + 2
        self.paired = sy_size == 2
        self.sides = 1 if self.paired else 2

    def rights(self, t):
        return [1 - t] if self.paired else [0, 1]

    def pair_starts(self, t):
        return [right * (self.tiles - 2) for right in self.rights(t)]

    def halo_tiles(self, t):
        return [right * (self.tiles - 1) for right in self.rights(t)]

    def edge_tiles(self, t):
        return [1 + right * (self.tiles - 3) for right in self.rights(t)]

    def first_parity(self, t):
        return 1 - t if self.paired else 0

    def mid_start(self, t):
        return 1 + t if self.paired else 2

    @property
    def mid_tiles(self):
        return self.tiles - 3 if self.paired else self.tiles - 4

    def across(self, values, axis_name="sy"):
        if self.paired:
            return [lax.ppermute(values[0], axis_name, [(0, 1), (1, 0)])]
        ends = self.sy_size - 1
        return [
            lax.ppermute(values[1], axis_name, [(i, i + 1) for i in range(ends)]),
            lax.ppermute(values[0], axis_name, [(i + 1, i) for i in range(ends)]),
        ]

    def far_rows(self, values):
        rows, columns = self.sx_size, self.sy_size
        pairs = [(i * columns + t, (i + 1) * columns + t) for i in range(1, rows - 1, 2) for t in range(columns)]
        for i in (0, rows - 1):
            pairs += [(i * columns + t, i * columns + t + 1) for t in range(0, columns - 1, 2)]
        return lax.ppermute(values, ("sx", "sy"), pairs + [(j, i) for i, j in pairs])

    def near_rows(self, values):
        return lax.ppermute(values, "sx", [(i, i ^ 1) for i in range(self.sx_size)])

    def outermost(self, s):
        return (s == 0) | (s == self.sx_size - 1)


def far_side(s):
    return 2 * (s % 2) - 1


def lanes(tile, count=1):
    if isinstance(tile, int):
        return pl.ds(tile * LANES, count * LANES)
    return pl.ds(pl.multiple_of(tile * LANES, LANES), count * LANES)


def pick_tile(plan, target, pieces, tile, t):
    rows = target.shape[1]
    if plan.paired:

        @pl.when(tile == (plan.tiles - 1) * t)
        def _():
            target[...] = jnp.zeros(target.shape, jnp.float32)

    for ref, offset, count, start in pieces:

        @pl.when((tile >= start) & (tile < start + count))
        def _(ref=ref, offset=offset, start=start):
            target[...] = ref[:, :rows, lanes(tile - start + offset)]


def lay_out(refs, starts):
    return [(ref, 0, ref.shape[2] // LANES, start) for ref, start in zip(refs, starts)]


def chunks(count):
    return [min(2, count - first) for first in range(0, count, 2)]


def chunk_starts(start, count):
    return [start + 2 * index for index in range(len(chunks(count)))]


def spread(source, targets):
    offset = 0
    for target in targets:
        columns = target.shape[2]
        target[...] = source[:, :, offset : offset + columns]
        offset += columns


def rows_at(ref, start, count):
    offset = start % 8
    values = ref[pl.ds(pl.multiple_of(start - offset, 8), count + 8)]
    return pltpu.roll(values, (count + 8 - offset) % (count + 8), 0)[:count]


def here():
    return lax.axis_index("sx"), lax.axis_index("sy")


def info_rows(centres, count):
    lane = lax.broadcasted_iota(jnp.int32, (8, LANES), 1)
    slots = centres.shape[0]
    values = [centres[slot, axis] for slot in range(slots) for axis in range(2)] + [count]
    line = jnp.zeros((8, LANES), jnp.int32)
    for index, value in enumerate(values):
        line = jnp.where(lane == index, value, line)
    return line.astype(jnp.float32)


def edge_message_kernel(plan, block, centres, counts, *rest):
    messages, sems = rest[: plan.sides], rest[plan.sides]
    s, t = here()
    half = block.shape[1]
    copies = [
        pltpu.make_async_copy(block.at[:, :, lanes(tile - 1)], message.at[:, :half], sems.at[side])
        for side, (message, tile) in enumerate(zip(messages, plan.edge_tiles(t)))
    ]
    for copy in copies:
        copy.start()
    rows = info_rows(centres, counts[s])
    for message in messages:
        message[0, half:] = rows
        message[1, half:] = rows
    for copy in copies:
        copy.wait()


def halo_message_kernel(plan, centres, counts, _, *rest):
    sides = plan.sides
    received, far, halos, infos = (rest[k * sides : (k + 1) * sides] for k in range(4))
    own = info_rows(centres, counts[lax.axis_index("sx")])
    rest[-1][...] = own
    upper_line = lax.broadcasted_iota(jnp.int32, own.shape, 0) == 0
    for source, message, halo, info in zip(received, far, halos, infos):
        rows = halo.shape[1]
        both = jnp.where(upper_line, own, pltpu.roll(source[0, rows : rows + 8], 1, 0))
        halo[...] = source[:, :rows]
        info[...] = both
        message[:, :rows] = source[:, :rows]
        message[0, rows:] = both
        message[1, rows:] = both


def pair_kernel(plan, base, early, inverse, middle, *rest):
    sides = plan.sides
    sums, received, results = (rest[k * sides : (k + 1) * sides] for k in range(3))
    near = rest[3 * sides :]
    _, t = here()
    for total, other, result, copy, start in zip(sums, received, results, near, plan.pair_starts(t)):
        where = lanes(start, 2)
        missing = total[...] + other[...] - early[:, :, where]
        values = base[:, :, where] - missing * inverse[:, where][None]
        result[...] = values
        copy[...] = values
    spread(middle, near[sides:])


def prepare_kernel(centres, probe, amps, order, rolled, ordered, padded):
    size = probe.shape[1]
    half = size // 2
    padded[:, :half] = jnp.zeros((2, half, size), jnp.float32)
    padded[:, half + size :] = jnp.zeros((2, half + 8, size), jnp.float32)
    padded[:, half : half + size] = probe[...]
    for slot in range(amps.shape[0]):
        row = centres[slot, 0]
        col = centres[slot, 1]
        for part in range(2):
            shape = padded.at[part]
            upper = rows_at(shape, half - row, half) + rows_at(shape, half + size - row, half)
            lower = rows_at(shape, size - row, half)
            rolled[slot, part] = pltpu.roll(jnp.concatenate([upper, lower], axis=0), col % LANES, 1)
        high, low = split(amps[slot])
        across = jnp.dot(
            jnp.concatenate([high, low], axis=1),
            jnp.concatenate([order[0], order[0]], axis=0),
            preferred_element_type=jnp.float32,
        )
        high, low = split(across)
        ordered[slot] = jnp.dot(
            jnp.concatenate([order[1], order[1]], axis=1),
            jnp.concatenate([high, low], axis=0),
            preferred_element_type=jnp.float32,
        )


def info_kernel(plan, *rest):
    home, far, other = (rest[k * plan.sides : (k + 1) * plan.sides] for k in range(3))
    _, info, known, sem = rest[3 * plan.sides :]
    s, _ = here()
    upper = s % 2 == 0
    width = plan.sides + 1

    def lines(messages):
        return [messages[0]] + [pltpu.roll(message, 7, 0) for message in messages]

    own = lines([line[...] for line in home])
    near = lines([line[...] for line in other])
    far = lines([jnp.where(plan.outermost(s), 0.0, message[0, plan.rows :]) for message in far])
    for turn in range(width):
        for kind, line in ((0, jnp.where(upper, far[turn], near[turn])), (1, own[turn]), (2, jnp.where(upper, near[turn], far[turn]))):
            known[kind * width + turn] = line.astype(jnp.int32)
    copy = pltpu.make_async_copy(known.at[:, 0], info, sem)
    copy.start()
    copy.wait()


def light_kernel(plan, slots, info, probe, _, inverse, padded, canvas):
    size = probe.shape[1]
    half = size // 2
    _, t = here()
    padded[:half] = jnp.zeros((half, size), jnp.float32)
    padded[half + size :] = jnp.zeros((half + 8, size), jnp.float32)
    padded[half : half + size] = probe[0] * probe[0] + probe[1] * probe[1]
    canvas[...] = jnp.zeros(canvas.shape, jnp.float32)
    reach = plan.sides + 1
    spare = jnp.zeros((half, LANES), jnp.float32)
    for down in (-1, 0, 1):

        def add(step, carry, down=down):
            turn = step // slots
            slot = step % slots
            over = turn * (1 - 2 * t) if plan.paired else jnp.where(turn == 0, 0, 2 * turn - 3)
            index = (down + 1) * reach + turn

            @pl.when(slot < info[index, 2 * slots])
            def _():
                row = info[index, 2 * slot]
                col = info[index, 2 * slot + 1]
                power = rows_at(padded, size - half * down - row, half)
                shifted = pltpu.roll(jnp.concatenate([power, spare], axis=1), col % LANES, 1)
                first = col // LANES + plan.own * (over + 1)
                canvas[:, lanes(first, 3)] += shifted

            return carry

        lax.fori_loop(0, reach * slots, add, 0)
    inverse[...] = 1.0 / (canvas[:, lanes(plan.own, plan.tiles)] + DAMPING)


def term_kernel(plan, slot, layout, pieces, copied, halves, slots, spot, *rest):
    refs, rest = rest[:pieces], rest[pieces:]
    earlier, (probe, amps, tables, inner), rest = rest[:copied], rest[copied : copied + 4], rest[copied + 4 :]
    if halves:
        outer, rest = rest[-1], rest[:-1]
    else:
        outer, rest = rest[0], rest[1:]
    outer_halves, near_outers, picked = rest[:halves], rest[halves:-1], rest[-1]
    size = probe.shape[2]
    half = size // 2
    s, t = here()
    line = spot[0:1]
    lane = lax.broadcasted_iota(jnp.int32, line.shape, 1)
    entries = (2 * slot, 2 * slot + 1, 2 * slots)
    row, col, count = (jnp.sum(jnp.where(lane == k, line, 0.0)).astype(jnp.int32) for k in entries)
    alive = slot < count

    @pl.when(jnp.logical_not(alive))
    def _():
        outer[...] = jnp.zeros(outer.shape, jnp.float32)
        inner[...] = jnp.zeros(inner.shape, jnp.float32)

    @pl.when(alive)
    def _():
        tile = col // LANES
        first = tile % 2
        rest_col = col % LANES
        from_tile = lax.broadcasted_iota(jnp.int32, (half, LANES), 1) >= rest_col
        from_upper = lax.broadcasted_iota(jnp.int32, (half, LANES), 0) >= row
        side = far_side(s)
        own, far, near = layout(refs, t)
        for kind, source in ((1, own), (1 + side, far), (1 - side, near)):
            for step in range(3):
                pick_tile(plan, picked.at[kind, step], source, tile + step, t)

        @pl.when(plan.outermost(s))
        def _():
            picked[1 + side] = jnp.zeros(picked.shape[1:], jnp.float32)

        def edge(kind, part):
            return jnp.where(from_tile, picked[kind, 0, part], picked[kind, 2, part])

        def across(edges, middles, rows):
            sums, differences = [], []
            shares = []
            for columns, (real, imag) in ((slice(0, half), edges), (slice(half, size), middles)):
                probe_real, probe_imag = probe[slot, 0, rows, columns], probe[slot, 1, rows, columns]
                shares.append((probe_real * real - probe_imag * imag, probe_real * imag + probe_imag * real))
            for part in range(2):
                sums.append(shares[0][part] + shares[1][part])
                differences.append(shares[0][part] - shares[1][part])
            return [
                times_table(jnp.concatenate(parts, axis=1), tables[parity, 0])
                for parity, parts in enumerate((sums, differences))
            ]

        lower = across(
            [edge(1, part) for part in range(2)], [picked[1, 1, part] for part in range(2)], slice(half, size)
        )
        upper = across(
            [jnp.where(from_upper, edge(0, part), edge(2, part)) for part in range(2)],
            [jnp.where(from_upper, picked[0, 1, part], picked[2, 1, part]) for part in range(2)],
            slice(0, half),
        )
        halves = []
        for sign in (1.0, -1.0):
            rows = [top + sign * bottom for top, bottom in zip(upper, lower)]
            halves.append(
                jnp.concatenate(
                    [jnp.concatenate([row[:, part] for row in rows], axis=1) for part in (slice(0, half), slice(half, size))],
                    axis=0,
                )
            )
        back = []
        for parity in range(2):
            pattern = table_times(tables[parity, 1], halves[parity])
            far_real = pattern[:half]
            far_imag = pattern[half:]
            amplitude = amps[slot, parity * half : (parity + 1) * half]
            factor = 1.0 - amplitude * lax.rsqrt(far_real * far_real + far_imag * far_imag + SMOOTH)
            miss = jnp.concatenate([far_real * factor, far_imag * factor], axis=0)
            back.append(table_times(tables[parity, 0], miss))
        real = jnp.concatenate([back[0][:half] + back[1][:half], back[0][:half] - back[1][:half]], axis=0)
        imag = jnp.concatenate([back[0][half:] + back[1][half:], back[0][half:] - back[1][half:]], axis=0)
        both = []
        for parity in range(2):
            columns = slice(parity * half, (parity + 1) * half)
            both.append(times_table(jnp.concatenate([real[:, columns], imag[:, columns]], axis=1), tables[parity, 1]))
        near_real = jnp.concatenate([both[0][:, :half] + both[1][:, :half], both[0][:, :half] - both[1][:, :half]], axis=1)
        near_imag = jnp.concatenate([both[0][:, half:] + both[1][:, half:], both[0][:, half:] - both[1][:, half:]], axis=1)
        probe_real = probe[slot, 0]
        probe_imag = probe[slot, 1]
        for part, term in enumerate((probe_real * near_real + probe_imag * near_imag, probe_real * near_imag - probe_imag * near_real)):
            for place, columns in ((first, slice(0, half)), (1 - first, slice(half, size))):
                outer[part, :, lanes(place)] = term[:half, columns]
                inner[part, :, lanes(place)] = term[half:, columns]

    for index, target in enumerate(outer_halves):
        first = plan.first_parity(t)
        target[...] = outer[:, :, lanes(first if index == 0 else 1 - first)]
    for index, source in enumerate((*earlier, outer)):
        line = 0
        for target in near_outers:
            rows = target.shape[1]
            target[2 * index : 2 * index + 2] = source[:, line : line + rows]
            line += rows


class Patch:
    def __init__(self, plan, info, s, patch, slot, down, far=False):
        runs = patch if isinstance(patch, (list, tuple)) else [patch]
        half = sum(run.shape[1] for run in runs)
        index = (1 if down is None else 1 + down) * (plan.sides + 1)
        row = info[index, 2 * slot]
        col = info[index, 2 * slot + 1]
        self.runs = runs
        self.tile = col // LANES
        self.first = self.tile % 2
        self.rest = col % LANES
        self.lane = lax.broadcasted_iota(jnp.int32, (half, LANES), 1)
        self.from_tile = self.lane >= self.rest
        self.rows = None
        if down is not None:
            line = lax.broadcasted_iota(jnp.int32, (half, LANES), 0)
            after = jnp.where(down > 0, half, row)
            if far:
                after = jnp.where(plan.outermost(s), 0, after)
            self.rows = (line >= jnp.where(down > 0, row, 0)) & (line < after)

    def lines(self, part, place):
        values = jnp.concatenate([run[part, :, lanes(place)] for run in self.runs], axis=0)
        return values if self.rows is None else jnp.where(self.rows, values, 0.0)

    def tiles(self, part):
        edge = self.lines(part, self.first)
        middle = self.lines(part, 1 - self.first)
        return jnp.where(self.from_tile, edge, 0.0), middle, jnp.where(self.from_tile, 0.0, edge)

    def add_to(self, canvas):
        for part in range(2):
            for step, values in enumerate(self.tiles(part)):
                canvas[part, :, lanes(self.tile + step)] += values

    def mask(self, tile):
        step = tile - self.tile
        first = jnp.where(step == 0, self.rest, 0)
        after = jnp.where(step == 2, self.rest, jnp.where((step < 0) | (step > 2), 0, LANES))
        inside = (self.lane >= first) & (self.lane < after)
        if self.rows is not None:
            inside = inside & self.rows
        return jnp.where(inside, 1.0, 0.0)


def part_of(plan, patch, mask, part, tile):
    if isinstance(patch, (list, tuple)):
        first = plan.first_parity(lax.axis_index("sy"))
        values = jnp.where(tile % 2 == first, patch[0][part], patch[1][part])
    else:
        values = patch[part, :, lanes(tile % 2)]
    return values * mask[:, lanes(tile)]


def early_sum_kernel(plan, slots, info, *rest):
    inner, near, canvas = rest[:slots], rest[slots:-1], rest[-1]
    s, _ = here()
    canvas[...] = jnp.zeros(canvas.shape, jnp.float32)
    for slot in range(slots):
        Patch(plan, info, s, inner[slot], slot, None).add_to(canvas)
        runs = [run.at[2 * slot : 2 * slot + 2] for run in near]
        Patch(plan, info, s, runs, slot, -far_side(s)).add_to(canvas)


def base_kernel(plan, slots, layout, pieces, info, early, inverse, *rest):
    far, refs, (canvas, base, mask) = rest[: slots - 1], rest[slots - 1 : slots - 1 + pieces], rest[slots - 1 + pieces :]
    s, t = here()
    canvas[...] = early[...]
    for slot in range(slots - 1):
        Patch(plan, info, s, far[slot], slot, far_side(s), True).add_to(canvas)
    last = Patch(plan, info, s, canvas, slots - 1, far_side(s), True)
    for tile in range(plan.tiles):
        where = lanes(tile)
        pick_tile(plan, base.at[:, :, where], layout(refs, t)[0], tile, t)
        base[:, :, where] -= canvas[:, :, where] * inverse[:, where][None]
        mask[:, where] = last.mask(tile)


def take_off(plan, patch, mask, target, base, inverse, tile):
    for part in range(2):
        target[part] = base[part, :, lanes(tile)] - part_of(plan, patch, mask, part, tile) * inverse[:, lanes(tile)]


def middle_kernel(plan, base, patch, mask, inverse, _, middle):
    _, t = here()
    for step in range(plan.mid_tiles):
        take_off(plan, patch, mask, middle.at[:, :, lanes(step)], base, inverse, plan.mid_start(t) + step)


def boundary_kernel(plan, early, patch, mask, *sums):
    _, t = here()
    for total, start in zip(sums, plan.pair_starts(t)):
        for step in range(2):
            tile = start + step
            for part in range(2):
                total[part, :, lanes(step)] = early[part, :, lanes(tile)] + part_of(plan, patch, mask, part, tile)


def halo_sum_kernel(plan, early, mask, *rest):
    halves, sums = rest[: plan.sides], rest[plan.sides :]
    _, t = here()
    for half, total, tile in zip(halves, sums, plan.halo_tiles(t)):
        for part in range(2):
            total[part] = early[part, :, lanes(tile)] + half[part] * mask[:, lanes(tile)]


def last_kernel(plan, base, mask, inverse, _, first, second, *rest):
    nearly, bases, (current, sems) = rest[0], rest[1 : 1 + plan.sides], rest[1 + plan.sides :]
    patch = [first, second]
    _, t = here()
    copies = []
    for step in range(plan.own):
        where = lanes(step)
        take_off(plan, patch, mask, current.at[:, :, where], base, inverse, 1 + step)
        copies.append(pltpu.make_async_copy(current.at[:, :, where], nearly.at[:, :, where], sems.at[step]))
        copies[-1].start()
    for edge, tile in zip(bases, plan.edge_tiles(t)):
        edge[...] = current[:, :, lanes(tile - 1)]
    for copy in copies:
        copy.wait()


def edge_kernel(plan, inverse, *rest):
    bases, received = rest[: plan.sides], rest[plan.sides : 2 * plan.sides]
    _, result, sums, sems = rest[2 * plan.sides :]
    _, t = here()
    copies = []
    for side, tile in enumerate(plan.edge_tiles(t)):
        sums[side] = bases[side][...] - received[side][...] * inverse[:, lanes(tile)][None]
        copies.append(pltpu.make_async_copy(sums.at[side], result.at[:, :, lanes(tile - 1)], sems.at[side]))
        copies[-1].start()
    for copy in copies:
        copy.wait()


def call(kernel, outs, scratch, ins, flops=10**5, size=10**4, in_specs=None, out_specs=None, **options):
    result = pl.pallas_call(
        kernel,
        out_shape=outs,
        in_specs=in_specs or [SMEM if value.dtype == jnp.int32 else VMEM for value in ins],
        out_specs=out_specs or jax.tree.map(lambda _: VMEM, outs),
        scratch_shapes=scratch,
        compiler_params=pltpu.CompilerParams(vmem_limit_bytes=VMEM_BYTES),
        cost_estimate=pl.CostEstimate(flops=flops, bytes_accessed=size, transcendentals=0),
        **options,
    )(*ins)
    return list(result) if isinstance(outs, list) else result


def on_device(plan, object_field, probe_field, amplitudes, centres, counts):
    f32 = jnp.float32
    shape = jax.ShapeDtypeStruct
    size = probe_field.shape[1]
    half = size // 2
    slots = amplitudes.shape[2]
    block_rows = object_field.shape[1]
    block_cols = object_field.shape[2]
    assert block_rows == half and block_cols % (2 * LANES) == 0 and half == LANES
    width = plan.tiles * LANES
    sides = plan.sides
    spots = centres[0, 0]
    counts = counts.reshape(-1)
    own_amps = amplitudes[0, 0]
    tables = jnp.asarray(dft_tables(size))
    order = jnp.asarray(parity_order(size))
    dma = pltpu.SemaphoreType.DMA

    messages = call(
        lambda *refs: edge_message_kernel(plan, *refs),
        [shape((2, half + 8, LANES), f32)] * sides,
        [dma((sides,))],
        [object_field, spots, counts],
        in_specs=[HBM, SMEM, SMEM],
    )
    halos = plan.across(messages)
    far_block = plan.far_rows(object_field)
    near_block = plan.near_rows(object_field)
    rolled, ordered = call(
        prepare_kernel,
        [shape((slots, 2, size, size), f32), shape((slots, size, size), f32)],
        [pltpu.VMEM((2, 2 * size + 8, size), f32)],
        [spots, probe_field, own_amps, order],
    )
    messages = call(
        lambda *refs: halo_message_kernel(plan, *refs),
        [shape((2, half + 8, LANES), f32)] * sides
        + [shape((2, half, LANES), f32)] * sides
        + [shape((8, LANES), f32)] * (sides + 1),
        [],
        [spots, counts, ordered, *halos],
        in_specs=[SMEM, SMEM, ANY] + [VMEM] * sides,
    )
    passed, lines, own_spot = messages[sides : 2 * sides], messages[2 * sides : -1], messages[-1]
    near_lines = [plan.near_rows(line) for line in lines]
    far = [far_block] + [plan.far_rows(message) for message in messages[:sides]]
    near = [plan.near_rows(message) for message in passed] + [near_block]
    own = [object_field] + passed
    def runs_layout(refs, main, count, side_starts):
        starts = [main] + side_starts
        own, far, near = refs[: 1 + sides], refs[1 + sides : 2 + 2 * sides], refs[2 + 2 * sides :]
        return lay_out(own, starts), lay_out(far, starts), lay_out(near, side_starts + (chunk_starts(main, count) if len(near) > 1 + sides else [main]))

    def first_layout(refs, t):
        return runs_layout(refs, 1, plan.own, plan.halo_tiles(t))

    def later_layout(refs, t):
        return runs_layout(refs, plan.mid_start(t), plan.mid_tiles, plan.pair_starts(t))

    layout = first_layout

    third = half // 24 * 8
    near_heights = [half - 2 * third, third, third]
    for sweep in range(ITERS):
        pieces = own + far + near
        inner, outer, outer_far = [], [], []
        for slot in range(slots):
            last = slot == slots - 1
            earlier = outer if last else []
            patch = shape((2, half, size), f32)
            halves = 2 if last and sweep == ITERS - 1 else 0
            inner_part, *copies = call(
                lambda *refs, slot=slot, layout=layout, copied=len(earlier), halves=halves: term_kernel(
                    plan, slot, layout, len(pieces), copied, halves, slots, *refs
                ),
                [patch]
                + ([shape((2, half, LANES), f32)] * halves or [patch])
                + [shape((2 * slots, rows, size), f32) for rows in near_heights if last],
                [pltpu.VMEM((3, 3, 2, half, LANES), f32)]
                + [pltpu.VMEM((2, half, size), f32)] * (halves > 0),
                [own_spot, *pieces, *earlier, rolled, ordered, tables],
            )
            outer_part = None if halves else copies.pop(0)
            outer_halves, copies = copies[:halves], copies[halves:]
            inner.append(inner_part)
            outer.append(outer_part)
            outer_far.append([plan.far_rows(part) for part in outer_halves] if halves else plan.far_rows(outer_part))
            if sweep == 0 and last:
                info = call(
                    lambda *refs: info_kernel(plan, *refs),
                    shape((3 * (sides + 1), LANES), jnp.int32),
                    [pltpu.VMEM((3 * (sides + 1), 8, LANES), jnp.int32), dma],
                    lines + far[1:] + near_lines + [outer_part],
                    in_specs=[VMEM] * (3 * sides) + [ANY],
                    out_specs=SMEM,
                )
        outer_near = [plan.near_rows(copy) for copy in copies]
        if sweep == 0:
            inverse = call(
                lambda *refs: light_kernel(plan, slots, *refs),
                shape((half, width), f32),
                [
                    pltpu.VMEM((2 * size + 8, size), f32),
                    pltpu.VMEM((half, width + 2 * plan.own * LANES), f32),
                ],
                [info, probe_field, copies[0]],
                in_specs=[SMEM, VMEM, ANY],
            )
        early = call(
            lambda *refs: early_sum_kernel(plan, slots, *refs),
            shape((2, half, width), f32),
            [],
            [info, *inner, *outer_near],
        )
        early, base, mask = call(
            lambda *refs, layout=layout: base_kernel(plan, slots, layout, len(pieces), *refs),
            [shape((2, half, width), f32)] * 2 + [shape((half, width), f32)],
            [],
            [info, early, inverse, *outer_far[:-1], *pieces],
        )
        if sweep < ITERS - 1:
            sums = call(
                lambda *refs: boundary_kernel(plan, *refs),
                [shape((2, half, 2 * LANES), f32)] * sides,
                [],
                [early, outer_far[-1], mask],
            )
            received = plan.across(sums)
            middle = call(
                lambda *refs: middle_kernel(plan, *refs),
                shape((2, half, plan.mid_tiles * LANES), f32),
                [],
                [base, outer_far[-1], mask, inverse, sums[0]],
                in_specs=[VMEM] * 4 + [ANY],
            )
            far_middle = plan.far_rows(middle)
            near_runs = [shape((2, half, count * LANES), f32) for count in chunks(plan.mid_tiles)]
            updated = call(
                lambda *refs: pair_kernel(plan, *refs),
                [shape((2, half, 2 * LANES), f32)] * (2 * sides) + near_runs,
                [],
                [base, early, inverse, middle, *sums, *received],
            )
            pairs = updated[:sides]
            own = [middle] + pairs
            far = [far_middle] + [plan.far_rows(piece) for piece in pairs]
            near = [plan.near_rows(piece) for piece in updated[sides:]]
            layout = later_layout
    sums = call(
        lambda *refs: halo_sum_kernel(plan, *refs),
        [shape((2, half, LANES), f32)] * sides,
        [],
        [early, mask, *outer_far[-1][:sides]],
    )
    nearly, *bases = call(
        lambda *refs: last_kernel(plan, *refs),
        [shape((2, half, block_cols), f32)] + [shape((2, half, LANES), f32)] * sides,
        [pltpu.VMEM((2, half, block_cols), f32), dma((plan.own,))],
        [base, mask, inverse, sums[0], *outer_far[-1]],
        in_specs=[VMEM] * 3 + [ANY] + [VMEM] * 2,
        out_specs=[HBM] + [VMEM] * sides,
    )
    received = plan.across(sums)
    return call(
        lambda *refs: edge_kernel(plan, *refs),
        shape(nearly.shape, f32),
        [pltpu.VMEM((sides, 2, half, LANES), f32), dma((sides,))],
        [inverse, *bases, *received, nearly],
        in_specs=[VMEM] * (1 + 2 * sides) + [HBM],
        out_specs=HBM,
        input_output_aliases={1 + 2 * sides: 0},
    )


def solution(mesh):
    sizes = dict(mesh.shape)

    def per_device(object_field, *rest):
        plan = Plan(sizes["sx"], sizes["sy"], *object_field.shape[1:])
        return on_device(plan, object_field, *rest)

    return jax.shard_map(
        per_device,
        mesh=mesh,
        in_specs=(
            P(None, "sx", "sy"),
            P(),
            P("sx", "sy", None, None, None),
            P("sx", "sy", None, None),
            P(None, "sy"),
        ),
        out_specs=P(None, "sx", "sy"),
        check_vma=False,
    )
```

```python
import math

import jax
import jax.numpy as jnp
import ml_dtypes
import numpy as np
from jax import lax
from jax.experimental import pallas as pl
from jax.experimental.pallas import tpu as pltpu
from jax.sharding import PartitionSpec as P

ITERS = 2
SMOOTH = 1.0
DAMPING = 1.0
LANES = 128
VMEM_BYTES = 12 * 1024 * 1024

VMEM = pl.BlockSpec(memory_space=pltpu.VMEM)
SMEM = pl.BlockSpec(memory_space=pltpu.SMEM)
HBM = pl.BlockSpec(memory_space=pltpu.HBM)
ANY = pl.BlockSpec(memory_space=pl.ANY)


def split_numpy(table):
    high = table.astype(np.float32).astype(ml_dtypes.bfloat16)
    low = (table - high.astype(np.float64)).astype(ml_dtypes.bfloat16)
    return high, low


def dft_tables(length):
    half = length // 2
    index = np.arange(half)
    tables = []
    for parity in range(2):
        angles = 2.0 * math.pi / length * (index[:, None] * (2 * index[None, :] + parity) % length)
        cosine = np.cos(angles) / math.sqrt(length)
        sine = np.sin(angles) / math.sqrt(length)
        forward = np.block([[cosine, -sine], [sine, cosine]])
        tables.append([split_numpy(forward), split_numpy(forward.T)])
    return np.array(tables, dtype=ml_dtypes.bfloat16)


def parity_order(length):
    half = length // 2
    order = np.zeros((length, length))
    for index in range(length):
        order[index, index % 2 * half + index // 2] = 1.0
    return np.stack([order, order.T]).astype(ml_dtypes.bfloat16)


def split(values):
    high = values.astype(jnp.bfloat16)
    low = (values - high.astype(jnp.float32)).astype(jnp.bfloat16)
    return high, low


def times_table(values, table):
    high, low = split(values)
    left = jnp.concatenate([high, low, high], axis=1)
    right = jnp.concatenate([table[0], table[0], table[1]], axis=0)
    return jnp.dot(left, right, preferred_element_type=jnp.float32)


def table_times(table, values):
    high, low = split(values)
    left = jnp.concatenate([table[0], table[0], table[1]], axis=1)
    right = jnp.concatenate([high, low, high], axis=0)
    return jnp.dot(left, right, preferred_element_type=jnp.float32)


class Plan:
    def __init__(self, sx_size, sy_size, block_rows, block_cols):
        self.rows = block_rows
        self.sx_size = sx_size
        self.sy_size = sy_size
        self.own = block_cols // LANES
        self.tiles = self.own + 2
        self.paired = sy_size == 2
        self.sides = 1 if self.paired else 2

    def rights(self, t):
        return [1 - t] if self.paired else [0, 1]

    def pair_starts(self, t):
        return [right * (self.tiles - 2) for right in self.rights(t)]

    def halo_tiles(self, t):
        return [right * (self.tiles - 1) for right in self.rights(t)]

    def edge_tiles(self, t):
        return [1 + right * (self.tiles - 3) for right in self.rights(t)]

    def first_parity(self, t):
        return 1 - t if self.paired else 0

    def mid_start(self, t):
        return 1 + t if self.paired else 2

    @property
    def mid_tiles(self):
        return self.tiles - 3 if self.paired else self.tiles - 4

    def across(self, values, axis_name="sy"):
        if self.paired:
            return [lax.ppermute(values[0], axis_name, [(0, 1), (1, 0)])]
        ends = self.sy_size - 1
        return [
            lax.ppermute(values[1], axis_name, [(i, i + 1) for i in range(ends)]),
            lax.ppermute(values[0], axis_name, [(i + 1, i) for i in range(ends)]),
        ]

    def far_rows(self, values):
        rows, columns = self.sx_size, self.sy_size
        pairs = [(i * columns + t, (i + 1) * columns + t) for i in range(1, rows - 1, 2) for t in range(columns)]
        for i in (0, rows - 1):
            pairs += [(i * columns + t, i * columns + t + 1) for t in range(0, columns - 1, 2)]
        return lax.ppermute(values, ("sx", "sy"), pairs + [(j, i) for i, j in pairs])

    def near_rows(self, values):
        return lax.ppermute(values, "sx", [(i, i ^ 1) for i in range(self.sx_size)])

    def outermost(self, s):
        return (s == 0) | (s == self.sx_size - 1)


def far_side(s):
    return 2 * (s % 2) - 1


def lanes(tile, count=1):
    if isinstance(tile, int):
        return pl.ds(tile * LANES, count * LANES)
    return pl.ds(pl.multiple_of(tile * LANES, LANES), count * LANES)


def pick_tile(plan, target, pieces, tile, t):
    rows = target.shape[1]
    if plan.paired:

        @pl.when(tile == (plan.tiles - 1) * t)
        def _():
            target[...] = jnp.zeros(target.shape, jnp.float32)

    for ref, offset, count, start in pieces:

        @pl.when((tile >= start) & (tile < start + count))
        def _(ref=ref, offset=offset, start=start):
            target[...] = ref[:, :rows, lanes(tile - start + offset)]


def lay_out(refs, starts):
    return [(ref, 0, ref.shape[2] // LANES, start) for ref, start in zip(refs, starts)]


def chunks(count):
    return [min(2, count - first) for first in range(0, count, 2)]


def chunk_starts(start, count):
    return [start + 2 * index for index in range(len(chunks(count)))]


def spread(source, targets):
    offset = 0
    for target in targets:
        columns = target.shape[2]
        target[...] = source[:, :, offset : offset + columns]
        offset += columns


def rows_at(ref, start, count):
    offset = start % 8
    values = ref[pl.ds(pl.multiple_of(start - offset, 8), count + 8)]
    return pltpu.roll(values, (count + 8 - offset) % (count + 8), 0)[:count]


def here():
    return lax.axis_index("sx"), lax.axis_index("sy")


def info_rows(centres, count):
    lane = lax.broadcasted_iota(jnp.int32, (8, LANES), 1)
    slots = centres.shape[0]
    values = [centres[slot, axis] for slot in range(slots) for axis in range(2)] + [count]
    line = jnp.zeros((8, LANES), jnp.int32)
    for index, value in enumerate(values):
        line = jnp.where(lane == index, value, line)
    return line.astype(jnp.float32)


def edge_message_kernel(plan, block, centres, counts, *rest):
    messages, sems = rest[: plan.sides], rest[plan.sides]
    s, t = here()
    half = block.shape[1]
    copies = [
        pltpu.make_async_copy(block.at[:, :, lanes(tile - 1)], message.at[:, :half], sems.at[side])
        for side, (message, tile) in enumerate(zip(messages, plan.edge_tiles(t)))
    ]
    for copy in copies:
        copy.start()
    rows = info_rows(centres, counts[s])
    for message in messages:
        message[0, half:] = rows
        message[1, half:] = rows
    for copy in copies:
        copy.wait()


def halo_message_kernel(plan, centres, counts, _, *rest):
    sides = plan.sides
    received, far, halos, infos = (rest[k * sides : (k + 1) * sides] for k in range(4))
    own = info_rows(centres, counts[lax.axis_index("sx")])
    rest[-1][...] = own
    upper_line = lax.broadcasted_iota(jnp.int32, own.shape, 0) == 0
    for source, message, halo, info in zip(received, far, halos, infos):
        rows = halo.shape[1]
        both = jnp.where(upper_line, own, pltpu.roll(source[0, rows : rows + 8], 1, 0))
        halo[...] = source[:, :rows]
        info[...] = both
        message[:, :rows] = source[:, :rows]
        message[0, rows:] = both
        message[1, rows:] = both


def pair_kernel(plan, base, early, inverse, middle, *rest):
    sides = plan.sides
    sums, received, results = (rest[k * sides : (k + 1) * sides] for k in range(3))
    near = rest[3 * sides :]
    _, t = here()
    for total, other, result, copy, start in zip(sums, received, results, near, plan.pair_starts(t)):
        where = lanes(start, 2)
        missing = total[...] + (other[1 - t] if plan.paired else other[...]) - early[:, :, where]
        values = base[:, :, where] - missing * inverse[:, where][None]
        result[...] = values
        copy[...] = values
    spread(middle, near[sides:])


def prepare_kernel(centres, probe, amps, order, rolled, ordered, padded):
    size = probe.shape[1]
    half = size // 2
    padded[:, :half] = jnp.zeros((2, half, size), jnp.float32)
    padded[:, half + size :] = jnp.zeros((2, half + 8, size), jnp.float32)
    padded[:, half : half + size] = probe[...]
    for slot in range(amps.shape[0]):
        row = centres[slot, 0]
        col = centres[slot, 1]
        for part in range(2):
            shape = padded.at[part]
            upper = rows_at(shape, half - row, half) + rows_at(shape, half + size - row, half)
            lower = rows_at(shape, size - row, half)
            rolled[slot, part] = pltpu.roll(jnp.concatenate([upper, lower], axis=0), col % LANES, 1)
        high, low = split(amps[slot])
        across = jnp.dot(
            jnp.concatenate([high, low], axis=1),
            jnp.concatenate([order[0], order[0]], axis=0),
            preferred_element_type=jnp.float32,
        )
        high, low = split(across)
        ordered[slot] = jnp.dot(
            jnp.concatenate([order[1], order[1]], axis=1),
            jnp.concatenate([high, low], axis=0),
            preferred_element_type=jnp.float32,
        )


def info_kernel(plan, *rest):
    home, far, other = (rest[k * plan.sides : (k + 1) * plan.sides] for k in range(3))
    _, info, known, sem = rest[3 * plan.sides :]
    s, _ = here()
    upper = s % 2 == 0
    width = plan.sides + 1

    def lines(messages):
        return [messages[0]] + [pltpu.roll(message, 7, 0) for message in messages]

    own = lines([line[...] for line in home])
    near = lines([line[...] for line in other])
    far = lines([jnp.where(plan.outermost(s), 0.0, message[0, plan.rows :]) for message in far])
    for turn in range(width):
        for kind, line in ((0, jnp.where(upper, far[turn], near[turn])), (1, own[turn]), (2, jnp.where(upper, near[turn], far[turn]))):
            known[kind * width + turn] = line.astype(jnp.int32)
    copy = pltpu.make_async_copy(known.at[:, 0], info, sem)
    copy.start()
    copy.wait()


def light_kernel(plan, slots, info, probe, _, inverse, padded, canvas):
    size = probe.shape[1]
    half = size // 2
    _, t = here()
    padded[:half] = jnp.zeros((half, size), jnp.float32)
    padded[half + size :] = jnp.zeros((half + 8, size), jnp.float32)
    padded[half : half + size] = probe[0] * probe[0] + probe[1] * probe[1]
    canvas[...] = jnp.zeros(canvas.shape, jnp.float32)
    reach = plan.sides + 1
    spare = jnp.zeros((half, LANES), jnp.float32)
    for down in (-1, 0, 1):

        def add(step, carry, down=down):
            turn = step // slots
            slot = step % slots
            over = turn * (1 - 2 * t) if plan.paired else jnp.where(turn == 0, 0, 2 * turn - 3)
            index = (down + 1) * reach + turn

            @pl.when(slot < info[index, 2 * slots])
            def _():
                row = info[index, 2 * slot]
                col = info[index, 2 * slot + 1]
                power = rows_at(padded, size - half * down - row, half)
                shifted = pltpu.roll(jnp.concatenate([power, spare], axis=1), col % LANES, 1)
                first = col // LANES + plan.own * (over + 1)
                canvas[:, lanes(first, 3)] += shifted

            return carry

        lax.fori_loop(0, reach * slots, add, 0)
    inverse[...] = 1.0 / (canvas[:, lanes(plan.own, plan.tiles)] + DAMPING)


def term_kernel(plan, slot, layout, pieces, copied, halves, slots, spot, *rest):
    refs, rest = rest[:pieces], rest[pieces:]
    earlier, (probe, amps, tables, inner), rest = rest[:copied], rest[copied : copied + 4], rest[copied + 4 :]
    if halves:
        outer, rest = rest[-1], rest[:-1]
    else:
        outer, rest = rest[0], rest[1:]
    outer_halves, near_outers, picked = rest[:halves], rest[halves:-1], rest[-1]
    size = probe.shape[2]
    half = size // 2
    s, t = here()
    line = spot[0:1]
    lane = lax.broadcasted_iota(jnp.int32, line.shape, 1)
    entries = (2 * slot, 2 * slot + 1, 2 * slots)
    row, col, count = (jnp.sum(jnp.where(lane == k, line, 0.0)).astype(jnp.int32) for k in entries)
    alive = slot < count

    @pl.when(jnp.logical_not(alive))
    def _():
        outer[...] = jnp.zeros(outer.shape, jnp.float32)
        inner[...] = jnp.zeros(inner.shape, jnp.float32)

    @pl.when(alive)
    def _():
        tile = col // LANES
        first = tile % 2
        rest_col = col % LANES
        from_tile = lax.broadcasted_iota(jnp.int32, (half, LANES), 1) >= rest_col
        from_upper = lax.broadcasted_iota(jnp.int32, (half, LANES), 0) >= row
        side = far_side(s)
        own, far, near = layout(refs, t)
        for kind, source in ((1, own), (1 + side, far), (1 - side, near)):
            for step in range(3):
                pick_tile(plan, picked.at[kind, step], source, tile + step, t)

        @pl.when(plan.outermost(s))
        def _():
            picked[1 + side] = jnp.zeros(picked.shape[1:], jnp.float32)

        def edge(kind, part):
            return jnp.where(from_tile, picked[kind, 0, part], picked[kind, 2, part])

        def across(edges, middles, rows):
            sums, differences = [], []
            shares = []
            for columns, (real, imag) in ((slice(0, half), edges), (slice(half, size), middles)):
                probe_real, probe_imag = probe[slot, 0, rows, columns], probe[slot, 1, rows, columns]
                shares.append((probe_real * real - probe_imag * imag, probe_real * imag + probe_imag * real))
            for part in range(2):
                sums.append(shares[0][part] + shares[1][part])
                differences.append(shares[0][part] - shares[1][part])
            return [
                times_table(jnp.concatenate(parts, axis=1), tables[parity, 0])
                for parity, parts in enumerate((sums, differences))
            ]

        lower = across(
            [edge(1, part) for part in range(2)], [picked[1, 1, part] for part in range(2)], slice(half, size)
        )
        upper = across(
            [jnp.where(from_upper, edge(0, part), edge(2, part)) for part in range(2)],
            [jnp.where(from_upper, picked[0, 1, part], picked[2, 1, part]) for part in range(2)],
            slice(0, half),
        )
        halves = []
        for sign in (1.0, -1.0):
            rows = [top + sign * bottom for top, bottom in zip(upper, lower)]
            halves.append(
                jnp.concatenate(
                    [jnp.concatenate([row[:, part] for row in rows], axis=1) for part in (slice(0, half), slice(half, size))],
                    axis=0,
                )
            )
        back = []
        for parity in range(2):
            pattern = table_times(tables[parity, 1], halves[parity])
            far_real = pattern[:half]
            far_imag = pattern[half:]
            amplitude = amps[slot, parity * half : (parity + 1) * half]
            factor = 1.0 - amplitude * lax.rsqrt(far_real * far_real + far_imag * far_imag + SMOOTH)
            miss = jnp.concatenate([far_real * factor, far_imag * factor], axis=0)
            back.append(table_times(tables[parity, 0], miss))
        real = jnp.concatenate([back[0][:half] + back[1][:half], back[0][:half] - back[1][:half]], axis=0)
        imag = jnp.concatenate([back[0][half:] + back[1][half:], back[0][half:] - back[1][half:]], axis=0)
        both = []
        for parity in range(2):
            columns = slice(parity * half, (parity + 1) * half)
            both.append(times_table(jnp.concatenate([real[:, columns], imag[:, columns]], axis=1), tables[parity, 1]))
        near_real = jnp.concatenate([both[0][:, :half] + both[1][:, :half], both[0][:, :half] - both[1][:, :half]], axis=1)
        near_imag = jnp.concatenate([both[0][:, half:] + both[1][:, half:], both[0][:, half:] - both[1][:, half:]], axis=1)
        probe_real = probe[slot, 0]
        probe_imag = probe[slot, 1]
        for part, term in enumerate((probe_real * near_real + probe_imag * near_imag, probe_real * near_imag - probe_imag * near_real)):
            for place, columns in ((first, slice(0, half)), (1 - first, slice(half, size))):
                outer[part, :, lanes(place)] = term[:half, columns]
                inner[part, :, lanes(place)] = term[half:, columns]

    for index, target in enumerate(outer_halves):
        first = plan.first_parity(t)
        target[...] = outer[:, :, lanes(first if index == 0 else 1 - first)]
    for index, source in enumerate((*earlier, outer)):
        line = 0
        for target in near_outers:
            rows = target.shape[1]
            target[2 * index : 2 * index + 2] = source[:, line : line + rows]
            line += rows


class Patch:
    def __init__(self, plan, info, s, patch, slot, down, far=False):
        runs = patch if isinstance(patch, (list, tuple)) else [patch]
        half = sum(run.shape[1] for run in runs)
        index = (1 if down is None else 1 + down) * (plan.sides + 1)
        row = info[index, 2 * slot]
        col = info[index, 2 * slot + 1]
        self.runs = runs
        self.tile = col // LANES
        self.first = self.tile % 2
        self.rest = col % LANES
        self.lane = lax.broadcasted_iota(jnp.int32, (half, LANES), 1)
        self.from_tile = self.lane >= self.rest
        self.rows = None
        if down is not None:
            line = lax.broadcasted_iota(jnp.int32, (half, LANES), 0)
            after = jnp.where(down > 0, half, row)
            if far:
                after = jnp.where(plan.outermost(s), 0, after)
            self.rows = (line >= jnp.where(down > 0, row, 0)) & (line < after)

    def lines(self, part, place):
        values = jnp.concatenate([run[part, :, lanes(place)] for run in self.runs], axis=0)
        return values if self.rows is None else jnp.where(self.rows, values, 0.0)

    def tiles(self, part):
        edge = self.lines(part, self.first)
        middle = self.lines(part, 1 - self.first)
        return jnp.where(self.from_tile, edge, 0.0), middle, jnp.where(self.from_tile, 0.0, edge)

    def add_to(self, canvas):
        for part in range(2):
            for step, values in enumerate(self.tiles(part)):
                canvas[part, :, lanes(self.tile + step)] += values

    def mask(self, tile):
        step = tile - self.tile
        first = jnp.where(step == 0, self.rest, 0)
        after = jnp.where(step == 2, self.rest, jnp.where((step < 0) | (step > 2), 0, LANES))
        inside = (self.lane >= first) & (self.lane < after)
        if self.rows is not None:
            inside = inside & self.rows
        return jnp.where(inside, 1.0, 0.0)


def part_of(plan, patch, mask, part, tile):
    if isinstance(patch, (list, tuple)):
        first = plan.first_parity(lax.axis_index("sy"))
        values = jnp.where(tile % 2 == first, patch[0][part], patch[1][part])
    else:
        values = patch[part, :, lanes(tile % 2)]
    return values * mask[:, lanes(tile)]


def early_sum_kernel(plan, slots, info, *rest):
    inner, near, canvas = rest[:slots], rest[slots:-1], rest[-1]
    s, _ = here()
    canvas[...] = jnp.zeros(canvas.shape, jnp.float32)
    for slot in range(slots):
        Patch(plan, info, s, inner[slot], slot, None).add_to(canvas)
        runs = [run.at[2 * slot : 2 * slot + 2] for run in near]
        Patch(plan, info, s, runs, slot, -far_side(s)).add_to(canvas)


def base_kernel(plan, slots, layout, pieces, info, early, inverse, *rest):
    far, refs, (canvas, base, mask) = rest[: slots - 1], rest[slots - 1 : slots - 1 + pieces], rest[slots - 1 + pieces :]
    s, t = here()
    canvas[...] = early[...]
    for slot in range(slots - 1):
        Patch(plan, info, s, far[slot], slot, far_side(s), True).add_to(canvas)
    last = Patch(plan, info, s, canvas, slots - 1, far_side(s), True)
    for tile in range(plan.tiles):
        where = lanes(tile)
        pick_tile(plan, base.at[:, :, where], layout(refs, t)[0], tile, t)
        base[:, :, where] -= canvas[:, :, where] * inverse[:, where][None]
        mask[:, where] = last.mask(tile)


def take_off(plan, patch, mask, target, base, inverse, tile):
    for part in range(2):
        target[part] = base[part, :, lanes(tile)] - part_of(plan, patch, mask, part, tile) * inverse[:, lanes(tile)]


def middle_kernel(plan, base, patch, mask, inverse, _, middle):
    _, t = here()
    for step in range(plan.mid_tiles):
        take_off(plan, patch, mask, middle.at[:, :, lanes(step)], base, inverse, plan.mid_start(t) + step)


def boundary_kernel(plan, early, patch, mask, *sums):
    _, t = here()
    for total, start in zip(sums, plan.pair_starts(t)):
        for step in range(2):
            tile = start + step
            for part in range(2):
                total[part, :, lanes(step)] = early[part, :, lanes(tile)] + part_of(plan, patch, mask, part, tile)


def halo_sum_kernel(plan, early, mask, *rest):
    halves, sums = rest[: plan.sides], rest[plan.sides :]
    _, t = here()
    for half, total, tile in zip(halves, sums, plan.halo_tiles(t)):
        for part in range(2):
            total[part] = early[part, :, lanes(tile)] + half[part] * mask[:, lanes(tile)]


def last_kernel(plan, base, mask, inverse, _, first, second, *rest):
    nearly, bases, (current, sems) = rest[0], rest[1 : 1 + plan.sides], rest[1 + plan.sides :]
    patch = [first, second]
    _, t = here()
    copies = []
    for step in range(plan.own):
        where = lanes(step)
        take_off(plan, patch, mask, current.at[:, :, where], base, inverse, 1 + step)
        copies.append(pltpu.make_async_copy(current.at[:, :, where], nearly.at[:, :, where], sems.at[step]))
        copies[-1].start()
    for edge, tile in zip(bases, plan.edge_tiles(t)):
        edge[...] = current[:, :, lanes(tile - 1)]
    for copy in copies:
        copy.wait()


def edge_kernel(plan, inverse, *rest):
    bases, received = rest[: plan.sides], rest[plan.sides : 2 * plan.sides]
    _, result, sums, sems = rest[2 * plan.sides :]
    _, t = here()
    copies = []
    for side, tile in enumerate(plan.edge_tiles(t)):
        sums[side] = bases[side][...] - received[side][...] * inverse[:, lanes(tile)][None]
        copies.append(pltpu.make_async_copy(sums.at[side], result.at[:, :, lanes(tile - 1)], sems.at[side]))
        copies[-1].start()
    for copy in copies:
        copy.wait()


def call(kernel, outs, scratch, ins, flops=10**5, size=10**4, in_specs=None, out_specs=None, **options):
    result = pl.pallas_call(
        kernel,
        out_shape=outs,
        in_specs=in_specs or [SMEM if value.dtype == jnp.int32 else VMEM for value in ins],
        out_specs=out_specs or jax.tree.map(lambda _: VMEM, outs),
        scratch_shapes=scratch,
        compiler_params=pltpu.CompilerParams(vmem_limit_bytes=VMEM_BYTES),
        cost_estimate=pl.CostEstimate(flops=flops, bytes_accessed=size, transcendentals=0),
        **options,
    )(*ins)
    return list(result) if isinstance(outs, list) else result


def on_device(plan, object_field, probe_field, amplitudes, centres, counts):
    f32 = jnp.float32
    shape = jax.ShapeDtypeStruct
    size = probe_field.shape[1]
    half = size // 2
    slots = amplitudes.shape[2]
    block_rows = object_field.shape[1]
    block_cols = object_field.shape[2]
    assert block_rows == half and block_cols % (2 * LANES) == 0 and half == LANES
    width = plan.tiles * LANES
    sides = plan.sides
    spots = centres[0, 0]
    counts = counts.reshape(-1)
    own_amps = amplitudes[0, 0]
    tables = jnp.asarray(dft_tables(size))
    order = jnp.asarray(parity_order(size))
    dma = pltpu.SemaphoreType.DMA

    messages = call(
        lambda *refs: edge_message_kernel(plan, *refs),
        [shape((2, half + 8, LANES), f32)] * sides,
        [dma((sides,))],
        [object_field, spots, counts],
        in_specs=[HBM, SMEM, SMEM],
    )
    halos = plan.across(messages)
    far_block = plan.far_rows(object_field)
    near_block = plan.near_rows(object_field)
    rolled, ordered = call(
        prepare_kernel,
        [shape((slots, 2, size, size), f32), shape((slots, size, size), f32)],
        [pltpu.VMEM((2, 2 * size + 8, size), f32)],
        [spots, probe_field, own_amps, order],
    )
    messages = call(
        lambda *refs: halo_message_kernel(plan, *refs),
        [shape((2, half + 8, LANES), f32)] * sides
        + [shape((2, half, LANES), f32)] * sides
        + [shape((8, LANES), f32)] * (sides + 1),
        [],
        [spots, counts, ordered, *halos],
        in_specs=[SMEM, SMEM, ANY] + [VMEM] * sides,
    )
    passed, lines, own_spot = messages[sides : 2 * sides], messages[2 * sides : -1], messages[-1]
    near_lines = [plan.near_rows(line) for line in lines]
    far = [far_block] + [plan.far_rows(message) for message in messages[:sides]]
    near = [plan.near_rows(message) for message in passed] + [near_block]
    own = [object_field] + passed
    def runs_layout(refs, main, count, side_starts):
        starts = [main] + side_starts
        own, far, near = refs[: 1 + sides], refs[1 + sides : 2 + 2 * sides], refs[2 + 2 * sides :]
        return lay_out(own, starts), lay_out(far, starts), lay_out(near, side_starts + (chunk_starts(main, count) if len(near) > 1 + sides else [main]))

    def first_layout(refs, t):
        return runs_layout(refs, 1, plan.own, plan.halo_tiles(t))

    def later_layout(refs, t):
        return runs_layout(refs, plan.mid_start(t), plan.mid_tiles, plan.pair_starts(t))

    layout = first_layout

    third = half // 24 * 8
    near_heights = [half - 2 * third, third, third]
    for sweep in range(ITERS):
        pieces = own + far + near
        inner, outer, outer_far = [], [], []
        for slot in range(slots):
            last = slot == slots - 1
            earlier = outer if last else []
            patch = shape((2, half, size), f32)
            halves = 2 if last and sweep == ITERS - 1 else 0
            inner_part, *copies = call(
                lambda *refs, slot=slot, layout=layout, copied=len(earlier), halves=halves: term_kernel(
                    plan, slot, layout, len(pieces), copied, halves, slots, *refs
                ),
                [patch]
                + ([shape((2, half, LANES), f32)] * halves or [patch])
                + [shape((2 * slots, rows, size), f32) for rows in near_heights if last],
                [pltpu.VMEM((3, 3, 2, half, LANES), f32)]
                + [pltpu.VMEM((2, half, size), f32)] * (halves > 0),
                [own_spot, *pieces, *earlier, rolled, ordered, tables],
            )
            outer_part = None if halves else copies.pop(0)
            outer_halves, copies = copies[:halves], copies[halves:]
            inner.append(inner_part)
            outer.append(outer_part)
            outer_far.append([plan.far_rows(part) for part in outer_halves] if halves else plan.far_rows(outer_part))
            if sweep == 0 and last:
                info = call(
                    lambda *refs: info_kernel(plan, *refs),
                    shape((3 * (sides + 1), LANES), jnp.int32),
                    [pltpu.VMEM((3 * (sides + 1), 8, LANES), jnp.int32), dma],
                    lines + far[1:] + near_lines + [outer_part],
                    in_specs=[VMEM] * (3 * sides) + [ANY],
                    out_specs=SMEM,
                )
        outer_near = [plan.near_rows(copy) for copy in copies]
        if sweep == 0:
            inverse = call(
                lambda *refs: light_kernel(plan, slots, *refs),
                shape((half, width), f32),
                [
                    pltpu.VMEM((2 * size + 8, size), f32),
                    pltpu.VMEM((half, width + 2 * plan.own * LANES), f32),
                ],
                [info, probe_field, copies[0]],
                in_specs=[SMEM, VMEM, ANY],
            )
        early = call(
            lambda *refs: early_sum_kernel(plan, slots, *refs),
            shape((2, half, width), f32),
            [],
            [info, *inner, *outer_near],
        )
        early, base, mask = call(
            lambda *refs, layout=layout: base_kernel(plan, slots, layout, len(pieces), *refs),
            [shape((2, half, width), f32)] * 2 + [shape((half, width), f32)],
            [],
            [info, early, inverse, *outer_far[:-1], *pieces],
        )
        if sweep < ITERS - 1:
            sums = call(
                lambda *refs: boundary_kernel(plan, *refs),
                [shape((2, half, 2 * LANES), f32)] * sides,
                [],
                [early, outer_far[-1], mask],
            )
            if plan.paired:
                received = [lax.all_gather(sums[0], "sy")]
            else:
                received = plan.across(sums)
            middle = call(
                lambda *refs: middle_kernel(plan, *refs),
                shape((2, half, plan.mid_tiles * LANES), f32),
                [],
                [base, outer_far[-1], mask, inverse, sums[0]],
                in_specs=[VMEM] * 4 + [ANY],
            )
            far_middle = plan.far_rows(middle)
            near_runs = [shape((2, half, count * LANES), f32) for count in chunks(plan.mid_tiles)]
            updated = call(
                lambda *refs: pair_kernel(plan, *refs),
                [shape((2, half, 2 * LANES), f32)] * (2 * sides) + near_runs,
                [],
                [base, early, inverse, middle, *sums, *received],
            )
            pairs = updated[:sides]
            own = [middle] + pairs
            far = [far_middle] + [plan.far_rows(piece) for piece in pairs]
            near = [plan.near_rows(piece) for piece in updated[sides:]]
            layout = later_layout
    sums = call(
        lambda *refs: halo_sum_kernel(plan, *refs),
        [shape((2, half, LANES), f32)] * sides,
        [],
        [early, mask, *outer_far[-1][:sides]],
    )
    nearly, *bases = call(
        lambda *refs: last_kernel(plan, *refs),
        [shape((2, half, block_cols), f32)] + [shape((2, half, LANES), f32)] * sides,
        [pltpu.VMEM((2, half, block_cols), f32), dma((plan.own,))],
        [base, mask, inverse, sums[0], *outer_far[-1]],
        in_specs=[VMEM] * 3 + [ANY] + [VMEM] * 2,
        out_specs=[HBM] + [VMEM] * sides,
    )
    received = plan.across(sums)
    return call(
        lambda *refs: edge_kernel(plan, *refs),
        shape(nearly.shape, f32),
        [pltpu.VMEM((sides, 2, half, LANES), f32), dma((sides,))],
        [inverse, *bases, *received, nearly],
        in_specs=[VMEM] * (1 + 2 * sides) + [HBM],
        out_specs=HBM,
        input_output_aliases={1 + 2 * sides: 0},
    )


def solution(mesh):
    sizes = dict(mesh.shape)

    def per_device(object_field, *rest):
        plan = Plan(sizes["sx"], sizes["sy"], *object_field.shape[1:])
        return on_device(plan, object_field, *rest)

    return jax.shard_map(
        per_device,
        mesh=mesh,
        in_specs=(
            P(None, "sx", "sy"),
            P(),
            P("sx", "sy", None, None, None),
            P("sx", "sy", None, None),
            P(None, "sy"),
        ),
        out_specs=P(None, "sx", "sy"),
        check_vma=False,
    )
```

```python
import math

import jax
import jax.numpy as jnp
import ml_dtypes
import numpy as np
from jax import lax
from jax.experimental import pallas as pl
from jax.experimental.pallas import tpu as pltpu
from jax.sharding import PartitionSpec as P

ITERS = 2
SMOOTH = 1.0
DAMPING = 1.0
LANES = 128
VMEM_BYTES = 12 * 1024 * 1024

VMEM = pl.BlockSpec(memory_space=pltpu.VMEM)
SMEM = pl.BlockSpec(memory_space=pltpu.SMEM)
HBM = pl.BlockSpec(memory_space=pltpu.HBM)
ANY = pl.BlockSpec(memory_space=pl.ANY)


def split_numpy(table):
    high = table.astype(np.float32).astype(ml_dtypes.bfloat16)
    low = (table - high.astype(np.float64)).astype(ml_dtypes.bfloat16)
    return high, low


def dft_tables(length):
    half = length // 2
    index = np.arange(half)
    tables = []
    for parity in range(2):
        angles = 2.0 * math.pi / length * (index[:, None] * (2 * index[None, :] + parity) % length)
        cosine = np.cos(angles) / math.sqrt(length)
        sine = np.sin(angles) / math.sqrt(length)
        forward = np.block([[cosine, -sine], [sine, cosine]])
        tables.append([split_numpy(forward), split_numpy(forward.T)])
    return np.array(tables, dtype=ml_dtypes.bfloat16)


def parity_order(length):
    half = length // 2
    order = np.zeros((length, length))
    for index in range(length):
        order[index, index % 2 * half + index // 2] = 1.0
    return np.stack([order, order.T]).astype(ml_dtypes.bfloat16)


def split(values):
    high = values.astype(jnp.bfloat16)
    low = (values - high.astype(jnp.float32)).astype(jnp.bfloat16)
    return high, low


def times_table(values, table):
    high, low = split(values)
    left = jnp.concatenate([high, low, high], axis=1)
    right = jnp.concatenate([table[0], table[0], table[1]], axis=0)
    return jnp.dot(left, right, preferred_element_type=jnp.float32)


def table_times(table, values):
    high, low = split(values)
    left = jnp.concatenate([table[0], table[0], table[1]], axis=1)
    right = jnp.concatenate([high, low, high], axis=0)
    return jnp.dot(left, right, preferred_element_type=jnp.float32)


class Plan:
    def __init__(self, sx_size, sy_size, block_rows, block_cols):
        self.rows = block_rows
        self.sx_size = sx_size
        self.sy_size = sy_size
        self.own = block_cols // LANES
        self.tiles = self.own + 2
        self.paired = sy_size == 2
        self.sides = 1 if self.paired else 2

    def rights(self, t):
        return [1 - t] if self.paired else [0, 1]

    def pair_starts(self, t):
        return [right * (self.tiles - 2) for right in self.rights(t)]

    def halo_tiles(self, t):
        return [right * (self.tiles - 1) for right in self.rights(t)]

    def edge_tiles(self, t):
        return [1 + right * (self.tiles - 3) for right in self.rights(t)]

    def first_parity(self, t):
        return 1 - t if self.paired else 0

    def mid_start(self, t):
        return 1 + t if self.paired else 2

    @property
    def mid_tiles(self):
        return self.tiles - 3 if self.paired else self.tiles - 4

    def across(self, values, axis_name="sy"):
        if self.paired:
            return [lax.ppermute(values[0], axis_name, [(0, 1), (1, 0)])]
        ends = self.sy_size - 1
        return [
            lax.ppermute(values[1], axis_name, [(i, i + 1) for i in range(ends)]),
            lax.ppermute(values[0], axis_name, [(i + 1, i) for i in range(ends)]),
        ]

    def far_rows(self, values):
        rows, columns = self.sx_size, self.sy_size
        pairs = [(i * columns + t, (i + 1) * columns + t) for i in range(1, rows - 1, 2) for t in range(columns)]
        for i in (0, rows - 1):
            pairs += [(i * columns + t, i * columns + t + 1) for t in range(0, columns - 1, 2)]
        return lax.ppermute(values, ("sx", "sy"), pairs + [(j, i) for i, j in pairs])

    def near_rows(self, values):
        return lax.ppermute(values, "sx", [(i, i ^ 1) for i in range(self.sx_size)])

    def outermost(self, s):
        return (s == 0) | (s == self.sx_size - 1)


def far_side(s):
    return 2 * (s % 2) - 1


def lanes(tile, count=1):
    if isinstance(tile, int):
        return pl.ds(tile * LANES, count * LANES)
    return pl.ds(pl.multiple_of(tile * LANES, LANES), count * LANES)


def pick_tile(plan, target, pieces, tile, t):
    rows = target.shape[1]
    if plan.paired:

        @pl.when(tile == (plan.tiles - 1) * t)
        def _():
            target[...] = jnp.zeros(target.shape, jnp.float32)

    for runs, offset, count, start in pieces:

        @pl.when((tile >= start) & (tile < start + count))
        def _(runs=runs, offset=offset, start=start):
            line = 0
            for run in runs:
                height = min(run.shape[1], rows - line)
                target[:, line : line + height] = run[:, :height, lanes(tile - start + offset)]
                line += height


def lay_out(refs, starts):
    return [([ref], 0, ref.shape[2] // LANES, start) for ref, start in zip(refs, starts)]


def lay_out_rows(runs, counts, starts):
    return [(runs, sum(counts[:k]), count, start) for k, (count, start) in enumerate(zip(counts, starts))]


def rows_at(ref, start, count):
    offset = start % 8
    values = ref[pl.ds(pl.multiple_of(start - offset, 8), count + 8)]
    return pltpu.roll(values, (count + 8 - offset) % (count + 8), 0)[:count]


def here():
    return lax.axis_index("sx"), lax.axis_index("sy")


def info_rows(centres, count):
    lane = lax.broadcasted_iota(jnp.int32, (8, LANES), 1)
    slots = centres.shape[0]
    values = [centres[slot, axis] for slot in range(slots) for axis in range(2)] + [count]
    line = jnp.zeros((8, LANES), jnp.int32)
    for index, value in enumerate(values):
        line = jnp.where(lane == index, value, line)
    return line.astype(jnp.float32)


def edge_message_kernel(plan, block, centres, counts, *rest):
    messages, sems = rest[: plan.sides], rest[plan.sides]
    s, t = here()
    half = block.shape[1]
    copies = [
        pltpu.make_async_copy(block.at[:, :, lanes(tile - 1)], message.at[:, :half], sems.at[side])
        for side, (message, tile) in enumerate(zip(messages, plan.edge_tiles(t)))
    ]
    for copy in copies:
        copy.start()
    rows = info_rows(centres, counts[s])
    for message in messages:
        message[0, half:] = rows
        message[1, half:] = rows
    for copy in copies:
        copy.wait()


def halo_message_kernel(plan, centres, counts, _, *rest):
    sides = plan.sides
    received, far, halos, infos = (rest[k * sides : (k + 1) * sides] for k in range(4))
    own = info_rows(centres, counts[lax.axis_index("sx")])
    rest[-1][...] = own
    upper_line = lax.broadcasted_iota(jnp.int32, own.shape, 0) == 0
    for source, message, halo, info in zip(received, far, halos, infos):
        rows = halo.shape[1]
        both = jnp.where(upper_line, own, pltpu.roll(source[0, rows : rows + 8], 1, 0))
        halo[...] = source[:, :rows]
        info[...] = both
        message[:, :rows] = source[:, :rows]
        message[0, rows:] = both
        message[1, rows:] = both


def pair_kernel(plan, base, early, inverse, middle, *rest):
    sides = plan.sides
    sums, received, results = (rest[k * sides : (k + 1) * sides] for k in range(3))
    near = rest[3 * sides :]
    _, t = here()

    def copy(values, offset):
        line = 0
        for run in near:
            rows = run.shape[1]
            run[:, :, offset : offset + values.shape[2]] = values[:, line : line + rows]
            line += rows

    for side, (total, other, result, start) in enumerate(zip(sums, received, results, plan.pair_starts(t))):
        where = lanes(start, 2)
        missing = total[...] + other[...] - early[:, :, where]
        result[...] = base[:, :, where] - missing * inverse[:, where][None]
        copy(result, 2 * LANES * side)
    copy(middle, 2 * LANES * sides)


def prepare_kernel(centres, probe, amps, order, rolled, ordered, padded):
    size = probe.shape[1]
    half = size // 2
    padded[:, :half] = jnp.zeros((2, half, size), jnp.float32)
    padded[:, half + size :] = jnp.zeros((2, half + 8, size), jnp.float32)
    padded[:, half : half + size] = probe[...]
    for slot in range(amps.shape[0]):
        row = centres[slot, 0]
        col = centres[slot, 1]
        for part in range(2):
            shape = padded.at[part]
            upper = rows_at(shape, half - row, half) + rows_at(shape, half + size - row, half)
            lower = rows_at(shape, size - row, half)
            rolled[slot, part] = pltpu.roll(jnp.concatenate([upper, lower], axis=0), col % LANES, 1)
        high, low = split(amps[slot])
        across = jnp.dot(
            jnp.concatenate([high, low], axis=1),
            jnp.concatenate([order[0], order[0]], axis=0),
            preferred_element_type=jnp.float32,
        )
        high, low = split(across)
        ordered[slot] = jnp.dot(
            jnp.concatenate([order[1], order[1]], axis=1),
            jnp.concatenate([high, low], axis=0),
            preferred_element_type=jnp.float32,
        )


def info_kernel(plan, *rest):
    home, far, other = (rest[k * plan.sides : (k + 1) * plan.sides] for k in range(3))
    _, info, known, sem = rest[3 * plan.sides :]
    s, _ = here()
    upper = s % 2 == 0
    width = plan.sides + 1

    def lines(messages):
        return [messages[0]] + [pltpu.roll(message, 7, 0) for message in messages]

    own = lines([line[...] for line in home])
    near = lines([line[...] for line in other])
    far = lines([jnp.where(plan.outermost(s), 0.0, message[0, plan.rows :]) for message in far])
    for turn in range(width):
        for kind, line in ((0, jnp.where(upper, far[turn], near[turn])), (1, own[turn]), (2, jnp.where(upper, near[turn], far[turn]))):
            known[kind * width + turn] = line.astype(jnp.int32)
    copy = pltpu.make_async_copy(known.at[:, 0], info, sem)
    copy.start()
    copy.wait()


def light_kernel(plan, slots, info, probe, _, inverse, padded, canvas):
    size = probe.shape[1]
    half = size // 2
    _, t = here()
    padded[:half] = jnp.zeros((half, size), jnp.float32)
    padded[half + size :] = jnp.zeros((half + 8, size), jnp.float32)
    padded[half : half + size] = probe[0] * probe[0] + probe[1] * probe[1]
    canvas[...] = jnp.zeros(canvas.shape, jnp.float32)
    reach = plan.sides + 1
    spare = jnp.zeros((half, LANES), jnp.float32)
    for down in (-1, 0, 1):

        def add(step, carry, down=down):
            turn = step // slots
            slot = step % slots
            over = turn * (1 - 2 * t) if plan.paired else jnp.where(turn == 0, 0, 2 * turn - 3)
            index = (down + 1) * reach + turn

            @pl.when(slot < info[index, 2 * slots])
            def _():
                row = info[index, 2 * slot]
                col = info[index, 2 * slot + 1]
                power = rows_at(padded, size - half * down - row, half)
                shifted = pltpu.roll(jnp.concatenate([power, spare], axis=1), col % LANES, 1)
                first = col // LANES + plan.own * (over + 1)
                canvas[:, lanes(first, 3)] += shifted

            return carry

        lax.fori_loop(0, reach * slots, add, 0)
    inverse[...] = 1.0 / (canvas[:, lanes(plan.own, plan.tiles)] + DAMPING)


def term_kernel(plan, slot, layout, pieces, copied, halves, slots, spot, *rest):
    refs, rest = rest[:pieces], rest[pieces:]
    earlier, (probe, amps, tables, inner), rest = rest[:copied], rest[copied : copied + 4], rest[copied + 4 :]
    if halves:
        outer, rest = rest[-1], rest[:-1]
    else:
        outer, rest = rest[0], rest[1:]
    outer_halves, near_outers, picked = rest[:halves], rest[halves:-1], rest[-1]
    size = probe.shape[2]
    half = size // 2
    s, t = here()
    line = spot[0:1]
    lane = lax.broadcasted_iota(jnp.int32, line.shape, 1)
    entries = (2 * slot, 2 * slot + 1, 2 * slots)
    row, col, count = (jnp.sum(jnp.where(lane == k, line, 0.0)).astype(jnp.int32) for k in entries)
    alive = slot < count

    @pl.when(jnp.logical_not(alive))
    def _():
        outer[...] = jnp.zeros(outer.shape, jnp.float32)
        inner[...] = jnp.zeros(inner.shape, jnp.float32)

    @pl.when(alive)
    def _():
        tile = col // LANES
        first = tile % 2
        rest_col = col % LANES
        from_tile = lax.broadcasted_iota(jnp.int32, (half, LANES), 1) >= rest_col
        from_upper = lax.broadcasted_iota(jnp.int32, (half, LANES), 0) >= row
        side = far_side(s)
        own, far, near = layout(refs, t)
        for kind, source in ((1, own), (1 + side, far), (1 - side, near)):
            for step in range(3):
                pick_tile(plan, picked.at[kind, step], source, tile + step, t)

        @pl.when(plan.outermost(s))
        def _():
            picked[1 + side] = jnp.zeros(picked.shape[1:], jnp.float32)

        def edge(kind, part):
            return jnp.where(from_tile, picked[kind, 0, part], picked[kind, 2, part])

        def across(edges, middles, rows):
            sums, differences = [], []
            shares = []
            for columns, (real, imag) in ((slice(0, half), edges), (slice(half, size), middles)):
                probe_real, probe_imag = probe[slot, 0, rows, columns], probe[slot, 1, rows, columns]
                shares.append((probe_real * real - probe_imag * imag, probe_real * imag + probe_imag * real))
            for part in range(2):
                sums.append(shares[0][part] + shares[1][part])
                differences.append(shares[0][part] - shares[1][part])
            return [
                times_table(jnp.concatenate(parts, axis=1), tables[parity, 0])
                for parity, parts in enumerate((sums, differences))
            ]

        lower = across(
            [edge(1, part) for part in range(2)], [picked[1, 1, part] for part in range(2)], slice(half, size)
        )
        upper = across(
            [jnp.where(from_upper, edge(0, part), edge(2, part)) for part in range(2)],
            [jnp.where(from_upper, picked[0, 1, part], picked[2, 1, part]) for part in range(2)],
            slice(0, half),
        )
        halves = []
        for sign in (1.0, -1.0):
            rows = [top + sign * bottom for top, bottom in zip(upper, lower)]
            halves.append(
                jnp.concatenate(
                    [jnp.concatenate([row[:, part] for row in rows], axis=1) for part in (slice(0, half), slice(half, size))],
                    axis=0,
                )
            )
        back = []
        for parity in range(2):
            pattern = table_times(tables[parity, 1], halves[parity])
            far_real = pattern[:half]
            far_imag = pattern[half:]
            amplitude = amps[slot, parity * half : (parity + 1) * half]
            factor = 1.0 - amplitude * lax.rsqrt(far_real * far_real + far_imag * far_imag + SMOOTH)
            miss = jnp.concatenate([far_real * factor, far_imag * factor], axis=0)
            back.append(table_times(tables[parity, 0], miss))
        real = jnp.concatenate([back[0][:half] + back[1][:half], back[0][:half] - back[1][:half]], axis=0)
        imag = jnp.concatenate([back[0][half:] + back[1][half:], back[0][half:] - back[1][half:]], axis=0)
        both = []
        for parity in range(2):
            columns = slice(parity * half, (parity + 1) * half)
            both.append(times_table(jnp.concatenate([real[:, columns], imag[:, columns]], axis=1), tables[parity, 1]))
        near_real = jnp.concatenate([both[0][:, :half] + both[1][:, :half], both[0][:, :half] - both[1][:, :half]], axis=1)
        near_imag = jnp.concatenate([both[0][:, half:] + both[1][:, half:], both[0][:, half:] - both[1][:, half:]], axis=1)
        probe_real = probe[slot, 0]
        probe_imag = probe[slot, 1]
        for part, term in enumerate((probe_real * near_real + probe_imag * near_imag, probe_real * near_imag - probe_imag * near_real)):
            for place, columns in ((first, slice(0, half)), (1 - first, slice(half, size))):
                outer[part, :, lanes(place)] = term[:half, columns]
                inner[part, :, lanes(place)] = term[half:, columns]

    for index, target in enumerate(outer_halves):
        first = plan.first_parity(t)
        target[...] = outer[:, :, lanes(first if index == 0 else 1 - first)]
    for index, source in enumerate((*earlier, outer)):
        line = 0
        for target in near_outers:
            rows = target.shape[1]
            target[2 * index : 2 * index + 2] = source[:, line : line + rows]
            line += rows


class Patch:
    def __init__(self, plan, info, s, patch, slot, down, far=False):
        runs = patch if isinstance(patch, (list, tuple)) else [patch]
        half = sum(run.shape[1] for run in runs)
        index = (1 if down is None else 1 + down) * (plan.sides + 1)
        row = info[index, 2 * slot]
        col = info[index, 2 * slot + 1]
        self.runs = runs
        self.tile = col // LANES
        self.first = self.tile % 2
        self.rest = col % LANES
        self.lane = lax.broadcasted_iota(jnp.int32, (half, LANES), 1)
        self.from_tile = self.lane >= self.rest
        self.rows = None
        if down is not None:
            line = lax.broadcasted_iota(jnp.int32, (half, LANES), 0)
            after = jnp.where(down > 0, half, row)
            if far:
                after = jnp.where(plan.outermost(s), 0, after)
            self.rows = (line >= jnp.where(down > 0, row, 0)) & (line < after)

    def lines(self, part, place):
        values = jnp.concatenate([run[part, :, lanes(place)] for run in self.runs], axis=0)
        return values if self.rows is None else jnp.where(self.rows, values, 0.0)

    def tiles(self, part):
        edge = self.lines(part, self.first)
        middle = self.lines(part, 1 - self.first)
        return jnp.where(self.from_tile, edge, 0.0), middle, jnp.where(self.from_tile, 0.0, edge)

    def add_to(self, canvas):
        for part in range(2):
            for step, values in enumerate(self.tiles(part)):
                canvas[part, :, lanes(self.tile + step)] += values

    def mask(self, tile):
        step = tile - self.tile
        first = jnp.where(step == 0, self.rest, 0)
        after = jnp.where(step == 2, self.rest, jnp.where((step < 0) | (step > 2), 0, LANES))
        inside = (self.lane >= first) & (self.lane < after)
        if self.rows is not None:
            inside = inside & self.rows
        return jnp.where(inside, 1.0, 0.0)


def part_of(plan, patch, mask, part, tile):
    if isinstance(patch, (list, tuple)):
        first = plan.first_parity(lax.axis_index("sy"))
        values = jnp.where(tile % 2 == first, patch[0][part], patch[1][part])
    else:
        values = patch[part, :, lanes(tile % 2)]
    return values * mask[:, lanes(tile)]


def early_sum_kernel(plan, slots, info, *rest):
    inner, near, canvas = rest[:slots], rest[slots:-1], rest[-1]
    s, _ = here()
    canvas[...] = jnp.zeros(canvas.shape, jnp.float32)
    for slot in range(slots):
        Patch(plan, info, s, inner[slot], slot, None).add_to(canvas)
        runs = [run.at[2 * slot : 2 * slot + 2] for run in near]
        Patch(plan, info, s, runs, slot, -far_side(s)).add_to(canvas)


def base_kernel(plan, slots, layout, pieces, info, early, inverse, *rest):
    far, refs, (canvas, base, mask) = rest[: slots - 1], rest[slots - 1 : slots - 1 + pieces], rest[slots - 1 + pieces :]
    s, t = here()
    canvas[...] = early[...]
    for slot in range(slots - 1):
        Patch(plan, info, s, far[slot], slot, far_side(s), True).add_to(canvas)
    last = Patch(plan, info, s, canvas, slots - 1, far_side(s), True)
    for tile in range(plan.tiles):
        where = lanes(tile)
        pick_tile(plan, base.at[:, :, where], layout(refs, t)[0], tile, t)
        base[:, :, where] -= canvas[:, :, where] * inverse[:, where][None]
        mask[:, where] = last.mask(tile)


def take_off(plan, patch, mask, target, base, inverse, tile):
    for part in range(2):
        target[part] = base[part, :, lanes(tile)] - part_of(plan, patch, mask, part, tile) * inverse[:, lanes(tile)]


def middle_kernel(plan, base, patch, mask, inverse, _, middle):
    _, t = here()
    for step in range(plan.mid_tiles):
        take_off(plan, patch, mask, middle.at[:, :, lanes(step)], base, inverse, plan.mid_start(t) + step)


def boundary_kernel(plan, early, patch, mask, *sums):
    _, t = here()
    for total, start in zip(sums, plan.pair_starts(t)):
        for step in range(2):
            tile = start + step
            for part in range(2):
                total[part, :, lanes(step)] = early[part, :, lanes(tile)] + part_of(plan, patch, mask, part, tile)


def halo_sum_kernel(plan, early, mask, *rest):
    halves, sums = rest[: plan.sides], rest[plan.sides :]
    _, t = here()
    for half, total, tile in zip(halves, sums, plan.halo_tiles(t)):
        for part in range(2):
            total[part] = early[part, :, lanes(tile)] + half[part] * mask[:, lanes(tile)]


def last_kernel(plan, base, mask, inverse, _, first, second, *rest):
    nearly, bases, (current, sems) = rest[0], rest[1 : 1 + plan.sides], rest[1 + plan.sides :]
    patch = [first, second]
    _, t = here()
    copies = []
    for step in range(plan.own):
        where = lanes(step)
        take_off(plan, patch, mask, current.at[:, :, where], base, inverse, 1 + step)
        copies.append(pltpu.make_async_copy(current.at[:, :, where], nearly.at[:, :, where], sems.at[step]))
        copies[-1].start()
    for edge, tile in zip(bases, plan.edge_tiles(t)):
        edge[...] = current[:, :, lanes(tile - 1)]
    for copy in copies:
        copy.wait()


def edge_kernel(plan, inverse, *rest):
    bases, received = rest[: plan.sides], rest[plan.sides : 2 * plan.sides]
    _, result, sums, sems = rest[2 * plan.sides :]
    _, t = here()
    copies = []
    for side, tile in enumerate(plan.edge_tiles(t)):
        sums[side] = bases[side][...] - received[side][...] * inverse[:, lanes(tile)][None]
        copies.append(pltpu.make_async_copy(sums.at[side], result.at[:, :, lanes(tile - 1)], sems.at[side]))
        copies[-1].start()
    for copy in copies:
        copy.wait()


def call(kernel, outs, scratch, ins, flops=10**5, size=10**4, in_specs=None, out_specs=None, **options):
    result = pl.pallas_call(
        kernel,
        out_shape=outs,
        in_specs=in_specs or [SMEM if value.dtype == jnp.int32 else VMEM for value in ins],
        out_specs=out_specs or jax.tree.map(lambda _: VMEM, outs),
        scratch_shapes=scratch,
        compiler_params=pltpu.CompilerParams(vmem_limit_bytes=VMEM_BYTES),
        cost_estimate=pl.CostEstimate(flops=flops, bytes_accessed=size, transcendentals=0),
        **options,
    )(*ins)
    return list(result) if isinstance(outs, list) else result


def on_device(plan, object_field, probe_field, amplitudes, centres, counts):
    f32 = jnp.float32
    shape = jax.ShapeDtypeStruct
    size = probe_field.shape[1]
    half = size // 2
    slots = amplitudes.shape[2]
    block_rows = object_field.shape[1]
    block_cols = object_field.shape[2]
    assert block_rows == half and block_cols % (2 * LANES) == 0 and half == LANES
    width = plan.tiles * LANES
    sides = plan.sides
    spots = centres[0, 0]
    counts = counts.reshape(-1)
    own_amps = amplitudes[0, 0]
    tables = jnp.asarray(dft_tables(size))
    order = jnp.asarray(parity_order(size))
    dma = pltpu.SemaphoreType.DMA

    messages = call(
        lambda *refs: edge_message_kernel(plan, *refs),
        [shape((2, half + 8, LANES), f32)] * sides,
        [dma((sides,))],
        [object_field, spots, counts],
        in_specs=[HBM, SMEM, SMEM],
    )
    halos = plan.across(messages)
    far_block = plan.far_rows(object_field)
    near_block = plan.near_rows(object_field)
    rolled, ordered = call(
        prepare_kernel,
        [shape((slots, 2, size, size), f32), shape((slots, size, size), f32)],
        [pltpu.VMEM((2, 2 * size + 8, size), f32)],
        [spots, probe_field, own_amps, order],
    )
    messages = call(
        lambda *refs: halo_message_kernel(plan, *refs),
        [shape((2, half + 8, LANES), f32)] * sides
        + [shape((2, half, LANES), f32)] * sides
        + [shape((8, LANES), f32)] * (sides + 1),
        [],
        [spots, counts, ordered, *halos],
        in_specs=[SMEM, SMEM, ANY] + [VMEM] * sides,
    )
    passed, lines, own_spot = messages[sides : 2 * sides], messages[2 * sides : -1], messages[-1]
    near_lines = [plan.near_rows(line) for line in lines]
    far = [far_block] + [plan.far_rows(message) for message in messages[:sides]]
    near = [plan.near_rows(message) for message in passed] + [near_block]
    own = [object_field] + passed
    def runs_layout(refs, main, side_starts):
        starts = [main] + side_starts
        return lay_out(refs[: 1 + sides], starts), lay_out(refs[1 + sides : 2 + 2 * sides], starts)

    def first_layout(refs, t):
        own, far = runs_layout(refs, 1, plan.halo_tiles(t))
        return own, far, lay_out(refs[2 + 2 * sides :], plan.halo_tiles(t) + [1])

    def later_layout(refs, t):
        own, far = runs_layout(refs, plan.mid_start(t), plan.pair_starts(t))
        counts = [2] * sides + [plan.mid_tiles]
        return own, far, lay_out_rows(refs[2 + 2 * sides :], counts, plan.pair_starts(t) + [plan.mid_start(t)])

    layout = first_layout

    third = half // 24 * 8
    near_heights = [half - 2 * third, third, third]
    for sweep in range(ITERS):
        pieces = own + far + near
        inner, outer, outer_far = [], [], []
        for slot in range(slots):
            last = slot == slots - 1
            earlier = outer if last else []
            patch = shape((2, half, size), f32)
            halves = 2 if last and sweep == ITERS - 1 else 0
            inner_part, *copies = call(
                lambda *refs, slot=slot, layout=layout, copied=len(earlier), halves=halves: term_kernel(
                    plan, slot, layout, len(pieces), copied, halves, slots, *refs
                ),
                [patch]
                + ([shape((2, half, LANES), f32)] * halves or [patch])
                + [shape((2 * slots, rows, size), f32) for rows in near_heights if last],
                [pltpu.VMEM((3, 3, 2, half, LANES), f32)]
                + [pltpu.VMEM((2, half, size), f32)] * (halves > 0),
                [own_spot, *pieces, *earlier, rolled, ordered, tables],
            )
            outer_part = None if halves else copies.pop(0)
            outer_halves, copies = copies[:halves], copies[halves:]
            inner.append(inner_part)
            outer.append(outer_part)
            outer_far.append([plan.far_rows(part) for part in outer_halves] if halves else plan.far_rows(outer_part))
            if sweep == 0 and last:
                info = call(
                    lambda *refs: info_kernel(plan, *refs),
                    shape((3 * (sides + 1), LANES), jnp.int32),
                    [pltpu.VMEM((3 * (sides + 1), 8, LANES), jnp.int32), dma],
                    lines + far[1:] + near_lines + [outer_part],
                    in_specs=[VMEM] * (3 * sides) + [ANY],
                    out_specs=SMEM,
                )
        outer_near = [plan.near_rows(copy) for copy in copies]
        if sweep == 0:
            inverse = call(
                lambda *refs: light_kernel(plan, slots, *refs),
                shape((half, width), f32),
                [
                    pltpu.VMEM((2 * size + 8, size), f32),
                    pltpu.VMEM((half, width + 2 * plan.own * LANES), f32),
                ],
                [info, probe_field, copies[0]],
                in_specs=[SMEM, VMEM, ANY],
            )
        early = call(
            lambda *refs: early_sum_kernel(plan, slots, *refs),
            shape((2, half, width), f32),
            [],
            [info, *inner, *outer_near],
        )
        early, base, mask = call(
            lambda *refs, layout=layout: base_kernel(plan, slots, layout, len(pieces), *refs),
            [shape((2, half, width), f32)] * 2 + [shape((half, width), f32)],
            [],
            [info, early, inverse, *outer_far[:-1], *pieces],
        )
        if sweep < ITERS - 1:
            sums = call(
                lambda *refs: boundary_kernel(plan, *refs),
                [shape((2, half, 2 * LANES), f32)] * sides,
                [],
                [early, outer_far[-1], mask],
            )
            received = plan.across(sums)
            middle = call(
                lambda *refs: middle_kernel(plan, *refs),
                shape((2, half, plan.mid_tiles * LANES), f32),
                [],
                [base, outer_far[-1], mask, inverse, sums[0]],
                in_specs=[VMEM] * 4 + [ANY],
            )
            far_middle = plan.far_rows(middle)
            near_runs = [shape((2, rows, (2 * sides + plan.mid_tiles) * LANES), f32) for rows in near_heights]
            updated = call(
                lambda *refs: pair_kernel(plan, *refs),
                [shape((2, half, 2 * LANES), f32)] * sides + near_runs,
                [],
                [base, early, inverse, middle, *sums, *received],
            )
            pairs = updated[:sides]
            own = [middle] + pairs
            far = [far_middle] + [plan.far_rows(piece) for piece in pairs]
            near = [plan.near_rows(piece) for piece in updated[sides:]]
            layout = later_layout
    sums = call(
        lambda *refs: halo_sum_kernel(plan, *refs),
        [shape((2, half, LANES), f32)] * sides,
        [],
        [early, mask, *outer_far[-1][:sides]],
    )
    nearly, *bases = call(
        lambda *refs: last_kernel(plan, *refs),
        [shape((2, half, block_cols), f32)] + [shape((2, half, LANES), f32)] * sides,
        [pltpu.VMEM((2, half, block_cols), f32), dma((plan.own,))],
        [base, mask, inverse, sums[0], *outer_far[-1]],
        in_specs=[VMEM] * 3 + [ANY] + [VMEM] * 2,
        out_specs=[HBM] + [VMEM] * sides,
    )
    received = plan.across(sums)
    return call(
        lambda *refs: edge_kernel(plan, *refs),
        shape(nearly.shape, f32),
        [pltpu.VMEM((sides, 2, half, LANES), f32), dma((sides,))],
        [inverse, *bases, *received, nearly],
        in_specs=[VMEM] * (1 + 2 * sides) + [HBM],
        out_specs=HBM,
        input_output_aliases={1 + 2 * sides: 0},
    )


def solution(mesh):
    sizes = dict(mesh.shape)

    def per_device(object_field, *rest):
        plan = Plan(sizes["sx"], sizes["sy"], *object_field.shape[1:])
        return on_device(plan, object_field, *rest)

    return jax.shard_map(
        per_device,
        mesh=mesh,
        in_specs=(
            P(None, "sx", "sy"),
            P(),
            P("sx", "sy", None, None, None),
            P("sx", "sy", None, None),
            P(None, "sy"),
        ),
        out_specs=P(None, "sx", "sy"),
        check_vma=False,
    )
```

```python
import math

import jax
import jax.numpy as jnp
import ml_dtypes
import numpy as np
from jax import lax
from jax.experimental import pallas as pl
from jax.experimental.pallas import tpu as pltpu
from jax.sharding import PartitionSpec as P

ITERS = 2
SMOOTH = 1.0
DAMPING = 1.0
LANES = 128
VMEM_BYTES = 12 * 1024 * 1024

VMEM = pl.BlockSpec(memory_space=pltpu.VMEM)
SMEM = pl.BlockSpec(memory_space=pltpu.SMEM)
HBM = pl.BlockSpec(memory_space=pltpu.HBM)
ANY = pl.BlockSpec(memory_space=pl.ANY)


def split_numpy(table):
    high = table.astype(np.float32).astype(ml_dtypes.bfloat16)
    low = (table - high.astype(np.float64)).astype(ml_dtypes.bfloat16)
    return high, low


def dft_tables(length):
    half = length // 2
    index = np.arange(half)
    tables = []
    for parity in range(2):
        angles = 2.0 * math.pi / length * (index[:, None] * (2 * index[None, :] + parity) % length)
        cosine = np.cos(angles) / math.sqrt(length)
        sine = np.sin(angles) / math.sqrt(length)
        forward = np.block([[cosine, -sine], [sine, cosine]])
        tables.append([split_numpy(forward), split_numpy(forward.T)])
    return np.array(tables, dtype=ml_dtypes.bfloat16)


def parity_order(length):
    half = length // 2
    order = np.zeros((length, length))
    for index in range(length):
        order[index, index % 2 * half + index // 2] = 1.0
    return np.stack([order, order.T]).astype(ml_dtypes.bfloat16)


def split(values):
    high = values.astype(jnp.bfloat16)
    low = (values - high.astype(jnp.float32)).astype(jnp.bfloat16)
    return high, low


def times_table(values, table):
    high, low = split(values)
    left = jnp.concatenate([high, low, high], axis=1)
    right = jnp.concatenate([table[0], table[0], table[1]], axis=0)
    return jnp.dot(left, right, preferred_element_type=jnp.float32)


def table_times(table, values):
    high, low = split(values)
    left = jnp.concatenate([table[0], table[0], table[1]], axis=1)
    right = jnp.concatenate([high, low, high], axis=0)
    return jnp.dot(left, right, preferred_element_type=jnp.float32)


class Plan:
    def __init__(self, sx_size, sy_size, block_rows, block_cols):
        self.rows = block_rows
        self.sx_size = sx_size
        self.sy_size = sy_size
        self.own = block_cols // LANES
        self.tiles = self.own + 2
        self.paired = sy_size == 2
        self.sides = 1 if self.paired else 2

    def rights(self, t):
        return [1 - t] if self.paired else [0, 1]

    def pair_starts(self, t):
        return [right * (self.tiles - 2) for right in self.rights(t)]

    def halo_tiles(self, t):
        return [right * (self.tiles - 1) for right in self.rights(t)]

    def edge_tiles(self, t):
        return [1 + right * (self.tiles - 3) for right in self.rights(t)]

    def first_parity(self, t):
        return 1 - t if self.paired else 0

    def mid_start(self, t):
        return 1 + t if self.paired else 2

    @property
    def mid_tiles(self):
        return self.tiles - 3 if self.paired else self.tiles - 4

    def across(self, values, axis_name="sy"):
        if self.paired:
            return [lax.ppermute(values[0], axis_name, [(0, 1), (1, 0)])]
        ends = self.sy_size - 1
        return [
            lax.ppermute(values[1], axis_name, [(i, i + 1) for i in range(ends)]),
            lax.ppermute(values[0], axis_name, [(i + 1, i) for i in range(ends)]),
        ]

    def far_rows(self, values):
        rows, columns = self.sx_size, self.sy_size
        pairs = [(i * columns + t, (i + 1) * columns + t) for i in range(1, rows - 1, 2) for t in range(columns)]
        for i in (0, rows - 1):
            pairs += [(i * columns + t, i * columns + t + 1) for t in range(0, columns - 1, 2)]
        return lax.ppermute(values, ("sx", "sy"), pairs + [(j, i) for i, j in pairs])

    def near_rows(self, values):
        return lax.ppermute(values, "sx", [(i, i ^ 1) for i in range(self.sx_size)])

    def outermost(self, s):
        return (s == 0) | (s == self.sx_size - 1)


def far_side(s):
    return 2 * (s % 2) - 1


def lanes(tile, count=1):
    if isinstance(tile, int):
        return pl.ds(tile * LANES, count * LANES)
    return pl.ds(pl.multiple_of(tile * LANES, LANES), count * LANES)


def pick_tile(plan, target, pieces, tile, t):
    rows = target.shape[1]
    if plan.paired:

        @pl.when(tile == (plan.tiles - 1) * t)
        def _():
            target[...] = jnp.zeros(target.shape, jnp.float32)

    for runs, offset, count, start in pieces:

        @pl.when((tile >= start) & (tile < start + count))
        def _(runs=runs, offset=offset, start=start):
            line = 0
            for run in runs:
                height = min(run.shape[1], rows - line)
                target[:, line : line + height] = run[:, :height, lanes(tile - start + offset)]
                line += height


def lay_out(refs, starts):
    return [([ref], 0, ref.shape[2] // LANES, start) for ref, start in zip(refs, starts)]


def lay_out_rows(runs, counts, starts):
    return [(runs, sum(counts[:k]), count, start) for k, (count, start) in enumerate(zip(counts, starts))]


def rows_at(ref, start, count):
    offset = start % 8
    values = ref[pl.ds(pl.multiple_of(start - offset, 8), count + 8)]
    return pltpu.roll(values, (count + 8 - offset) % (count + 8), 0)[:count]


def here():
    return lax.axis_index("sx"), lax.axis_index("sy")


def info_rows(centres, count):
    lane = lax.broadcasted_iota(jnp.int32, (8, LANES), 1)
    slots = centres.shape[0]
    values = [centres[slot, axis] for slot in range(slots) for axis in range(2)] + [count]
    line = jnp.zeros((8, LANES), jnp.int32)
    for index, value in enumerate(values):
        line = jnp.where(lane == index, value, line)
    return line.astype(jnp.float32)


def edge_message_kernel(plan, block, centres, counts, *rest):
    messages, sems = rest[: plan.sides], rest[plan.sides]
    s, t = here()
    half = block.shape[1]
    copies = [
        pltpu.make_async_copy(block.at[:, :, lanes(tile - 1)], message.at[:, :half], sems.at[side])
        for side, (message, tile) in enumerate(zip(messages, plan.edge_tiles(t)))
    ]
    for copy in copies:
        copy.start()
    rows = info_rows(centres, counts[s])
    for message in messages:
        message[0, half:] = rows
        message[1, half:] = rows
    for copy in copies:
        copy.wait()


def halo_message_kernel(plan, centres, counts, _, *rest):
    sides = plan.sides
    received, far, halos, infos = (rest[k * sides : (k + 1) * sides] for k in range(4))
    own = info_rows(centres, counts[lax.axis_index("sx")])
    rest[-1][...] = own
    upper_line = lax.broadcasted_iota(jnp.int32, own.shape, 0) == 0
    for source, message, halo, info in zip(received, far, halos, infos):
        rows = halo.shape[1]
        both = jnp.where(upper_line, own, pltpu.roll(source[0, rows : rows + 8], 1, 0))
        halo[...] = source[:, :rows]
        info[...] = both
        message[:, :rows] = source[:, :rows]
        message[0, rows:] = both
        message[1, rows:] = both


def pair_kernel(plan, base, early, inverse, first, second, *rest):
    sides = plan.sides
    sums, received, results = (rest[k * sides : (k + 1) * sides] for k in range(3))
    near = rest[3 * sides :]
    _, t = here()

    def copy(values, offset):
        line = 0
        for run in near:
            rows = run.shape[1]
            run[:, :, offset : offset + values.shape[2]] = values[:, line : line + rows]
            line += rows

    for side, (total, other, result, start) in enumerate(zip(sums, received, results, plan.pair_starts(t))):
        where = lanes(start, 2)
        missing = total[...] + other[...] - early[:, :, where]
        result[...] = base[:, :, where] - missing * inverse[:, where][None]
        copy(result, 2 * LANES * side)
    for step in range(plan.mid_tiles):
        copy((first, second)[step % 2].at[:, :, lanes(step // 2)], LANES * (2 * sides + step))


def spot_kernel(spot, _, copy):
    copy[...] = spot[...]


def prepare_kernel(centres, probe, amps, order, rolled, ordered, padded):
    size = probe.shape[1]
    half = size // 2
    padded[:, :half] = jnp.zeros((2, half, size), jnp.float32)
    padded[:, half + size :] = jnp.zeros((2, half + 8, size), jnp.float32)
    padded[:, half : half + size] = probe[...]
    for slot in range(amps.shape[0]):
        row = centres[slot, 0]
        col = centres[slot, 1]
        for part in range(2):
            shape = padded.at[part]
            upper = rows_at(shape, half - row, half) + rows_at(shape, half + size - row, half)
            lower = rows_at(shape, size - row, half)
            rolled[slot, part] = pltpu.roll(jnp.concatenate([upper, lower], axis=0), col % LANES, 1)
        high, low = split(amps[slot])
        across = jnp.dot(
            jnp.concatenate([high, low], axis=1),
            jnp.concatenate([order[0], order[0]], axis=0),
            preferred_element_type=jnp.float32,
        )
        high, low = split(across)
        ordered[slot] = jnp.dot(
            jnp.concatenate([order[1], order[1]], axis=1),
            jnp.concatenate([high, low], axis=0),
            preferred_element_type=jnp.float32,
        )


def info_kernel(plan, *rest):
    home, far, other = (rest[k * plan.sides : (k + 1) * plan.sides] for k in range(3))
    _, info, known, sem = rest[3 * plan.sides :]
    s, _ = here()
    upper = s % 2 == 0
    width = plan.sides + 1

    def lines(messages):
        return [messages[0]] + [pltpu.roll(message, 7, 0) for message in messages]

    own = lines([line[...] for line in home])
    near = lines([line[...] for line in other])
    far = lines([jnp.where(plan.outermost(s), 0.0, message[0, plan.rows :]) for message in far])
    for turn in range(width):
        for kind, line in ((0, jnp.where(upper, far[turn], near[turn])), (1, own[turn]), (2, jnp.where(upper, near[turn], far[turn]))):
            known[kind * width + turn] = line.astype(jnp.int32)
    copy = pltpu.make_async_copy(known.at[:, 0], info, sem)
    copy.start()
    copy.wait()


def light_kernel(plan, slots, info, probe, _, inverse, padded, canvas):
    size = probe.shape[1]
    half = size // 2
    _, t = here()
    padded[:half] = jnp.zeros((half, size), jnp.float32)
    padded[half + size :] = jnp.zeros((half + 8, size), jnp.float32)
    padded[half : half + size] = probe[0] * probe[0] + probe[1] * probe[1]
    canvas[...] = jnp.zeros(canvas.shape, jnp.float32)
    reach = plan.sides + 1
    spare = jnp.zeros((half, LANES), jnp.float32)
    for down in (-1, 0, 1):

        def add(step, carry, down=down):
            turn = step // slots
            slot = step % slots
            over = turn * (1 - 2 * t) if plan.paired else jnp.where(turn == 0, 0, 2 * turn - 3)
            index = (down + 1) * reach + turn

            @pl.when(slot < info[index, 2 * slots])
            def _():
                row = info[index, 2 * slot]
                col = info[index, 2 * slot + 1]
                power = rows_at(padded, size - half * down - row, half)
                shifted = pltpu.roll(jnp.concatenate([power, spare], axis=1), col % LANES, 1)
                first = col // LANES + plan.own * (over + 1)
                canvas[:, lanes(first, 3)] += shifted

            return carry

        lax.fori_loop(0, reach * slots, add, 0)
    inverse[...] = 1.0 / (canvas[:, lanes(plan.own, plan.tiles)] + DAMPING)


def term_kernel(plan, slot, layout, pieces, copied, halves, slots, spot, *rest):
    refs, rest = rest[:pieces], rest[pieces:]
    earlier, (probe, amps, tables, inner), rest = rest[:copied], rest[copied : copied + 4], rest[copied + 4 :]
    if halves:
        outer, rest = rest[-1], rest[:-1]
    else:
        outer, rest = rest[0], rest[1:]
    outer_halves, near_outers, picked = rest[:halves], rest[halves:-1], rest[-1]
    size = probe.shape[2]
    half = size // 2
    s, t = here()
    line = spot[0:1]
    lane = lax.broadcasted_iota(jnp.int32, line.shape, 1)
    entries = (2 * slot, 2 * slot + 1, 2 * slots)
    row, col, count = (jnp.sum(jnp.where(lane == k, line, 0.0)).astype(jnp.int32) for k in entries)
    alive = slot < count

    @pl.when(jnp.logical_not(alive))
    def _():
        outer[...] = jnp.zeros(outer.shape, jnp.float32)
        inner[...] = jnp.zeros(inner.shape, jnp.float32)

    @pl.when(alive)
    def _():
        tile = col // LANES
        first = tile % 2
        rest_col = col % LANES
        from_tile = lax.broadcasted_iota(jnp.int32, (half, LANES), 1) >= rest_col
        from_upper = lax.broadcasted_iota(jnp.int32, (half, LANES), 0) >= row
        side = far_side(s)
        own, far, near = layout(refs, t)
        for kind, source in ((1, own), (1 + side, far), (1 - side, near)):
            for step in range(3):
                pick_tile(plan, picked.at[kind, step], source, tile + step, t)

        @pl.when(plan.outermost(s))
        def _():
            picked[1 + side] = jnp.zeros(picked.shape[1:], jnp.float32)

        def edge(kind, part):
            return jnp.where(from_tile, picked[kind, 0, part], picked[kind, 2, part])

        def across(edges, middles, rows):
            sums, differences = [], []
            shares = []
            for columns, (real, imag) in ((slice(0, half), edges), (slice(half, size), middles)):
                probe_real, probe_imag = probe[slot, 0, rows, columns], probe[slot, 1, rows, columns]
                shares.append((probe_real * real - probe_imag * imag, probe_real * imag + probe_imag * real))
            for part in range(2):
                sums.append(shares[0][part] + shares[1][part])
                differences.append(shares[0][part] - shares[1][part])
            return [
                times_table(jnp.concatenate(parts, axis=1), tables[parity, 0])
                for parity, parts in enumerate((sums, differences))
            ]

        lower = across(
            [edge(1, part) for part in range(2)], [picked[1, 1, part] for part in range(2)], slice(half, size)
        )
        upper = across(
            [jnp.where(from_upper, edge(0, part), edge(2, part)) for part in range(2)],
            [jnp.where(from_upper, picked[0, 1, part], picked[2, 1, part]) for part in range(2)],
            slice(0, half),
        )
        halves = []
        for sign in (1.0, -1.0):
            rows = [top + sign * bottom for top, bottom in zip(upper, lower)]
            halves.append(
                jnp.concatenate(
                    [jnp.concatenate([row[:, part] for row in rows], axis=1) for part in (slice(0, half), slice(half, size))],
                    axis=0,
                )
            )
        back = []
        for parity in range(2):
            pattern = table_times(tables[parity, 1], halves[parity])
            far_real = pattern[:half]
            far_imag = pattern[half:]
            amplitude = amps[slot, parity * half : (parity + 1) * half]
            factor = 1.0 - amplitude * lax.rsqrt(far_real * far_real + far_imag * far_imag + SMOOTH)
            miss = jnp.concatenate([far_real * factor, far_imag * factor], axis=0)
            back.append(table_times(tables[parity, 0], miss))
        real = jnp.concatenate([back[0][:half] + back[1][:half], back[0][:half] - back[1][:half]], axis=0)
        imag = jnp.concatenate([back[0][half:] + back[1][half:], back[0][half:] - back[1][half:]], axis=0)
        both = []
        for parity in range(2):
            columns = slice(parity * half, (parity + 1) * half)
            both.append(times_table(jnp.concatenate([real[:, columns], imag[:, columns]], axis=1), tables[parity, 1]))
        near_real = jnp.concatenate([both[0][:, :half] + both[1][:, :half], both[0][:, :half] - both[1][:, :half]], axis=1)
        near_imag = jnp.concatenate([both[0][:, half:] + both[1][:, half:], both[0][:, half:] - both[1][:, half:]], axis=1)
        probe_real = probe[slot, 0]
        probe_imag = probe[slot, 1]
        for part, term in enumerate((probe_real * near_real + probe_imag * near_imag, probe_real * near_imag - probe_imag * near_real)):
            for place, columns in ((first, slice(0, half)), (1 - first, slice(half, size))):
                outer[part, :, lanes(place)] = term[:half, columns]
                inner[part, :, lanes(place)] = term[half:, columns]

    for index, target in enumerate(outer_halves):
        first = plan.first_parity(t)
        target[...] = outer[:, :, lanes(first if index == 0 else 1 - first)]
    for index, source in enumerate((*earlier, outer)):
        line = 0
        for target in near_outers:
            rows = target.shape[1]
            target[2 * index : 2 * index + 2] = source[:, line : line + rows]
            line += rows


class Patch:
    def __init__(self, plan, info, s, patch, slot, down, far=False):
        runs = patch if isinstance(patch, (list, tuple)) else [patch]
        half = sum(run.shape[1] for run in runs)
        index = (1 if down is None else 1 + down) * (plan.sides + 1)
        row = info[index, 2 * slot]
        col = info[index, 2 * slot + 1]
        self.runs = runs
        self.tile = col // LANES
        self.first = self.tile % 2
        self.rest = col % LANES
        self.lane = lax.broadcasted_iota(jnp.int32, (half, LANES), 1)
        self.from_tile = self.lane >= self.rest
        self.rows = None
        if down is not None:
            line = lax.broadcasted_iota(jnp.int32, (half, LANES), 0)
            after = jnp.where(down > 0, half, row)
            if far:
                after = jnp.where(plan.outermost(s), 0, after)
            self.rows = (line >= jnp.where(down > 0, row, 0)) & (line < after)

    def lines(self, part, place):
        values = jnp.concatenate([run[part, :, lanes(place)] for run in self.runs], axis=0)
        return values if self.rows is None else jnp.where(self.rows, values, 0.0)

    def tiles(self, part):
        edge = self.lines(part, self.first)
        middle = self.lines(part, 1 - self.first)
        return jnp.where(self.from_tile, edge, 0.0), middle, jnp.where(self.from_tile, 0.0, edge)

    def add_to(self, canvas):
        for part in range(2):
            for step, values in enumerate(self.tiles(part)):
                canvas[part, :, lanes(self.tile + step)] += values

    def mask(self, tile):
        step = tile - self.tile
        first = jnp.where(step == 0, self.rest, 0)
        after = jnp.where(step == 2, self.rest, jnp.where((step < 0) | (step > 2), 0, LANES))
        inside = (self.lane >= first) & (self.lane < after)
        if self.rows is not None:
            inside = inside & self.rows
        return jnp.where(inside, 1.0, 0.0)


def part_of(plan, patch, mask, part, tile):
    first = plan.first_parity(lax.axis_index("sy"))
    return jnp.where(tile % 2 == first, patch[0][part], patch[1][part]) * mask[:, lanes(tile)]


def early_sum_kernel(plan, slots, info, *rest):
    inner, near, canvas = rest[:slots], rest[slots:-1], rest[-1]
    s, _ = here()
    canvas[...] = jnp.zeros(canvas.shape, jnp.float32)
    for slot in range(slots):
        Patch(plan, info, s, inner[slot], slot, None).add_to(canvas)
        runs = [run.at[2 * slot : 2 * slot + 2] for run in near]
        Patch(plan, info, s, runs, slot, -far_side(s)).add_to(canvas)


def base_kernel(plan, slots, layout, pieces, info, early, inverse, *rest):
    far, refs, (canvas, base, mask) = rest[: slots - 1], rest[slots - 1 : slots - 1 + pieces], rest[slots - 1 + pieces :]
    s, t = here()
    canvas[...] = early[...]
    for slot in range(slots - 1):
        Patch(plan, info, s, far[slot], slot, far_side(s), True).add_to(canvas)
    last = Patch(plan, info, s, canvas, slots - 1, far_side(s), True)
    for tile in range(plan.tiles):
        where = lanes(tile)
        pick_tile(plan, base.at[:, :, where], layout(refs, t)[0], tile, t)
        base[:, :, where] -= canvas[:, :, where] * inverse[:, where][None]
        mask[:, where] = last.mask(tile)


def take_off(plan, patch, mask, target, base, inverse, tile):
    for part in range(2):
        target[part] = base[part, :, lanes(tile)] - part_of(plan, patch, mask, part, tile) * inverse[:, lanes(tile)]


def middle_kernel(plan, parity, base, half, mask, inverse, _, middle):
    _, t = here()
    for index, step in enumerate(range(parity, plan.mid_tiles, 2)):
        tile = plan.mid_start(t) + step
        for part in range(2):
            terms = half[part] * mask[:, lanes(tile)] * inverse[:, lanes(tile)]
            middle[part, : terms.shape[0], lanes(index)] = base[part, :, lanes(tile)] - terms
    spare = middle.shape[1] - base.shape[1]
    if spare:
        middle[:, base.shape[1] :] = jnp.zeros((2, spare, middle.shape[2]), jnp.float32)


def boundary_kernel(plan, early, first, second, mask, *sums):
    _, t = here()
    for total, start in zip(sums, plan.pair_starts(t)):
        for step in range(2):
            tile = start + step
            for part in range(2):
                total[part, :, lanes(step)] = early[part, :, lanes(tile)] + part_of(plan, [first, second], mask, part, tile)


def halo_sum_kernel(plan, early, mask, *rest):
    halves, sums = rest[: plan.sides], rest[plan.sides :]
    _, t = here()
    for half, total, tile in zip(halves, sums, plan.halo_tiles(t)):
        for part in range(2):
            total[part] = early[part, :, lanes(tile)] + half[part] * mask[:, lanes(tile)]


def last_kernel(plan, base, mask, inverse, _, first, second, *rest):
    nearly, bases, (current, sems) = rest[0], rest[1 : 1 + plan.sides], rest[1 + plan.sides :]
    patch = [first, second]
    _, t = here()
    copies = []
    for step in range(plan.own):
        where = lanes(step)
        take_off(plan, patch, mask, current.at[:, :, where], base, inverse, 1 + step)
        copies.append(pltpu.make_async_copy(current.at[:, :, where], nearly.at[:, :, where], sems.at[step]))
        copies[-1].start()
    for edge, tile in zip(bases, plan.edge_tiles(t)):
        edge[...] = current[:, :, lanes(tile - 1)]
    for copy in copies:
        copy.wait()


def edge_kernel(plan, inverse, *rest):
    bases, received = rest[: plan.sides], rest[plan.sides : 2 * plan.sides]
    _, result, sums, sems = rest[2 * plan.sides :]
    _, t = here()
    copies = []
    for side, tile in enumerate(plan.edge_tiles(t)):
        sums[side] = bases[side][...] - received[side][...] * inverse[:, lanes(tile)][None]
        copies.append(pltpu.make_async_copy(sums.at[side], result.at[:, :, lanes(tile - 1)], sems.at[side]))
        copies[-1].start()
    for copy in copies:
        copy.wait()


def call(kernel, outs, scratch, ins, flops=10**5, size=10**4, in_specs=None, out_specs=None, **options):
    result = pl.pallas_call(
        kernel,
        out_shape=outs,
        in_specs=in_specs or [SMEM if value.dtype == jnp.int32 else VMEM for value in ins],
        out_specs=out_specs or jax.tree.map(lambda _: VMEM, outs),
        scratch_shapes=scratch,
        compiler_params=pltpu.CompilerParams(vmem_limit_bytes=VMEM_BYTES),
        cost_estimate=pl.CostEstimate(flops=flops, bytes_accessed=size, transcendentals=0),
        **options,
    )(*ins)
    return list(result) if isinstance(outs, list) else result


def on_device(plan, object_field, probe_field, amplitudes, centres, counts):
    f32 = jnp.float32
    shape = jax.ShapeDtypeStruct
    size = probe_field.shape[1]
    half = size // 2
    slots = amplitudes.shape[2]
    block_rows = object_field.shape[1]
    block_cols = object_field.shape[2]
    assert block_rows == half and block_cols % (2 * LANES) == 0 and half == LANES
    width = plan.tiles * LANES
    sides = plan.sides
    spots = centres[0, 0]
    counts = counts.reshape(-1)
    own_amps = amplitudes[0, 0]
    tables = jnp.asarray(dft_tables(size))
    order = jnp.asarray(parity_order(size))
    dma = pltpu.SemaphoreType.DMA

    messages = call(
        lambda *refs: edge_message_kernel(plan, *refs),
        [shape((2, half + 8, LANES), f32)] * sides,
        [dma((sides,))],
        [object_field, spots, counts],
        in_specs=[HBM, SMEM, SMEM],
    )
    halos = plan.across(messages)
    far_block = plan.far_rows(object_field)
    near_block = plan.near_rows(object_field)
    rolled, ordered = call(
        prepare_kernel,
        [shape((slots, 2, size, size), f32), shape((slots, size, size), f32)],
        [pltpu.VMEM((2, 2 * size + 8, size), f32)],
        [spots, probe_field, own_amps, order],
    )
    messages = call(
        lambda *refs: halo_message_kernel(plan, *refs),
        [shape((2, half + 8, LANES), f32)] * sides
        + [shape((2, half, LANES), f32)] * sides
        + [shape((8, LANES), f32)] * (sides + 1),
        [],
        [spots, counts, ordered, *halos],
        in_specs=[SMEM, SMEM, ANY] + [VMEM] * sides,
    )
    passed, lines, own_spot = messages[sides : 2 * sides], messages[2 * sides : -1], messages[-1]
    near_lines = [plan.near_rows(line) for line in lines]
    own_spot = call(spot_kernel, shape(own_spot.shape, f32), [], [own_spot, near_lines[0]], in_specs=[VMEM, ANY])
    far = [far_block] + [plan.far_rows(message) for message in messages[:sides]]
    near = [plan.near_rows(message) for message in passed] + [near_block]
    own = [object_field] + passed
    def first_layout(refs, t):
        starts = [1] + plan.halo_tiles(t)
        own, far, near = refs[: 1 + sides], refs[1 + sides : 2 + 2 * sides], refs[2 + 2 * sides :]
        return lay_out(own, starts), lay_out(far, starts), lay_out(near, plan.halo_tiles(t) + [1])

    def later_layout(refs, t):
        own, far, near = refs[: 2 + sides], refs[2 + sides : 4 + 2 * sides], refs[4 + 2 * sides :]

        def tiles(group):
            middle = [([group[step % 2]], step // 2, 1, plan.mid_start(t) + step) for step in range(plan.mid_tiles)]
            return middle + lay_out(group[2:], plan.pair_starts(t))

        counts = [2] * sides + [plan.mid_tiles]
        return tiles(own), tiles(far), lay_out_rows(near, counts, plan.pair_starts(t) + [plan.mid_start(t)])

    layout = first_layout

    third = half // 24 * 8
    near_heights = [half - 2 * third, third, third]
    patch_heights = [third + 16, third - 16, half - 2 * third]
    for sweep in range(ITERS):
        pieces = own + far + near
        inner, outer, outer_far = [], [], []
        for slot in range(slots):
            last = slot == slots - 1
            earlier = outer if last else []
            patch = shape((2, half, size), f32)
            halves = 2 if last else 0
            inner_part, *copies = call(
                lambda *refs, slot=slot, layout=layout, copied=len(earlier), halves=halves: term_kernel(
                    plan, slot, layout, len(pieces), copied, halves, slots, *refs
                ),
                [patch]
                + ([shape((2, half, LANES), f32)] * halves or [patch])
                + [shape((2 * slots, rows, size), f32) for rows in patch_heights if last],
                [pltpu.VMEM((3, 3, 2, half, LANES), f32)]
                + [pltpu.VMEM((2, half, size), f32)] * (halves > 0),
                [own_spot, *pieces, *earlier, rolled, ordered, tables],
            )
            outer_part = None if halves else copies.pop(0)
            outer_halves, copies = copies[:halves], copies[halves:]
            inner.append(inner_part)
            outer.append(outer_part)
            outer_far.append([plan.far_rows(part) for part in outer_halves] if halves else plan.far_rows(outer_part))
            if sweep == 0 and last:
                info = call(
                    lambda *refs: info_kernel(plan, *refs),
                    shape((3 * (sides + 1), LANES), jnp.int32),
                    [pltpu.VMEM((3 * (sides + 1), 8, LANES), jnp.int32), dma],
                    lines + far[1:] + near_lines + [inner_part],
                    in_specs=[VMEM] * (3 * sides) + [ANY],
                    out_specs=SMEM,
                )
        outer_near = [plan.near_rows(copy) for copy in copies]
        if sweep == 0:
            inverse = call(
                lambda *refs: light_kernel(plan, slots, *refs),
                shape((half, width), f32),
                [
                    pltpu.VMEM((2 * size + 8, size), f32),
                    pltpu.VMEM((half, width + 2 * plan.own * LANES), f32),
                ],
                [info, probe_field, copies[0]],
                in_specs=[SMEM, VMEM, ANY],
            )
        early = call(
            lambda *refs: early_sum_kernel(plan, slots, *refs),
            shape((2, half, width), f32),
            [],
            [info, *inner, *outer_near],
        )
        early, base, mask = call(
            lambda *refs, layout=layout: base_kernel(plan, slots, layout, len(pieces), *refs),
            [shape((2, half, width), f32)] * 2 + [shape((half, width), f32)],
            [],
            [info, early, inverse, *outer_far[:-1], *pieces],
        )
        if sweep < ITERS - 1:
            sums = call(
                lambda *refs: boundary_kernel(plan, *refs),
                [shape((2, half, 2 * LANES), f32)] * sides,
                [],
                [early, *outer_far[-1], mask],
            )
            received = plan.across(sums)
            middles = [
                call(
                    lambda *refs, parity=parity: middle_kernel(plan, parity, *refs),
                    shape((2, half + 8 * (1 - parity), (plan.mid_tiles + 1 - parity) // 2 * LANES), f32),
                    [],
                    [base, outer_far[-1][parity], mask, inverse, after],
                    in_specs=[VMEM] * 4 + [ANY],
                )
                for parity, after in ((0, base), (1, sums[0]))
            ]
            far_middles = [plan.far_rows(middle) for middle in middles]
            near_runs = [shape((2, rows, (2 * sides + plan.mid_tiles) * LANES), f32) for rows in near_heights]
            updated = call(
                lambda *refs: pair_kernel(plan, *refs),
                [shape((2, half, 2 * LANES), f32)] * sides + near_runs,
                [],
                [base, early, inverse, *middles, *sums, *received],
            )
            pairs = updated[:sides]
            own = middles + pairs
            far = far_middles + [plan.far_rows(piece) for piece in pairs]
            near = [plan.near_rows(piece) for piece in updated[sides:]]
            layout = later_layout
            own_spot = call(
                spot_kernel,
                shape(own_spot.shape, f32),
                [],
                [own_spot, far_middles[0]],
                in_specs=[VMEM, ANY],
                flops=10**11,
            )
    sums = call(
        lambda *refs: halo_sum_kernel(plan, *refs),
        [shape((2, half, LANES), f32)] * sides,
        [],
        [early, mask, *outer_far[-1][:sides]],
    )
    nearly, *bases = call(
        lambda *refs: last_kernel(plan, *refs),
        [shape((2, half, block_cols), f32)] + [shape((2, half, LANES), f32)] * sides,
        [pltpu.VMEM((2, half, block_cols), f32), dma((plan.own,))],
        [base, mask, inverse, sums[0], *outer_far[-1]],
        in_specs=[VMEM] * 3 + [ANY] + [VMEM] * 2,
        out_specs=[HBM] + [VMEM] * sides,
    )
    received = plan.across(sums)
    return call(
        lambda *refs: edge_kernel(plan, *refs),
        shape(nearly.shape, f32),
        [pltpu.VMEM((sides, 2, half, LANES), f32), dma((sides,))],
        [inverse, *bases, *received, nearly],
        in_specs=[VMEM] * (1 + 2 * sides) + [HBM],
        out_specs=HBM,
        input_output_aliases={1 + 2 * sides: 0},
    )


def solution(mesh):
    sizes = dict(mesh.shape)

    def per_device(object_field, *rest):
        plan = Plan(sizes["sx"], sizes["sy"], *object_field.shape[1:])
        return on_device(plan, object_field, *rest)

    return jax.shard_map(
        per_device,
        mesh=mesh,
        in_specs=(
            P(None, "sx", "sy"),
            P(),
            P("sx", "sy", None, None, None),
            P("sx", "sy", None, None),
            P(None, "sy"),
        ),
        out_specs=P(None, "sx", "sy"),
        check_vma=False,
    )
```

```python
import math

import jax
import jax.numpy as jnp
import ml_dtypes
import numpy as np
from jax import lax
from jax.experimental import pallas as pl
from jax.experimental.pallas import tpu as pltpu
from jax.sharding import PartitionSpec as P

ITERS = 2
SMOOTH = 1.0
DAMPING = 1.0
LANES = 128
VMEM_BYTES = 12 * 1024 * 1024

VMEM = pl.BlockSpec(memory_space=pltpu.VMEM)
SMEM = pl.BlockSpec(memory_space=pltpu.SMEM)
HBM = pl.BlockSpec(memory_space=pltpu.HBM)
ANY = pl.BlockSpec(memory_space=pl.ANY)


def split_numpy(table):
    high = table.astype(np.float32).astype(ml_dtypes.bfloat16)
    low = (table - high.astype(np.float64)).astype(ml_dtypes.bfloat16)
    return high, low


def dft_tables(length):
    half = length // 2
    index = np.arange(half)
    tables = []
    for parity in range(2):
        angles = 2.0 * math.pi / length * (index[:, None] * (2 * index[None, :] + parity) % length)
        cosine = np.cos(angles) / math.sqrt(length)
        sine = np.sin(angles) / math.sqrt(length)
        forward = np.block([[cosine, -sine], [sine, cosine]])
        tables.append([split_numpy(forward), split_numpy(forward.T)])
    return np.array(tables, dtype=ml_dtypes.bfloat16)


def parity_order(length):
    half = length // 2
    order = np.zeros((length, length))
    for index in range(length):
        order[index, index % 2 * half + index // 2] = 1.0
    return np.stack([order, order.T]).astype(ml_dtypes.bfloat16)


def split(values):
    high = values.astype(jnp.bfloat16)
    low = (values - high.astype(jnp.float32)).astype(jnp.bfloat16)
    return high, low


def times_table(values, table):
    high, low = split(values)
    left = jnp.concatenate([high, low, high], axis=1)
    right = jnp.concatenate([table[0], table[0], table[1]], axis=0)
    return jnp.dot(left, right, preferred_element_type=jnp.float32)


def table_times(table, values):
    high, low = split(values)
    left = jnp.concatenate([table[0], table[0], table[1]], axis=1)
    right = jnp.concatenate([high, low, high], axis=0)
    return jnp.dot(left, right, preferred_element_type=jnp.float32)


class Plan:
    def __init__(self, sx_size, sy_size, block_rows, block_cols):
        self.rows = block_rows
        self.sx_size = sx_size
        self.sy_size = sy_size
        self.own = block_cols // LANES
        self.tiles = self.own + 2
        self.paired = sy_size == 2
        self.sides = 1 if self.paired else 2

    def rights(self, t):
        return [1 - t] if self.paired else [0, 1]

    def pair_starts(self, t):
        return [right * (self.tiles - 2) for right in self.rights(t)]

    def halo_tiles(self, t):
        return [right * (self.tiles - 1) for right in self.rights(t)]

    def edge_tiles(self, t):
        return [1 + right * (self.tiles - 3) for right in self.rights(t)]

    def first_parity(self, t):
        return 1 - t if self.paired else 0

    def mid_start(self, t):
        return 1 + t if self.paired else 2

    @property
    def mid_tiles(self):
        return self.tiles - 3 if self.paired else self.tiles - 4

    def across(self, values, axis_name="sy"):
        if self.paired:
            return [lax.ppermute(values[0], axis_name, [(0, 1), (1, 0)])]
        ends = self.sy_size - 1
        return [
            lax.ppermute(values[1], axis_name, [(i, i + 1) for i in range(ends)]),
            lax.ppermute(values[0], axis_name, [(i + 1, i) for i in range(ends)]),
        ]

    def far_rows(self, values):
        rows, columns = self.sx_size, self.sy_size
        pairs = [(i * columns + t, (i + 1) * columns + t) for i in range(1, rows - 1, 2) for t in range(columns)]
        for i in (0, rows - 1):
            pairs += [(i * columns + t, i * columns + t + 1) for t in range(0, columns - 1, 2)]
        return lax.ppermute(values, ("sx", "sy"), pairs + [(j, i) for i, j in pairs])

    def near_rows(self, values):
        return lax.ppermute(values, "sx", [(i, i ^ 1) for i in range(self.sx_size)])

    def outermost(self, s):
        return (s == 0) | (s == self.sx_size - 1)


def far_side(s):
    return 2 * (s % 2) - 1


def lanes(tile, count=1):
    if isinstance(tile, int):
        return pl.ds(tile * LANES, count * LANES)
    return pl.ds(pl.multiple_of(tile * LANES, LANES), count * LANES)


def pick_tile(plan, target, pieces, tile, t):
    rows = target.shape[1]
    if plan.paired:

        @pl.when(tile == (plan.tiles - 1) * t)
        def _():
            target[...] = jnp.zeros(target.shape, jnp.float32)

    for runs, offset, count, start in pieces:

        @pl.when((tile >= start) & (tile < start + count))
        def _(runs=runs, offset=offset, start=start):
            line = 0
            for run in runs:
                height = min(run.shape[1], rows - line)
                target[:, line : line + height] = run[:, :height, lanes(tile - start + offset)]
                line += height


def lay_out(refs, starts):
    return [([ref], 0, ref.shape[2] // LANES, start) for ref, start in zip(refs, starts)]


def lay_out_rows(runs, counts, starts):
    return [(runs, sum(counts[:k]), count, start) for k, (count, start) in enumerate(zip(counts, starts))]


def rows_at(ref, start, count):
    offset = start % 8
    values = ref[pl.ds(pl.multiple_of(start - offset, 8), count + 8)]
    return pltpu.roll(values, (count + 8 - offset) % (count + 8), 0)[:count]


def here():
    return lax.axis_index("sx"), lax.axis_index("sy")


def info_rows(centres, count):
    lane = lax.broadcasted_iota(jnp.int32, (8, LANES), 1)
    slots = centres.shape[0]
    values = [centres[slot, axis] for slot in range(slots) for axis in range(2)] + [count]
    line = jnp.zeros((8, LANES), jnp.int32)
    for index, value in enumerate(values):
        line = jnp.where(lane == index, value, line)
    return line.astype(jnp.float32)


def edge_message_kernel(plan, block, centres, counts, *rest):
    messages, sems = rest[: plan.sides], rest[plan.sides]
    s, t = here()
    half = block.shape[1]
    copies = [
        pltpu.make_async_copy(block.at[:, :, lanes(tile - 1)], message.at[:, :half], sems.at[side])
        for side, (message, tile) in enumerate(zip(messages, plan.edge_tiles(t)))
    ]
    for copy in copies:
        copy.start()
    rows = info_rows(centres, counts[s])
    for message in messages:
        message[0, half:] = rows
        message[1, half:] = rows
    for copy in copies:
        copy.wait()


def halo_message_kernel(plan, centres, counts, block, _, *rest):
    sides = plan.sides
    received, far, halos, infos = (rest[k * sides : (k + 1) * sides] for k in range(4))
    near = rest[4 * sides : -1]
    own = info_rows(centres, counts[lax.axis_index("sx")])
    rest[-1][...] = own
    upper_line = lax.broadcasted_iota(jnp.int32, own.shape, 0) == 0
    for source, message, halo, info in zip(received, far, halos, infos):
        rows = halo.shape[1]
        both = jnp.where(upper_line, own, pltpu.roll(source[0, rows : rows + 8], 1, 0))
        halo[...] = source[:, :rows]
        info[...] = both
        message[:, :rows] = source[:, :rows]
        message[0, rows:] = both
        message[1, rows:] = both
    line = 0
    for run in near:
        rows = run.shape[1]
        for side, halo in enumerate(halos):
            run[:, :, side * LANES : (side + 1) * LANES] = halo[:, line : line + rows]
        run[:, :, sides * LANES :] = block[:, line : line + rows]
        line += rows


def pair_kernel(plan, base, early, inverse, middle, *rest):
    sides = plan.sides
    sums, received, results = (rest[k * sides : (k + 1) * sides] for k in range(3))
    near = rest[3 * sides :]
    _, t = here()

    def copy(values, offset):
        line = 0
        for run in near:
            rows = run.shape[1]
            run[:, :, offset : offset + values.shape[2]] = values[:, line : line + rows]
            line += rows

    for side, (total, other, result, start) in enumerate(zip(sums, received, results, plan.pair_starts(t))):
        where = lanes(start, 2)
        missing = total[...] + other[...] - early[:, :, where]
        result[...] = base[:, :, where] - missing * inverse[:, where][None]
        copy(result, 2 * LANES * side)
    copy(middle, 2 * LANES * sides)


def prepare_kernel(centres, probe, amps, order, rolled, ordered, padded):
    size = probe.shape[1]
    half = size // 2
    padded[:, :half] = jnp.zeros((2, half, size), jnp.float32)
    padded[:, half + size :] = jnp.zeros((2, half + 8, size), jnp.float32)
    padded[:, half : half + size] = probe[...]
    for slot in range(amps.shape[0]):
        row = centres[slot, 0]
        col = centres[slot, 1]
        for part in range(2):
            shape = padded.at[part]
            upper = rows_at(shape, half - row, half) + rows_at(shape, half + size - row, half)
            lower = rows_at(shape, size - row, half)
            rolled[slot, part] = pltpu.roll(jnp.concatenate([upper, lower], axis=0), col % LANES, 1)
        high, low = split(amps[slot])
        across = jnp.dot(
            jnp.concatenate([high, low], axis=1),
            jnp.concatenate([order[0], order[0]], axis=0),
            preferred_element_type=jnp.float32,
        )
        high, low = split(across)
        ordered[slot] = jnp.dot(
            jnp.concatenate([order[1], order[1]], axis=1),
            jnp.concatenate([high, low], axis=0),
            preferred_element_type=jnp.float32,
        )


def info_kernel(plan, *rest):
    home, far, other = (rest[k * plan.sides : (k + 1) * plan.sides] for k in range(3))
    _, info, known, sem = rest[3 * plan.sides :]
    s, _ = here()
    upper = s % 2 == 0
    width = plan.sides + 1

    def lines(messages):
        return [messages[0]] + [pltpu.roll(message, 7, 0) for message in messages]

    own = lines([line[...] for line in home])
    near = lines([line[...] for line in other])
    far = lines([jnp.where(plan.outermost(s), 0.0, message[0, plan.rows :]) for message in far])
    for turn in range(width):
        for kind, line in ((0, jnp.where(upper, far[turn], near[turn])), (1, own[turn]), (2, jnp.where(upper, near[turn], far[turn]))):
            known[kind * width + turn] = line.astype(jnp.int32)
    copy = pltpu.make_async_copy(known.at[:, 0], info, sem)
    copy.start()
    copy.wait()


def light_kernel(plan, slots, info, probe, _, inverse, padded, canvas):
    size = probe.shape[1]
    half = size // 2
    _, t = here()
    padded[:half] = jnp.zeros((half, size), jnp.float32)
    padded[half + size :] = jnp.zeros((half + 8, size), jnp.float32)
    padded[half : half + size] = probe[0] * probe[0] + probe[1] * probe[1]
    canvas[...] = jnp.zeros(canvas.shape, jnp.float32)
    reach = plan.sides + 1
    spare = jnp.zeros((half, LANES), jnp.float32)
    for down in (-1, 0, 1):

        def add(step, carry, down=down):
            turn = step // slots
            slot = step % slots
            over = turn * (1 - 2 * t) if plan.paired else jnp.where(turn == 0, 0, 2 * turn - 3)
            index = (down + 1) * reach + turn

            @pl.when(slot < info[index, 2 * slots])
            def _():
                row = info[index, 2 * slot]
                col = info[index, 2 * slot + 1]
                power = rows_at(padded, size - half * down - row, half)
                shifted = pltpu.roll(jnp.concatenate([power, spare], axis=1), col % LANES, 1)
                first = col // LANES + plan.own * (over + 1)
                canvas[:, lanes(first, 3)] += shifted

            return carry

        lax.fori_loop(0, reach * slots, add, 0)
    inverse[...] = 1.0 / (canvas[:, lanes(plan.own, plan.tiles)] + DAMPING)


def term_kernel(plan, slot, layout, pieces, copied, halves, slots, spot, *rest):
    refs, rest = rest[:pieces], rest[pieces:]
    earlier, (probe, amps, tables, inner), rest = rest[:copied], rest[copied : copied + 4], rest[copied + 4 :]
    if halves:
        outer, rest = rest[-1], rest[:-1]
    else:
        outer, rest = rest[0], rest[1:]
    outer_halves, near_outers, picked = rest[:halves], rest[halves:-1], rest[-1]
    size = probe.shape[2]
    half = size // 2
    s, t = here()
    line = spot[0:1]
    lane = lax.broadcasted_iota(jnp.int32, line.shape, 1)
    entries = (2 * slot, 2 * slot + 1, 2 * slots)
    row, col, count = (jnp.sum(jnp.where(lane == k, line, 0.0)).astype(jnp.int32) for k in entries)
    alive = slot < count

    @pl.when(jnp.logical_not(alive))
    def _():
        outer[...] = jnp.zeros(outer.shape, jnp.float32)
        inner[...] = jnp.zeros(inner.shape, jnp.float32)

    @pl.when(alive)
    def _():
        tile = col // LANES
        first = tile % 2
        rest_col = col % LANES
        from_tile = lax.broadcasted_iota(jnp.int32, (half, LANES), 1) >= rest_col
        from_upper = lax.broadcasted_iota(jnp.int32, (half, LANES), 0) >= row
        side = far_side(s)
        own, far, near = layout(refs, t)
        for kind, source in ((1, own), (1 + side, far), (1 - side, near)):
            for step in range(3):
                pick_tile(plan, picked.at[kind, step], source, tile + step, t)

        @pl.when(plan.outermost(s))
        def _():
            picked[1 + side] = jnp.zeros(picked.shape[1:], jnp.float32)

        def edge(kind, part):
            return jnp.where(from_tile, picked[kind, 0, part], picked[kind, 2, part])

        def across(edges, middles, rows):
            sums, differences = [], []
            shares = []
            for columns, (real, imag) in ((slice(0, half), edges), (slice(half, size), middles)):
                probe_real, probe_imag = probe[slot, 0, rows, columns], probe[slot, 1, rows, columns]
                shares.append((probe_real * real - probe_imag * imag, probe_real * imag + probe_imag * real))
            for part in range(2):
                sums.append(shares[0][part] + shares[1][part])
                differences.append(shares[0][part] - shares[1][part])
            return [
                times_table(jnp.concatenate(parts, axis=1), tables[parity, 0])
                for parity, parts in enumerate((sums, differences))
            ]

        lower = across(
            [edge(1, part) for part in range(2)], [picked[1, 1, part] for part in range(2)], slice(half, size)
        )
        upper = across(
            [jnp.where(from_upper, edge(0, part), edge(2, part)) for part in range(2)],
            [jnp.where(from_upper, picked[0, 1, part], picked[2, 1, part]) for part in range(2)],
            slice(0, half),
        )
        halves = []
        for sign in (1.0, -1.0):
            rows = [top + sign * bottom for top, bottom in zip(upper, lower)]
            halves.append(
                jnp.concatenate(
                    [jnp.concatenate([row[:, part] for row in rows], axis=1) for part in (slice(0, half), slice(half, size))],
                    axis=0,
                )
            )
        back = []
        for parity in range(2):
            pattern = table_times(tables[parity, 1], halves[parity])
            far_real = pattern[:half]
            far_imag = pattern[half:]
            amplitude = amps[slot, parity * half : (parity + 1) * half]
            factor = 1.0 - amplitude * lax.rsqrt(far_real * far_real + far_imag * far_imag + SMOOTH)
            miss = jnp.concatenate([far_real * factor, far_imag * factor], axis=0)
            back.append(table_times(tables[parity, 0], miss))
        real = jnp.concatenate([back[0][:half] + back[1][:half], back[0][:half] - back[1][:half]], axis=0)
        imag = jnp.concatenate([back[0][half:] + back[1][half:], back[0][half:] - back[1][half:]], axis=0)
        both = []
        for parity in range(2):
            columns = slice(parity * half, (parity + 1) * half)
            both.append(times_table(jnp.concatenate([real[:, columns], imag[:, columns]], axis=1), tables[parity, 1]))
        near_real = jnp.concatenate([both[0][:, :half] + both[1][:, :half], both[0][:, :half] - both[1][:, :half]], axis=1)
        near_imag = jnp.concatenate([both[0][:, half:] + both[1][:, half:], both[0][:, half:] - both[1][:, half:]], axis=1)
        probe_real = probe[slot, 0]
        probe_imag = probe[slot, 1]
        for part, term in enumerate((probe_real * near_real + probe_imag * near_imag, probe_real * near_imag - probe_imag * near_real)):
            for place, columns in ((first, slice(0, half)), (1 - first, slice(half, size))):
                outer[part, :, lanes(place)] = term[:half, columns]
                inner[part, :, lanes(place)] = term[half:, columns]

    for index, target in enumerate(outer_halves):
        first = plan.first_parity(t)
        target[...] = outer[:, :, lanes(first if index == 0 else 1 - first)]
    for index, source in enumerate((*earlier, outer)):
        line = 0
        for target in near_outers:
            rows = target.shape[1]
            target[2 * index : 2 * index + 2] = source[:, line : line + rows]
            line += rows


class Patch:
    def __init__(self, plan, info, s, patch, slot, down, far=False):
        runs = patch if isinstance(patch, (list, tuple)) else [patch]
        half = sum(run.shape[1] for run in runs)
        index = (1 if down is None else 1 + down) * (plan.sides + 1)
        row = info[index, 2 * slot]
        col = info[index, 2 * slot + 1]
        self.runs = runs
        self.tile = col // LANES
        self.first = self.tile % 2
        self.rest = col % LANES
        self.lane = lax.broadcasted_iota(jnp.int32, (half, LANES), 1)
        self.from_tile = self.lane >= self.rest
        self.rows = None
        if down is not None:
            line = lax.broadcasted_iota(jnp.int32, (half, LANES), 0)
            after = jnp.where(down > 0, half, row)
            if far:
                after = jnp.where(plan.outermost(s), 0, after)
            self.rows = (line >= jnp.where(down > 0, row, 0)) & (line < after)

    def lines(self, part, place):
        values = jnp.concatenate([run[part, :, lanes(place)] for run in self.runs], axis=0)
        return values if self.rows is None else jnp.where(self.rows, values, 0.0)

    def tiles(self, part):
        edge = self.lines(part, self.first)
        middle = self.lines(part, 1 - self.first)
        return jnp.where(self.from_tile, edge, 0.0), middle, jnp.where(self.from_tile, 0.0, edge)

    def add_to(self, canvas):
        for part in range(2):
            for step, values in enumerate(self.tiles(part)):
                canvas[part, :, lanes(self.tile + step)] += values

    def mask(self, tile):
        step = tile - self.tile
        first = jnp.where(step == 0, self.rest, 0)
        after = jnp.where(step == 2, self.rest, jnp.where((step < 0) | (step > 2), 0, LANES))
        inside = (self.lane >= first) & (self.lane < after)
        if self.rows is not None:
            inside = inside & self.rows
        return jnp.where(inside, 1.0, 0.0)


def part_of(plan, patch, mask, part, tile):
    if isinstance(patch, (list, tuple)):
        first = plan.first_parity(lax.axis_index("sy"))
        values = jnp.where(tile % 2 == first, patch[0][part], patch[1][part])
    else:
        values = patch[part, :, lanes(tile % 2)]
    return values * mask[:, lanes(tile)]


def early_sum_kernel(plan, slots, info, *rest):
    inner, near, canvas = rest[:slots], rest[slots:-1], rest[-1]
    s, _ = here()
    canvas[...] = jnp.zeros(canvas.shape, jnp.float32)
    for slot in range(slots):
        Patch(plan, info, s, inner[slot], slot, None).add_to(canvas)
        runs = [run.at[2 * slot : 2 * slot + 2] for run in near]
        Patch(plan, info, s, runs, slot, -far_side(s)).add_to(canvas)


def base_kernel(plan, slots, layout, pieces, info, early, inverse, *rest):
    far, refs, (canvas, base, mask) = rest[: slots - 1], rest[slots - 1 : slots - 1 + pieces], rest[slots - 1 + pieces :]
    s, t = here()
    canvas[...] = early[...]
    for slot in range(slots - 1):
        Patch(plan, info, s, far[slot], slot, far_side(s), True).add_to(canvas)
    last = Patch(plan, info, s, canvas, slots - 1, far_side(s), True)
    for tile in range(plan.tiles):
        where = lanes(tile)
        pick_tile(plan, base.at[:, :, where], layout(refs, t)[0], tile, t)
        base[:, :, where] -= canvas[:, :, where] * inverse[:, where][None]
        mask[:, where] = last.mask(tile)


def take_off(plan, patch, mask, target, base, inverse, tile):
    for part in range(2):
        target[part] = base[part, :, lanes(tile)] - part_of(plan, patch, mask, part, tile) * inverse[:, lanes(tile)]


def middle_kernel(plan, base, patch, mask, inverse, _, middle):
    _, t = here()
    for step in range(plan.mid_tiles):
        take_off(plan, patch, mask, middle.at[:, :, lanes(step)], base, inverse, plan.mid_start(t) + step)


def boundary_kernel(plan, early, patch, mask, *sums):
    _, t = here()
    for total, start in zip(sums, plan.pair_starts(t)):
        for step in range(2):
            tile = start + step
            for part in range(2):
                total[part, :, lanes(step)] = early[part, :, lanes(tile)] + part_of(plan, patch, mask, part, tile)


def halo_sum_kernel(plan, early, mask, *rest):
    halves, sums = rest[: plan.sides], rest[plan.sides :]
    _, t = here()
    for half, total, tile in zip(halves, sums, plan.halo_tiles(t)):
        for part in range(2):
            total[part] = early[part, :, lanes(tile)] + half[part] * mask[:, lanes(tile)]


def last_kernel(plan, base, mask, inverse, _, first, second, *rest):
    nearly, bases, (current, sems) = rest[0], rest[1 : 1 + plan.sides], rest[1 + plan.sides :]
    patch = [first, second]
    _, t = here()
    copies = []
    for step in range(plan.own):
        where = lanes(step)
        take_off(plan, patch, mask, current.at[:, :, where], base, inverse, 1 + step)
        copies.append(pltpu.make_async_copy(current.at[:, :, where], nearly.at[:, :, where], sems.at[step]))
        copies[-1].start()
    for edge, tile in zip(bases, plan.edge_tiles(t)):
        edge[...] = current[:, :, lanes(tile - 1)]
    for copy in copies:
        copy.wait()


def edge_kernel(plan, inverse, *rest):
    bases, received = rest[: plan.sides], rest[plan.sides : 2 * plan.sides]
    _, result, sums, sems = rest[2 * plan.sides :]
    _, t = here()
    copies = []
    for side, tile in enumerate(plan.edge_tiles(t)):
        sums[side] = bases[side][...] - received[side][...] * inverse[:, lanes(tile)][None]
        copies.append(pltpu.make_async_copy(sums.at[side], result.at[:, :, lanes(tile - 1)], sems.at[side]))
        copies[-1].start()
    for copy in copies:
        copy.wait()


def call(kernel, outs, scratch, ins, flops=10**5, size=10**4, in_specs=None, out_specs=None, **options):
    result = pl.pallas_call(
        kernel,
        out_shape=outs,
        in_specs=in_specs or [SMEM if value.dtype == jnp.int32 else VMEM for value in ins],
        out_specs=out_specs or jax.tree.map(lambda _: VMEM, outs),
        scratch_shapes=scratch,
        compiler_params=pltpu.CompilerParams(vmem_limit_bytes=VMEM_BYTES),
        cost_estimate=pl.CostEstimate(flops=flops, bytes_accessed=size, transcendentals=0),
        **options,
    )(*ins)
    return list(result) if isinstance(outs, list) else result


def on_device(plan, object_field, probe_field, amplitudes, centres, counts):
    f32 = jnp.float32
    shape = jax.ShapeDtypeStruct
    size = probe_field.shape[1]
    half = size // 2
    slots = amplitudes.shape[2]
    block_rows = object_field.shape[1]
    block_cols = object_field.shape[2]
    assert block_rows == half and block_cols % (2 * LANES) == 0 and half == LANES
    width = plan.tiles * LANES
    sides = plan.sides
    spots = centres[0, 0]
    counts = counts.reshape(-1)
    own_amps = amplitudes[0, 0]
    tables = jnp.asarray(dft_tables(size))
    order = jnp.asarray(parity_order(size))
    dma = pltpu.SemaphoreType.DMA

    messages = call(
        lambda *refs: edge_message_kernel(plan, *refs),
        [shape((2, half + 8, LANES), f32)] * sides,
        [dma((sides,))],
        [object_field, spots, counts],
        in_specs=[HBM, SMEM, SMEM],
    )
    halos = plan.across(messages)
    far_block = plan.far_rows(object_field)
    rolled, ordered = call(
        prepare_kernel,
        [shape((slots, 2, size, size), f32), shape((slots, size, size), f32)],
        [pltpu.VMEM((2, 2 * size + 8, size), f32)],
        [spots, probe_field, own_amps, order],
    )
    third = half // 24 * 8
    near_heights = [half - 2 * third, third, third]
    patch_heights = [third + 16, third - 16, half - 2 * third]
    messages = call(
        lambda *refs: halo_message_kernel(plan, *refs),
        [shape((2, half + 8, LANES), f32)] * sides
        + [shape((2, half, LANES), f32)] * sides
        + [shape((8, LANES), f32)] * sides
        + [shape((2, rows, (sides + plan.own) * LANES), f32) for rows in near_heights]
        + [shape((8, LANES), f32)],
        [],
        [spots, counts, object_field, ordered, *halos],
        in_specs=[SMEM, SMEM, VMEM, ANY] + [VMEM] * sides,
    )
    passed, lines, own_spot = messages[sides : 2 * sides], messages[2 * sides : 3 * sides], messages[-1]
    near_lines = [plan.near_rows(line) for line in lines]
    far = [far_block] + [plan.far_rows(message) for message in messages[:sides]]
    near = [plan.near_rows(run) for run in messages[3 * sides : -1]]
    own = [object_field] + passed
    def runs_layout(refs, main, side_starts):
        starts = [main] + side_starts
        return lay_out(refs[: 1 + sides], starts), lay_out(refs[1 + sides : 2 + 2 * sides], starts)

    def first_layout(refs, t):
        own, far = runs_layout(refs, 1, plan.halo_tiles(t))
        counts = [1] * sides + [plan.own]
        return own, far, lay_out_rows(refs[2 + 2 * sides :], counts, plan.halo_tiles(t) + [1])

    def later_layout(refs, t):
        own, far = runs_layout(refs, plan.mid_start(t), plan.pair_starts(t))
        counts = [2] * sides + [plan.mid_tiles]
        return own, far, lay_out_rows(refs[2 + 2 * sides :], counts, plan.pair_starts(t) + [plan.mid_start(t)])

    layout = first_layout

    for sweep in range(ITERS):
        pieces = own + far + near
        inner, outer, outer_far = [], [], []
        for slot in range(slots):
            last = slot == slots - 1
            earlier = outer if last else []
            patch = shape((2, half, size), f32)
            halves = 2 if last and sweep == ITERS - 1 else 0
            inner_part, *copies = call(
                lambda *refs, slot=slot, layout=layout, copied=len(earlier), halves=halves: term_kernel(
                    plan, slot, layout, len(pieces), copied, halves, slots, *refs
                ),
                [patch]
                + ([shape((2, half, LANES), f32)] * halves or [patch])
                + [shape((2 * slots, rows, size), f32) for rows in patch_heights if last],
                [pltpu.VMEM((3, 3, 2, half, LANES), f32)]
                + [pltpu.VMEM((2, half, size), f32)] * (halves > 0),
                [own_spot, *pieces, *earlier, rolled, ordered, tables],
            )
            outer_part = None if halves else copies.pop(0)
            outer_halves, copies = copies[:halves], copies[halves:]
            inner.append(inner_part)
            outer.append(outer_part)
            outer_far.append([plan.far_rows(part) for part in outer_halves] if halves else plan.far_rows(outer_part))
            if sweep == 0 and last:
                info = call(
                    lambda *refs: info_kernel(plan, *refs),
                    shape((3 * (sides + 1), LANES), jnp.int32),
                    [pltpu.VMEM((3 * (sides + 1), 8, LANES), jnp.int32), dma],
                    lines + far[1:] + near_lines + [outer_part],
                    in_specs=[VMEM] * (3 * sides) + [ANY],
                    out_specs=SMEM,
                )
        outer_near = [plan.near_rows(copy) for copy in copies]
        if sweep == 0:
            inverse = call(
                lambda *refs: light_kernel(plan, slots, *refs),
                shape((half, width), f32),
                [
                    pltpu.VMEM((2 * size + 8, size), f32),
                    pltpu.VMEM((half, width + 2 * plan.own * LANES), f32),
                ],
                [info, probe_field, copies[0]],
                in_specs=[SMEM, VMEM, ANY],
            )
        early = call(
            lambda *refs: early_sum_kernel(plan, slots, *refs),
            shape((2, half, width), f32),
            [],
            [info, *inner, *outer_near],
        )
        early, base, mask = call(
            lambda *refs, layout=layout: base_kernel(plan, slots, layout, len(pieces), *refs),
            [shape((2, half, width), f32)] * 2 + [shape((half, width), f32)],
            [],
            [info, early, inverse, *outer_far[:-1], *pieces],
        )
        if sweep < ITERS - 1:
            sums = call(
                lambda *refs: boundary_kernel(plan, *refs),
                [shape((2, half, 2 * LANES), f32)] * sides,
                [],
                [early, outer_far[-1], mask],
            )
            received = plan.across(sums)
            middle = call(
                lambda *refs: middle_kernel(plan, *refs),
                shape((2, half, plan.mid_tiles * LANES), f32),
                [],
                [base, outer_far[-1], mask, inverse, sums[0]],
                in_specs=[VMEM] * 4 + [ANY],
            )
            far_middle = plan.far_rows(middle)
            near_runs = [shape((2, rows, (2 * sides + plan.mid_tiles) * LANES), f32) for rows in near_heights]
            updated = call(
                lambda *refs: pair_kernel(plan, *refs),
                [shape((2, half, 2 * LANES), f32)] * sides + near_runs,
                [],
                [base, early, inverse, middle, *sums, *received],
            )
            pairs = updated[:sides]
            own = [middle] + pairs
            far = [far_middle] + [plan.far_rows(piece) for piece in pairs]
            near = [plan.near_rows(piece) for piece in updated[sides:]]
            layout = later_layout
    sums = call(
        lambda *refs: halo_sum_kernel(plan, *refs),
        [shape((2, half, LANES), f32)] * sides,
        [],
        [early, mask, *outer_far[-1][:sides]],
    )
    nearly, *bases = call(
        lambda *refs: last_kernel(plan, *refs),
        [shape((2, half, block_cols), f32)] + [shape((2, half, LANES), f32)] * sides,
        [pltpu.VMEM((2, half, block_cols), f32), dma((plan.own,))],
        [base, mask, inverse, sums[0], *outer_far[-1]],
        in_specs=[VMEM] * 3 + [ANY] + [VMEM] * 2,
        out_specs=[HBM] + [VMEM] * sides,
    )
    received = plan.across(sums)
    return call(
        lambda *refs: edge_kernel(plan, *refs),
        shape(nearly.shape, f32),
        [pltpu.VMEM((sides, 2, half, LANES), f32), dma((sides,))],
        [inverse, *bases, *received, nearly],
        in_specs=[VMEM] * (1 + 2 * sides) + [HBM],
        out_specs=HBM,
        input_output_aliases={1 + 2 * sides: 0},
    )


def solution(mesh):
    sizes = dict(mesh.shape)

    def per_device(object_field, *rest):
        plan = Plan(sizes["sx"], sizes["sy"], *object_field.shape[1:])
        return on_device(plan, object_field, *rest)

    return jax.shard_map(
        per_device,
        mesh=mesh,
        in_specs=(
            P(None, "sx", "sy"),
            P(),
            P("sx", "sy", None, None, None),
            P("sx", "sy", None, None),
            P(None, "sy"),
        ),
        out_specs=P(None, "sx", "sy"),
        check_vma=False,
    )
```

```python
import math

import jax
import jax.numpy as jnp
import ml_dtypes
import numpy as np
from jax import lax
from jax.experimental import pallas as pl
from jax.experimental.pallas import tpu as pltpu
from jax.sharding import PartitionSpec as P

ITERS = 2
SMOOTH = 1.0
DAMPING = 1.0
LANES = 128
VMEM_BYTES = 12 * 1024 * 1024

VMEM = pl.BlockSpec(memory_space=pltpu.VMEM)
SMEM = pl.BlockSpec(memory_space=pltpu.SMEM)
HBM = pl.BlockSpec(memory_space=pltpu.HBM)
ANY = pl.BlockSpec(memory_space=pl.ANY)


def split_numpy(table):
    high = table.astype(np.float32).astype(ml_dtypes.bfloat16)
    low = (table - high.astype(np.float64)).astype(ml_dtypes.bfloat16)
    return high, low


def dft_tables(length):
    half = length // 2
    index = np.arange(half)
    tables = []
    for parity in range(2):
        angles = 2.0 * math.pi / length * (index[:, None] * (2 * index[None, :] + parity) % length)
        cosine = np.cos(angles) / math.sqrt(length)
        sine = np.sin(angles) / math.sqrt(length)
        forward = np.block([[cosine, -sine], [sine, cosine]])
        tables.append([split_numpy(forward), split_numpy(forward.T)])
    return np.array(tables, dtype=ml_dtypes.bfloat16)


def parity_order(length):
    half = length // 2
    order = np.zeros((length, length))
    for index in range(length):
        order[index, index % 2 * half + index // 2] = 1.0
    return np.stack([order, order.T]).astype(ml_dtypes.bfloat16)


def split(values):
    high = values.astype(jnp.bfloat16)
    low = (values - high.astype(jnp.float32)).astype(jnp.bfloat16)
    return high, low


def times_table(values, table):
    high, low = split(values)
    left = jnp.concatenate([high, low, high], axis=1)
    right = jnp.concatenate([table[0], table[0], table[1]], axis=0)
    return jnp.dot(left, right, preferred_element_type=jnp.float32)


def table_times(table, values):
    high, low = split(values)
    left = jnp.concatenate([table[0], table[0], table[1]], axis=1)
    right = jnp.concatenate([high, low, high], axis=0)
    return jnp.dot(left, right, preferred_element_type=jnp.float32)


class Plan:
    def __init__(self, sx_size, sy_size, block_rows, block_cols):
        self.rows = block_rows
        self.sx_size = sx_size
        self.sy_size = sy_size
        self.own = block_cols // LANES
        self.tiles = self.own + 2
        self.paired = sy_size == 2
        self.sides = 1 if self.paired else 2

    def rights(self, t):
        return [1 - t] if self.paired else [0, 1]

    def pair_starts(self, t):
        return [right * (self.tiles - 2) for right in self.rights(t)]

    def halo_tiles(self, t):
        return [right * (self.tiles - 1) for right in self.rights(t)]

    def edge_tiles(self, t):
        return [1 + right * (self.tiles - 3) for right in self.rights(t)]

    def first_parity(self, t):
        return 1 - t if self.paired else 0

    def mid_start(self, t):
        return 1 + t if self.paired else 2

    @property
    def mid_tiles(self):
        return self.tiles - 3 if self.paired else self.tiles - 4

    def across(self, values, axis_name="sy"):
        if self.paired:
            return [lax.ppermute(values[0], axis_name, [(0, 1), (1, 0)])]
        ends = self.sy_size - 1
        return [
            lax.ppermute(values[1], axis_name, [(i, i + 1) for i in range(ends)]),
            lax.ppermute(values[0], axis_name, [(i + 1, i) for i in range(ends)]),
        ]

    def far_rows(self, values):
        rows, columns = self.sx_size, self.sy_size
        pairs = [(i * columns + t, (i + 1) * columns + t) for i in range(1, rows - 1, 2) for t in range(columns)]
        for i in (0, rows - 1):
            pairs += [(i * columns + t, i * columns + t + 1) for t in range(0, columns - 1, 2)]
        return lax.ppermute(values, ("sx", "sy"), pairs + [(j, i) for i, j in pairs])

    def near_rows(self, values):
        return lax.ppermute(values, "sx", [(i, i ^ 1) for i in range(self.sx_size)])

    def outermost(self, s):
        return (s == 0) | (s == self.sx_size - 1)


def far_side(s):
    return 2 * (s % 2) - 1


def lanes(tile, count=1):
    if isinstance(tile, int):
        return pl.ds(tile * LANES, count * LANES)
    return pl.ds(pl.multiple_of(tile * LANES, LANES), count * LANES)


def pick_tile(plan, target, pieces, tile, t):
    rows = target.shape[1]
    if plan.paired:

        @pl.when(tile == (plan.tiles - 1) * t)
        def _():
            target[...] = jnp.zeros(target.shape, jnp.float32)

    for runs, offset, count, start in pieces:

        @pl.when((tile >= start) & (tile < start + count))
        def _(runs=runs, offset=offset, start=start):
            line = 0
            for run in runs:
                height = min(run.shape[1], rows - line)
                target[:, line : line + height] = run[:, :height, lanes(tile - start + offset)]
                line += height


def lay_out(refs, starts):
    return [([ref], 0, ref.shape[2] // LANES, start) for ref, start in zip(refs, starts)]


def lay_out_rows(runs, counts, starts):
    return [(runs, sum(counts[:k]), count, start) for k, (count, start) in enumerate(zip(counts, starts))]


def rows_at(ref, start, count):
    offset = start % 8
    values = ref[pl.ds(pl.multiple_of(start - offset, 8), count + 8)]
    return pltpu.roll(values, (count + 8 - offset) % (count + 8), 0)[:count]


def here():
    return lax.axis_index("sx"), lax.axis_index("sy")


def info_rows(centres, count):
    lane = lax.broadcasted_iota(jnp.int32, (8, LANES), 1)
    slots = centres.shape[0]
    values = [centres[slot, axis] for slot in range(slots) for axis in range(2)] + [count]
    line = jnp.zeros((8, LANES), jnp.int32)
    for index, value in enumerate(values):
        line = jnp.where(lane == index, value, line)
    return line.astype(jnp.float32)


def edge_message_kernel(plan, block, centres, counts, *rest):
    messages, sems = rest[: plan.sides], rest[plan.sides]
    s, t = here()
    half = block.shape[1]
    copies = [
        pltpu.make_async_copy(block.at[:, :, lanes(tile - 1)], message.at[:, :half], sems.at[side])
        for side, (message, tile) in enumerate(zip(messages, plan.edge_tiles(t)))
    ]
    for copy in copies:
        copy.start()
    rows = info_rows(centres, counts[s])
    for message in messages:
        message[0, half:] = rows
        message[1, half:] = rows
    for copy in copies:
        copy.wait()


def halo_message_kernel(plan, centres, counts, _, *rest):
    sides = plan.sides
    received, far, halos, infos = (rest[k * sides : (k + 1) * sides] for k in range(4))
    own = info_rows(centres, counts[lax.axis_index("sx")])
    rest[-1][...] = own
    upper_line = lax.broadcasted_iota(jnp.int32, own.shape, 0) == 0
    for source, message, halo, info in zip(received, far, halos, infos):
        rows = halo.shape[1]
        both = jnp.where(upper_line, own, pltpu.roll(source[0, rows : rows + 8], 1, 0))
        halo[...] = source[:, :rows]
        info[...] = both
        message[:, :rows] = source[:, :rows]
        message[0, rows:] = both
        message[1, rows:] = both


def pair_kernel(plan, base, early, inverse, middle, *rest):
    sides = plan.sides
    sums, received, results = (rest[k * sides : (k + 1) * sides] for k in range(3))
    near = rest[3 * sides :]
    _, t = here()

    def copy(values, offset):
        line = 0
        for run in near:
            rows = run.shape[1]
            run[:, :, offset : offset + values.shape[2]] = values[:, line : line + rows]
            line += rows

    for side, (total, other, result, start) in enumerate(zip(sums, received, results, plan.pair_starts(t))):
        where = lanes(start, 2)
        missing = total[...] + other[...] - early[:, :, where]
        result[...] = base[:, :, where] - missing * inverse[:, where][None]
        copy(result, 2 * LANES * side)
    copy(middle, 2 * LANES * sides)


def spot_kernel(spot, _, copy):
    copy[...] = spot[...]


def prepare_kernel(centres, probe, amps, order, rolled, ordered, padded):
    size = probe.shape[1]
    half = size // 2
    padded[:, :half] = jnp.zeros((2, half, size), jnp.float32)
    padded[:, half + size :] = jnp.zeros((2, half + 8, size), jnp.float32)
    padded[:, half : half + size] = probe[...]
    for slot in range(amps.shape[0]):
        row = centres[slot, 0]
        col = centres[slot, 1]
        for part in range(2):
            shape = padded.at[part]
            upper = rows_at(shape, half - row, half) + rows_at(shape, half + size - row, half)
            lower = rows_at(shape, size - row, half)
            rolled[slot, part] = pltpu.roll(jnp.concatenate([upper, lower], axis=0), col % LANES, 1)
        high, low = split(amps[slot])
        across = jnp.dot(
            jnp.concatenate([high, low], axis=1),
            jnp.concatenate([order[0], order[0]], axis=0),
            preferred_element_type=jnp.float32,
        )
        high, low = split(across)
        ordered[slot] = jnp.dot(
            jnp.concatenate([order[1], order[1]], axis=1),
            jnp.concatenate([high, low], axis=0),
            preferred_element_type=jnp.float32,
        )


def info_kernel(plan, *rest):
    home, far, other = (rest[k * plan.sides : (k + 1) * plan.sides] for k in range(3))
    _, info, known, sem = rest[3 * plan.sides :]
    s, _ = here()
    upper = s % 2 == 0
    width = plan.sides + 1

    def lines(messages):
        return [messages[0]] + [pltpu.roll(message, 7, 0) for message in messages]

    own = lines([line[...] for line in home])
    near = lines([line[...] for line in other])
    far = lines([jnp.where(plan.outermost(s), 0.0, message[0, plan.rows :]) for message in far])
    for turn in range(width):
        for kind, line in ((0, jnp.where(upper, far[turn], near[turn])), (1, own[turn]), (2, jnp.where(upper, near[turn], far[turn]))):
            known[kind * width + turn] = line.astype(jnp.int32)
    copy = pltpu.make_async_copy(known.at[:, 0], info, sem)
    copy.start()
    copy.wait()


def light_kernel(plan, slots, info, probe, _, inverse, padded, canvas):
    size = probe.shape[1]
    half = size // 2
    _, t = here()
    padded[:half] = jnp.zeros((half, size), jnp.float32)
    padded[half + size :] = jnp.zeros((half + 8, size), jnp.float32)
    padded[half : half + size] = probe[0] * probe[0] + probe[1] * probe[1]
    canvas[...] = jnp.zeros(canvas.shape, jnp.float32)
    reach = plan.sides + 1
    spare = jnp.zeros((half, LANES), jnp.float32)
    for down in (-1, 0, 1):

        def add(step, carry, down=down):
            turn = step // slots
            slot = step % slots
            over = turn * (1 - 2 * t) if plan.paired else jnp.where(turn == 0, 0, 2 * turn - 3)
            index = (down + 1) * reach + turn

            @pl.when(slot < info[index, 2 * slots])
            def _():
                row = info[index, 2 * slot]
                col = info[index, 2 * slot + 1]
                power = rows_at(padded, size - half * down - row, half)
                shifted = pltpu.roll(jnp.concatenate([power, spare], axis=1), col % LANES, 1)
                first = col // LANES + plan.own * (over + 1)
                canvas[:, lanes(first, 3)] += shifted

            return carry

        lax.fori_loop(0, reach * slots, add, 0)
    inverse[...] = 1.0 / (canvas[:, lanes(plan.own, plan.tiles)] + DAMPING)


def term_kernel(plan, slot, layout, pieces, copied, halves, slots, spot, *rest):
    refs, rest = rest[:pieces], rest[pieces:]
    earlier, (probe, amps, tables, inner), rest = rest[:copied], rest[copied : copied + 4], rest[copied + 4 :]
    if halves:
        outer, rest = rest[-1], rest[:-1]
    else:
        outer, rest = rest[0], rest[1:]
    outer_halves, near_outers, picked = rest[:halves], rest[halves:-1], rest[-1]
    size = probe.shape[2]
    half = size // 2
    s, t = here()
    line = spot[0:1]
    lane = lax.broadcasted_iota(jnp.int32, line.shape, 1)
    entries = (2 * slot, 2 * slot + 1, 2 * slots)
    row, col, count = (jnp.sum(jnp.where(lane == k, line, 0.0)).astype(jnp.int32) for k in entries)
    alive = slot < count

    @pl.when(jnp.logical_not(alive))
    def _():
        outer[...] = jnp.zeros(outer.shape, jnp.float32)
        inner[...] = jnp.zeros(inner.shape, jnp.float32)

    @pl.when(alive)
    def _():
        tile = col // LANES
        first = tile % 2
        rest_col = col % LANES
        from_tile = lax.broadcasted_iota(jnp.int32, (half, LANES), 1) >= rest_col
        from_upper = lax.broadcasted_iota(jnp.int32, (half, LANES), 0) >= row
        side = far_side(s)
        own, far, near = layout(refs, t)
        for kind, source in ((1, own), (1 + side, far), (1 - side, near)):
            for step in range(3):
                pick_tile(plan, picked.at[kind, step], source, tile + step, t)

        @pl.when(plan.outermost(s))
        def _():
            picked[1 + side] = jnp.zeros(picked.shape[1:], jnp.float32)

        def edge(kind, part):
            return jnp.where(from_tile, picked[kind, 0, part], picked[kind, 2, part])

        def across(edges, middles, rows):
            sums, differences = [], []
            shares = []
            for columns, (real, imag) in ((slice(0, half), edges), (slice(half, size), middles)):
                probe_real, probe_imag = probe[slot, 0, rows, columns], probe[slot, 1, rows, columns]
                shares.append((probe_real * real - probe_imag * imag, probe_real * imag + probe_imag * real))
            for part in range(2):
                sums.append(shares[0][part] + shares[1][part])
                differences.append(shares[0][part] - shares[1][part])
            return [
                times_table(jnp.concatenate(parts, axis=1), tables[parity, 0])
                for parity, parts in enumerate((sums, differences))
            ]

        lower = across(
            [edge(1, part) for part in range(2)], [picked[1, 1, part] for part in range(2)], slice(half, size)
        )
        upper = across(
            [jnp.where(from_upper, edge(0, part), edge(2, part)) for part in range(2)],
            [jnp.where(from_upper, picked[0, 1, part], picked[2, 1, part]) for part in range(2)],
            slice(0, half),
        )
        halves = []
        for sign in (1.0, -1.0):
            rows = [top + sign * bottom for top, bottom in zip(upper, lower)]
            halves.append(
                jnp.concatenate(
                    [jnp.concatenate([row[:, part] for row in rows], axis=1) for part in (slice(0, half), slice(half, size))],
                    axis=0,
                )
            )
        back = []
        for parity in range(2):
            pattern = table_times(tables[parity, 1], halves[parity])
            far_real = pattern[:half]
            far_imag = pattern[half:]
            amplitude = amps[slot, parity * half : (parity + 1) * half]
            factor = 1.0 - amplitude * lax.rsqrt(far_real * far_real + far_imag * far_imag + SMOOTH)
            miss = jnp.concatenate([far_real * factor, far_imag * factor], axis=0)
            back.append(table_times(tables[parity, 0], miss))
        real = jnp.concatenate([back[0][:half] + back[1][:half], back[0][:half] - back[1][:half]], axis=0)
        imag = jnp.concatenate([back[0][half:] + back[1][half:], back[0][half:] - back[1][half:]], axis=0)
        both = []
        for parity in range(2):
            columns = slice(parity * half, (parity + 1) * half)
            both.append(times_table(jnp.concatenate([real[:, columns], imag[:, columns]], axis=1), tables[parity, 1]))
        near_real = jnp.concatenate([both[0][:, :half] + both[1][:, :half], both[0][:, :half] - both[1][:, :half]], axis=1)
        near_imag = jnp.concatenate([both[0][:, half:] + both[1][:, half:], both[0][:, half:] - both[1][:, half:]], axis=1)
        probe_real = probe[slot, 0]
        probe_imag = probe[slot, 1]
        for part, term in enumerate((probe_real * near_real + probe_imag * near_imag, probe_real * near_imag - probe_imag * near_real)):
            for place, columns in ((first, slice(0, half)), (1 - first, slice(half, size))):
                outer[part, :, lanes(place)] = term[:half, columns]
                inner[part, :, lanes(place)] = term[half:, columns]

    for index, target in enumerate(outer_halves):
        first = plan.first_parity(t)
        target[...] = outer[:, :, lanes(first if index == 0 else 1 - first)]
    for index, source in enumerate((*earlier, outer)):
        line = 0
        for target in near_outers:
            rows = target.shape[1]
            target[2 * index : 2 * index + 2] = source[:, line : line + rows]
            line += rows


class Patch:
    def __init__(self, plan, info, s, patch, slot, down, far=False):
        runs = patch if isinstance(patch, (list, tuple)) else [patch]
        half = sum(run.shape[1] for run in runs)
        index = (1 if down is None else 1 + down) * (plan.sides + 1)
        row = info[index, 2 * slot]
        col = info[index, 2 * slot + 1]
        self.runs = runs
        self.tile = col // LANES
        self.first = self.tile % 2
        self.rest = col % LANES
        self.lane = lax.broadcasted_iota(jnp.int32, (half, LANES), 1)
        self.from_tile = self.lane >= self.rest
        self.rows = None
        if down is not None:
            line = lax.broadcasted_iota(jnp.int32, (half, LANES), 0)
            after = jnp.where(down > 0, half, row)
            if far:
                after = jnp.where(plan.outermost(s), 0, after)
            self.rows = (line >= jnp.where(down > 0, row, 0)) & (line < after)

    def lines(self, part, place):
        values = jnp.concatenate([run[part, :, lanes(place)] for run in self.runs], axis=0)
        return values if self.rows is None else jnp.where(self.rows, values, 0.0)

    def tiles(self, part):
        edge = self.lines(part, self.first)
        middle = self.lines(part, 1 - self.first)
        return jnp.where(self.from_tile, edge, 0.0), middle, jnp.where(self.from_tile, 0.0, edge)

    def add_to(self, canvas):
        for part in range(2):
            for step, values in enumerate(self.tiles(part)):
                canvas[part, :, lanes(self.tile + step)] += values

    def mask(self, tile):
        step = tile - self.tile
        first = jnp.where(step == 0, self.rest, 0)
        after = jnp.where(step == 2, self.rest, jnp.where((step < 0) | (step > 2), 0, LANES))
        inside = (self.lane >= first) & (self.lane < after)
        if self.rows is not None:
            inside = inside & self.rows
        return jnp.where(inside, 1.0, 0.0)


def part_of(plan, patch, mask, part, tile):
    if isinstance(patch, (list, tuple)):
        first = plan.first_parity(lax.axis_index("sy"))
        values = jnp.where(tile % 2 == first, patch[0][part], patch[1][part])
    else:
        values = patch[part, :, lanes(tile % 2)]
    return values * mask[:, lanes(tile)]


def early_sum_kernel(plan, slots, info, *rest):
    inner, near, canvas = rest[:slots], rest[slots:-1], rest[-1]
    s, _ = here()
    canvas[...] = jnp.zeros(canvas.shape, jnp.float32)
    for slot in range(slots):
        Patch(plan, info, s, inner[slot], slot, None).add_to(canvas)
        runs = [run.at[2 * slot : 2 * slot + 2] for run in near]
        Patch(plan, info, s, runs, slot, -far_side(s)).add_to(canvas)


def base_kernel(plan, slots, layout, pieces, info, early, inverse, *rest):
    far, refs, (canvas, base, mask) = rest[: slots - 1], rest[slots - 1 : slots - 1 + pieces], rest[slots - 1 + pieces :]
    s, t = here()
    canvas[...] = early[...]
    for slot in range(slots - 1):
        Patch(plan, info, s, far[slot], slot, far_side(s), True).add_to(canvas)
    last = Patch(plan, info, s, canvas, slots - 1, far_side(s), True)
    for tile in range(plan.tiles):
        where = lanes(tile)
        pick_tile(plan, base.at[:, :, where], layout(refs, t)[0], tile, t)
        base[:, :, where] -= canvas[:, :, where] * inverse[:, where][None]
        mask[:, where] = last.mask(tile)


def take_off(plan, patch, mask, target, base, inverse, tile):
    for part in range(2):
        target[part] = base[part, :, lanes(tile)] - part_of(plan, patch, mask, part, tile) * inverse[:, lanes(tile)]


def middle_kernel(plan, base, patch, mask, inverse, _, middle):
    _, t = here()
    for step in range(plan.mid_tiles):
        take_off(plan, patch, mask, middle.at[:, :, lanes(step)], base, inverse, plan.mid_start(t) + step)


def boundary_kernel(plan, early, patch, mask, *sums):
    _, t = here()
    for total, start in zip(sums, plan.pair_starts(t)):
        for step in range(2):
            tile = start + step
            for part in range(2):
                total[part, :, lanes(step)] = early[part, :, lanes(tile)] + part_of(plan, patch, mask, part, tile)


def halo_sum_kernel(plan, early, mask, *rest):
    halves, sums = rest[: plan.sides], rest[plan.sides :]
    _, t = here()
    for half, total, tile in zip(halves, sums, plan.halo_tiles(t)):
        for part in range(2):
            total[part] = early[part, :, lanes(tile)] + half[part] * mask[:, lanes(tile)]


def last_kernel(plan, base, mask, inverse, _, first, second, *rest):
    nearly, bases, (current, sems) = rest[0], rest[1 : 1 + plan.sides], rest[1 + plan.sides :]
    patch = [first, second]
    _, t = here()
    copies = []
    for step in range(plan.own):
        where = lanes(step)
        take_off(plan, patch, mask, current.at[:, :, where], base, inverse, 1 + step)
        copies.append(pltpu.make_async_copy(current.at[:, :, where], nearly.at[:, :, where], sems.at[step]))
        copies[-1].start()
    for edge, tile in zip(bases, plan.edge_tiles(t)):
        edge[...] = current[:, :, lanes(tile - 1)]
    for copy in copies:
        copy.wait()


def edge_kernel(plan, inverse, *rest):
    bases, received = rest[: plan.sides], rest[plan.sides : 2 * plan.sides]
    _, result, sums, sems = rest[2 * plan.sides :]
    _, t = here()
    copies = []
    for side, tile in enumerate(plan.edge_tiles(t)):
        sums[side] = bases[side][...] - received[side][...] * inverse[:, lanes(tile)][None]
        copies.append(pltpu.make_async_copy(sums.at[side], result.at[:, :, lanes(tile - 1)], sems.at[side]))
        copies[-1].start()
    for copy in copies:
        copy.wait()


def call(kernel, outs, scratch, ins, flops=10**5, size=10**4, in_specs=None, out_specs=None, **options):
    result = pl.pallas_call(
        kernel,
        out_shape=outs,
        in_specs=in_specs or [SMEM if value.dtype == jnp.int32 else VMEM for value in ins],
        out_specs=out_specs or jax.tree.map(lambda _: VMEM, outs),
        scratch_shapes=scratch,
        compiler_params=pltpu.CompilerParams(vmem_limit_bytes=VMEM_BYTES),
        cost_estimate=pl.CostEstimate(flops=flops, bytes_accessed=size, transcendentals=0),
        **options,
    )(*ins)
    return list(result) if isinstance(outs, list) else result


def on_device(plan, object_field, probe_field, amplitudes, centres, counts):
    f32 = jnp.float32
    shape = jax.ShapeDtypeStruct
    size = probe_field.shape[1]
    half = size // 2
    slots = amplitudes.shape[2]
    block_rows = object_field.shape[1]
    block_cols = object_field.shape[2]
    assert block_rows == half and block_cols % (2 * LANES) == 0 and half == LANES
    width = plan.tiles * LANES
    sides = plan.sides
    spots = centres[0, 0]
    counts = counts.reshape(-1)
    own_amps = amplitudes[0, 0]
    tables = jnp.asarray(dft_tables(size))
    order = jnp.asarray(parity_order(size))
    dma = pltpu.SemaphoreType.DMA

    messages = call(
        lambda *refs: edge_message_kernel(plan, *refs),
        [shape((2, half + 8, LANES), f32)] * sides,
        [dma((sides,))],
        [object_field, spots, counts],
        in_specs=[HBM, SMEM, SMEM],
    )
    halos = plan.across(messages)
    far_block = plan.far_rows(object_field)
    near_block = plan.near_rows(object_field)
    rolled, ordered = call(
        prepare_kernel,
        [shape((slots, 2, size, size), f32), shape((slots, size, size), f32)],
        [pltpu.VMEM((2, 2 * size + 8, size), f32)],
        [spots, probe_field, own_amps, order],
    )
    messages = call(
        lambda *refs: halo_message_kernel(plan, *refs),
        [shape((2, half + 8, LANES), f32)] * sides
        + [shape((2, half, LANES), f32)] * sides
        + [shape((8, LANES), f32)] * (sides + 1),
        [],
        [spots, counts, ordered, *halos],
        in_specs=[SMEM, SMEM, ANY] + [VMEM] * sides,
    )
    passed, lines, own_spot = messages[sides : 2 * sides], messages[2 * sides : -1], messages[-1]
    near_lines = [plan.near_rows(line) for line in lines]
    own_spot = call(spot_kernel, shape(own_spot.shape, f32), [], [own_spot, near_lines[0]], in_specs=[VMEM, ANY])
    far = [far_block] + [plan.far_rows(message) for message in messages[:sides]]
    near = [plan.near_rows(message) for message in passed] + [near_block]
    own = [object_field] + passed
    def runs_layout(refs, main, side_starts):
        starts = [main] + side_starts
        return lay_out(refs[: 1 + sides], starts), lay_out(refs[1 + sides : 2 + 2 * sides], starts)

    def first_layout(refs, t):
        own, far = runs_layout(refs, 1, plan.halo_tiles(t))
        return own, far, lay_out(refs[2 + 2 * sides :], plan.halo_tiles(t) + [1])

    def later_layout(refs, t):
        own, far = runs_layout(refs, plan.mid_start(t), plan.pair_starts(t))
        counts = [2] * sides + [plan.mid_tiles]
        return own, far, lay_out_rows(refs[2 + 2 * sides :], counts, plan.pair_starts(t) + [plan.mid_start(t)])

    layout = first_layout

    third = half // 24 * 8
    near_heights = [half - 2 * third, third, third]
    for sweep in range(ITERS):
        pieces = own + far + near
        inner, outer, outer_far = [], [], []
        for slot in range(slots):
            last = slot == slots - 1
            earlier = outer if last else []
            patch = shape((2, half, size), f32)
            halves = 2 if last and sweep == ITERS - 1 else 0
            inner_part, *copies = call(
                lambda *refs, slot=slot, layout=layout, copied=len(earlier), halves=halves: term_kernel(
                    plan, slot, layout, len(pieces), copied, halves, slots, *refs
                ),
                [patch]
                + ([shape((2, half, LANES), f32)] * halves or [patch])
                + [shape((2 * slots, rows, size), f32) for rows in near_heights if last],
                [pltpu.VMEM((3, 3, 2, half, LANES), f32)]
                + [pltpu.VMEM((2, half, size), f32)] * (halves > 0),
                [own_spot, *pieces, *earlier, rolled, ordered, tables],
            )
            outer_part = None if halves else copies.pop(0)
            outer_halves, copies = copies[:halves], copies[halves:]
            inner.append(inner_part)
            outer.append(outer_part)
            outer_far.append([plan.far_rows(part) for part in outer_halves] if halves else plan.far_rows(outer_part))
            if sweep == 0 and last:
                info = call(
                    lambda *refs: info_kernel(plan, *refs),
                    shape((3 * (sides + 1), LANES), jnp.int32),
                    [pltpu.VMEM((3 * (sides + 1), 8, LANES), jnp.int32), dma],
                    lines + far[1:] + near_lines + [outer_part],
                    in_specs=[VMEM] * (3 * sides) + [ANY],
                    out_specs=SMEM,
                )
        outer_near = [plan.near_rows(copy) for copy in copies]
        if sweep == 0:
            inverse = call(
                lambda *refs: light_kernel(plan, slots, *refs),
                shape((half, width), f32),
                [
                    pltpu.VMEM((2 * size + 8, size), f32),
                    pltpu.VMEM((half, width + 2 * plan.own * LANES), f32),
                ],
                [info, probe_field, copies[0]],
                in_specs=[SMEM, VMEM, ANY],
            )
        early = call(
            lambda *refs: early_sum_kernel(plan, slots, *refs),
            shape((2, half, width), f32),
            [],
            [info, *inner, *outer_near],
        )
        early, base, mask = call(
            lambda *refs, layout=layout: base_kernel(plan, slots, layout, len(pieces), *refs),
            [shape((2, half, width), f32)] * 2 + [shape((half, width), f32)],
            [],
            [info, early, inverse, *outer_far[:-1], *pieces],
        )
        if sweep < ITERS - 1:
            sums = call(
                lambda *refs: boundary_kernel(plan, *refs),
                [shape((2, half, 2 * LANES), f32)] * sides,
                [],
                [early, outer_far[-1], mask],
            )
            received = plan.across(sums)
            middle = call(
                lambda *refs: middle_kernel(plan, *refs),
                shape((2, half, plan.mid_tiles * LANES), f32),
                [],
                [base, outer_far[-1], mask, inverse, sums[0]],
                in_specs=[VMEM] * 4 + [ANY],
            )
            far_middle = plan.far_rows(middle)
            near_runs = [shape((2, rows, (2 * sides + plan.mid_tiles) * LANES), f32) for rows in near_heights]
            updated = call(
                lambda *refs: pair_kernel(plan, *refs),
                [shape((2, half, 2 * LANES), f32)] * sides + near_runs,
                [],
                [base, early, inverse, middle, *sums, *received],
            )
            pairs = updated[:sides]
            own = [middle] + pairs
            far = [far_middle] + [plan.far_rows(piece) for piece in pairs]
            near = [plan.near_rows(piece) for piece in updated[sides:]]
            layout = later_layout
    sums = call(
        lambda *refs: halo_sum_kernel(plan, *refs),
        [shape((2, half, LANES), f32)] * sides,
        [],
        [early, mask, *outer_far[-1][:sides]],
    )
    nearly, *bases = call(
        lambda *refs: last_kernel(plan, *refs),
        [shape((2, half, block_cols), f32)] + [shape((2, half, LANES), f32)] * sides,
        [pltpu.VMEM((2, half, block_cols), f32), dma((plan.own,))],
        [base, mask, inverse, sums[0], *outer_far[-1]],
        in_specs=[VMEM] * 3 + [ANY] + [VMEM] * 2,
        out_specs=[HBM] + [VMEM] * sides,
    )
    received = plan.across(sums)
    return call(
        lambda *refs: edge_kernel(plan, *refs),
        shape(nearly.shape, f32),
        [pltpu.VMEM((sides, 2, half, LANES), f32), dma((sides,))],
        [inverse, *bases, *received, nearly],
        in_specs=[VMEM] * (1 + 2 * sides) + [HBM],
        out_specs=HBM,
        input_output_aliases={1 + 2 * sides: 0},
    )


def solution(mesh):
    sizes = dict(mesh.shape)

    def per_device(object_field, *rest):
        plan = Plan(sizes["sx"], sizes["sy"], *object_field.shape[1:])
        return on_device(plan, object_field, *rest)

    return jax.shard_map(
        per_device,
        mesh=mesh,
        in_specs=(
            P(None, "sx", "sy"),
            P(),
            P("sx", "sy", None, None, None),
            P("sx", "sy", None, None),
            P(None, "sy"),
        ),
        out_specs=P(None, "sx", "sy"),
        check_vma=False,
    )
```

```python
import math

import jax
import jax.numpy as jnp
import ml_dtypes
import numpy as np
from jax import lax
from jax.experimental import pallas as pl
from jax.experimental.pallas import tpu as pltpu
from jax.sharding import PartitionSpec as P

ITERS = 2
SMOOTH = 1.0
DAMPING = 1.0
LANES = 128
VMEM_BYTES = 12 * 1024 * 1024

VMEM = pl.BlockSpec(memory_space=pltpu.VMEM)
SMEM = pl.BlockSpec(memory_space=pltpu.SMEM)
HBM = pl.BlockSpec(memory_space=pltpu.HBM)
ANY = pl.BlockSpec(memory_space=pl.ANY)


def split_numpy(table):
    high = table.astype(np.float32).astype(ml_dtypes.bfloat16)
    low = (table - high.astype(np.float64)).astype(ml_dtypes.bfloat16)
    return high, low


def dft_tables(length):
    half = length // 2
    index = np.arange(half)
    tables = []
    for parity in range(2):
        angles = 2.0 * math.pi / length * (index[:, None] * (2 * index[None, :] + parity) % length)
        cosine = np.cos(angles) / math.sqrt(length)
        sine = np.sin(angles) / math.sqrt(length)
        forward = np.block([[cosine, -sine], [sine, cosine]])
        tables.append([split_numpy(forward), split_numpy(forward.T)])
    return np.array(tables, dtype=ml_dtypes.bfloat16)


def parity_order(length):
    half = length // 2
    order = np.zeros((length, length))
    for index in range(length):
        order[index, index % 2 * half + index // 2] = 1.0
    return np.stack([order, order.T]).astype(ml_dtypes.bfloat16)


def split(values):
    high = values.astype(jnp.bfloat16)
    low = (values - high.astype(jnp.float32)).astype(jnp.bfloat16)
    return high, low


def times_table(values, table):
    high, low = split(values)
    left = jnp.concatenate([high, low, high], axis=1)
    right = jnp.concatenate([table[0], table[0], table[1]], axis=0)
    return jnp.dot(left, right, preferred_element_type=jnp.float32)


def table_times(table, values):
    high, low = split(values)
    left = jnp.concatenate([table[0], table[0], table[1]], axis=1)
    right = jnp.concatenate([high, low, high], axis=0)
    return jnp.dot(left, right, preferred_element_type=jnp.float32)


class Plan:
    def __init__(self, sx_size, sy_size, block_rows, block_cols):
        self.rows = block_rows
        self.sx_size = sx_size
        self.sy_size = sy_size
        self.own = block_cols // LANES
        self.tiles = self.own + 2
        self.paired = sy_size == 2
        self.sides = 1 if self.paired else 2

    def rights(self, t):
        return [1 - t] if self.paired else [0, 1]

    def pair_starts(self, t):
        return [right * (self.tiles - 2) for right in self.rights(t)]

    def halo_tiles(self, t):
        return [right * (self.tiles - 1) for right in self.rights(t)]

    def edge_tiles(self, t):
        return [1 + right * (self.tiles - 3) for right in self.rights(t)]

    def first_parity(self, t):
        return 1 - t if self.paired else 0

    def mid_start(self, t):
        return 1 + t if self.paired else 2

    @property
    def mid_tiles(self):
        return self.tiles - 3 if self.paired else self.tiles - 4

    def across(self, values, axis_name="sy"):
        if self.paired:
            return [lax.ppermute(values[0], axis_name, [(0, 1), (1, 0)])]
        ends = self.sy_size - 1
        return [
            lax.ppermute(values[1], axis_name, [(i, i + 1) for i in range(ends)]),
            lax.ppermute(values[0], axis_name, [(i + 1, i) for i in range(ends)]),
        ]

    def far_rows(self, values):
        rows, columns = self.sx_size, self.sy_size
        pairs = [(i * columns + t, (i + 1) * columns + t) for i in range(1, rows - 1, 2) for t in range(columns)]
        for i in (0, rows - 1):
            pairs += [(i * columns + t, i * columns + t + 1) for t in range(0, columns - 1, 2)]
        return lax.ppermute(values, ("sx", "sy"), pairs + [(j, i) for i, j in pairs])

    def near_rows(self, values):
        return lax.ppermute(values, "sx", [(i, i ^ 1) for i in range(self.sx_size)])

    def outermost(self, s):
        return (s == 0) | (s == self.sx_size - 1)


def far_side(s):
    return 2 * (s % 2) - 1


def lanes(tile, count=1):
    if isinstance(tile, int):
        return pl.ds(tile * LANES, count * LANES)
    return pl.ds(pl.multiple_of(tile * LANES, LANES), count * LANES)


def pick_tile(plan, target, pieces, tile, t):
    rows = target.shape[1]
    if plan.paired:

        @pl.when(tile == (plan.tiles - 1) * t)
        def _():
            target[...] = jnp.zeros(target.shape, jnp.float32)

    for runs, offset, count, start in pieces:

        @pl.when((tile >= start) & (tile < start + count))
        def _(runs=runs, offset=offset, start=start):
            line = 0
            for run in runs:
                height = min(run.shape[1], rows - line)
                target[:, line : line + height] = run[:, :height, lanes(tile - start + offset)]
                line += height


def lay_out(refs, starts):
    return [([ref], 0, ref.shape[2] // LANES, start) for ref, start in zip(refs, starts)]


def lay_out_rows(runs, counts, starts):
    return [(runs, sum(counts[:k]), count, start) for k, (count, start) in enumerate(zip(counts, starts))]


def rows_at(ref, start, count):
    offset = start % 8
    values = ref[pl.ds(pl.multiple_of(start - offset, 8), count + 8)]
    return pltpu.roll(values, (count + 8 - offset) % (count + 8), 0)[:count]


def here():
    return lax.axis_index("sx"), lax.axis_index("sy")


def info_rows(centres, count):
    lane = lax.broadcasted_iota(jnp.int32, (8, LANES), 1)
    slots = centres.shape[0]
    values = [centres[slot, axis] for slot in range(slots) for axis in range(2)] + [count]
    line = jnp.zeros((8, LANES), jnp.int32)
    for index, value in enumerate(values):
        line = jnp.where(lane == index, value, line)
    return line.astype(jnp.float32)


def edge_message_kernel(plan, block, centres, counts, *rest):
    messages, sems = rest[: plan.sides], rest[plan.sides]
    s, t = here()
    half = block.shape[1]
    copies = [
        pltpu.make_async_copy(block.at[:, :, lanes(tile - 1)], message.at[:, :half], sems.at[side])
        for side, (message, tile) in enumerate(zip(messages, plan.edge_tiles(t)))
    ]
    for copy in copies:
        copy.start()
    rows = info_rows(centres, counts[s])
    for message in messages:
        message[0, half:] = rows
        message[1, half:] = rows
    for copy in copies:
        copy.wait()


def halo_message_kernel(plan, centres, counts, _, *rest):
    sides = plan.sides
    received, far, halos, infos = (rest[k * sides : (k + 1) * sides] for k in range(4))
    own = info_rows(centres, counts[lax.axis_index("sx")])
    rest[-1][...] = own
    upper_line = lax.broadcasted_iota(jnp.int32, own.shape, 0) == 0
    for source, message, halo, info in zip(received, far, halos, infos):
        rows = halo.shape[1]
        both = jnp.where(upper_line, own, pltpu.roll(source[0, rows : rows + 8], 1, 0))
        halo[...] = source[:, :rows]
        info[...] = both
        message[:, :rows] = source[:, :rows]
        message[0, rows:] = both
        message[1, rows:] = both


def pair_kernel(plan, base, early, inverse, middle, *rest):
    sides = plan.sides
    sums, received, results = (rest[k * sides : (k + 1) * sides] for k in range(3))
    near = rest[3 * sides :]
    _, t = here()

    def copy(values, offset):
        line = 0
        for run in near:
            rows = run.shape[1]
            run[:, :, offset : offset + values.shape[2]] = values[:, line : line + rows]
            line += rows

    for side, (total, other, result, start) in enumerate(zip(sums, received, results, plan.pair_starts(t))):
        where = lanes(start, 2)
        missing = total[...] + other[...] - early[:, :, where]
        result[...] = base[:, :, where] - missing * inverse[:, where][None]
        copy(result, 2 * LANES * side)
    copy(middle, 2 * LANES * sides)


def spot_kernel(spot, _, copy):
    copy[...] = spot[...]


def prepare_kernel(centres, probe, amps, order, rolled, ordered, padded):
    size = probe.shape[1]
    half = size // 2
    padded[:, :half] = jnp.zeros((2, half, size), jnp.float32)
    padded[:, half + size :] = jnp.zeros((2, half + 8, size), jnp.float32)
    padded[:, half : half + size] = probe[...]
    for slot in range(amps.shape[0]):
        row = centres[slot, 0]
        col = centres[slot, 1]
        for part in range(2):
            shape = padded.at[part]
            upper = rows_at(shape, half - row, half) + rows_at(shape, half + size - row, half)
            lower = rows_at(shape, size - row, half)
            rolled[slot, part] = pltpu.roll(jnp.concatenate([upper, lower], axis=0), col % LANES, 1)
        high, low = split(amps[slot])
        across = jnp.dot(
            jnp.concatenate([high, low], axis=1),
            jnp.concatenate([order[0], order[0]], axis=0),
            preferred_element_type=jnp.float32,
        )
        high, low = split(across)
        ordered[slot] = jnp.dot(
            jnp.concatenate([order[1], order[1]], axis=1),
            jnp.concatenate([high, low], axis=0),
            preferred_element_type=jnp.float32,
        )


def gather_info(plan, home, far, other, info, known, sem):
    s, _ = here()
    upper = s % 2 == 0
    width = plan.sides + 1

    def lines(messages):
        return [messages[0]] + [pltpu.roll(message, 7, 0) for message in messages]

    own = lines([line[...] for line in home])
    near = lines([line[...] for line in other])
    far = lines([jnp.where(plan.outermost(s), 0.0, message[0, plan.rows :]) for message in far])
    for turn in range(width):
        for kind, line in ((0, jnp.where(upper, far[turn], near[turn])), (1, own[turn]), (2, jnp.where(upper, near[turn], far[turn]))):
            known[kind * width + turn] = line.astype(jnp.int32)
    copy = pltpu.make_async_copy(known.at[:, 0], info, sem)
    copy.start()
    copy.wait()


def light_kernel(plan, slots, *rest):
    groups = [rest[k * plan.sides : (k + 1) * plan.sides] for k in range(3)]
    probe, _, inverse, info, padded, canvas, known, sem = rest[3 * plan.sides :]
    gather_info(plan, *groups, info, known, sem)
    size = probe.shape[1]
    half = size // 2
    _, t = here()
    padded[:half] = jnp.zeros((half, size), jnp.float32)
    padded[half + size :] = jnp.zeros((half + 8, size), jnp.float32)
    padded[half : half + size] = probe[0] * probe[0] + probe[1] * probe[1]
    canvas[...] = jnp.zeros(canvas.shape, jnp.float32)
    reach = plan.sides + 1
    spare = jnp.zeros((half, LANES), jnp.float32)
    for down in (-1, 0, 1):

        def add(step, carry, down=down):
            turn = step // slots
            slot = step % slots
            over = turn * (1 - 2 * t) if plan.paired else jnp.where(turn == 0, 0, 2 * turn - 3)
            index = (down + 1) * reach + turn

            @pl.when(slot < info[index, 2 * slots])
            def _():
                row = info[index, 2 * slot]
                col = info[index, 2 * slot + 1]
                power = rows_at(padded, size - half * down - row, half)
                shifted = pltpu.roll(jnp.concatenate([power, spare], axis=1), col % LANES, 1)
                first = col // LANES + plan.own * (over + 1)
                canvas[:, lanes(first, 3)] += shifted

            return carry

        lax.fori_loop(0, reach * slots, add, 0)
    inverse[...] = 1.0 / (canvas[:, lanes(plan.own, plan.tiles)] + DAMPING)


def term_kernel(plan, slot, layout, pieces, copied, halves, slots, spot, *rest):
    refs, rest = rest[:pieces], rest[pieces:]
    earlier, (probe, amps, tables, inner), rest = rest[:copied], rest[copied : copied + 4], rest[copied + 4 :]
    if halves:
        outer, rest = rest[-1], rest[:-1]
    else:
        outer, rest = rest[0], rest[1:]
    outer_halves, near_outers, picked = rest[:halves], rest[halves:-1], rest[-1]
    size = probe.shape[2]
    half = size // 2
    s, t = here()
    line = spot[0:1]
    lane = lax.broadcasted_iota(jnp.int32, line.shape, 1)
    entries = (2 * slot, 2 * slot + 1, 2 * slots)
    row, col, count = (jnp.sum(jnp.where(lane == k, line, 0.0)).astype(jnp.int32) for k in entries)
    alive = slot < count

    @pl.when(jnp.logical_not(alive))
    def _():
        outer[...] = jnp.zeros(outer.shape, jnp.float32)
        inner[...] = jnp.zeros(inner.shape, jnp.float32)

    @pl.when(alive)
    def _():
        tile = col // LANES
        first = tile % 2
        rest_col = col % LANES
        from_tile = lax.broadcasted_iota(jnp.int32, (half, LANES), 1) >= rest_col
        from_upper = lax.broadcasted_iota(jnp.int32, (half, LANES), 0) >= row
        side = far_side(s)
        own, far, near = layout(refs, t)
        for kind, source in ((1, own), (1 + side, far), (1 - side, near)):
            for step in range(3):
                pick_tile(plan, picked.at[kind, step], source, tile + step, t)

        @pl.when(plan.outermost(s))
        def _():
            picked[1 + side] = jnp.zeros(picked.shape[1:], jnp.float32)

        def edge(kind, part):
            return jnp.where(from_tile, picked[kind, 0, part], picked[kind, 2, part])

        def across(edges, middles, rows):
            sums, differences = [], []
            shares = []
            for columns, (real, imag) in ((slice(0, half), edges), (slice(half, size), middles)):
                probe_real, probe_imag = probe[slot, 0, rows, columns], probe[slot, 1, rows, columns]
                shares.append((probe_real * real - probe_imag * imag, probe_real * imag + probe_imag * real))
            for part in range(2):
                sums.append(shares[0][part] + shares[1][part])
                differences.append(shares[0][part] - shares[1][part])
            return [
                times_table(jnp.concatenate(parts, axis=1), tables[parity, 0])
                for parity, parts in enumerate((sums, differences))
            ]

        lower = across(
            [edge(1, part) for part in range(2)], [picked[1, 1, part] for part in range(2)], slice(half, size)
        )
        upper = across(
            [jnp.where(from_upper, edge(0, part), edge(2, part)) for part in range(2)],
            [jnp.where(from_upper, picked[0, 1, part], picked[2, 1, part]) for part in range(2)],
            slice(0, half),
        )
        halves = []
        for sign in (1.0, -1.0):
            rows = [top + sign * bottom for top, bottom in zip(upper, lower)]
            halves.append(
                jnp.concatenate(
                    [jnp.concatenate([row[:, part] for row in rows], axis=1) for part in (slice(0, half), slice(half, size))],
                    axis=0,
                )
            )
        back = []
        for parity in range(2):
            pattern = table_times(tables[parity, 1], halves[parity])
            far_real = pattern[:half]
            far_imag = pattern[half:]
            amplitude = amps[slot, parity * half : (parity + 1) * half]
            factor = 1.0 - amplitude * lax.rsqrt(far_real * far_real + far_imag * far_imag + SMOOTH)
            miss = jnp.concatenate([far_real * factor, far_imag * factor], axis=0)
            back.append(table_times(tables[parity, 0], miss))
        real = jnp.concatenate([back[0][:half] + back[1][:half], back[0][:half] - back[1][:half]], axis=0)
        imag = jnp.concatenate([back[0][half:] + back[1][half:], back[0][half:] - back[1][half:]], axis=0)
        both = []
        for parity in range(2):
            columns = slice(parity * half, (parity + 1) * half)
            both.append(times_table(jnp.concatenate([real[:, columns], imag[:, columns]], axis=1), tables[parity, 1]))
        near_real = jnp.concatenate([both[0][:, :half] + both[1][:, :half], both[0][:, :half] - both[1][:, :half]], axis=1)
        near_imag = jnp.concatenate([both[0][:, half:] + both[1][:, half:], both[0][:, half:] - both[1][:, half:]], axis=1)
        probe_real = probe[slot, 0]
        probe_imag = probe[slot, 1]
        for part, term in enumerate((probe_real * near_real + probe_imag * near_imag, probe_real * near_imag - probe_imag * near_real)):
            for place, columns in ((first, slice(0, half)), (1 - first, slice(half, size))):
                outer[part, :, lanes(place)] = term[:half, columns]
                inner[part, :, lanes(place)] = term[half:, columns]

    for index, target in enumerate(outer_halves):
        first = plan.first_parity(t)
        target[...] = outer[:, :, lanes(first if index == 0 else 1 - first)]
    for index, source in enumerate((*earlier, outer)):
        line = 0
        for target in near_outers:
            rows = target.shape[1]
            target[2 * index : 2 * index + 2] = source[:, line : line + rows]
            line += rows


class Patch:
    def __init__(self, plan, info, s, patch, slot, down, far=False):
        runs = patch if isinstance(patch, (list, tuple)) else [patch]
        half = sum(run.shape[1] for run in runs)
        index = (1 if down is None else 1 + down) * (plan.sides + 1)
        row = info[index, 2 * slot]
        col = info[index, 2 * slot + 1]
        self.runs = runs
        self.tile = col // LANES
        self.first = self.tile % 2
        self.rest = col % LANES
        self.lane = lax.broadcasted_iota(jnp.int32, (half, LANES), 1)
        self.from_tile = self.lane >= self.rest
        self.rows = None
        if down is not None:
            line = lax.broadcasted_iota(jnp.int32, (half, LANES), 0)
            after = jnp.where(down > 0, half, row)
            if far:
                after = jnp.where(plan.outermost(s), 0, after)
            self.rows = (line >= jnp.where(down > 0, row, 0)) & (line < after)

    def lines(self, part, place):
        values = jnp.concatenate([run[part, :, lanes(place)] for run in self.runs], axis=0)
        return values if self.rows is None else jnp.where(self.rows, values, 0.0)

    def tiles(self, part):
        edge = self.lines(part, self.first)
        middle = self.lines(part, 1 - self.first)
        return jnp.where(self.from_tile, edge, 0.0), middle, jnp.where(self.from_tile, 0.0, edge)

    def add_to(self, canvas):
        for part in range(2):
            for step, values in enumerate(self.tiles(part)):
                canvas[part, :, lanes(self.tile + step)] += values

    def mask(self, tile):
        step = tile - self.tile
        first = jnp.where(step == 0, self.rest, 0)
        after = jnp.where(step == 2, self.rest, jnp.where((step < 0) | (step > 2), 0, LANES))
        inside = (self.lane >= first) & (self.lane < after)
        if self.rows is not None:
            inside = inside & self.rows
        return jnp.where(inside, 1.0, 0.0)


def part_of(plan, patch, mask, part, tile):
    if isinstance(patch, (list, tuple)):
        first = plan.first_parity(lax.axis_index("sy"))
        values = jnp.where(tile % 2 == first, patch[0][part], patch[1][part])
    else:
        values = patch[part, :, lanes(tile % 2)]
    return values * mask[:, lanes(tile)]


def early_sum_kernel(plan, slots, info, *rest):
    inner, near, canvas = rest[:slots], rest[slots:-1], rest[-1]
    s, _ = here()
    canvas[...] = jnp.zeros(canvas.shape, jnp.float32)
    for slot in range(slots):
        Patch(plan, info, s, inner[slot], slot, None).add_to(canvas)
        runs = [run.at[2 * slot : 2 * slot + 2] for run in near]
        Patch(plan, info, s, runs, slot, -far_side(s)).add_to(canvas)


def base_kernel(plan, slots, layout, pieces, info, early, inverse, *rest):
    far, refs, (canvas, base, mask) = rest[: slots - 1], rest[slots - 1 : slots - 1 + pieces], rest[slots - 1 + pieces :]
    s, t = here()
    canvas[...] = early[...]
    for slot in range(slots - 1):
        Patch(plan, info, s, far[slot], slot, far_side(s), True).add_to(canvas)
    last = Patch(plan, info, s, canvas, slots - 1, far_side(s), True)
    for tile in range(plan.tiles):
        where = lanes(tile)
        pick_tile(plan, base.at[:, :, where], layout(refs, t)[0], tile, t)
        base[:, :, where] -= canvas[:, :, where] * inverse[:, where][None]
        mask[:, where] = last.mask(tile)


def take_off(plan, patch, mask, target, base, inverse, tile):
    for part in range(2):
        target[part] = base[part, :, lanes(tile)] - part_of(plan, patch, mask, part, tile) * inverse[:, lanes(tile)]


def middle_kernel(plan, base, patch, mask, inverse, _, middle):
    _, t = here()
    for step in range(plan.mid_tiles):
        take_off(plan, patch, mask, middle.at[:, :, lanes(step)], base, inverse, plan.mid_start(t) + step)


def boundary_kernel(plan, early, patch, mask, *sums):
    _, t = here()
    for total, start in zip(sums, plan.pair_starts(t)):
        for step in range(2):
            tile = start + step
            for part in range(2):
                total[part, :, lanes(step)] = early[part, :, lanes(tile)] + part_of(plan, patch, mask, part, tile)


def halo_sum_kernel(plan, early, mask, *rest):
    halves, sums = rest[: plan.sides], rest[plan.sides :]
    _, t = here()
    for half, total, tile in zip(halves, sums, plan.halo_tiles(t)):
        for part in range(2):
            total[part] = early[part, :, lanes(tile)] + half[part] * mask[:, lanes(tile)]


def last_kernel(plan, base, mask, inverse, _, first, second, *rest):
    nearly, bases, (current, sems) = rest[0], rest[1 : 1 + plan.sides], rest[1 + plan.sides :]
    patch = [first, second]
    _, t = here()
    copies = []
    for step in range(plan.own):
        where = lanes(step)
        take_off(plan, patch, mask, current.at[:, :, where], base, inverse, 1 + step)
        copies.append(pltpu.make_async_copy(current.at[:, :, where], nearly.at[:, :, where], sems.at[step]))
        copies[-1].start()
    for edge, tile in zip(bases, plan.edge_tiles(t)):
        edge[...] = current[:, :, lanes(tile - 1)]
    for copy in copies:
        copy.wait()


def edge_kernel(plan, inverse, *rest):
    bases, received = rest[: plan.sides], rest[plan.sides : 2 * plan.sides]
    _, result, sums, sems = rest[2 * plan.sides :]
    _, t = here()
    copies = []
    for side, tile in enumerate(plan.edge_tiles(t)):
        sums[side] = bases[side][...] - received[side][...] * inverse[:, lanes(tile)][None]
        copies.append(pltpu.make_async_copy(sums.at[side], result.at[:, :, lanes(tile - 1)], sems.at[side]))
        copies[-1].start()
    for copy in copies:
        copy.wait()


def call(kernel, outs, scratch, ins, flops=10**5, size=10**4, in_specs=None, out_specs=None, **options):
    result = pl.pallas_call(
        kernel,
        out_shape=outs,
        in_specs=in_specs or [SMEM if value.dtype == jnp.int32 else VMEM for value in ins],
        out_specs=out_specs or jax.tree.map(lambda _: VMEM, outs),
        scratch_shapes=scratch,
        compiler_params=pltpu.CompilerParams(vmem_limit_bytes=VMEM_BYTES),
        cost_estimate=pl.CostEstimate(flops=flops, bytes_accessed=size, transcendentals=0),
        **options,
    )(*ins)
    return list(result) if isinstance(outs, list) else result


def on_device(plan, object_field, probe_field, amplitudes, centres, counts):
    f32 = jnp.float32
    shape = jax.ShapeDtypeStruct
    size = probe_field.shape[1]
    half = size // 2
    slots = amplitudes.shape[2]
    block_rows = object_field.shape[1]
    block_cols = object_field.shape[2]
    assert block_rows == half and block_cols % (2 * LANES) == 0 and half == LANES
    width = plan.tiles * LANES
    sides = plan.sides
    spots = centres[0, 0]
    counts = counts.reshape(-1)
    own_amps = amplitudes[0, 0]
    tables = jnp.asarray(dft_tables(size))
    order = jnp.asarray(parity_order(size))
    dma = pltpu.SemaphoreType.DMA

    messages = call(
        lambda *refs: edge_message_kernel(plan, *refs),
        [shape((2, half + 8, LANES), f32)] * sides,
        [dma((sides,))],
        [object_field, spots, counts],
        in_specs=[HBM, SMEM, SMEM],
    )
    halos = plan.across(messages)
    far_block = plan.far_rows(object_field)
    near_block = plan.near_rows(object_field)
    rolled, ordered = call(
        prepare_kernel,
        [shape((slots, 2, size, size), f32), shape((slots, size, size), f32)],
        [pltpu.VMEM((2, 2 * size + 8, size), f32)],
        [spots, probe_field, own_amps, order],
    )
    messages = call(
        lambda *refs: halo_message_kernel(plan, *refs),
        [shape((2, half + 8, LANES), f32)] * sides
        + [shape((2, half, LANES), f32)] * sides
        + [shape((8, LANES), f32)] * (sides + 1),
        [],
        [spots, counts, ordered, *halos],
        in_specs=[SMEM, SMEM, ANY] + [VMEM] * sides,
    )
    passed, lines, own_spot = messages[sides : 2 * sides], messages[2 * sides : -1], messages[-1]
    near_lines = [plan.near_rows(line) for line in lines]
    own_spot = call(spot_kernel, shape(own_spot.shape, f32), [], [own_spot, near_lines[0]], in_specs=[VMEM, ANY])
    far = [far_block] + [plan.far_rows(message) for message in messages[:sides]]
    near = [plan.near_rows(message) for message in passed] + [near_block]
    own = [object_field] + passed
    def runs_layout(refs, main, side_starts):
        starts = [main] + side_starts
        return lay_out(refs[: 1 + sides], starts), lay_out(refs[1 + sides : 2 + 2 * sides], starts)

    def first_layout(refs, t):
        own, far = runs_layout(refs, 1, plan.halo_tiles(t))
        return own, far, lay_out(refs[2 + 2 * sides :], plan.halo_tiles(t) + [1])

    def later_layout(refs, t):
        own, far = runs_layout(refs, plan.mid_start(t), plan.pair_starts(t))
        counts = [2] * sides + [plan.mid_tiles]
        return own, far, lay_out_rows(refs[2 + 2 * sides :], counts, plan.pair_starts(t) + [plan.mid_start(t)])

    layout = first_layout

    third = half // 24 * 8
    near_heights = [half - 2 * third, third, third]
    for sweep in range(ITERS):
        pieces = own + far + near
        inner, outer, outer_far = [], [], []
        for slot in range(slots):
            last = slot == slots - 1
            earlier = outer if last else []
            patch = shape((2, half, size), f32)
            halves = 2 if last and sweep == ITERS - 1 else 0
            inner_part, *copies = call(
                lambda *refs, slot=slot, layout=layout, copied=len(earlier), halves=halves: term_kernel(
                    plan, slot, layout, len(pieces), copied, halves, slots, *refs
                ),
                [patch]
                + ([shape((2, half, LANES), f32)] * halves or [patch])
                + [shape((2 * slots, rows, size), f32) for rows in near_heights if last],
                [pltpu.VMEM((3, 3, 2, half, LANES), f32)]
                + [pltpu.VMEM((2, half, size), f32)] * (halves > 0),
                [own_spot, *pieces, *earlier, rolled, ordered, tables],
            )
            outer_part = None if halves else copies.pop(0)
            outer_halves, copies = copies[:halves], copies[halves:]
            inner.append(inner_part)
            outer.append(outer_part)
            outer_far.append([plan.far_rows(part) for part in outer_halves] if halves else plan.far_rows(outer_part))
        outer_near = [plan.near_rows(copy) for copy in copies]
        if sweep == 0:
            inverse, info = call(
                lambda *refs: light_kernel(plan, slots, *refs),
                [shape((half, width), f32), shape((3 * (sides + 1), LANES), jnp.int32)],
                [
                    pltpu.VMEM((2 * size + 8, size), f32),
                    pltpu.VMEM((half, width + 2 * plan.own * LANES), f32),
                    pltpu.VMEM((3 * (sides + 1), 8, LANES), jnp.int32),
                    dma,
                ],
                lines + far[1:] + near_lines + [probe_field, copies[0]],
                in_specs=[VMEM] * (3 * sides + 1) + [ANY],
                out_specs=[VMEM, SMEM],
            )
        early = call(
            lambda *refs: early_sum_kernel(plan, slots, *refs),
            shape((2, half, width), f32),
            [],
            [info, *inner, *outer_near],
        )
        early, base, mask = call(
            lambda *refs, layout=layout: base_kernel(plan, slots, layout, len(pieces), *refs),
            [shape((2, half, width), f32)] * 2 + [shape((half, width), f32)],
            [],
            [info, early, inverse, *outer_far[:-1], *pieces],
        )
        if sweep < ITERS - 1:
            sums = call(
                lambda *refs: boundary_kernel(plan, *refs),
                [shape((2, half, 2 * LANES), f32)] * sides,
                [],
                [early, outer_far[-1], mask],
            )
            received = plan.across(sums)
            middle = call(
                lambda *refs: middle_kernel(plan, *refs),
                shape((2, half, plan.mid_tiles * LANES), f32),
                [],
                [base, outer_far[-1], mask, inverse, sums[0]],
                in_specs=[VMEM] * 4 + [ANY],
            )
            far_middle = plan.far_rows(middle)
            near_runs = [shape((2, rows, (2 * sides + plan.mid_tiles) * LANES), f32) for rows in near_heights]
            updated = call(
                lambda *refs: pair_kernel(plan, *refs),
                [shape((2, half, 2 * LANES), f32)] * sides + near_runs,
                [],
                [base, early, inverse, middle, *sums, *received],
            )
            pairs = updated[:sides]
            own = [middle] + pairs
            far = [far_middle] + [plan.far_rows(piece) for piece in pairs]
            near = [plan.near_rows(piece) for piece in updated[sides:]]
            layout = later_layout
    sums = call(
        lambda *refs: halo_sum_kernel(plan, *refs),
        [shape((2, half, LANES), f32)] * sides,
        [],
        [early, mask, *outer_far[-1][:sides]],
    )
    nearly, *bases = call(
        lambda *refs: last_kernel(plan, *refs),
        [shape((2, half, block_cols), f32)] + [shape((2, half, LANES), f32)] * sides,
        [pltpu.VMEM((2, half, block_cols), f32), dma((plan.own,))],
        [base, mask, inverse, sums[0], *outer_far[-1]],
        in_specs=[VMEM] * 3 + [ANY] + [VMEM] * 2,
        out_specs=[HBM] + [VMEM] * sides,
    )
    received = plan.across(sums)
    return call(
        lambda *refs: edge_kernel(plan, *refs),
        shape(nearly.shape, f32),
        [pltpu.VMEM((sides, 2, half, LANES), f32), dma((sides,))],
        [inverse, *bases, *received, nearly],
        in_specs=[VMEM] * (1 + 2 * sides) + [HBM],
        out_specs=HBM,
        input_output_aliases={1 + 2 * sides: 0},
    )


def solution(mesh):
    sizes = dict(mesh.shape)

    def per_device(object_field, *rest):
        plan = Plan(sizes["sx"], sizes["sy"], *object_field.shape[1:])
        return on_device(plan, object_field, *rest)

    return jax.shard_map(
        per_device,
        mesh=mesh,
        in_specs=(
            P(None, "sx", "sy"),
            P(),
            P("sx", "sy", None, None, None),
            P("sx", "sy", None, None),
            P(None, "sy"),
        ),
        out_specs=P(None, "sx", "sy"),
        check_vma=False,
    )
```

```python
import math

import jax
import jax.numpy as jnp
import ml_dtypes
import numpy as np
from jax import lax
from jax.experimental import pallas as pl
from jax.experimental.pallas import tpu as pltpu
from jax.sharding import PartitionSpec as P

ITERS = 2
SMOOTH = 1.0
DAMPING = 1.0
LANES = 128
VMEM_BYTES = 12 * 1024 * 1024

VMEM = pl.BlockSpec(memory_space=pltpu.VMEM)
SMEM = pl.BlockSpec(memory_space=pltpu.SMEM)
HBM = pl.BlockSpec(memory_space=pltpu.HBM)
ANY = pl.BlockSpec(memory_space=pl.ANY)


def split_numpy(table):
    high = table.astype(np.float32).astype(ml_dtypes.bfloat16)
    low = (table - high.astype(np.float64)).astype(ml_dtypes.bfloat16)
    return high, low


def dft_tables(length):
    half = length // 2
    index = np.arange(half)
    tables = []
    for parity in range(2):
        angles = 2.0 * math.pi / length * (index[:, None] * (2 * index[None, :] + parity) % length)
        cosine = np.cos(angles) / math.sqrt(length)
        sine = np.sin(angles) / math.sqrt(length)
        forward = np.block([[cosine, -sine], [sine, cosine]])
        tables.append([split_numpy(forward), split_numpy(forward.T)])
    return np.array(tables, dtype=ml_dtypes.bfloat16)


def parity_order(length):
    half = length // 2
    order = np.zeros((length, length))
    for index in range(length):
        order[index, index % 2 * half + index // 2] = 1.0
    return np.stack([order, order.T]).astype(ml_dtypes.bfloat16)


def split(values):
    high = values.astype(jnp.bfloat16)
    low = (values - high.astype(jnp.float32)).astype(jnp.bfloat16)
    return high, low


def times_table(values, table):
    high, low = split(values)
    left = jnp.concatenate([high, low, high], axis=1)
    right = jnp.concatenate([table[0], table[0], table[1]], axis=0)
    return jnp.dot(left, right, preferred_element_type=jnp.float32)


def table_times(table, values):
    high, low = split(values)
    left = jnp.concatenate([table[0], table[0], table[1]], axis=1)
    right = jnp.concatenate([high, low, high], axis=0)
    return jnp.dot(left, right, preferred_element_type=jnp.float32)


class Plan:
    def __init__(self, sx_size, sy_size, block_rows, block_cols):
        self.rows = block_rows
        self.sx_size = sx_size
        self.sy_size = sy_size
        self.own = block_cols // LANES
        self.tiles = self.own + 2
        self.paired = sy_size == 2
        self.sides = 1 if self.paired else 2

    def rights(self, t):
        return [1 - t] if self.paired else [0, 1]

    def pair_starts(self, t):
        return [right * (self.tiles - 2) for right in self.rights(t)]

    def halo_tiles(self, t):
        return [right * (self.tiles - 1) for right in self.rights(t)]

    def edge_tiles(self, t):
        return [1 + right * (self.tiles - 3) for right in self.rights(t)]

    def first_parity(self, t):
        return 1 - t if self.paired else 0

    def mid_start(self, t):
        return 1 + t if self.paired else 2

    @property
    def mid_tiles(self):
        return self.tiles - 3 if self.paired else self.tiles - 4

    def across(self, values, axis_name="sy"):
        if self.paired:
            return [lax.ppermute(values[0], axis_name, [(0, 1), (1, 0)])]
        ends = self.sy_size - 1
        return [
            lax.ppermute(values[1], axis_name, [(i, i + 1) for i in range(ends)]),
            lax.ppermute(values[0], axis_name, [(i + 1, i) for i in range(ends)]),
        ]

    def far_rows(self, values):
        rows, columns = self.sx_size, self.sy_size
        pairs = [(i * columns + t, (i + 1) * columns + t) for i in range(1, rows - 1, 2) for t in range(columns)]
        for i in (0, rows - 1):
            pairs += [(i * columns + t, i * columns + t + 1) for t in range(0, columns - 1, 2)]
        return lax.ppermute(values, ("sx", "sy"), pairs + [(j, i) for i, j in pairs])

    def near_rows(self, values):
        return lax.ppermute(values, "sx", [(i, i ^ 1) for i in range(self.sx_size)])

    def outermost(self, s):
        return (s == 0) | (s == self.sx_size - 1)


def far_side(s):
    return 2 * (s % 2) - 1


def lanes(tile, count=1):
    if isinstance(tile, int):
        return pl.ds(tile * LANES, count * LANES)
    return pl.ds(pl.multiple_of(tile * LANES, LANES), count * LANES)


def pick_tile(plan, target, pieces, tile, t):
    rows = target.shape[1]
    if plan.paired:

        @pl.when(tile == (plan.tiles - 1) * t)
        def _():
            target[...] = jnp.zeros(target.shape, jnp.float32)

    for ref, offset, count, start in pieces:

        @pl.when((tile >= start) & (tile < start + count))
        def _(ref=ref, offset=offset, start=start):
            target[...] = ref[:, :rows, lanes(tile - start + offset)]


def lay_out(refs, starts):
    return [(ref, 0, ref.shape[2] // LANES, start) for ref, start in zip(refs, starts)]


def chunks(count):
    return [min(2, count - first) for first in range(0, count, 2)]


def chunk_starts(start, count):
    return [start + 2 * index for index in range(len(chunks(count)))]


def spread(source, targets):
    offset = 0
    for target in targets:
        columns = target.shape[2]
        target[...] = source[:, :, offset : offset + columns]
        offset += columns


def rows_at(ref, start, count):
    offset = start % 8
    values = ref[pl.ds(pl.multiple_of(start - offset, 8), count + 8)]
    return pltpu.roll(values, (count + 8 - offset) % (count + 8), 0)[:count]


def here():
    return lax.axis_index("sx"), lax.axis_index("sy")


def info_rows(centres, count):
    lane = lax.broadcasted_iota(jnp.int32, (8, LANES), 1)
    slots = centres.shape[0]
    values = [centres[slot, axis] for slot in range(slots) for axis in range(2)] + [count]
    line = jnp.zeros((8, LANES), jnp.int32)
    for index, value in enumerate(values):
        line = jnp.where(lane == index, value, line)
    return line.astype(jnp.float32)


def edge_message_kernel(plan, block, centres, counts, *rest):
    messages, sems = rest[: plan.sides], rest[plan.sides]
    s, t = here()
    half = block.shape[1]
    copies = [
        pltpu.make_async_copy(block.at[:, :, lanes(tile - 1)], message.at[:, :half], sems.at[side])
        for side, (message, tile) in enumerate(zip(messages, plan.edge_tiles(t)))
    ]
    for copy in copies:
        copy.start()
    rows = info_rows(centres, counts[s])
    for message in messages:
        message[0, half:] = rows
        message[1, half:] = rows
    for copy in copies:
        copy.wait()


def halo_message_kernel(plan, centres, counts, _, *rest):
    sides = plan.sides
    received, far, halos, infos = (rest[k * sides : (k + 1) * sides] for k in range(4))
    own = info_rows(centres, counts[lax.axis_index("sx")])
    rest[-1][...] = own
    upper_line = lax.broadcasted_iota(jnp.int32, own.shape, 0) == 0
    for source, message, halo, info in zip(received, far, halos, infos):
        rows = halo.shape[1]
        both = jnp.where(upper_line, own, pltpu.roll(source[0, rows : rows + 8], 1, 0))
        halo[...] = source[:, :rows]
        info[...] = both
        message[:, :rows] = source[:, :rows]
        message[0, rows:] = both
        message[1, rows:] = both


def pair_kernel(plan, base, early, inverse, middle, *rest):
    sides = plan.sides
    sums, received, results = (rest[k * sides : (k + 1) * sides] for k in range(3))
    near = rest[3 * sides :]
    _, t = here()
    for total, other, result, copy, start in zip(sums, received, results, near, plan.pair_starts(t)):
        where = lanes(start, 2)
        missing = total[...] + other[...] - early[:, :, where]
        values = base[:, :, where] - missing * inverse[:, where][None]
        result[...] = values
        copy[...] = values
    spread(middle, near[sides:])


def spot_kernel(spot, _, copy):
    copy[...] = spot[...]


def prepare_kernel(centres, probe, amps, order, rolled, ordered, padded):
    size = probe.shape[1]
    half = size // 2
    padded[:, :half] = jnp.zeros((2, half, size), jnp.float32)
    padded[:, half + size :] = jnp.zeros((2, half + 8, size), jnp.float32)
    padded[:, half : half + size] = probe[...]
    for slot in range(amps.shape[0]):
        row = centres[slot, 0]
        col = centres[slot, 1]
        for part in range(2):
            shape = padded.at[part]
            upper = rows_at(shape, half - row, half) + rows_at(shape, half + size - row, half)
            lower = rows_at(shape, size - row, half)
            rolled[slot, part] = pltpu.roll(jnp.concatenate([upper, lower], axis=0), col % LANES, 1)
        high, low = split(amps[slot])
        across = jnp.dot(
            jnp.concatenate([high, low], axis=1),
            jnp.concatenate([order[0], order[0]], axis=0),
            preferred_element_type=jnp.float32,
        )
        high, low = split(across)
        ordered[slot] = jnp.dot(
            jnp.concatenate([order[1], order[1]], axis=1),
            jnp.concatenate([high, low], axis=0),
            preferred_element_type=jnp.float32,
        )


def info_kernel(plan, *rest):
    home, far, other = (rest[k * plan.sides : (k + 1) * plan.sides] for k in range(3))
    _, info, known, sem = rest[3 * plan.sides :]
    s, _ = here()
    upper = s % 2 == 0
    width = plan.sides + 1

    def lines(messages):
        return [messages[0]] + [pltpu.roll(message, 7, 0) for message in messages]

    own = lines([line[...] for line in home])
    near = lines([line[...] for line in other])
    far = lines([jnp.where(plan.outermost(s), 0.0, message[0, plan.rows :]) for message in far])
    for turn in range(width):
        for kind, line in ((0, jnp.where(upper, far[turn], near[turn])), (1, own[turn]), (2, jnp.where(upper, near[turn], far[turn]))):
            known[kind * width + turn] = line.astype(jnp.int32)
    copy = pltpu.make_async_copy(known.at[:, 0], info, sem)
    copy.start()
    copy.wait()


def light_kernel(plan, slots, info, probe, _, inverse, padded, canvas):
    size = probe.shape[1]
    half = size // 2
    _, t = here()
    padded[:half] = jnp.zeros((half, size), jnp.float32)
    padded[half + size :] = jnp.zeros((half + 8, size), jnp.float32)
    padded[half : half + size] = probe[0] * probe[0] + probe[1] * probe[1]
    canvas[...] = jnp.zeros(canvas.shape, jnp.float32)
    reach = plan.sides + 1
    spare = jnp.zeros((half, LANES), jnp.float32)
    for down in (-1, 0, 1):

        def add(step, carry, down=down):
            turn = step // slots
            slot = step % slots
            over = turn * (1 - 2 * t) if plan.paired else jnp.where(turn == 0, 0, 2 * turn - 3)
            index = (down + 1) * reach + turn

            @pl.when(slot < info[index, 2 * slots])
            def _():
                row = info[index, 2 * slot]
                col = info[index, 2 * slot + 1]
                power = rows_at(padded, size - half * down - row, half)
                shifted = pltpu.roll(jnp.concatenate([power, spare], axis=1), col % LANES, 1)
                first = col // LANES + plan.own * (over + 1)
                canvas[:, lanes(first, 3)] += shifted

            return carry

        lax.fori_loop(0, reach * slots, add, 0)
    inverse[...] = 1.0 / (canvas[:, lanes(plan.own, plan.tiles)] + DAMPING)


def term_kernel(plan, slot, layout, pieces, copied, halves, slots, spot, *rest):
    refs, rest = rest[:pieces], rest[pieces:]
    earlier, (probe, amps, tables, inner), rest = rest[:copied], rest[copied : copied + 4], rest[copied + 4 :]
    if halves:
        outer, rest = rest[-1], rest[:-1]
    else:
        outer, rest = rest[0], rest[1:]
    outer_halves, near_outers, picked = rest[:halves], rest[halves:-1], rest[-1]
    size = probe.shape[2]
    half = size // 2
    s, t = here()
    line = spot[0:1]
    lane = lax.broadcasted_iota(jnp.int32, line.shape, 1)
    entries = (2 * slot, 2 * slot + 1, 2 * slots)
    row, col, count = (jnp.sum(jnp.where(lane == k, line, 0.0)).astype(jnp.int32) for k in entries)
    alive = slot < count

    @pl.when(jnp.logical_not(alive))
    def _():
        outer[...] = jnp.zeros(outer.shape, jnp.float32)
        inner[...] = jnp.zeros(inner.shape, jnp.float32)

    @pl.when(alive)
    def _():
        tile = col // LANES
        first = tile % 2
        rest_col = col % LANES
        from_tile = lax.broadcasted_iota(jnp.int32, (half, LANES), 1) >= rest_col
        from_upper = lax.broadcasted_iota(jnp.int32, (half, LANES), 0) >= row
        side = far_side(s)
        own, far, near = layout(refs, t)
        for kind, source in ((1, own), (1 + side, far), (1 - side, near)):
            for step in range(3):
                pick_tile(plan, picked.at[kind, step], source, tile + step, t)

        @pl.when(plan.outermost(s))
        def _():
            picked[1 + side] = jnp.zeros(picked.shape[1:], jnp.float32)

        def edge(kind, part):
            return jnp.where(from_tile, picked[kind, 0, part], picked[kind, 2, part])

        def across(edges, middles, rows):
            sums, differences = [], []
            shares = []
            for columns, (real, imag) in ((slice(0, half), edges), (slice(half, size), middles)):
                probe_real, probe_imag = probe[slot, 0, rows, columns], probe[slot, 1, rows, columns]
                shares.append((probe_real * real - probe_imag * imag, probe_real * imag + probe_imag * real))
            for part in range(2):
                sums.append(shares[0][part] + shares[1][part])
                differences.append(shares[0][part] - shares[1][part])
            return [
                times_table(jnp.concatenate(parts, axis=1), tables[parity, 0])
                for parity, parts in enumerate((sums, differences))
            ]

        lower = across(
            [edge(1, part) for part in range(2)], [picked[1, 1, part] for part in range(2)], slice(half, size)
        )
        upper = across(
            [jnp.where(from_upper, edge(0, part), edge(2, part)) for part in range(2)],
            [jnp.where(from_upper, picked[0, 1, part], picked[2, 1, part]) for part in range(2)],
            slice(0, half),
        )
        halves = []
        for sign in (1.0, -1.0):
            rows = [top + sign * bottom for top, bottom in zip(upper, lower)]
            halves.append(
                jnp.concatenate(
                    [jnp.concatenate([row[:, part] for row in rows], axis=1) for part in (slice(0, half), slice(half, size))],
                    axis=0,
                )
            )
        back = []
        for parity in range(2):
            pattern = table_times(tables[parity, 1], halves[parity])
            far_real = pattern[:half]
            far_imag = pattern[half:]
            amplitude = amps[slot, parity * half : (parity + 1) * half]
            factor = 1.0 - amplitude * lax.rsqrt(far_real * far_real + far_imag * far_imag + SMOOTH)
            miss = jnp.concatenate([far_real * factor, far_imag * factor], axis=0)
            back.append(table_times(tables[parity, 0], miss))
        real = jnp.concatenate([back[0][:half] + back[1][:half], back[0][:half] - back[1][:half]], axis=0)
        imag = jnp.concatenate([back[0][half:] + back[1][half:], back[0][half:] - back[1][half:]], axis=0)
        both = []
        for parity in range(2):
            columns = slice(parity * half, (parity + 1) * half)
            both.append(times_table(jnp.concatenate([real[:, columns], imag[:, columns]], axis=1), tables[parity, 1]))
        near_real = jnp.concatenate([both[0][:, :half] + both[1][:, :half], both[0][:, :half] - both[1][:, :half]], axis=1)
        near_imag = jnp.concatenate([both[0][:, half:] + both[1][:, half:], both[0][:, half:] - both[1][:, half:]], axis=1)
        probe_real = probe[slot, 0]
        probe_imag = probe[slot, 1]
        for part, term in enumerate((probe_real * near_real + probe_imag * near_imag, probe_real * near_imag - probe_imag * near_real)):
            for place, columns in ((first, slice(0, half)), (1 - first, slice(half, size))):
                outer[part, :, lanes(place)] = term[:half, columns]
                inner[part, :, lanes(place)] = term[half:, columns]

    for index, target in enumerate(outer_halves):
        first = plan.first_parity(t)
        target[...] = outer[:, :, lanes(first if index == 0 else 1 - first)]
    for index, source in enumerate((*earlier, outer)):
        line = 0
        for target in near_outers:
            rows = target.shape[1]
            target[2 * index : 2 * index + 2] = source[:, line : line + rows]
            line += rows


class Patch:
    def __init__(self, plan, info, s, patch, slot, down, far=False):
        runs = patch if isinstance(patch, (list, tuple)) else [patch]
        half = sum(run.shape[1] for run in runs)
        index = (1 if down is None else 1 + down) * (plan.sides + 1)
        row = info[index, 2 * slot]
        col = info[index, 2 * slot + 1]
        self.runs = runs
        self.tile = col // LANES
        self.first = self.tile % 2
        self.rest = col % LANES
        self.lane = lax.broadcasted_iota(jnp.int32, (half, LANES), 1)
        self.from_tile = self.lane >= self.rest
        self.rows = None
        if down is not None:
            line = lax.broadcasted_iota(jnp.int32, (half, LANES), 0)
            after = jnp.where(down > 0, half, row)
            if far:
                after = jnp.where(plan.outermost(s), 0, after)
            self.rows = (line >= jnp.where(down > 0, row, 0)) & (line < after)

    def lines(self, part, place):
        values = jnp.concatenate([run[part, :, lanes(place)] for run in self.runs], axis=0)
        return values if self.rows is None else jnp.where(self.rows, values, 0.0)

    def tiles(self, part):
        edge = self.lines(part, self.first)
        middle = self.lines(part, 1 - self.first)
        return jnp.where(self.from_tile, edge, 0.0), middle, jnp.where(self.from_tile, 0.0, edge)

    def add_to(self, canvas):
        for part in range(2):
            for step, values in enumerate(self.tiles(part)):
                canvas[part, :, lanes(self.tile + step)] += values

    def mask(self, tile):
        step = tile - self.tile
        first = jnp.where(step == 0, self.rest, 0)
        after = jnp.where(step == 2, self.rest, jnp.where((step < 0) | (step > 2), 0, LANES))
        inside = (self.lane >= first) & (self.lane < after)
        if self.rows is not None:
            inside = inside & self.rows
        return jnp.where(inside, 1.0, 0.0)


def part_of(plan, patch, mask, part, tile):
    if isinstance(patch, (list, tuple)):
        first = plan.first_parity(lax.axis_index("sy"))
        values = jnp.where(tile % 2 == first, patch[0][part], patch[1][part])
    else:
        values = patch[part, :, lanes(tile % 2)]
    return values * mask[:, lanes(tile)]


def early_sum_kernel(plan, slots, info, *rest):
    inner, near, canvas = rest[:slots], rest[slots:-1], rest[-1]
    s, _ = here()
    canvas[...] = jnp.zeros(canvas.shape, jnp.float32)
    for slot in range(slots):
        Patch(plan, info, s, inner[slot], slot, None).add_to(canvas)
        runs = [run.at[2 * slot : 2 * slot + 2] for run in near]
        Patch(plan, info, s, runs, slot, -far_side(s)).add_to(canvas)


def base_kernel(plan, slots, layout, pieces, info, early, inverse, *rest):
    far, refs, (canvas, base, mask) = rest[: slots - 1], rest[slots - 1 : slots - 1 + pieces], rest[slots - 1 + pieces :]
    s, t = here()
    canvas[...] = early[...]
    for slot in range(slots - 1):
        Patch(plan, info, s, far[slot], slot, far_side(s), True).add_to(canvas)
    last = Patch(plan, info, s, canvas, slots - 1, far_side(s), True)
    for tile in range(plan.tiles):
        where = lanes(tile)
        pick_tile(plan, base.at[:, :, where], layout(refs, t)[0], tile, t)
        base[:, :, where] -= canvas[:, :, where] * inverse[:, where][None]
        mask[:, where] = last.mask(tile)


def take_off(plan, patch, mask, target, base, inverse, tile):
    for part in range(2):
        target[part] = base[part, :, lanes(tile)] - part_of(plan, patch, mask, part, tile) * inverse[:, lanes(tile)]


def middle_kernel(plan, base, patch, mask, inverse, _, middle):
    _, t = here()
    for step in range(plan.mid_tiles):
        take_off(plan, patch, mask, middle.at[:, :, lanes(step)], base, inverse, plan.mid_start(t) + step)


def boundary_kernel(plan, early, patch, mask, *sums):
    _, t = here()
    for total, start in zip(sums, plan.pair_starts(t)):
        for step in range(2):
            tile = start + step
            for part in range(2):
                total[part, :, lanes(step)] = early[part, :, lanes(tile)] + part_of(plan, patch, mask, part, tile)


def halo_sum_kernel(plan, early, mask, *rest):
    halves, sums = rest[: plan.sides], rest[plan.sides :]
    _, t = here()
    for half, total, tile in zip(halves, sums, plan.halo_tiles(t)):
        for part in range(2):
            total[part] = early[part, :, lanes(tile)] + half[part] * mask[:, lanes(tile)]


def last_kernel(plan, base, mask, inverse, _, first, second, *rest):
    nearly, bases, (current, sems) = rest[0], rest[1 : 1 + plan.sides], rest[1 + plan.sides :]
    patch = [first, second]
    _, t = here()
    copies = []
    for step in range(plan.own):
        where = lanes(step)
        take_off(plan, patch, mask, current.at[:, :, where], base, inverse, 1 + step)
        copies.append(pltpu.make_async_copy(current.at[:, :, where], nearly.at[:, :, where], sems.at[step]))
        copies[-1].start()
    for edge, tile in zip(bases, plan.edge_tiles(t)):
        edge[...] = current[:, :, lanes(tile - 1)]
    for copy in copies:
        copy.wait()


def edge_kernel(plan, inverse, *rest):
    bases, received = rest[: plan.sides], rest[plan.sides : 2 * plan.sides]
    _, result, sums, sems = rest[2 * plan.sides :]
    _, t = here()
    copies = []
    for side, tile in enumerate(plan.edge_tiles(t)):
        sums[side] = bases[side][...] - received[side][...] * inverse[:, lanes(tile)][None]
        copies.append(pltpu.make_async_copy(sums.at[side], result.at[:, :, lanes(tile - 1)], sems.at[side]))
        copies[-1].start()
    for copy in copies:
        copy.wait()


def call(kernel, outs, scratch, ins, flops=10**5, size=10**4, in_specs=None, out_specs=None, **options):
    result = pl.pallas_call(
        kernel,
        out_shape=outs,
        in_specs=in_specs or [SMEM if value.dtype == jnp.int32 else VMEM for value in ins],
        out_specs=out_specs or jax.tree.map(lambda _: VMEM, outs),
        scratch_shapes=scratch,
        compiler_params=pltpu.CompilerParams(vmem_limit_bytes=VMEM_BYTES),
        cost_estimate=pl.CostEstimate(flops=flops, bytes_accessed=size, transcendentals=0),
        **options,
    )(*ins)
    return list(result) if isinstance(outs, list) else result


def on_device(plan, object_field, probe_field, amplitudes, centres, counts):
    f32 = jnp.float32
    shape = jax.ShapeDtypeStruct
    size = probe_field.shape[1]
    half = size // 2
    slots = amplitudes.shape[2]
    block_rows = object_field.shape[1]
    block_cols = object_field.shape[2]
    assert block_rows == half and block_cols % (2 * LANES) == 0 and half == LANES
    width = plan.tiles * LANES
    sides = plan.sides
    spots = centres[0, 0]
    counts = counts.reshape(-1)
    own_amps = amplitudes[0, 0]
    tables = jnp.asarray(dft_tables(size))
    order = jnp.asarray(parity_order(size))
    dma = pltpu.SemaphoreType.DMA

    messages = call(
        lambda *refs: edge_message_kernel(plan, *refs),
        [shape((2, half + 8, LANES), f32)] * sides,
        [dma((sides,))],
        [object_field, spots, counts],
        in_specs=[HBM, SMEM, SMEM],
    )
    halos = plan.across(messages)
    far_block = plan.far_rows(object_field)
    near_block = plan.near_rows(object_field)
    rolled, ordered = call(
        prepare_kernel,
        [shape((slots, 2, size, size), f32), shape((slots, size, size), f32)],
        [pltpu.VMEM((2, 2 * size + 8, size), f32)],
        [spots, probe_field, own_amps, order],
    )
    messages = call(
        lambda *refs: halo_message_kernel(plan, *refs),
        [shape((2, half + 8, LANES), f32)] * sides
        + [shape((2, half, LANES), f32)] * sides
        + [shape((8, LANES), f32)] * (sides + 1),
        [],
        [spots, counts, ordered, *halos],
        in_specs=[SMEM, SMEM, ANY] + [VMEM] * sides,
    )
    passed, lines, own_spot = messages[sides : 2 * sides], messages[2 * sides : -1], messages[-1]
    near_lines = [plan.near_rows(line) for line in lines]
    own_spot = call(spot_kernel, shape(own_spot.shape, f32), [], [own_spot, near_lines[0]], in_specs=[VMEM, ANY])
    far = [far_block] + [plan.far_rows(message) for message in messages[:sides]]
    near = [plan.near_rows(message) for message in passed] + [near_block]
    own = [object_field] + passed
    def runs_layout(refs, main, count, side_starts):
        starts = [main] + side_starts
        own, far, near = refs[: 1 + sides], refs[1 + sides : 2 + 2 * sides], refs[2 + 2 * sides :]
        return lay_out(own, starts), lay_out(far, starts), lay_out(near, side_starts + (chunk_starts(main, count) if len(near) > 1 + sides else [main]))

    def first_layout(refs, t):
        return runs_layout(refs, 1, plan.own, plan.halo_tiles(t))

    def later_layout(refs, t):
        return runs_layout(refs, plan.mid_start(t), plan.mid_tiles, plan.pair_starts(t))

    layout = first_layout

    third = half // 24 * 8
    near_heights = [half - 2 * third, third, third]
    for sweep in range(ITERS):
        pieces = own + far + near
        inner, outer, outer_far = [], [], []
        for slot in range(slots):
            last = slot == slots - 1
            earlier = outer if last else []
            patch = shape((2, half, size), f32)
            halves = 2 if last and sweep == ITERS - 1 else 0
            inner_part, *copies = call(
                lambda *refs, slot=slot, layout=layout, copied=len(earlier), halves=halves: term_kernel(
                    plan, slot, layout, len(pieces), copied, halves, slots, *refs
                ),
                [patch]
                + ([shape((2, half, LANES), f32)] * halves or [patch])
                + [shape((2 * slots, rows, size), f32) for rows in near_heights if last],
                [pltpu.VMEM((3, 3, 2, half, LANES), f32)]
                + [pltpu.VMEM((2, half, size), f32)] * (halves > 0),
                [own_spot, *pieces, *earlier, rolled, ordered, tables],
            )
            outer_part = None if halves else copies.pop(0)
            outer_halves, copies = copies[:halves], copies[halves:]
            inner.append(inner_part)
            outer.append(outer_part)
            outer_far.append([plan.far_rows(part) for part in outer_halves] if halves else plan.far_rows(outer_part))
            if sweep == 0 and last:
                info = call(
                    lambda *refs: info_kernel(plan, *refs),
                    shape((3 * (sides + 1), LANES), jnp.int32),
                    [pltpu.VMEM((3 * (sides + 1), 8, LANES), jnp.int32), dma],
                    lines + far[1:] + near_lines + [outer_part],
                    in_specs=[VMEM] * (3 * sides) + [ANY],
                    out_specs=SMEM,
                )
        outer_near = [plan.near_rows(copy) for copy in copies]
        if sweep == 0:
            inverse = call(
                lambda *refs: light_kernel(plan, slots, *refs),
                shape((half, width), f32),
                [
                    pltpu.VMEM((2 * size + 8, size), f32),
                    pltpu.VMEM((half, width + 2 * plan.own * LANES), f32),
                ],
                [info, probe_field, copies[0]],
                in_specs=[SMEM, VMEM, ANY],
            )
        early = call(
            lambda *refs: early_sum_kernel(plan, slots, *refs),
            shape((2, half, width), f32),
            [],
            [info, *inner, *outer_near],
        )
        early, base, mask = call(
            lambda *refs, layout=layout: base_kernel(plan, slots, layout, len(pieces), *refs),
            [shape((2, half, width), f32)] * 2 + [shape((half, width), f32)],
            [],
            [info, early, inverse, *outer_far[:-1], *pieces],
        )
        if sweep < ITERS - 1:
            sums = call(
                lambda *refs: boundary_kernel(plan, *refs),
                [shape((2, half, 2 * LANES), f32)] * sides,
                [],
                [early, outer_far[-1], mask],
            )
            received = plan.across(sums)
            middle = call(
                lambda *refs: middle_kernel(plan, *refs),
                shape((2, half, plan.mid_tiles * LANES), f32),
                [],
                [base, outer_far[-1], mask, inverse, sums[0]],
                in_specs=[VMEM] * 4 + [ANY],
            )
            far_middle = plan.far_rows(middle)
            near_runs = [shape((2, half, count * LANES), f32) for count in chunks(plan.mid_tiles)]
            updated = call(
                lambda *refs: pair_kernel(plan, *refs),
                [shape((2, half, 2 * LANES), f32)] * (2 * sides) + near_runs,
                [],
                [base, early, inverse, middle, *sums, *received],
            )
            pairs = updated[:sides]
            own = [middle] + pairs
            far = [far_middle] + [plan.far_rows(piece) for piece in pairs]
            near = [plan.near_rows(piece) for piece in updated[sides:]]
            layout = later_layout
    sums = call(
        lambda *refs: halo_sum_kernel(plan, *refs),
        [shape((2, half, LANES), f32)] * sides,
        [],
        [early, mask, *outer_far[-1][:sides]],
    )
    nearly, *bases = call(
        lambda *refs: last_kernel(plan, *refs),
        [shape((2, half, block_cols), f32)] + [shape((2, half, LANES), f32)] * sides,
        [pltpu.VMEM((2, half, block_cols), f32), dma((plan.own,))],
        [base, mask, inverse, sums[0], *outer_far[-1]],
        in_specs=[VMEM] * 3 + [ANY] + [VMEM] * 2,
        out_specs=[HBM] + [VMEM] * sides,
    )
    received = plan.across(sums)
    return call(
        lambda *refs: edge_kernel(plan, *refs),
        shape(nearly.shape, f32),
        [pltpu.VMEM((sides, 2, half, LANES), f32), dma((sides,))],
        [inverse, *bases, *received, nearly],
        in_specs=[VMEM] * (1 + 2 * sides) + [HBM],
        out_specs=HBM,
        input_output_aliases={1 + 2 * sides: 0},
    )


def solution(mesh):
    sizes = dict(mesh.shape)

    def per_device(object_field, *rest):
        plan = Plan(sizes["sx"], sizes["sy"], *object_field.shape[1:])
        return on_device(plan, object_field, *rest)

    return jax.shard_map(
        per_device,
        mesh=mesh,
        in_specs=(
            P(None, "sx", "sy"),
            P(),
            P("sx", "sy", None, None, None),
            P("sx", "sy", None, None),
            P(None, "sy"),
        ),
        out_specs=P(None, "sx", "sy"),
        check_vma=False,
    )
```

```python
import math

import jax
import jax.numpy as jnp
import ml_dtypes
import numpy as np
from jax import lax
from jax.experimental import pallas as pl
from jax.experimental.pallas import tpu as pltpu
from jax.sharding import PartitionSpec as P

ITERS = 2
SMOOTH = 1.0
DAMPING = 1.0
LANES = 128
VMEM_BYTES = 12 * 1024 * 1024

VMEM = pl.BlockSpec(memory_space=pltpu.VMEM)
SMEM = pl.BlockSpec(memory_space=pltpu.SMEM)
HBM = pl.BlockSpec(memory_space=pltpu.HBM)
ANY = pl.BlockSpec(memory_space=pl.ANY)


def split_numpy(table):
    high = table.astype(np.float32).astype(ml_dtypes.bfloat16)
    low = (table - high.astype(np.float64)).astype(ml_dtypes.bfloat16)
    return high, low


def dft_tables(length):
    half = length // 2
    index = np.arange(half)
    tables = []
    for parity in range(2):
        angles = 2.0 * math.pi / length * (index[:, None] * (2 * index[None, :] + parity) % length)
        cosine = np.cos(angles) / math.sqrt(length)
        sine = np.sin(angles) / math.sqrt(length)
        forward = np.block([[cosine, -sine], [sine, cosine]])
        tables.append([split_numpy(forward), split_numpy(forward.T)])
    return np.array(tables, dtype=ml_dtypes.bfloat16)


def parity_order(length):
    half = length // 2
    order = np.zeros((length, length))
    for index in range(length):
        order[index, index % 2 * half + index // 2] = 1.0
    return np.stack([order, order.T]).astype(ml_dtypes.bfloat16)


def split(values):
    high = values.astype(jnp.bfloat16)
    low = (values - high.astype(jnp.float32)).astype(jnp.bfloat16)
    return high, low


def times_table(values, table):
    high, low = split(values)
    left = jnp.concatenate([high, low, high], axis=1)
    right = jnp.concatenate([table[0], table[0], table[1]], axis=0)
    return jnp.dot(left, right, preferred_element_type=jnp.float32)


def table_times(table, values):
    high, low = split(values)
    left = jnp.concatenate([table[0], table[0], table[1]], axis=1)
    right = jnp.concatenate([high, low, high], axis=0)
    return jnp.dot(left, right, preferred_element_type=jnp.float32)


class Plan:
    def __init__(self, sx_size, sy_size, block_rows, block_cols):
        self.rows = block_rows
        self.sx_size = sx_size
        self.sy_size = sy_size
        self.own = block_cols // LANES
        self.tiles = self.own + 2
        self.paired = sy_size == 2
        self.sides = 1 if self.paired else 2

    def rights(self, t):
        return [1 - t] if self.paired else [0, 1]

    def pair_starts(self, t):
        return [right * (self.tiles - 2) for right in self.rights(t)]

    def halo_tiles(self, t):
        return [right * (self.tiles - 1) for right in self.rights(t)]

    def edge_tiles(self, t):
        return [1 + right * (self.tiles - 3) for right in self.rights(t)]

    def first_parity(self, t):
        return 1 - t if self.paired else 0

    def mid_start(self, t):
        return 1 + t if self.paired else 2

    @property
    def mid_tiles(self):
        return self.tiles - 3 if self.paired else self.tiles - 4

    def across(self, values, axis_name="sy"):
        if self.paired:
            return [lax.ppermute(values[0], axis_name, [(0, 1), (1, 0)])]
        ends = self.sy_size - 1
        return [
            lax.ppermute(values[1], axis_name, [(i, i + 1) for i in range(ends)]),
            lax.ppermute(values[0], axis_name, [(i + 1, i) for i in range(ends)]),
        ]

    def far_rows(self, values):
        rows, columns = self.sx_size, self.sy_size
        pairs = [(i * columns + t, (i + 1) * columns + t) for i in range(1, rows - 1, 2) for t in range(columns)]
        for i in (0, rows - 1):
            pairs += [(i * columns + t, i * columns + t + 1) for t in range(0, columns - 1, 2)]
        return lax.ppermute(values, ("sx", "sy"), pairs + [(j, i) for i, j in pairs])

    def near_rows(self, values):
        return lax.ppermute(values, "sx", [(i, i ^ 1) for i in range(self.sx_size)])

    def outermost(self, s):
        return (s == 0) | (s == self.sx_size - 1)


def far_side(s):
    return 2 * (s % 2) - 1


def lanes(tile, count=1):
    if isinstance(tile, int):
        return pl.ds(tile * LANES, count * LANES)
    return pl.ds(pl.multiple_of(tile * LANES, LANES), count * LANES)


def pick_tile(plan, target, pieces, tile, t):
    rows = target.shape[1]
    if plan.paired:

        @pl.when(tile == (plan.tiles - 1) * t)
        def _():
            target[...] = jnp.zeros(target.shape, jnp.float32)

    for ref, offset, count, start in pieces:

        @pl.when((tile >= start) & (tile < start + count))
        def _(ref=ref, offset=offset, start=start):
            target[...] = ref[:, :rows, lanes(tile - start + offset)]


def lay_out(refs, starts):
    return [(ref, 0, ref.shape[2] // LANES, start) for ref, start in zip(refs, starts)]


def chunks(count):
    return [min(2, count - first) for first in range(0, count, 2)]


def chunk_starts(start, count):
    return [start + 2 * index for index in range(len(chunks(count)))]


def spread(source, targets):
    offset = 0
    for target in targets:
        columns = target.shape[2]
        target[...] = source[:, :, offset : offset + columns]
        offset += columns


def rows_at(ref, start, count):
    offset = start % 8
    values = ref[pl.ds(pl.multiple_of(start - offset, 8), count + 8)]
    return pltpu.roll(values, (count + 8 - offset) % (count + 8), 0)[:count]


def here():
    return lax.axis_index("sx"), lax.axis_index("sy")


def info_rows(centres, count):
    lane = lax.broadcasted_iota(jnp.int32, (8, LANES), 1)
    slots = centres.shape[0]
    values = [centres[slot, axis] for slot in range(slots) for axis in range(2)] + [count]
    line = jnp.zeros((8, LANES), jnp.int32)
    for index, value in enumerate(values):
        line = jnp.where(lane == index, value, line)
    return line.astype(jnp.float32)


def edge_message_kernel(plan, block, centres, counts, *rest):
    messages, sems = rest[: plan.sides], rest[plan.sides]
    s, t = here()
    half = block.shape[1]
    copies = [
        pltpu.make_async_copy(block.at[:, :, lanes(tile - 1)], message.at[:, :half], sems.at[side])
        for side, (message, tile) in enumerate(zip(messages, plan.edge_tiles(t)))
    ]
    for copy in copies:
        copy.start()
    rows = info_rows(centres, counts[s])
    for message in messages:
        message[0, half:] = rows
        message[1, half:] = rows
    for copy in copies:
        copy.wait()


def halo_message_kernel(plan, centres, counts, _, *rest):
    sides = plan.sides
    received, far, halos, infos = (rest[k * sides : (k + 1) * sides] for k in range(4))
    own = info_rows(centres, counts[lax.axis_index("sx")])
    rest[-1][...] = own
    upper_line = lax.broadcasted_iota(jnp.int32, own.shape, 0) == 0
    for source, message, halo, info in zip(received, far, halos, infos):
        rows = halo.shape[1]
        both = jnp.where(upper_line, own, pltpu.roll(source[0, rows : rows + 8], 1, 0))
        halo[...] = source[:, :rows]
        info[...] = both
        message[:, :rows] = source[:, :rows]
        message[0, rows:] = both
        message[1, rows:] = both


def pair_kernel(plan, base, early, inverse, middle, *rest):
    sides = plan.sides
    sums, received, results = (rest[k * sides : (k + 1) * sides] for k in range(3))
    near = rest[3 * sides :]
    _, t = here()
    for total, other, result, copy, start in zip(sums, received, results, near, plan.pair_starts(t)):
        where = lanes(start, 2)
        missing = total[...] + other[...] - early[:, :, where]
        values = base[:, :, where] - missing * inverse[:, where][None]
        result[...] = values
        copy[...] = values
    spread(middle, near[sides:])


def spot_kernel(spot, _, copy):
    copy[...] = spot[...]


def prepare_kernel(centres, probe, amps, order, rolled, ordered, padded):
    size = probe.shape[1]
    half = size // 2
    padded[:, :half] = jnp.zeros((2, half, size), jnp.float32)
    padded[:, half + size :] = jnp.zeros((2, half + 8, size), jnp.float32)
    padded[:, half : half + size] = probe[...]
    for slot in range(amps.shape[0]):
        row = centres[slot, 0]
        col = centres[slot, 1]
        for part in range(2):
            shape = padded.at[part]
            upper = rows_at(shape, half - row, half) + rows_at(shape, half + size - row, half)
            lower = rows_at(shape, size - row, half)
            rolled[slot, part] = pltpu.roll(jnp.concatenate([upper, lower], axis=0), col % LANES, 1)
        high, low = split(amps[slot])
        across = jnp.dot(
            jnp.concatenate([high, low], axis=1),
            jnp.concatenate([order[0], order[0]], axis=0),
            preferred_element_type=jnp.float32,
        )
        high, low = split(across)
        ordered[slot] = jnp.dot(
            jnp.concatenate([order[1], order[1]], axis=1),
            jnp.concatenate([high, low], axis=0),
            preferred_element_type=jnp.float32,
        )


def gather_info(plan, home, far, other, info, known, sem):
    s, _ = here()
    upper = s % 2 == 0
    width = plan.sides + 1

    def lines(messages):
        return [messages[0]] + [pltpu.roll(message, 7, 0) for message in messages]

    own = lines([line[...] for line in home])
    near = lines([line[...] for line in other])
    far = lines([jnp.where(plan.outermost(s), 0.0, message[0, plan.rows :]) for message in far])
    for turn in range(width):
        for kind, line in ((0, jnp.where(upper, far[turn], near[turn])), (1, own[turn]), (2, jnp.where(upper, near[turn], far[turn]))):
            known[kind * width + turn] = line.astype(jnp.int32)
    copy = pltpu.make_async_copy(known.at[:, 0], info, sem)
    copy.start()
    copy.wait()


def light_kernel(plan, slots, *rest):
    groups = [rest[k * plan.sides : (k + 1) * plan.sides] for k in range(3)]
    probe, _, inverse, info, padded, canvas, known, sem = rest[3 * plan.sides :]
    gather_info(plan, *groups, info, known, sem)
    size = probe.shape[1]
    half = size // 2
    _, t = here()
    padded[:half] = jnp.zeros((half, size), jnp.float32)
    padded[half + size :] = jnp.zeros((half + 8, size), jnp.float32)
    padded[half : half + size] = probe[0] * probe[0] + probe[1] * probe[1]
    canvas[...] = jnp.zeros(canvas.shape, jnp.float32)
    reach = plan.sides + 1
    spare = jnp.zeros((half, LANES), jnp.float32)
    for down in (-1, 0, 1):

        def add(step, carry, down=down):
            turn = step // slots
            slot = step % slots
            over = turn * (1 - 2 * t) if plan.paired else jnp.where(turn == 0, 0, 2 * turn - 3)
            index = (down + 1) * reach + turn

            @pl.when(slot < info[index, 2 * slots])
            def _():
                row = info[index, 2 * slot]
                col = info[index, 2 * slot + 1]
                power = rows_at(padded, size - half * down - row, half)
                shifted = pltpu.roll(jnp.concatenate([power, spare], axis=1), col % LANES, 1)
                first = col // LANES + plan.own * (over + 1)
                canvas[:, lanes(first, 3)] += shifted

            return carry

        lax.fori_loop(0, reach * slots, add, 0)
    inverse[...] = 1.0 / (canvas[:, lanes(plan.own, plan.tiles)] + DAMPING)


def term_kernel(plan, slot, layout, pieces, copied, halves, slots, spot, *rest):
    refs, rest = rest[:pieces], rest[pieces:]
    earlier, (probe, amps, tables, inner), rest = rest[:copied], rest[copied : copied + 4], rest[copied + 4 :]
    if halves:
        outer, rest = rest[-1], rest[:-1]
    else:
        outer, rest = rest[0], rest[1:]
    outer_halves, near_outers, picked = rest[:halves], rest[halves:-1], rest[-1]
    size = probe.shape[2]
    half = size // 2
    s, t = here()
    line = spot[0:1]
    lane = lax.broadcasted_iota(jnp.int32, line.shape, 1)
    entries = (2 * slot, 2 * slot + 1, 2 * slots)
    row, col, count = (jnp.sum(jnp.where(lane == k, line, 0.0)).astype(jnp.int32) for k in entries)
    alive = slot < count

    @pl.when(jnp.logical_not(alive))
    def _():
        outer[...] = jnp.zeros(outer.shape, jnp.float32)
        inner[...] = jnp.zeros(inner.shape, jnp.float32)

    @pl.when(alive)
    def _():
        tile = col // LANES
        first = tile % 2
        rest_col = col % LANES
        from_tile = lax.broadcasted_iota(jnp.int32, (half, LANES), 1) >= rest_col
        from_upper = lax.broadcasted_iota(jnp.int32, (half, LANES), 0) >= row
        side = far_side(s)
        own, far, near = layout(refs, t)
        for kind, source in ((1, own), (1 + side, far), (1 - side, near)):
            for step in range(3):
                pick_tile(plan, picked.at[kind, step], source, tile + step, t)

        @pl.when(plan.outermost(s))
        def _():
            picked[1 + side] = jnp.zeros(picked.shape[1:], jnp.float32)

        def edge(kind, part):
            return jnp.where(from_tile, picked[kind, 0, part], picked[kind, 2, part])

        def across(edges, middles, rows):
            sums, differences = [], []
            shares = []
            for columns, (real, imag) in ((slice(0, half), edges), (slice(half, size), middles)):
                probe_real, probe_imag = probe[slot, 0, rows, columns], probe[slot, 1, rows, columns]
                shares.append((probe_real * real - probe_imag * imag, probe_real * imag + probe_imag * real))
            for part in range(2):
                sums.append(shares[0][part] + shares[1][part])
                differences.append(shares[0][part] - shares[1][part])
            return [
                times_table(jnp.concatenate(parts, axis=1), tables[parity, 0])
                for parity, parts in enumerate((sums, differences))
            ]

        lower = across(
            [edge(1, part) for part in range(2)], [picked[1, 1, part] for part in range(2)], slice(half, size)
        )
        upper = across(
            [jnp.where(from_upper, edge(0, part), edge(2, part)) for part in range(2)],
            [jnp.where(from_upper, picked[0, 1, part], picked[2, 1, part]) for part in range(2)],
            slice(0, half),
        )
        halves = []
        for sign in (1.0, -1.0):
            rows = [top + sign * bottom for top, bottom in zip(upper, lower)]
            halves.append(
                jnp.concatenate(
                    [jnp.concatenate([row[:, part] for row in rows], axis=1) for part in (slice(0, half), slice(half, size))],
                    axis=0,
                )
            )
        back = []
        for parity in range(2):
            pattern = table_times(tables[parity, 1], halves[parity])
            far_real = pattern[:half]
            far_imag = pattern[half:]
            amplitude = amps[slot, parity * half : (parity + 1) * half]
            factor = 1.0 - amplitude * lax.rsqrt(far_real * far_real + far_imag * far_imag + SMOOTH)
            miss = jnp.concatenate([far_real * factor, far_imag * factor], axis=0)
            back.append(table_times(tables[parity, 0], miss))
        real = jnp.concatenate([back[0][:half] + back[1][:half], back[0][:half] - back[1][:half]], axis=0)
        imag = jnp.concatenate([back[0][half:] + back[1][half:], back[0][half:] - back[1][half:]], axis=0)
        both = []
        for parity in range(2):
            columns = slice(parity * half, (parity + 1) * half)
            both.append(times_table(jnp.concatenate([real[:, columns], imag[:, columns]], axis=1), tables[parity, 1]))
        near_real = jnp.concatenate([both[0][:, :half] + both[1][:, :half], both[0][:, :half] - both[1][:, :half]], axis=1)
        near_imag = jnp.concatenate([both[0][:, half:] + both[1][:, half:], both[0][:, half:] - both[1][:, half:]], axis=1)
        probe_real = probe[slot, 0]
        probe_imag = probe[slot, 1]
        for part, term in enumerate((probe_real * near_real + probe_imag * near_imag, probe_real * near_imag - probe_imag * near_real)):
            for place, columns in ((first, slice(0, half)), (1 - first, slice(half, size))):
                outer[part, :, lanes(place)] = term[:half, columns]
                inner[part, :, lanes(place)] = term[half:, columns]

    for index, target in enumerate(outer_halves):
        first = plan.first_parity(t)
        target[...] = outer[:, :, lanes(first if index == 0 else 1 - first)]
    for index, source in enumerate((*earlier, outer)):
        line = 0
        for target in near_outers:
            rows = target.shape[1]
            target[2 * index : 2 * index + 2] = source[:, line : line + rows]
            line += rows


class Patch:
    def __init__(self, plan, info, s, patch, slot, down, far=False):
        runs = patch if isinstance(patch, (list, tuple)) else [patch]
        half = sum(run.shape[1] for run in runs)
        index = (1 if down is None else 1 + down) * (plan.sides + 1)
        row = info[index, 2 * slot]
        col = info[index, 2 * slot + 1]
        self.runs = runs
        self.tile = col // LANES
        self.first = self.tile % 2
        self.rest = col % LANES
        self.lane = lax.broadcasted_iota(jnp.int32, (half, LANES), 1)
        self.from_tile = self.lane >= self.rest
        self.rows = None
        if down is not None:
            line = lax.broadcasted_iota(jnp.int32, (half, LANES), 0)
            after = jnp.where(down > 0, half, row)
            if far:
                after = jnp.where(plan.outermost(s), 0, after)
            self.rows = (line >= jnp.where(down > 0, row, 0)) & (line < after)

    def lines(self, part, place):
        values = jnp.concatenate([run[part, :, lanes(place)] for run in self.runs], axis=0)
        return values if self.rows is None else jnp.where(self.rows, values, 0.0)

    def tiles(self, part):
        edge = self.lines(part, self.first)
        middle = self.lines(part, 1 - self.first)
        return jnp.where(self.from_tile, edge, 0.0), middle, jnp.where(self.from_tile, 0.0, edge)

    def add_to(self, canvas):
        for part in range(2):
            for step, values in enumerate(self.tiles(part)):
                canvas[part, :, lanes(self.tile + step)] += values

    def mask(self, tile):
        step = tile - self.tile
        first = jnp.where(step == 0, self.rest, 0)
        after = jnp.where(step == 2, self.rest, jnp.where((step < 0) | (step > 2), 0, LANES))
        inside = (self.lane >= first) & (self.lane < after)
        if self.rows is not None:
            inside = inside & self.rows
        return jnp.where(inside, 1.0, 0.0)


def part_of(plan, patch, mask, part, tile):
    if isinstance(patch, (list, tuple)):
        first = plan.first_parity(lax.axis_index("sy"))
        values = jnp.where(tile % 2 == first, patch[0][part], patch[1][part])
    else:
        values = patch[part, :, lanes(tile % 2)]
    return values * mask[:, lanes(tile)]


def early_sum_kernel(plan, slots, info, *rest):
    inner, near, canvas = rest[:slots], rest[slots:-1], rest[-1]
    s, _ = here()
    canvas[...] = jnp.zeros(canvas.shape, jnp.float32)
    for slot in range(slots):
        Patch(plan, info, s, inner[slot], slot, None).add_to(canvas)
        runs = [run.at[2 * slot : 2 * slot + 2] for run in near]
        Patch(plan, info, s, runs, slot, -far_side(s)).add_to(canvas)


def base_kernel(plan, slots, layout, pieces, info, early, inverse, *rest):
    far, refs, (canvas, base, mask) = rest[: slots - 1], rest[slots - 1 : slots - 1 + pieces], rest[slots - 1 + pieces :]
    s, t = here()
    canvas[...] = early[...]
    for slot in range(slots - 1):
        Patch(plan, info, s, far[slot], slot, far_side(s), True).add_to(canvas)
    last = Patch(plan, info, s, canvas, slots - 1, far_side(s), True)
    for tile in range(plan.tiles):
        where = lanes(tile)
        pick_tile(plan, base.at[:, :, where], layout(refs, t)[0], tile, t)
        base[:, :, where] -= canvas[:, :, where] * inverse[:, where][None]
        mask[:, where] = last.mask(tile)


def take_off(plan, patch, mask, target, base, inverse, tile):
    for part in range(2):
        target[part] = base[part, :, lanes(tile)] - part_of(plan, patch, mask, part, tile) * inverse[:, lanes(tile)]


def middle_kernel(plan, base, patch, mask, inverse, _, middle):
    _, t = here()
    for step in range(plan.mid_tiles):
        take_off(plan, patch, mask, middle.at[:, :, lanes(step)], base, inverse, plan.mid_start(t) + step)


def boundary_kernel(plan, early, patch, mask, *sums):
    _, t = here()
    for total, start in zip(sums, plan.pair_starts(t)):
        for step in range(2):
            tile = start + step
            for part in range(2):
                total[part, :, lanes(step)] = early[part, :, lanes(tile)] + part_of(plan, patch, mask, part, tile)


def halo_sum_kernel(plan, early, mask, *rest):
    halves, sums = rest[: plan.sides], rest[plan.sides :]
    _, t = here()
    for half, total, tile in zip(halves, sums, plan.halo_tiles(t)):
        for part in range(2):
            total[part] = early[part, :, lanes(tile)] + half[part] * mask[:, lanes(tile)]


def last_kernel(plan, base, mask, inverse, _, first, second, *rest):
    nearly, bases, (current, sems) = rest[0], rest[1 : 1 + plan.sides], rest[1 + plan.sides :]
    patch = [first, second]
    _, t = here()
    copies = []
    for step in range(plan.own):
        where = lanes(step)
        take_off(plan, patch, mask, current.at[:, :, where], base, inverse, 1 + step)
        copies.append(pltpu.make_async_copy(current.at[:, :, where], nearly.at[:, :, where], sems.at[step]))
        copies[-1].start()
    for edge, tile in zip(bases, plan.edge_tiles(t)):
        edge[...] = current[:, :, lanes(tile - 1)]
    for copy in copies:
        copy.wait()


def edge_kernel(plan, inverse, *rest):
    bases, received = rest[: plan.sides], rest[plan.sides : 2 * plan.sides]
    _, result, sums, sems = rest[2 * plan.sides :]
    _, t = here()
    copies = []
    for side, tile in enumerate(plan.edge_tiles(t)):
        sums[side] = bases[side][...] - received[side][...] * inverse[:, lanes(tile)][None]
        copies.append(pltpu.make_async_copy(sums.at[side], result.at[:, :, lanes(tile - 1)], sems.at[side]))
        copies[-1].start()
    for copy in copies:
        copy.wait()


def call(kernel, outs, scratch, ins, flops=10**5, size=10**4, in_specs=None, out_specs=None, **options):
    result = pl.pallas_call(
        kernel,
        out_shape=outs,
        in_specs=in_specs or [SMEM if value.dtype == jnp.int32 else VMEM for value in ins],
        out_specs=out_specs or jax.tree.map(lambda _: VMEM, outs),
        scratch_shapes=scratch,
        compiler_params=pltpu.CompilerParams(vmem_limit_bytes=VMEM_BYTES),
        cost_estimate=pl.CostEstimate(flops=flops, bytes_accessed=size, transcendentals=0),
        **options,
    )(*ins)
    return list(result) if isinstance(outs, list) else result


def on_device(plan, object_field, probe_field, amplitudes, centres, counts):
    f32 = jnp.float32
    shape = jax.ShapeDtypeStruct
    size = probe_field.shape[1]
    half = size // 2
    slots = amplitudes.shape[2]
    block_rows = object_field.shape[1]
    block_cols = object_field.shape[2]
    assert block_rows == half and block_cols % (2 * LANES) == 0 and half == LANES
    width = plan.tiles * LANES
    sides = plan.sides
    spots = centres[0, 0]
    counts = counts.reshape(-1)
    own_amps = amplitudes[0, 0]
    tables = jnp.asarray(dft_tables(size))
    order = jnp.asarray(parity_order(size))
    dma = pltpu.SemaphoreType.DMA

    messages = call(
        lambda *refs: edge_message_kernel(plan, *refs),
        [shape((2, half + 8, LANES), f32)] * sides,
        [dma((sides,))],
        [object_field, spots, counts],
        in_specs=[HBM, SMEM, SMEM],
    )
    halos = plan.across(messages)
    far_block = plan.far_rows(object_field)
    near_block = plan.near_rows(object_field)
    rolled, ordered = call(
        prepare_kernel,
        [shape((slots, 2, size, size), f32), shape((slots, size, size), f32)],
        [pltpu.VMEM((2, 2 * size + 8, size), f32)],
        [spots, probe_field, own_amps, order],
    )
    messages = call(
        lambda *refs: halo_message_kernel(plan, *refs),
        [shape((2, half + 8, LANES), f32)] * sides
        + [shape((2, half, LANES), f32)] * sides
        + [shape((8, LANES), f32)] * (sides + 1),
        [],
        [spots, counts, ordered, *halos],
        in_specs=[SMEM, SMEM, ANY] + [VMEM] * sides,
    )
    passed, lines, own_spot = messages[sides : 2 * sides], messages[2 * sides : -1], messages[-1]
    near_lines = [plan.near_rows(line) for line in lines]
    own_spot = call(spot_kernel, shape(own_spot.shape, f32), [], [own_spot, near_lines[0]], in_specs=[VMEM, ANY])
    far = [far_block] + [plan.far_rows(message) for message in messages[:sides]]
    near = [plan.near_rows(message) for message in passed] + [near_block]
    own = [object_field] + passed
    def runs_layout(refs, main, count, side_starts):
        starts = [main] + side_starts
        own, far, near = refs[: 1 + sides], refs[1 + sides : 2 + 2 * sides], refs[2 + 2 * sides :]
        return lay_out(own, starts), lay_out(far, starts), lay_out(near, side_starts + (chunk_starts(main, count) if len(near) > 1 + sides else [main]))

    def first_layout(refs, t):
        return runs_layout(refs, 1, plan.own, plan.halo_tiles(t))

    def later_layout(refs, t):
        return runs_layout(refs, plan.mid_start(t), plan.mid_tiles, plan.pair_starts(t))

    layout = first_layout

    third = half // 24 * 8
    near_heights = [half - 2 * third, third, third]
    for sweep in range(ITERS):
        pieces = own + far + near
        inner, outer, outer_far = [], [], []
        for slot in range(slots):
            last = slot == slots - 1
            earlier = outer if last else []
            patch = shape((2, half, size), f32)
            halves = 2 if last and sweep == ITERS - 1 else 0
            inner_part, *copies = call(
                lambda *refs, slot=slot, layout=layout, copied=len(earlier), halves=halves: term_kernel(
                    plan, slot, layout, len(pieces), copied, halves, slots, *refs
                ),
                [patch]
                + ([shape((2, half, LANES), f32)] * halves or [patch])
                + [shape((2 * slots, rows, size), f32) for rows in near_heights if last],
                [pltpu.VMEM((3, 3, 2, half, LANES), f32)]
                + [pltpu.VMEM((2, half, size), f32)] * (halves > 0),
                [own_spot, *pieces, *earlier, rolled, ordered, tables],
            )
            outer_part = None if halves else copies.pop(0)
            outer_halves, copies = copies[:halves], copies[halves:]
            inner.append(inner_part)
            outer.append(outer_part)
            outer_far.append([plan.far_rows(part) for part in outer_halves] if halves else plan.far_rows(outer_part))
        outer_near = [plan.near_rows(copy) for copy in copies]
        if sweep == 0:
            inverse, info = call(
                lambda *refs: light_kernel(plan, slots, *refs),
                [shape((half, width), f32), shape((3 * (sides + 1), LANES), jnp.int32)],
                [
                    pltpu.VMEM((2 * size + 8, size), f32),
                    pltpu.VMEM((half, width + 2 * plan.own * LANES), f32),
                    pltpu.VMEM((3 * (sides + 1), 8, LANES), jnp.int32),
                    dma,
                ],
                lines + far[1:] + near_lines + [probe_field, copies[0]],
                in_specs=[VMEM] * (3 * sides + 1) + [ANY],
                out_specs=[VMEM, SMEM],
            )
        early = call(
            lambda *refs: early_sum_kernel(plan, slots, *refs),
            shape((2, half, width), f32),
            [],
            [info, *inner, *outer_near],
        )
        early, base, mask = call(
            lambda *refs, layout=layout: base_kernel(plan, slots, layout, len(pieces), *refs),
            [shape((2, half, width), f32)] * 2 + [shape((half, width), f32)],
            [],
            [info, early, inverse, *outer_far[:-1], *pieces],
        )
        if sweep < ITERS - 1:
            sums = call(
                lambda *refs: boundary_kernel(plan, *refs),
                [shape((2, half, 2 * LANES), f32)] * sides,
                [],
                [early, outer_far[-1], mask],
            )
            received = plan.across(sums)
            middle = call(
                lambda *refs: middle_kernel(plan, *refs),
                shape((2, half, plan.mid_tiles * LANES), f32),
                [],
                [base, outer_far[-1], mask, inverse, sums[0]],
                in_specs=[VMEM] * 4 + [ANY],
            )
            far_middle = plan.far_rows(middle)
            near_runs = [shape((2, half, count * LANES), f32) for count in chunks(plan.mid_tiles)]
            updated = call(
                lambda *refs: pair_kernel(plan, *refs),
                [shape((2, half, 2 * LANES), f32)] * (2 * sides) + near_runs,
                [],
                [base, early, inverse, middle, *sums, *received],
            )
            pairs = updated[:sides]
            own = [middle] + pairs
            far = [far_middle] + [plan.far_rows(piece) for piece in pairs]
            near = [plan.near_rows(piece) for piece in updated[sides:]]
            layout = later_layout
    sums = call(
        lambda *refs: halo_sum_kernel(plan, *refs),
        [shape((2, half, LANES), f32)] * sides,
        [],
        [early, mask, *outer_far[-1][:sides]],
    )
    nearly, *bases = call(
        lambda *refs: last_kernel(plan, *refs),
        [shape((2, half, block_cols), f32)] + [shape((2, half, LANES), f32)] * sides,
        [pltpu.VMEM((2, half, block_cols), f32), dma((plan.own,))],
        [base, mask, inverse, sums[0], *outer_far[-1]],
        in_specs=[VMEM] * 3 + [ANY] + [VMEM] * 2,
        out_specs=[HBM] + [VMEM] * sides,
    )
    received = plan.across(sums)
    return call(
        lambda *refs: edge_kernel(plan, *refs),
        shape(nearly.shape, f32),
        [pltpu.VMEM((sides, 2, half, LANES), f32), dma((sides,))],
        [inverse, *bases, *received, nearly],
        in_specs=[VMEM] * (1 + 2 * sides) + [HBM],
        out_specs=HBM,
        input_output_aliases={1 + 2 * sides: 0},
    )


def solution(mesh):
    sizes = dict(mesh.shape)

    def per_device(object_field, *rest):
        plan = Plan(sizes["sx"], sizes["sy"], *object_field.shape[1:])
        return on_device(plan, object_field, *rest)

    return jax.shard_map(
        per_device,
        mesh=mesh,
        in_specs=(
            P(None, "sx", "sy"),
            P(),
            P("sx", "sy", None, None, None),
            P("sx", "sy", None, None),
            P(None, "sy"),
        ),
        out_specs=P(None, "sx", "sy"),
        check_vma=False,
    )
```
